32 devices in a mesh: expert: 8 (over z, core), seq: 4 (over y, x).
Axes of the slice: x: 2, y: 2, z: 4, core: 2. Of those that a mesh axis runs over, the one named last changes fastest.
Arguments:
- tokens: bfloat16 [8192, 1024], P(('expert', 'seq')), may hold values from -45 to 45
- cotangent: bfloat16 [8192, 1024], P(('expert', 'seq')), may hold values from -6 to 6
- expert_ids: int32 [8192, 2], P(('expert', 'seq')), may hold values from 0 to 7, all different within a row; in each aligned block of 256 rows (0 to 255, 256 to 511, ...) at most 160 rows name the same one
- segment_lengths: int32 [8, 13], P('expert'), may hold values from 1 to 409, 1024 in all within a row
- segment_parents: int32 [8, 13], P('expert'), may hold values from 0 to 11, as said below
- attention_gain: bfloat16 [1024], P(('expert', 'seq')), may hold values from 0.5 to 1.5
- query_weight: bfloat16 [1024, 1024], P(('expert', 'seq')), may hold values from -0.1875 to 0.1875
- key_weight: bfloat16 [1024, 1024], P(('expert', 'seq')), may hold values from -0.1875 to 0.1875
- value_weight: bfloat16 [1024, 1024], P(('expert', 'seq')), may hold values from -0.1875 to 0.1875
- output_weight: bfloat16 [1024, 1024], P(('expert', 'seq')), may hold values from -0.75 to 0.75
- bias_table: bfloat16 [512], P(('expert', 'seq')), may hold values from -4 to 4
- feedforward_gain: bfloat16 [1024], P(('expert', 'seq')), may hold values from 0.5 to 1.5
- router_weight: bfloat16 [1024, 8], P(('expert', 'seq')), may hold values from -0.1875 to 0.1875
- gate_weight: bfloat16 [8, 2816, 1024], P('expert', 'seq'), may hold values from -0.1875 to 0.1875
- up_weight: bfloat16 [8, 2816, 1024], P('expert', 'seq'), may hold values from -0.1875 to 0.1875
- down_weight: bfloat16 [8, 2816, 1024], P('expert', 'seq'), may hold values from -0.21875 to 0.21875
Outputs:
- layer_out: bfloat16 [8192, 1024], P(('expert', 'seq'))
- tokens_grad: float32 [8192, 1024], P(('expert', 'seq'))
- attention_gain_grad: float32 [1024], P(('expert', 'seq'))
- query_grad: float32 [1024, 1024], P(('expert', 'seq'))
- key_grad: float32 [1024, 1024], P(('expert', 'seq'))
- value_grad: float32 [1024, 1024], P(('expert', 'seq'))
- output_grad: float32 [1024, 1024], P(('expert', 'seq'))
- bias_table_grad: float32 [512], P(('expert', 'seq'))
- feedforward_gain_grad: float32 [1024], P(('expert', 'seq'))
- router_grad: float32 [1024, 8], P(('expert', 'seq'))
- gate_grad: float32 [8, 2816, 1024], P('expert', 'seq')
- up_grad: float32 [8, 2816, 1024], P('expert', 'seq')
- down_grad: float32 [8, 2816, 1024], P('expert', 'seq')
- root_mean_squares: float32 [2], replicated
The draws below stay inside these ranges and needn't reach their ends.
Inputs may be any that keep to these rules, and one draw needn't show every extreme that they name: `expert_ids`: the two ids of a token differ. In the rows of one device no expert is named more than 2 * 80 times. `segment_lengths`: each tree's lengths sum to 1024. `segment_parents`: segment 0 is the root and its own parent; every other segment has a parent with a lower number; the last segment's parent is the one before it.
All inputs are finite; a program needn't handle non-finite values.
Results may differ from the reference program's by a relative error of at most 0.025.
Values may be sent and summed in bfloat16 or wider, within the bound.
A program may use at most 256 MiB of HBM per device.

```python
import math
import jax
import jax.numpy as jnp
import numpy as np
from jax import lax

D = 1024
HEADS = 16
HDIM = 64
FF = 2816
BUCKETS = 32
MAXDIST = 128
SEGS = 13
EXPERTS = 8
TREE = 1024
ROWS = 256
TREES = 8
TOKENS = 8192
CAP = 80


def draw_tokens(key, part):
    key = jax.random.fold_in(key, 11)
    base_key, column_key = jax.random.split(key, 2)
    rising = 1.0 + 2.0 * jnp.arange(TOKENS, dtype=jnp.float32)[:, None] / (TOKENS - 1)
    column = jnp.exp(jax.random.uniform(column_key, (1, D), jnp.float32, math.log(0.3), math.log(3.0)))
    base_draw = jnp.clip(jax.random.normal(base_key, (TOKENS, D), jnp.float32), -5.0, 5.0)
    return (base_draw * rising * column).astype(jnp.bfloat16)


def draw_segment_parents(key, part):
    key = jax.random.fold_in(key, 23)
    ordinal = jnp.arange(SEGS, dtype=jnp.int32)
    raw_picks = jax.random.randint(key, (TREES, SEGS), 0, 1 << 20)
    parents = (raw_picks % jnp.maximum(ordinal, 1)[None, :]).astype(jnp.int32)
    parents = jnp.where(ordinal[None, :] == SEGS - 1, SEGS - 2, parents)
    return parents.astype(jnp.int32)


def steps_of(key, dims, cuts, smallest, largest):
    factor_of = 1.0
    for dim, shards_of in cuts:
        steps = jax.random.uniform(jax.random.fold_in(jax.random.fold_in(key, 6), dim), (shards_of,), jnp.float32, smallest / len(cuts), largest / len(cuts))
        factor_of = factor_of * jnp.repeat(jnp.exp(steps), dims[dim] // shards_of).reshape((-1,) + (1,) * (len(dims) - 1 - dim))
    return factor_of


def split_up(count, total, limit, skew):
    loads = [(1 << 20) // math.isqrt(rank ** skew) + 1 for rank in range(2, count + 1)]
    rest, given = total - limit - (count - 1), [1] * (count - 1)
    while rest > 0:
        movable = [i for i in range(count - 1) if given[i] < limit]
        mass, left = sum([loads[i] for i in movable]), rest
        for i in movable:
            more = min(limit - given[i], max(1, left * loads[i] // mass), rest)
            given[i] = given[i] + more
            rest = rest - more
    return np.array([limit] + given)


def ragged_sizes(own_key, number_of, total, limit, slope):
    if number_of == 2:
        one = jax.random.randint(own_key, (), max(1, total - limit), min(limit, total - 1) + 1)
        return jnp.stack([one, total - one])
    sizes = jnp.asarray(split_up(number_of, total, limit, slope), jnp.int32)
    twos = (number_of - 1) // 2
    giver, taker = sizes[1:1 + 2 * twos:2], sizes[2:2 + 2 * twos:2]
    slack = jnp.minimum(giver - 1, limit - taker)
    shifted = jax.random.randint(jax.random.fold_in(own_key, 1), (twos,), 0, 1 << 20) % (slack + 1)
    sizes = sizes.at[1:1 + 2 * twos:2].set(giver - shifted).at[2:2 + 2 * twos:2].set(taker + shifted)
    return sizes[jax.random.permutation(jax.random.fold_in(own_key, 2), number_of)]


def routed_block(rng, own, number, rows, amount, top, reach, skew):
    sequence = jax.random.permutation(rng, amount)
    heavy_load, ordinary = load_shares(amount, rows * top, reach, skew, True), load_shares(amount, rows * top, reach, skew, False)
    places = jnp.arange(amount)

    def named(sizes, turn):
        used = int((sizes > 0).sum())
        fixed = max(1, used // 4)
        shifted = fixed + (places - fixed + turn * (used - fixed)) % max(1, amount - fixed)
        return jnp.zeros((amount,), jnp.int32).at[sequence[jnp.where(places < fixed, places, shifted)]].set(jnp.asarray(sizes, jnp.int32))

    sizes = jnp.where(number % 4 == 0, named(heavy_load, number // 4), named(ordinary, number - number // 4 - 1))
    mixed = jax.random.permutation(jax.random.fold_in(own, 3), amount)
    donor, receiver = mixed[0:amount // 2 * 2:2], mixed[1:amount // 2 * 2:2]
    slack = jnp.minimum(sizes[donor] - 1, reach - sizes[receiver]) // 2
    slack = jnp.where((donor == sequence[0]) | (receiver == sequence[0]) | (sizes[receiver] == 0), 0, jnp.maximum(slack, 0))
    shifted = jax.random.randint(jax.random.fold_in(own, 4), (amount // 2,), 0, 1 << 20) % (slack + 1)
    sizes = sizes.at[donor].add(-shifted).at[receiver].add(shifted)
    members = jnp.searchsorted(jnp.cumsum(sizes), jnp.arange(rows * top), side="right").astype(jnp.int32)
    grid = members.reshape(top, rows).T
    grid = grid[jax.random.permutation(jax.random.fold_in(own, 1), rows)]
    turn = jax.random.randint(jax.random.fold_in(own, 2), (rows, 1), 0, top)
    return jnp.take_along_axis(grid, (jnp.arange(top)[None, :] + turn) % top, axis=1)


def load_shares(amount, total, reach, skew, full):
    loads = [(1 << 20) // math.isqrt(grade ** skew) + 1 for grade in range(1, amount + 1)]
    largest = reach if full else min(reach, max(-(-total // amount), total * loads[0] // sum(loads)))
    least = 1 if total - largest >= amount - 1 else 0
    counts, spare = [largest] + [least] * (amount - 1), total - largest - least * (amount - 1)
    while spare > 0:
        candidates = [i for i in range(1, amount) if counts[i] < largest] or [i for i in range(1, amount) if counts[i] < reach]
        pool, remaining = sum([loads[i] for i in candidates]), spare
        for i in candidates:
            addition = min(reach - counts[i], max(1, remaining * loads[i] // pool), spare)
            counts[i] = counts[i] + addition
            spare = spare - addition
    return np.array(counts)


def centred(key, dims, spread, limit, shards=(), kind=jnp.bfloat16):
    level = steps_of(key, dims, shards, -0.22, 0.18) if shards else 1.0
    array = jax.random.normal(key, dims, jnp.float32) * spread * level
    return jnp.minimum(jnp.maximum(array, -limit), limit).astype(kind)


def setup_inputs(seed: int = 0) -> dict:
    keys = jax.random.split(jax.random.key(seed), 17)
    tokens = draw_tokens(jax.random.fold_in(keys[16], 71), 0)
    cotangent = centred(keys[1], (TOKENS, D), 1.0, 6.0, ((0, 32),))
    expert_ids_keys = jax.random.split(jax.random.fold_in(keys[2], 1), TOKENS // ROWS)
    expert_ids_turns = jax.random.permutation(jax.random.fold_in(keys[2], 3), TOKENS // ROWS)
    expert_ids = jax.vmap(lambda own, number: routed_block(jax.random.fold_in(keys[2], 2), own, number, ROWS, EXPERTS, 2, 2 * CAP, 1))(expert_ids_keys, expert_ids_turns).reshape((TOKENS, 2))
    segment_lengths = jax.vmap(lambda own: ragged_sizes(own, SEGS, TREE, 2 * TREE // 5, 2))(jax.random.split(keys[3], TREES)).reshape((TREES, SEGS)).astype(jnp.int32)
    segment_parents = draw_segment_parents(jax.random.fold_in(keys[16], 71), 0)
    attention_gain = jnp.clip(1.0 + 0.1 * jax.random.normal(keys[5], (D,), jnp.float32), 0.5, 1.5).astype(jnp.bfloat16)
    query_weight = centred(keys[6], (D, D), D ** -0.5, 0.1875, ((0, 32),))
    key_weight = centred(keys[7], (D, D), D ** -0.5, 0.1875, ((0, 32),))
    value_weight = centred(keys[8], (D, D), D ** -0.5, 0.1875, ((0, 32),))
    output_weight = centred(keys[9], (D, D), (D // 16) ** -0.5, 0.75, ((0, 32),))
    bias_table = centred(keys[10], (BUCKETS * HEADS,), 1.0, 4.0, ((0, 32),))
    feedforward_gain = jnp.clip(1.0 + 0.1 * jax.random.normal(keys[11], (D,), jnp.float32), 0.5, 1.5).astype(jnp.bfloat16)
    router_weight = centred(keys[12], (D, EXPERTS), D ** -0.5, 0.1875, ((0, 32),))
    gate_weight = centred(keys[13], (EXPERTS, FF, D), D ** -0.5, 0.1875, ((0, 8), (1, 4)))
    up_weight = centred(keys[14], (EXPERTS, FF, D), D ** -0.5, 0.1875, ((0, 8), (1, 4)))
    down_weight = centred(keys[15], (EXPERTS, FF, D), (FF // 4) ** -0.5, 0.21875, ((0, 8), (1, 4)))
    return {"tokens": tokens, "cotangent": cotangent, "expert_ids": expert_ids, "segment_lengths": segment_lengths, "segment_parents": segment_parents, "attention_gain": attention_gain, "query_weight": query_weight, "key_weight": key_weight, "value_weight": value_weight, "output_weight": output_weight, "bias_table": bias_table, "feedforward_gain": feedforward_gain, "router_weight": router_weight, "gate_weight": gate_weight, "up_weight": up_weight, "down_weight": down_weight}


@jax.custom_vjp
def low(v):
    return lax.optimization_barrier(v.astype(jnp.bfloat16)).astype(jnp.float32)

@jax.custom_vjp
def low_back(v):
    return v

def low_keep(v):
    return (low(v), None)

def low_pass(kept, grad):
    return (grad,)

def back_keep(v):
    return (v, None)

def back_low(kept, grad):
    return (low(grad),)
low.defvjp(low_keep, low_pass)
low_back.defvjp(back_keep, back_low)
EPSILON = 1e-06
NEGATIVE = -1e+30

def matmul_high(left, right):
    return jnp.dot(left, right, preferred_element_type=jnp.float32, precision=lax.Precision.HIGHEST)

def root_norm(values, gain):
    return values * lax.rsqrt(lax.optimization_barrier(jnp.mean(values * values, axis=-1, keepdims=True)) + EPSILON) * gain

def bucket_of(distance):
    exact_span = BUCKETS // 2
    above = jnp.zeros(distance.shape, jnp.int32)
    for number in range(exact_span):
        threshold = int(math.ceil(exact_span * (MAXDIST / exact_span) ** (number / exact_span)))
        above = above + (distance >= threshold).astype(jnp.int32)
    return jnp.where(distance < exact_span, distance, exact_span - 1 + above).astype(jnp.int32)

def tree_tables(lengths, parents):
    ordinal = jnp.arange(lengths.shape[0], dtype=jnp.int32)
    starts = (jnp.cumsum(lengths) - lengths).astype(jnp.int32)

    def chase(number, running):
        current, reaches = running
        current = lax.optimization_barrier(jnp.sum(jnp.where(current[:, None] == ordinal[None, :], parents[None, :], 0), axis=1)).astype(jnp.int32)
        reaches = jnp.maximum(reaches, (current[:, None] == ordinal[None, :]).astype(jnp.int32))
        return (current, reaches)
    begin = (ordinal, (ordinal[:, None] == ordinal[None, :]).astype(jnp.int32))
    unused, reaches = lax.fori_loop(0, lengths.shape[0], chase, begin)
    before = (lax.optimization_barrier(jnp.sum(reaches * lengths[None, :], axis=1)) - lengths).astype(jnp.int32)
    return (starts, before, reaches)

def token_info(token_rows, starts, before, reaches):
    ordinal = jnp.arange(starts.shape[0], dtype=jnp.int32)
    segment = lax.optimization_barrier(jnp.sum((token_rows[:, None] >= starts[None, :]).astype(jnp.int32), axis=1)) - 1
    member = segment[:, None] == ordinal[None, :]
    position = (token_rows + lax.optimization_barrier(jnp.sum(jnp.where(member, (before - starts)[None, :], 0), axis=1))).astype(jnp.int32)
    lineage = lax.optimization_barrier(jnp.sum(jnp.where(member[:, :, None], reaches[None, :, :], 0), axis=1)).astype(jnp.int32)
    return (member, position, lineage)

def tree_attention(queries, key_tree, value_tree, bias_grid, starts, before, reaches):
    tree_len = queries.shape[0]
    block_rows = math.gcd(tree_len, 512)
    key_rows = jnp.arange(tree_len, dtype=jnp.int32)
    key_member, key_position, unused = token_info(key_rows, starts, before, reaches)
    key_hot = key_member.astype(jnp.float32)

    def one_block(block_number):
        first_row = (block_number * block_rows).astype(jnp.int32)
        query_rows = first_row + jnp.arange(block_rows, dtype=jnp.int32)
        query_block = lax.dynamic_slice_in_dim(queries, first_row, block_rows, 0)
        unused_member, query_position, lineage = token_info(query_rows, starts, before, reaches)
        visible = matmul_high(lineage.astype(jnp.float32), key_hot.T) > 0.5
        visible = visible & (key_rows[None, :] <= query_rows[:, None])
        distance = jnp.maximum(query_position[:, None] - key_position[None, :], 0)
        pair_bias = jnp.transpose(jnp.take(bias_grid, bucket_of(distance), axis=0), (2, 0, 1))
        scores = jnp.einsum('qhd,khd->hqk', query_block, key_tree, precision=lax.Precision.HIGHEST) * HDIM ** (-0.5) + pair_bias
        scores = jnp.where(visible[None], low_back(scores), NEGATIVE)
        soft_weights = low(jax.nn.softmax(scores, axis=-1))
        return jnp.einsum('hqk,khd->qhd', soft_weights, value_tree, precision=lax.Precision.HIGHEST)
    blocks = lax.map(jax.checkpoint(one_block), jnp.arange(tree_len // block_rows, dtype=jnp.int32))
    return blocks.reshape(tree_len, queries.shape[1], queries.shape[2])

def reference(tokens, cotangent, expert_ids, segment_lengths, segment_parents, attention_gain, query_weight, key_weight, value_weight, output_weight, bias_table, feedforward_gain, router_weight, gate_weight, up_weight, down_weight):
    starts, before, reaches = jax.vmap(tree_tables)(segment_lengths, segment_parents)
    devices = TOKENS // ROWS
    expert_range = jnp.arange(EXPERTS, dtype=jnp.int32)
    hot_int = (expert_ids[:, :, None] == expert_range[None, None, :]).astype(jnp.int32)
    per_device = hot_int.reshape(devices, ROWS * 2, EXPERTS)
    earlier = (jnp.cumsum(per_device, axis=1) - per_device).astype(jnp.int32)
    slot_number = lax.optimization_barrier(jnp.sum(earlier * per_device, axis=2)).astype(jnp.int32).reshape(TOKENS, 2)
    kept_copy = slot_number < CAP
    buffer_rows = devices * CAP
    owner = (jnp.arange(TOKENS, dtype=jnp.int32) // ROWS)[:, None]
    target = jnp.where(kept_copy, expert_ids * buffer_rows + owner * CAP + slot_number, EXPERTS * buffer_rows).astype(jnp.int32)
    source = jnp.broadcast_to(jnp.arange(TOKENS, dtype=jnp.int32)[:, None], (TOKENS, 2))
    slot_token = jnp.full((EXPERTS * buffer_rows + 1,), TOKENS, jnp.int32).at[target.reshape(-1)].set(source.reshape(-1))
    slot_token = slot_token[:EXPERTS * buffer_rows].reshape(EXPERTS, buffer_rows)
    fetch_index = jnp.minimum(target, EXPERTS * buffer_rows - 1).astype(jnp.int32)
    kept_float = kept_copy.astype(jnp.float32)
    pick_hot = hot_int.astype(jnp.float32)

    def forward(tokens_in, gain_one, query_full, key_full, value_full, output_full, bias_flat, gain_two, router_full, gate_full, up_full, down_full):
        normed_one = low(root_norm(tokens_in, gain_one))
        queries = low_back(low(matmul_high(normed_one, query_full)))
        keys_all = low_back(low(matmul_high(normed_one, key_full)))
        values_all = low_back(low(matmul_high(normed_one, value_full)))
        bias_grid = bias_flat.reshape(BUCKETS, HEADS)

        def one_tree(unused, pieces):
            query_tree, key_tree, value_tree, tree_starts, tree_before, tree_reaches = pieces
            return (unused, tree_attention(query_tree, key_tree, value_tree, bias_grid, tree_starts, tree_before, tree_reaches))
        shaped = (queries.reshape(TREES, TREE, HEADS, HDIM), keys_all.reshape(TREES, TREE, HEADS, HDIM), values_all.reshape(TREES, TREE, HEADS, HDIM), starts, before, reaches)
        unused, attended = lax.scan(one_tree, jnp.zeros((), jnp.float32), shaped)
        attended = low_back(low(attended.reshape(TOKENS, D)))
        residual = tokens_in + low_back(matmul_high(attended, output_full))
        normed_two = low(root_norm(residual, gain_two))
        router_prob = jax.nn.softmax(matmul_high(normed_two, router_full), axis=-1)
        chosen = lax.optimization_barrier(jnp.sum(pick_hot * router_prob[:, None, :], axis=2))
        gate_shares = chosen / lax.optimization_barrier(jnp.sum(chosen, axis=1, keepdims=True))
        padded = jnp.concatenate([normed_two, jnp.zeros((1, D), jnp.float32)], axis=0)

        def one_expert(number):
            rows_in = low_back(jnp.take(padded, slot_token[number], axis=0))
            gate_pre = low_back(matmul_high(rows_in, gate_full[number].T))
            up_pre = low_back(matmul_high(rows_in, up_full[number].T))
            active = low(jax.nn.gelu(gate_pre, approximate=True) * up_pre)
            return low_back(low(matmul_high(active, down_full[number])))
        expert_out = lax.map(jax.checkpoint(one_expert), expert_range)
        picked = jnp.take(expert_out.reshape(EXPERTS * buffer_rows, D), fetch_index.reshape(-1), axis=0).reshape(TOKENS, 2, D)
        mixture = lax.optimization_barrier(jnp.sum((gate_shares * kept_float)[:, :, None] * picked, axis=1))
        return (residual + mixture, (jnp.sum(residual * residual), jnp.sum(mixture * mixture)))
    layer_out, pullback, sums = jax.vjp(forward, tokens.astype(jnp.float32), attention_gain.astype(jnp.float32), query_weight.astype(jnp.float32), key_weight.astype(jnp.float32), value_weight.astype(jnp.float32), output_weight.astype(jnp.float32), bias_table.astype(jnp.float32), feedforward_gain.astype(jnp.float32), router_weight.astype(jnp.float32), gate_weight.astype(jnp.float32), up_weight.astype(jnp.float32), down_weight.astype(jnp.float32), has_aux=True)
    grads = pullback(cotangent.astype(jnp.float32))
    roots = jnp.sqrt(jnp.stack([sums[0], sums[1]]) / (TOKENS * D))
    return (layer_out.astype(jnp.bfloat16), grads[0], grads[1], grads[2], grads[3], grads[4], grads[5], grads[6], grads[7], grads[8], grads[9], grads[10], grads[11], roots)
```

```python
import math

import jax
import jax.numpy as jnp
from jax import lax
from jax.experimental import pallas as pl
from jax.experimental.pallas import tpu as pltpu
from jax.sharding import PartitionSpec as P

SPEC_0 = "qkb,bh->hqk"
SPEC_1 = "qhd,khd->hqk"
SPEC_2 = "hqk,khd->qhd"
SPEC_3 = "rd,fd->rf"
SPEC_4 = "rf,rd->fd"
SPEC_5 = "rd,re->de"
SPEC_6 = "re,de->rd"
SPEC_7 = "qkb,hqk->bh"
SPEC_8 = "hqk,qhd->khd"
MESH = pl.DeviceIdType.MESH
VMEM_LIMIT = 62 << 20
EXPERT, SEQ = "expert", "seq"
BOTH = (EXPERT, SEQ)

D = 1024
HEADS = 16
HDIM = 64
BUCKETS = 32
MAXDIST = 128


EPSILON = 1e-06
NEGATIVE = -1e30


def norm_factor(values):
    return lax.rsqrt(jnp.mean(values * values, axis=-1, keepdims=True) + EPSILON)


def gelu_tanh(values):
    return jax.nn.gelu(values, approximate=True)


def bucket_of(distance):
    exact_span = BUCKETS // 2
    above = jnp.zeros(distance.shape, jnp.int32)
    for number in range(exact_span):
        threshold = int(math.ceil(exact_span * (MAXDIST / exact_span) ** (number / exact_span)))
        above = above + (distance >= threshold).astype(jnp.int32)
    return jnp.where(distance < exact_span, distance, exact_span - 1 + above)


def tree_tables(lengths, parents):
    ordinal = jnp.arange(lengths.shape[0], dtype=jnp.int32)
    starts = jnp.cumsum(lengths) - lengths

    def chase(number, running):
        current, reaches = running
        current = jnp.sum(
            jnp.where(current[:, None] == ordinal[None, :], parents[None, :], 0), axis=1
        )
        reaches = jnp.maximum(reaches, (current[:, None] == ordinal[None, :]).astype(jnp.int32))
        return (current, reaches)

    begin = (ordinal, (ordinal[:, None] == ordinal[None, :]).astype(jnp.int32))
    unused, reaches = lax.fori_loop(0, lengths.shape[0], chase, begin)
    before = jnp.sum(reaches * lengths[None, :], axis=1) - lengths
    return (starts, before, reaches)


def token_info(token_rows, starts, before, reaches):
    ordinal = jnp.arange(starts.shape[0], dtype=jnp.int32)
    segment = jnp.sum((token_rows[:, None] >= starts[None, :]).astype(jnp.int32), axis=1) - 1
    member = segment[:, None] == ordinal[None, :]
    position = token_rows + jnp.sum(jnp.where(member, (before - starts)[None, :], 0), axis=1)
    lineage = jnp.sum(jnp.where(member[:, :, None], reaches[None, :, :], 0), axis=1)
    return (member.astype(jnp.float32), position, lineage.astype(jnp.float32))


def pair_terms(query_meta, key_meta, query_rows, key_rows, bias_grid):
    visible = jnp.dot(query_meta[2], key_meta[0].T, preferred_element_type=jnp.float32) > 0.5
    visible = visible & (key_rows[None, :] <= query_rows[:, None])
    distance = jnp.maximum(query_meta[1][:, None] - key_meta[1][None, :], 0)
    onehot = (
        bucket_of(distance)[:, :, None] == jnp.arange(BUCKETS, dtype=jnp.int32)[None, None, :]
    ).astype(jnp.bfloat16)
    pair_bias = jnp.einsum(SPEC_0, onehot, bias_grid, preferred_element_type=jnp.float32)
    return (visible, onehot, pair_bias)


def masked_scores(query_block, key_block, visible, pair_bias):
    scores = (
        jnp.einsum(SPEC_1, query_block, key_block, preferred_element_type=jnp.float32)
        * HDIM ** (-0.5)
        + pair_bias
    )
    return jnp.where(visible[None], scores, NEGATIVE)


def contract(left, right, dims):
    return lax.dot_general(left, right, (dims, ((), ())), preferred_element_type=jnp.float32)


def gelu_parts(values):
    root = 0.7978845608028654
    square = values * values
    swing = jnp.tanh(root * values * (1.0 + 0.044715 * square))
    half = 0.5 * (1.0 + swing)
    slope = half + 0.5 * values * (1.0 - swing * swing) * (root * (1.0 + 3 * 0.044715 * square))
    return values * half, slope


ORDER = (0, 1, 4, 5, 2, 3, 6, 7)


def expert_kernel(
    xs, gs, wg, wu, wd, ret_o, ret_b, dwg, dwu, dwd,
    xr, gr, act, gb, ub, po, pb, ro, rb, ro2, rb2, stage,
    in_send, in_recv, hop_send, hop_recv, rs_send, rs_recv, out_send, out_recv, stage_sem,
):
    e = lax.axis_index(EXPERT)
    s = lax.axis_index(SEQ)
    cap = xs.shape[0] // 8
    near_x, near_y = (e, s ^ 1), (e, s ^ 2)
    barrier = pltpu.get_barrier_semaphore()
    peers = [near_x, near_y] + [(e ^ d, s) for d in range(1, 8)]
    for peer in peers:
        pl.semaphore_signal(barrier, inc=1, device_id=peer, device_id_type=MESH)
    pl.semaphore_wait(barrier, len(peers))

    def remote(src, dst, send, recv, peer):
        return pltpu.make_async_remote_copy(
            src_ref=src, dst_ref=dst, send_sem=send, recv_sem=recv,
            device_id=peer, device_id_type=MESH,
        )

    def block(index):
        return pl.ds(pl.multiple_of(index * cap, 16), cap)

    tensors = ((xs, xr), (gs, gr))

    def entry(kind, place):
        src, dst = tensors[kind]
        d = ORDER[place]
        return remote(src.at[block(e ^ d)], dst.at[0, place], in_send.at[kind, place],
                      in_recv.at[kind, place], (e ^ d, s))

    def hop(kind, which, pair):
        buf = tensors[kind][1]
        two = pl.ds(2 * pair, 2)
        if which == 0:
            src, dst, peer = buf.at[0, two], buf.at[1, two], near_x
        elif which == 1:
            src, dst, peer = buf.at[0, two], buf.at[2, two], near_y
        elif kind == 0:
            src, dst, peer = buf.at[1, two], buf.at[3, two], near_y
        else:
            src, dst, peer = buf.at[2, two], buf.at[3, two], near_x
        return remote(src, dst, hop_send.at[kind, which, pair], hop_recv.at[kind, which, pair], peer)

    def rs(kind, which, c):
        part, one, two = ((po, ro, ro2), (pb, rb, rb2))[kind]
        first, second = ((near_x, near_y), (near_y, near_x))[kind]
        mine = 1 + kind
        if which == 0:
            src, dst, peer = part.at[mine, c], one.at[0, c], first
        elif which == 1:
            src, dst, peer = part.at[3, c], one.at[1, c], first
        else:
            src, dst, peer = part.at[2 - kind, c], two.at[c], second
        return remote(src, dst, rs_send.at[kind, which, c], rs_recv.at[kind, which, c], peer)

    def back(kind, place):
        part = (po, pb)[kind]
        ret = (ret_o, ret_b)[kind]
        c, i = place // 4, place % 4
        return remote(part.at[0, c, pl.ds(i * cap, cap)], ret.at[block(e)],
                      out_send.at[kind, place], out_recv.at[kind, place], (e ^ ORDER[place], s))

    def start_entries(c):
        for i in range(4):
            for kind in range(2):
                if ORDER[4 * c + i]:
                    entry(kind, 4 * c + i).start()

    def forward_pair(pair):
        for kind in range(2):
            for place in (2 * pair, 2 * pair + 1):
                if ORDER[place]:
                    entry(kind, place).wait_recv()
            hop(kind, 0, pair).start()
            hop(kind, 1, pair).start()

    def forward_corner(c):
        for pair in (2 * c, 2 * c + 1):
            hop(0, 0, pair).wait_recv()
            hop(0, 2, pair).start()
            hop(1, 1, pair).wait_recv()
            hop(1, 2, pair).start()

    def wait_hops(kind, which, c):
        for pair in (2 * c, 2 * c + 1):
            hop(kind, which, pair).wait_recv()

    def add_second(kind, c):
        rs(kind, 1, c).wait_recv()
        part, one = ((po, ro), (pb, rb))[kind]
        group = 2 - kind
        part[group, c] = (part[group, c].astype(jnp.float32) + one[1, c].astype(jnp.float32)).astype(jnp.bfloat16)
        rs(kind, 2, c).start()

    def finish(kind, c):
        rs(kind, 0, c).wait_recv()
        rs(kind, 2, c).wait_recv()
        part, one, two = ((po, ro, ro2), (pb, rb, rb2))[kind]
        part[0, c] = (
            part[0, c].astype(jnp.float32) + one[0, c].astype(jnp.float32) + two[c].astype(jnp.float32)
        ).astype(jnp.bfloat16)
        for i in range(4):
            if ORDER[4 * c + i]:
                back(kind, 4 * c + i).start()
            else:
                (ret_o, ret_b)[kind][block(e), :] = part[0, c, i * cap:(i + 1) * cap]

    start_entries(0)
    for src, dst in tensors:
        dst[0, 0] = src[block(e), :]
    forward_pair(0)
    forward_pair(1)
    start_entries(1)

    def unit(u, carry):
        q, c = lax.rem(u, 4), u // 4

        @pl.when(u == 1)
        def _():
            forward_corner(0)
            wait_hops(1, 0, 0)
            wait_hops(0, 1, 0)

        @pl.when(u == 3)
        def _():
            forward_pair(2)
            wait_hops(0, 2, 0)
            wait_hops(1, 2, 0)

        @pl.when(u == 4)
        def _():
            forward_pair(3)

        @pl.when(u == 5)
        def _():
            forward_corner(1)
            add_second(0, 0)
            add_second(1, 0)
            wait_hops(1, 0, 1)
            wait_hops(0, 1, 1)

        @pl.when(u == 7)
        def _():
            finish(0, 0)
            finish(1, 0)
            wait_hops(0, 2, 1)
            wait_hops(1, 2, 1)

        rows = 4 * cap
        x = xr[q, pl.ds(4 * c, 4)].reshape(rows, xs.shape[1])
        g = gr[q, pl.ds(4 * c, 4)].reshape(rows, xs.shape[1])
        gate = contract(x, wg[...], ((1,), (1,)))
        up = contract(x, wu[...], ((1,), (1,)))
        ag = contract(g, wd[...], ((1,), (1,)))
        value, slope = gelu_parts(gate)
        active = (value * up).astype(jnp.bfloat16)
        gate_back = (ag * up * slope).astype(jnp.bfloat16)
        up_back = (ag * value).astype(jnp.bfloat16)
        act[q, c] = active
        gb[q, c] = gate_back
        ub[q, c] = up_back
        po[q, c] = contract(active, wd[...], ((1,), (0,))).astype(jnp.bfloat16)
        pb[q, c] = (
            contract(gate_back, wg[...], ((1,), (0,))) + contract(up_back, wu[...], ((1,), (0,)))
        ).astype(jnp.bfloat16)

        for k, (kind, which) in ((1, (0, 0)), (2, (1, 0)), (3, (0, 1)), (3, (1, 1))):
            for half in range(2):
                @pl.when(u == k + 4 * half)
                def _():
                    rs(kind, which, half).start()
        return carry

    lax.fori_loop(0, 8, unit, 0)

    rows = 4 * cap

    def grads(left, right, dst):
        def part(u):
            q, c = lax.rem(u, 4), u // 4
            return contract(left[q, c], right[q, pl.ds(4 * c, 4)].reshape(rows, xs.shape[1]), ((0,), (0,)))

        def more(u, carry):
            stage[...] += part(u)
            return carry

        stage[...] = part(0)
        lax.fori_loop(1, 8, more, 0)
        done = pltpu.make_async_copy(stage, dst, stage_sem)
        done.start()
        return done

    gate_done = grads(gb, xr, dwg)
    add_second(0, 1)
    add_second(1, 1)
    gate_done.wait()
    up_done = grads(ub, xr, dwu)
    finish(0, 1)
    finish(1, 1)
    up_done.wait()
    grads(act, gr, dwd).wait()

    for kind in range(2):
        for place in range(8):
            if ORDER[place]:
                entry(kind, place).wait_send()
                back(kind, place).wait()
        for which in range(3):
            for pair in range(4):
                hop(kind, which, pair).wait_send()
            for c in range(2):
                rs(kind, which, c).wait_send()


def experts(send_rows, grad_rows, gate_weight, up_weight, down_weight):
    rows, width = send_rows.shape
    units = gate_weight.shape[0]
    cap = rows // 8
    low, full = jnp.bfloat16, jnp.float32
    vmem = pl.BlockSpec(memory_space=pltpu.VMEM)
    hbm = pl.BlockSpec(memory_space=pl.ANY)
    dma = pltpu.SemaphoreType.DMA
    return pl.pallas_call(
        expert_kernel,
        out_shape=(
            jax.ShapeDtypeStruct((rows, width), low),
            jax.ShapeDtypeStruct((rows, width), low),
        ) + (jax.ShapeDtypeStruct((units, width), full),) * 3,
        in_specs=[vmem] * 5,
        out_specs=(vmem, vmem, hbm, hbm, hbm),
        scratch_shapes=[
            pltpu.VMEM((4, 8, cap, width), low),
            pltpu.VMEM((4, 8, cap, width), low),
            pltpu.VMEM((4, 2, 4 * cap, units), low),
            pltpu.VMEM((4, 2, 4 * cap, units), low),
            pltpu.VMEM((4, 2, 4 * cap, units), low),
            pltpu.VMEM((4, 2, 4 * cap, width), low),
            pltpu.VMEM((4, 2, 4 * cap, width), low),
            pltpu.VMEM((2, 2, 4 * cap, width), low),
            pltpu.VMEM((2, 2, 4 * cap, width), low),
            pltpu.VMEM((2, 4 * cap, width), low),
            pltpu.VMEM((2, 4 * cap, width), low),
            pltpu.VMEM((units, width), full),
            dma((2, 8)), dma((2, 8)),
            dma((2, 3, 4)), dma((2, 3, 4)),
            dma((2, 3, 2)), dma((2, 3, 2)),
            dma((2, 8)), dma((2, 8)),
            dma,
        ],
        compiler_params=pltpu.CompilerParams(
            collective_id=1, has_side_effects=True, vmem_limit_bytes=VMEM_LIMIT
        ),
        cost_estimate=pl.CostEstimate(flops=2 * 9 * 4 * rows * units * width, bytes_accessed=20 << 20, transcendentals=4 * rows * units),
        name="experts",
    )(send_rows, grad_rows, gate_weight, up_weight, down_weight)


def remote(src, dst, send, recv, peer):
    return pltpu.make_async_remote_copy(
        src_ref=src, dst_ref=dst, send_sem=send, recv_sem=recv,
        device_id=peer, device_id_type=MESH,
    )


def greet(peers):
    barrier = pltpu.get_barrier_semaphore()
    for peer in peers:
        pl.semaphore_signal(barrier, inc=1, device_id=peer, device_id_type=MESH)
    pl.semaphore_wait(barrier, len(peers))


def aligned(index, size):
    return pl.ds(pl.multiple_of(index * size, size), size)


ZHOPS = (2, 4, 6)


def project_kernel(
    tokens, wq, wk, wv, misc, all_tokens, qkv, cols, params,
    part, tags, tag_sum, all_tags,
    t_send, t_recv, w_send, w_recv, m_send, m_recv, c_send, c_recv, n_send, n_recv,
):
    e, s = lax.axis_index(EXPERT), lax.axis_index(SEQ)
    near_x, near_y, corner = (e, s ^ 1), (e, s ^ 2), (e, s ^ 3)
    around = (near_x, near_y, corner)
    along = [(e ^ d, s) for d in (1,) + ZHOPS]
    greet(list(around) + along)
    rows, width = tokens.shape
    slim = wq.shape[0]
    shard = width // 4
    weights = (wq, wk, wv)

    def send_tokens(k):
        return remote(tokens, all_tokens.at[aligned(s, rows)], t_send.at[k], t_recv.at[k], around[k])

    def pass_tokens(k):
        piece = pl.ds(pl.multiple_of((s ^ (1 + k)) * rows + k * (rows // 2), rows // 2), rows // 2)
        view = all_tokens.at[piece]
        return remote(view, view, t_send.at[2 + k], t_recv.at[2 + k], around[1 - k])

    def send_cols(k, m):
        return remote(
            weights[m].at[:, aligned(s ^ (k + 1), shard)], part.at[m, aligned(s, slim)],
            w_send.at[k, m], w_recv.at[k, m], around[k],
        )

    def send_tags(k):
        return remote(misc, tags.at[k], m_send.at[k], m_recv.at[k], around[k])

    hops = (1,) + ZHOPS

    def share(k):
        return remote(part, cols.at[:, aligned(e, 4 * slim)], c_send.at[k], c_recv.at[k], (e ^ hops[k], s))

    def share_tags(k):
        return remote(tag_sum, all_tags.at[k], n_send.at[k], n_recv.at[k], (e ^ hops[k], s))

    def relay(k):
        view = cols.at[:, aligned(e ^ hops[k], 4 * slim)]
        return remote(view, view, c_send.at[3 + k], c_recv.at[3 + k], (e ^ 1, s))

    def relay_tags(k):
        return remote(all_tags.at[k], all_tags.at[3 + k], n_send.at[3 + k], n_recv.at[3 + k], (e ^ 1, s))

    for k in range(3):
        for m in range(3):
            send_cols(k, m).start()
        send_tags(k).start()
    for k in range(2):
        send_tokens(k).start()
    for m in range(3):
        part[m, aligned(s, slim), :] = weights[m][:, aligned(s, shard)]
    all_tokens[aligned(s, rows), :] = tokens[...]
    total = misc[...].astype(jnp.float32)
    for k in range(3):
        send_tags(k).wait_recv()
        total += tags[k].astype(jnp.float32)
    tag_sum[...] = total.astype(jnp.bfloat16)
    for k in range(3):
        for m in range(3):
            send_cols(k, m).wait_recv()
    for k in range(4):
        share_tags(k).start()
        share(k).start()
    cols[:, aligned(e, 4 * slim), :] = part[...]
    for k in range(2):
        send_tokens(k).wait_recv()
        pass_tokens(k).start()
    for k in range(1, 4):
        share_tags(k).wait_recv()
        relay_tags(k).start()
        share(k).wait_recv()
        relay(k).start()
    share_tags(0).wait_recv()
    share(0).wait_recv()
    for k in range(1, 4):
        relay_tags(k).wait_recv()
        relay(k).wait_recv()
    for k in range(7):
        total += all_tags[k].astype(jnp.float32)
    params[...] = total
    gain = total[0:1]

    def group(q, carry):
        @pl.when(q == 3)
        def _():
            for k in range(2):
                pass_tokens(k).wait_recv()
        place = aligned(s ^ q, rows)
        values = all_tokens[place, :].astype(jnp.float32)
        normed = (values * norm_factor(values) * gain).astype(jnp.bfloat16)
        for m in range(3):
            out = contract(normed, cols[m], ((1,), (0,)))
            if m == 0:
                out = out.astype(jnp.bfloat16).astype(jnp.float32) * HDIM ** (-0.5)
            qkv[place, m * shard:(m + 1) * shard] = out.astype(jnp.bfloat16)
        return carry

    lax.fori_loop(0, 4, group, 0)
    for k in range(2):
        send_tokens(k).wait_send()
        pass_tokens(k).wait_send()
    for k in range(3):
        for m in range(3):
            send_cols(k, m).wait_send()
        send_tags(k).wait_send()
    for k in range(4):
        share(k).wait_send()
        share_tags(k).wait_send()
    for k in range(1, 4):
        relay(k).wait_send()
        relay_tags(k).wait_send()


def project(tokens, wq, wk, wv, misc):
    rows, width = tokens.shape
    slim, shard = wq.shape[0], width // 4
    low, full = jnp.bfloat16, jnp.float32
    vmem = pl.BlockSpec(memory_space=pltpu.VMEM)
    dma = pltpu.SemaphoreType.DMA
    return pl.pallas_call(
        project_kernel,
        out_shape=(
            jax.ShapeDtypeStruct((4 * rows, width), low),
            jax.ShapeDtypeStruct((4 * rows, 3 * shard), low),
            jax.ShapeDtypeStruct((3, width, shard), low),
            jax.ShapeDtypeStruct(misc.shape, full),
        ),
        in_specs=[vmem] * 5,
        out_specs=(vmem,) * 4,
        scratch_shapes=[
            pltpu.VMEM((3, 4 * slim, shard), low),
            pltpu.VMEM((3,) + misc.shape, low),
            pltpu.VMEM(misc.shape, low),
            pltpu.VMEM((7,) + misc.shape, low),
            dma((4,)), dma((4,)), dma((3, 3)), dma((3, 3)), dma((3,)), dma((3,)),
            dma((7,)), dma((7,)), dma((7,)), dma((7,)),
        ],
        compiler_params=pltpu.CompilerParams(
            collective_id=2, has_side_effects=True, vmem_limit_bytes=VMEM_LIMIT
        ),
        cost_estimate=pl.CostEstimate(flops=24 * rows * width * shard, bytes_accessed=10 << 20, transcendentals=0),
        name="project",
    )(tokens, wq, wk, wv, misc)


def segment_scalars(lengths, parents, before_mem, reach_mem):
    count = lengths.shape[1]
    start = jnp.int32(0)
    found = []
    for k in range(count):
        length = lengths[0, k]
        if k == 0:
            before, reach = jnp.int32(0), jnp.int32(1)
        else:
            parent = parents[0, k]
            before = before_mem[parent] + lengths[0, parent]
            reach = reach_mem[parent] | (1 << k)
        before_mem[k] = before
        reach_mem[k] = reach
        found.append((start, before, reach, length))
        start = start + length
    return found


def token_columns(found, ids):
    offset = jnp.zeros(ids.shape, jnp.int32)
    reach = jnp.full(ids.shape, 1, jnp.int32)
    own = jnp.full(ids.shape, 1, jnp.int32)
    for k, (start, before, bits, _) in enumerate(found):
        if k:
            after = ids >= start
            offset = jnp.where(after, before - start, offset)
            reach = jnp.where(after, bits, reach)
            own = jnp.where(after, 1 << k, own)
    return ids + offset, reach, own


LAST = 127


def bias_tables(params, s):
    flat = params[2:3, 0:BUCKETS * HEADS]
    lane = lax.broadcasted_iota(jnp.int32, (8, BUCKETS * HEADS), 1)
    head = lax.broadcasted_iota(jnp.int32, (8, BUCKETS * HEADS), 0)
    heads_here = HEADS // 4
    chosen = jnp.where((lane % HEADS) == s * heads_here + head, jnp.broadcast_to(flat, lane.shape), 0.0)
    entry = lax.broadcasted_iota(jnp.int32, (BUCKETS * HEADS, LAST + 1), 0) // HEADS
    distance = lax.broadcasted_iota(jnp.int32, (BUCKETS * HEADS, LAST + 1), 1)
    hot = jnp.where(entry == bucket_of(distance), 1.0, 0.0)
    table = contract(chosen.astype(jnp.bfloat16), hot.astype(jnp.bfloat16), ((1,), (0,)))
    spot = lax.broadcasted_iota(jnp.int32, table.shape, 1)
    return jnp.where(spot == LAST, NEGATIVE, table)


def pair_index(found, first, rows, count):
    ids = first + lax.broadcasted_iota(jnp.int32, (rows, 1), 0)
    keys = lax.broadcasted_iota(jnp.int32, (1, count), 1)
    place, reach, _ = token_columns(found, ids)
    key_place, _, key_own = token_columns(found, keys)
    seen = ((reach & key_own) != 0) & (keys <= ids)
    return jnp.where(seen, jnp.minimum(place - key_place, LAST - 1), LAST), place, reach


def looked_up(row, index):
    rows, count = index.shape
    table = jnp.broadcast_to(row, (rows, LAST + 1))
    pieces = [
        jnp.take_along_axis(table, index[:, k * 128:(k + 1) * 128], axis=1)
        for k in range(count // 128)
    ]
    return jnp.concatenate(pieces, axis=1)


def attend_kernel(lengths, parents, qkv, params, out, index, table, before_mem, reach_mem):
    s = lax.axis_index(SEQ)
    found = segment_scalars(lengths, parents, before_mem, reach_mem)
    table[...] = bias_tables(params, s)
    total = qkv.shape[0]
    block = 256
    shard = qkv.shape[1] // 3
    for r in range(total // block):
        count = (r + 1) * block
        index[:, :count] = pair_index(found, r * block, block, count)[0]

        def pair(h, carry):
            place = aligned(h, 128)
            q = qkv[r * block:count, place]
            k = qkv[0:count, aligned(h + shard // 128, 128)]
            v = qkv[0:count, aligned(h + 2 * shard // 128, 128)]
            lane = lax.broadcasted_iota(jnp.int32, (block, 128), 1)
            results = []
            for side in range(2):
                mine = (lane // HDIM) == side
                scores = contract(jnp.where(mine, q, jnp.zeros_like(q)), k, ((1,), (1,)))
                scores = scores + looked_up(table[pl.ds(2 * h + side, 1), :], index[:, :count])
                expo = jnp.exp(scores - jnp.max(scores, axis=1, keepdims=True))
                probs = (expo / jnp.sum(expo, axis=1, keepdims=True)).astype(jnp.bfloat16)
                results.append(contract(probs, v, ((1,), (0,))))
            out[r * block:count, place] = jnp.where((lane // HDIM) == 0, results[0], results[1]).astype(jnp.bfloat16)
            return carry

        lax.fori_loop(0, shard // 128, pair, 0)


def attend(lengths, parents, qkv, params):
    total, shard = qkv.shape[0], qkv.shape[1] // 3
    vmem, smem = pl.BlockSpec(memory_space=pltpu.VMEM), pl.BlockSpec(memory_space=pltpu.SMEM)
    return pl.pallas_call(
        attend_kernel,
        out_shape=jax.ShapeDtypeStruct((total, shard), jnp.bfloat16),
        in_specs=[smem, smem, vmem, vmem],
        out_specs=vmem,
        scratch_shapes=[
            pltpu.VMEM((256, total), jnp.int32), pltpu.VMEM((8, 128), jnp.float32),
            pltpu.SMEM((16,), jnp.int32), pltpu.SMEM((16,), jnp.int32),
        ],
        compiler_params=pltpu.CompilerParams(vmem_limit_bytes=VMEM_LIMIT),
        cost_estimate=pl.CostEstimate(flops=4 * total * total * shard, bytes_accessed=4 << 20, transcendentals=2 * total * total),
        name="attend",
    )(lengths, parents, qkv, params)


def attend_back_kernel(lengths, parents, qkv, params, grad, dqkv, bias_grad,
                       index, spots, table, near, dk, dv, before_mem, reach_mem):
    s = lax.axis_index(SEQ)
    found = segment_scalars(lengths, parents, before_mem, reach_mem)
    table[...] = bias_tables(params, s)
    total = qkv.shape[0]
    block = 256
    shard = qkv.shape[1] // 3
    dk[...] = jnp.zeros_like(dk)
    dv[...] = jnp.zeros_like(dv)
    near[...] = jnp.zeros_like(near)
    for r in range(total // block):
        count = (r + 1) * block
        here, place, reach = pair_index(found, r * block, block, count)
        index[:, :count] = here
        step = lax.broadcasted_iota(jnp.int32, (block, 128), 1)
        wanted = place - step
        spot = jnp.full((block, 128), -1, jnp.int32)
        for k, (start, before, _, length) in enumerate(found):
            inside = ((reach & (1 << k)) != 0) & (wanted >= before) & (wanted < before + length)
            spot = jnp.where(inside, wanted + (start - before), spot)
        spots[...] = jnp.where(step == LAST, -1, spot)

        def pair(h, carry):
            lanes = aligned(h, 128)
            q = qkv[r * block:count, lanes]
            k = qkv[0:count, aligned(h + shard // 128, 128)]
            v = qkv[0:count, aligned(h + 2 * shard // 128, 128)]
            g = grad[r * block:count, lanes]
            lane = lax.broadcasted_iota(jnp.int32, (block, 128), 1)
            dq = None
            key_sum, value_sum = 0.0, 0.0
            for side in range(2):
                mine = (lane // HDIM) == side
                q_side = jnp.where(mine, q, jnp.zeros_like(q))
                g_side = jnp.where(mine, g, jnp.zeros_like(g))
                scores = contract(q_side, k, ((1,), (1,)))
                scores = scores + looked_up(table[pl.ds(2 * h + side, 1), :], index[:, :count])
                expo = jnp.exp(scores - jnp.max(scores, axis=1, keepdims=True))
                soft = expo / jnp.sum(expo, axis=1, keepdims=True)
                dprob = contract(g_side, v, ((1,), (1,)))
                delta = jnp.sum(soft * dprob, axis=1, keepdims=True)
                score_grad = (soft * (dprob - delta)).astype(jnp.bfloat16)
                wide = score_grad.astype(jnp.float32)
                part = contract(score_grad, k, ((1,), (0,)))
                dq = part if side == 0 else jnp.where(mine, part, dq)
                key_sum = key_sum + contract(score_grad, q_side, ((0,), (0,)))
                value_sum = value_sum + contract(soft.astype(jnp.bfloat16), g_side, ((0,), (0,)))
                close = jnp.zeros((block, 128), jnp.float32)
                everything = jnp.zeros((block, 128), jnp.float32)
                for b in range(count // 128):
                    piece = wide[:, b * 128:(b + 1) * 128]
                    local = spots[...] - b * 128
                    there = (local >= 0) & (local < 128)
                    taken = jnp.take_along_axis(piece, jnp.where(there, local, 0), axis=1)
                    close = close + jnp.where(there, taken, 0.0)
                    everything = everything + piece
                for kind, values in enumerate((close, everything)):
                    near[kind, 2 * h + side] += jnp.sum(values.reshape(block // 8, 8, 128), axis=0)
            dqkv[r * block:count, lanes] = (dq * HDIM ** (-0.5)).astype(jnp.bfloat16)
            dk[0:count, lanes] += key_sum
            dv[0:count, lanes] += value_sum
            return carry

        lax.fori_loop(0, shard // 128, pair, 0)
    dqkv[:, shard:2 * shard] = dk[...].astype(jnp.bfloat16)
    dqkv[:, 2 * shard:3 * shard] = dv[...].astype(jnp.bfloat16)
    close, everything = (
        jnp.concatenate([jnp.sum(near[kind, h], axis=0, keepdims=True) for h in range(8)], axis=0) for kind in range(2)
    )
    far = jnp.sum(everything, axis=1, keepdims=True) - jnp.sum(close, axis=1, keepdims=True)
    spot = lax.broadcasted_iota(jnp.int32, close.shape, 1)
    by_distance = jnp.where(spot == LAST, far, close)
    lane = lax.broadcasted_iota(jnp.int32, (128, BUCKETS * HEADS), 1)
    distance = lax.broadcasted_iota(jnp.int32, (128, BUCKETS * HEADS), 0)
    hot = jnp.where((lane // HEADS) == bucket_of(distance), 1.0, 0.0)
    spread = lax.dot_general(by_distance, hot, (((1,), (0,)), ((), ())),
                             precision=lax.Precision.HIGHEST, preferred_element_type=jnp.float32)
    head = lax.broadcasted_iota(jnp.int32, spread.shape, 0)
    lane = lax.broadcasted_iota(jnp.int32, spread.shape, 1)
    here = ((lane % HEADS) == s * (HEADS // 4) + head) & (head < HEADS // 4)
    bias_grad[...] = jnp.broadcast_to(jnp.sum(jnp.where(here, spread, 0.0), axis=0, keepdims=True), bias_grad.shape)


def attend_back(lengths, parents, qkv, params, grad):
    total, shard = qkv.shape[0], qkv.shape[1] // 3
    full = jnp.float32
    vmem, smem = pl.BlockSpec(memory_space=pltpu.VMEM), pl.BlockSpec(memory_space=pltpu.SMEM)
    return pl.pallas_call(
        attend_back_kernel,
        out_shape=(
            jax.ShapeDtypeStruct((total, 3 * shard), jnp.bfloat16),
            jax.ShapeDtypeStruct((8, BUCKETS * HEADS), full),
        ),
        in_specs=[smem, smem, vmem, vmem, vmem],
        out_specs=(vmem, vmem),
        scratch_shapes=[
            pltpu.VMEM((256, total), jnp.int32), pltpu.VMEM((256, 128), jnp.int32),
            pltpu.VMEM((8, 128), full), pltpu.VMEM((2, 8, 8, 128), full),
            pltpu.VMEM((total, shard), full), pltpu.VMEM((total, shard), full),
            pltpu.SMEM((16,), jnp.int32), pltpu.SMEM((16,), jnp.int32),
        ],
        compiler_params=pltpu.CompilerParams(vmem_limit_bytes=VMEM_LIMIT),
        cost_estimate=pl.CostEstimate(flops=10 * total * total * shard, bytes_accessed=6 << 20, transcendentals=2 * total * total),
        name="attend_back",
    )(lengths, parents, qkv, params, grad)


def routing(residual, params, ids, ids_row, cap):
    rows = residual.shape[0]
    full = jnp.float32
    scale = norm_factor(residual)
    unit = residual * scale
    normed = (unit * params[1:2]).astype(jnp.bfloat16)
    router = params[8:16]
    logits = contract(normed, router.astype(jnp.bfloat16), ((1,), (1,)))
    expo = jnp.exp(logits - jnp.max(logits, axis=1, keepdims=True))
    prob = expo / jnp.sum(expo, axis=1, keepdims=True)
    lane = lax.broadcasted_iota(jnp.int32, (rows, 8), 1)
    hot = [jnp.where(ids[:, k:k + 1] == lane, 1.0, 0.0).astype(full) for k in range(2)]
    chosen = [jnp.sum(h * prob, axis=1, keepdims=True) for h in hot]
    chosen_sum = chosen[0] + chosen[1]
    shares = [c / chosen_sum for c in chosen]
    down = lax.broadcasted_iota(jnp.int32, (rows, rows), 0)
    across = lax.broadcasted_iota(jnp.int32, (rows, rows), 1)
    before = jnp.where(across < down, 1.0, 0.0).astype(jnp.bfloat16)
    earlier = contract(before, (hot[0] + hot[1]).astype(jnp.bfloat16), ((1,), (0,)))
    slots = [jnp.sum(h * earlier, axis=1, keepdims=True) for h in hot]
    kept = [jnp.where(slot < cap, 1.0, 0.0) for slot in slots]
    target = [
        jnp.where(slots[k] < cap, ids[:, k:k + 1] * cap + slots[k].astype(jnp.int32), -1) for k in range(2)
    ]
    level = lax.broadcasted_iota(jnp.int32, (8, rows), 0)
    hot_row = [jnp.where(ids_row[k:k + 1] == level, 1.0, 0.0).astype(full) for k in range(2)]
    after = jnp.where(down < across, 1.0, 0.0).astype(jnp.bfloat16)
    earlier_row = contract((hot_row[0] + hot_row[1]).astype(jnp.bfloat16), after, ((1,), (0,)))
    slot_row = [jnp.sum(h * earlier_row, axis=0, keepdims=True) for h in hot_row]
    target_row = [
        jnp.where(slot_row[k] < cap, ids_row[k:k + 1] * cap + slot_row[k].astype(jnp.int32), -1) for k in range(2)
    ]
    return scale, unit, normed, router, prob, hot, chosen_sum, shares, kept, target, target_row


def dispatch_kernel(att, wo, tokens, cotangent, params, ids, ids_row, xs, gs, residual, landed, send, recv):
    e, s = lax.axis_index(EXPERT), lax.axis_index(SEQ)
    around = [(e, s ^ k) for k in range(1, 4)]
    greet(around)
    rows, width = tokens.shape
    shard = att.shape[1]
    cap = xs.shape[0] // 8

    def give(k):
        return remote(att.at[aligned(s ^ (k + 1), rows)], landed.at[s], send.at[k], recv.at[k], around[k])

    for k in (2, 0, 1):
        give(k).start()
    landed[s] = att[aligned(s, rows), :]
    total = tokens[...].astype(jnp.float32)
    total += contract(landed[s], wo[aligned(s, shard), :], ((1,), (0,)))
    for k in range(3):
        give(k).wait_recv()
        total += contract(landed[s ^ (k + 1)], wo[aligned(s ^ (k + 1), shard), :], ((1,), (0,)))
    residual[...] = total
    _, _, normed, _, _, _, _, shares, kept, _, target_row = routing(total, params[...], ids[...], ids_row[...], cap)
    place = lax.broadcasted_iota(jnp.int32, (8 * cap, rows), 0)
    hot = [jnp.where(place == target_row[k], 1.0, 0.0).astype(jnp.bfloat16) for k in range(2)]
    xs[...] = contract(hot[0] + hot[1], normed, ((1,), (0,))).astype(jnp.bfloat16)
    grad = cotangent[...].astype(jnp.float32)
    weighted = [((shares[k] * kept[k]) * grad).astype(jnp.bfloat16) for k in range(2)]
    gs[...] = (
        contract(hot[0], weighted[0], ((1,), (0,))) + contract(hot[1], weighted[1], ((1,), (0,)))
    ).astype(jnp.bfloat16)
    for k in range(3):
        give(k).wait_send()


def dispatch(att, wo, tokens, cotangent, params, ids, ids_row):
    rows, width = tokens.shape
    cap = 10 * rows // 32
    low, full = jnp.bfloat16, jnp.float32
    vmem = pl.BlockSpec(memory_space=pltpu.VMEM)
    dma = pltpu.SemaphoreType.DMA
    return pl.pallas_call(
        dispatch_kernel,
        out_shape=(
            jax.ShapeDtypeStruct((8 * cap, width), low),
            jax.ShapeDtypeStruct((8 * cap, width), low),
            jax.ShapeDtypeStruct((rows, width), full),
        ),
        in_specs=[vmem] * 7,
        out_specs=(vmem,) * 3,
        scratch_shapes=[pltpu.VMEM((4, rows, att.shape[1]), low), dma((3,)), dma((3,))],
        compiler_params=pltpu.CompilerParams(
            collective_id=3, has_side_effects=True, vmem_limit_bytes=VMEM_LIMIT
        ),
        cost_estimate=pl.CostEstimate(flops=6 * rows * width * width, bytes_accessed=8 << 20, transcendentals=rows * 8),
        name="dispatch",
    )(att, wo, tokens, cotangent, params, ids, ids_row)


def combine_kernel(ret_o, ret_b, residual, cotangent, wo, params, ids, ids_row,
                   layer_out, residual_grad, datt, aog_cols, small,
                   datt_own, aog_own, send, recv):
    e, s = lax.axis_index(EXPERT), lax.axis_index(SEQ)
    around = [(e, s ^ k) for k in range(1, 4)]
    greet(around)
    rows, width = residual.shape
    shard = datt.shape[1]
    cap = ret_o.shape[0] // 8
    full = jnp.float32
    high = lax.Precision.HIGHEST
    held = residual[...]
    scale, unit, normed, router, prob, hot, chosen_sum, shares, kept, target, _ = routing(
        held, params[...], ids[...], ids_row[...], cap
    )
    place = lax.broadcasted_iota(jnp.int32, (rows, 8 * cap), 1)
    pick = [jnp.where(place == target[k], 1.0, 0.0).astype(jnp.bfloat16) for k in range(2)]
    grad = cotangent[...].astype(full)
    mixture = jnp.zeros((rows, width), full)
    share_grad = []
    for k in range(2):
        picked = contract(pick[k], ret_o[...], ((1,), (0,)))
        mixture += (shares[k] * kept[k]) * picked
        share_grad.append(jnp.sum(grad * picked, axis=1, keepdims=True) * kept[k])
    layer_out[...] = (held + mixture).astype(jnp.bfloat16)
    inner = shares[0] * share_grad[0] + shares[1] * share_grad[1]
    prob_grad = sum(hot[k] * ((share_grad[k] - inner) / chosen_sum) for k in range(2))
    logit_grad = prob * (prob_grad - jnp.sum(prob * prob_grad, axis=1, keepdims=True))
    router_term = lax.dot_general(logit_grad, normed.astype(full), (((0,), (0,)), ((), ())),
                                  precision=high, preferred_element_type=full)
    normed_grad = contract(pick[0] + pick[1], ret_b[...], ((1,), (0,))) + lax.dot_general(
        logit_grad, router, (((1,), (0,)), ((), ())), precision=high, preferred_element_type=full
    )
    gain_term = jnp.sum(normed_grad * unit, axis=0, keepdims=True)
    unit_grad = normed_grad * params[1:2]
    back = grad + scale * (unit_grad - unit * jnp.mean(unit_grad * unit, axis=1, keepdims=True))
    residual_grad[...] = back
    rounded = back.astype(jnp.bfloat16)
    aog_own[...] = rounded
    datt_own[...] = contract(rounded, wo[...], ((1,), (1,))).astype(jnp.bfloat16)

    def give(kind, k):
        src, dst = ((datt_own, datt), (aog_own, aog_cols))[kind]
        return remote(src.at[:, aligned(s ^ (k + 1), shard)], dst.at[aligned(s, rows)],
                      send.at[kind, k], recv.at[kind, k], around[k])

    for kind in range(2):
        for k in (2, 0, 1):
            give(kind, k).start()
    datt[aligned(s, rows), :] = datt_own[:, aligned(s, shard)]
    aog_cols[aligned(s, rows), :] = aog_own[:, aligned(s, shard)]
    lane = lax.broadcasted_iota(jnp.int32, (1, width), 1)
    sums = jnp.where(lane == 0, jnp.sum(held * held), jnp.where(lane == 1, jnp.sum(mixture * mixture), 0.0))
    small[0:8, :] = jnp.zeros((8, width), full)
    small[1:2, :] = gain_term
    small[3:4, :] = sums
    small[8:16, :] = router_term
    for kind in range(2):
        for k in range(3):
            give(kind, k).wait()


def combine(ret_o, ret_b, residual, cotangent, wo, params, ids, ids_row):
    rows, width = residual.shape
    shard = width // 4
    low, full = jnp.bfloat16, jnp.float32
    vmem = pl.BlockSpec(memory_space=pltpu.VMEM)
    dma = pltpu.SemaphoreType.DMA
    return pl.pallas_call(
        combine_kernel,
        out_shape=(
            jax.ShapeDtypeStruct((rows, width), low),
            jax.ShapeDtypeStruct((rows, width), full),
            jax.ShapeDtypeStruct((4 * rows, shard), low),
            jax.ShapeDtypeStruct((4 * rows, shard), low),
            jax.ShapeDtypeStruct((16, width), full),
        ),
        in_specs=[vmem] * 8,
        out_specs=(vmem,) * 5,
        scratch_shapes=[pltpu.VMEM((rows, width), low), pltpu.VMEM((rows, width), low), dma((2, 3)), dma((2, 3))],
        compiler_params=pltpu.CompilerParams(
            collective_id=4, has_side_effects=True, vmem_limit_bytes=VMEM_LIMIT
        ),
        cost_estimate=pl.CostEstimate(flops=6 * rows * width * width, bytes_accessed=12 << 20, transcendentals=rows * 8),
        name="combine",
    )(ret_o, ret_b, residual, cotangent, wo, params, ids, ids_row)


def finish_kernel(
    all_tokens, dqkv, cols, att_full, aog_cols, residual_grad, params, small, bias_grad,
    tokens_grad, dwq, dwk, dwv, dwo, small_sum,
    halves, core_got, sums, z_got, final, parts, first_got, second_got, mine, normed, tally, tally_got,
    core_send, core_recv, z_send, z_recv, a_send, a_recv, n_send, n_recv, m_send, m_recv,
):
    e, s = lax.axis_index(EXPERT), lax.axis_index(SEQ)
    z, c = e // 2, lax.rem(e, 2)
    near_x, near_y = (e, s ^ 1), (e, s ^ 2)
    around = [(e, s ^ k) for k in range(1, 4)]
    hops = (1,) + ZHOPS
    greet(around + [(e ^ d, s) for d in hops])
    full, low = jnp.float32, jnp.bfloat16
    rows, width = residual_grad.shape
    shard = cols.shape[2]
    slim = dwq.shape[0]
    outs = (dwo, dwv, dwk, dwq)
    gain = params[0:1]

    def units(q):
        values = all_tokens[aligned(s ^ q, rows), :].astype(full)
        scale = norm_factor(values)
        return values * scale, scale

    def core_copy(m):
        return remote(halves.at[1 - c, m], core_got.at[m], core_send.at[m], core_recv.at[m], (e ^ 1, s))

    def z_copy(m, k):
        return remote(sums.at[m, z ^ k], z_got.at[k - 1, m], z_send.at[m, k - 1], z_recv.at[m, k - 1], (e ^ (2 * k), s))

    def a_copy(m, k):
        return remote(final.at[m, aligned(s ^ (k + 1), slim)], outs[m].at[:, aligned(s, shard)],
                      a_send.at[m, k], a_recv.at[m, k], around[k])

    def n_copy(kind, which):
        first, second = ((near_x, near_y), (near_y, near_x))[kind]
        if which < 2:
            src = parts.at[(1 + kind, 3)[which], kind]
            return remote(src, first_got.at[kind, which], n_send.at[kind, which], n_recv.at[kind, which], first)
        return remote(parts.at[2 - kind, kind], second_got.at[kind], n_send.at[kind, 2], n_recv.at[kind, 2], second)

    def store_halves(m, zone, block):
        for half in range(2):
            halves[half, m, zone] = block[half * (shard // 2):(half + 1) * (shard // 2)].astype(low)

    def norm_block(q, carry):
        unit, _ = units(q)
        normed[aligned(s ^ q, rows), :] = (unit * gain).astype(low)
        return carry

    def output_zone(j, carry):
        store_halves(0, j, contract(att_full[:, aligned(j, shard)], aog_cols[...], ((0,), (0,))))
        return carry

    lax.fori_loop(0, 4, output_zone, 0)
    core_copy(0).start()
    lax.fori_loop(0, 4, norm_block, 0)

    def qkv_zone(j, carry):
        block = contract(normed[:, aligned(j, shard)], dqkv[...], ((0,), (0,)))
        for m in range(3):
            store_halves(3 - m, j, block[:, m * shard:(m + 1) * shard])
        return carry

    lax.fori_loop(0, 4, qkv_zone, 0)
    for m in range(1, 4):
        core_copy(m).start()

    def add_core(m):
        core_copy(m).wait_recv()
        for j in range(4):
            sums[m, j] = (halves[c, m, j].astype(full) + core_got[m, j].astype(full)).astype(low)
        for k in range(1, 4):
            z_copy(m, k).start()

    add_core(0)
    tally[0] = small[...]
    tally[0, 0:1] = jnp.zeros((1, width), full)
    tally[0, 2:3, 0:BUCKETS * HEADS] = bias_grad[0:1]

    def back_block(i, carry):
        q = 3 - i
        place = aligned(s ^ q, rows)
        d = dqkv[place, :]
        total = jnp.zeros((rows, width), full)
        for m in range(3):
            total += contract(d[:, m * shard:(m + 1) * shard], cols[m], ((1,), (1,)))
        unit, _ = units(q)
        tally[0, 0:1] += jnp.sum(total * unit, axis=0, keepdims=True)
        mine[...] = total
        for kind in range(2):
            parts[q, kind] = total[:, kind * (width // 2):(kind + 1) * (width // 2)].astype(low)

        @pl.when(i == 0)
        def _():
            n_copy(0, 1).start()
            n_copy(1, 1).start()
            for m in range(1, 4):
                add_core(m)

        @pl.when(i == 1)
        def _():
            n_copy(1, 0).start()

        @pl.when(i == 2)
        def _():
            n_copy(0, 0).start()
        return carry

    lax.fori_loop(0, 4, back_block, 0)

    def m_copy(stage, k):
        slot = (0, 3, 4)[stage] + k
        peer = (around[k], (e ^ 1, s), (e ^ (2 * (k + 1)), s))[stage]
        return remote(tally.at[stage], tally_got.at[slot], m_send.at[slot], m_recv.at[slot], peer)

    for k in range(3):
        m_copy(0, k).start()

    for kind in range(2):
        n_copy(kind, 1).wait_recv()
        group = 2 - kind
        parts[group, kind] = (parts[group, kind].astype(full) + first_got[kind, 1].astype(full)).astype(low)
        n_copy(kind, 2).start()

    total = tally[0]
    for k in range(3):
        m_copy(0, k).wait_recv()
        total += tally_got[k]
    tally[1] = total
    m_copy(1, 0).start()

    def finish_grad(m):
        block = sums[m, z].astype(full)
        for k in range(1, 4):
            z_copy(m, k).wait_recv()
            block += z_got[k - 1, m].astype(full)
        final[m] = block
        for k in range(3):
            a_copy(m, k).start()
        outs[m][:, aligned(s, shard)] = final[m, aligned(s, slim)]

    finish_grad(0)
    m_copy(1, 0).wait_recv()
    total = total + tally_got[3]
    tally[2] = total
    for k in range(3):
        m_copy(2, k).start()
    for m in range(1, 4):
        finish_grad(m)

    for kind in range(2):
        n_copy(kind, 0).wait_recv()
        n_copy(kind, 2).wait_recv()
        lanes = slice(kind * (width // 2), (kind + 1) * (width // 2))
        mine[:, lanes] += first_got[kind, 0].astype(full) + second_got[kind].astype(full)
    unit, scale = units(0)
    unit_grad = mine[...] * gain
    tokens_grad[...] = residual_grad[...] + scale * (
        unit_grad - unit * jnp.mean(unit_grad * unit, axis=1, keepdims=True)
    )
    for k in range(3):
        m_copy(2, k).wait_recv()
        total += tally_got[4 + k]
    small_sum[...] = total
    for m in range(4):
        core_copy(m).wait_send()
        for k in range(3):
            z_copy(m, k + 1).wait_send()
            a_copy(m, k).wait()
    for kind in range(2):
        for which in range(3):
            n_copy(kind, which).wait_send()
    for stage, amount in ((0, 3), (1, 1), (2, 3)):
        for k in range(amount):
            m_copy(stage, k).wait_send()


def finish_grads(all_tokens, dqkv, cols, att_full, aog_cols, residual_grad, params, small, bias_grad):
    rows, width = residual_grad.shape
    shard = cols.shape[2]
    slim = width // 32
    low, full = jnp.bfloat16, jnp.float32
    vmem = pl.BlockSpec(memory_space=pltpu.VMEM)
    dma = pltpu.SemaphoreType.DMA
    return pl.pallas_call(
        finish_kernel,
        out_shape=(jax.ShapeDtypeStruct((rows, width), full),)
        + (jax.ShapeDtypeStruct((slim, width), full),) * 4
        + (jax.ShapeDtypeStruct((16, width), full),),
        in_specs=[vmem] * 9,
        out_specs=(vmem,) * 6,
        scratch_shapes=[
            pltpu.VMEM((2, 4, 4, shard // 2, shard), low),
            pltpu.VMEM((4, 4, shard // 2, shard), low),
            pltpu.VMEM((4, 4, shard // 2, shard), low),
            pltpu.VMEM((3, 4, shard // 2, shard), low),
            pltpu.VMEM((4, shard // 2, shard), full),
            pltpu.VMEM((4, 2, rows, width // 2), low),
            pltpu.VMEM((2, 2, rows, width // 2), low),
            pltpu.VMEM((2, rows, width // 2), low),
            pltpu.VMEM((rows, width), full),
            pltpu.VMEM((4 * rows, width), low),
            pltpu.VMEM((3, 16, width), full),
            pltpu.VMEM((7, 16, width), full),
            dma((4,)), dma((4,)), dma((4, 3)), dma((4, 3)), dma((4, 3)), dma((4, 3)),
            dma((2, 3)), dma((2, 3)), dma((7,)), dma((7,)),
        ],
        compiler_params=pltpu.CompilerParams(
            collective_id=5, has_side_effects=True, vmem_limit_bytes=VMEM_LIMIT
        ),
        cost_estimate=pl.CostEstimate(flops=60 * rows * width * shard, bytes_accessed=14 << 20, transcendentals=0),
        name="finish_grads",
    )(all_tokens, dqkv, cols, att_full, aog_cols, residual_grad, params, small, bias_grad)


def per_device_kernels(
    tokens, cotangent, expert_ids, segment_lengths, segment_parents, attention_gain,
    query_weight, key_weight, value_weight, output_weight, bias_table, feedforward_gain,
    router_weight, gate_weight, up_weight, down_weight,
):
    place = lax.axis_index(EXPERT) * lax.axis_size(SEQ) + lax.axis_index(SEQ)
    count = lax.axis_size(EXPERT) * lax.axis_size(SEQ)
    rows = tokens.shape[0]
    output_full = lax.all_gather(output_weight, BOTH, axis=0, tiled=True)

    def spread(values):
        length = values.shape[-1]
        lane = jnp.arange(count * length, dtype=jnp.int32) // length
        wide = jnp.where(lane == place, jnp.tile(values, (1, count)), jnp.zeros((), values.dtype))
        return jnp.pad(wide, ((0, 0), (0, D - wide.shape[1])))

    misc = jnp.concatenate([
        spread(attention_gain[None]), spread(feedforward_gain[None]), spread(bias_table[None]),
        jnp.zeros((5, D), jnp.bfloat16), spread(router_weight.T),
    ], axis=0)
    all_tokens, qkv, cols, params = project(tokens, query_weight, key_weight, value_weight, misc)
    attended = attend(segment_lengths, segment_parents, qkv, params)
    attended_full = lax.all_gather(attended, SEQ, axis=1, tiled=True)
    ids_row = expert_ids.T
    send_rows, grad_rows, residual = dispatch(
        attended, output_full, tokens, cotangent, params, expert_ids, ids_row
    )
    returned, grad_back, gate_term, up_term, down_term = experts(
        send_rows, grad_rows, gate_weight[0], up_weight[0], down_weight[0]
    )
    layer_out, residual_grad, attended_grad, out_grad_cols, small = combine(
        returned, grad_back, residual, cotangent, output_full, params, expert_ids, ids_row
    )
    dqkv, bias_grad = attend_back(segment_lengths, segment_parents, qkv, params, attended_grad)
    tokens_grad, dwq, dwk, dwv, dwo, totals = finish_grads(
        all_tokens, dqkv, cols, attended_full, out_grad_cols, residual_grad, params, small, bias_grad
    )

    def own(values, length):
        return lax.dynamic_slice_in_dim(values, place * length, length, values.ndim - 1)

    slim = D // count
    return (
        layer_out,
        tokens_grad,
        own(totals[0], slim),
        dwq,
        dwk,
        dwv,
        dwo,
        own(totals[2], BUCKETS * HEADS // count),
        own(totals[1], slim),
        own(totals[8:16], slim).T,
        gate_term[None],
        up_term[None],
        down_term[None],
        jnp.sqrt(totals[3, 0:2] / (rows * count * D)),
    )


def per_device_general(
    tokens,
    cotangent,
    expert_ids,
    segment_lengths,
    segment_parents,
    attention_gain,
    query_weight,
    key_weight,
    value_weight,
    output_weight,
    bias_table,
    feedforward_gain,
    router_weight,
    gate_weight,
    up_weight,
    down_weight,
):
    seq_count = lax.axis_size(SEQ)
    seq_place = lax.axis_index(SEQ)
    all_count = lax.axis_size(EXPERT) * seq_count
    row_count = tokens.shape[0]
    experts = lax.axis_size(EXPERT) * gate_weight.shape[0]
    capacity = 10 * row_count // (4 * experts)
    score_scale = HDIM ** (-0.5)
    gathered = (
        lax.all_gather(attention_gain, BOTH, axis=0, tiled=True),
        lax.all_gather(query_weight, BOTH, axis=0, tiled=True),
        lax.all_gather(key_weight, BOTH, axis=0, tiled=True),
        lax.all_gather(value_weight, BOTH, axis=0, tiled=True),
        lax.all_gather(output_weight, BOTH, axis=0, tiled=True),
        lax.all_gather(bias_table, BOTH, axis=0, tiled=True),
        lax.all_gather(feedforward_gain, BOTH, axis=0, tiled=True),
        lax.all_gather(router_weight, BOTH, axis=0, tiled=True),
    )
    gain_one, query_full, key_full, value_full, output_full, bias_flat, gain_two, router_full = (
        gathered
    )
    bias_grid = bias_flat.reshape(BUCKETS, HEADS)
    starts, before, reaches = tree_tables(segment_lengths[0], segment_parents[0])
    own_rows = seq_place * row_count + jnp.arange(row_count, dtype=jnp.int32)
    own_meta = token_info(own_rows, starts, before, reaches)
    tokens_float = tokens.astype(jnp.float32)
    scale_one = norm_factor(tokens_float)
    unit_one = tokens_float * scale_one
    normed_one = (unit_one * gain_one.astype(jnp.float32)).astype(jnp.bfloat16)
    queries = (
        jnp.dot(normed_one, query_full, preferred_element_type=jnp.float32)
        .astype(jnp.bfloat16)
        .reshape(row_count, HEADS, HDIM)
    )
    keys_own = (
        jnp.dot(normed_one, key_full, preferred_element_type=jnp.float32)
        .astype(jnp.bfloat16)
        .reshape(row_count, HEADS, HDIM)
    )
    values_own = (
        jnp.dot(normed_one, value_full, preferred_element_type=jnp.float32)
        .astype(jnp.bfloat16)
        .reshape(row_count, HEADS, HDIM)
    )
    row_peak = jnp.full((HEADS, row_count), NEGATIVE, jnp.float32)
    key_piece = lax.all_gather(keys_own, SEQ, axis=0, tiled=True)
    value_piece = lax.all_gather(values_own, SEQ, axis=0, tiled=True)
    key_rows = jnp.arange(key_piece.shape[0], dtype=jnp.int32)
    visible, onehot, pair_bias = pair_terms(
        own_meta, token_info(key_rows, starts, before, reaches), own_rows, key_rows, bias_grid
    )
    scores = masked_scores(queries, key_piece, visible, pair_bias)
    new_peak = jnp.maximum(row_peak, jnp.max(scores, axis=-1))
    expo = jnp.exp(scores - new_peak[:, :, None])
    row_total = jnp.sum(expo, axis=-1)
    summed = jnp.einsum(
        SPEC_2, expo.astype(jnp.bfloat16), value_piece, preferred_element_type=jnp.float32
    )
    row_peak, row_total, summed = (new_peak, row_total, summed)
    log_total = row_peak + jnp.log(row_total)
    attended_float = summed / jnp.transpose(row_total)[:, :, None]
    attended = attended_float.astype(jnp.bfloat16).reshape(row_count, D)
    residual = tokens_float + jnp.dot(attended, output_full, preferred_element_type=jnp.float32)
    scale_two = norm_factor(residual)
    unit_two = residual * scale_two
    normed_two = (unit_two * gain_two.astype(jnp.float32)).astype(jnp.bfloat16)
    router_prob = jax.nn.softmax(
        jnp.dot(normed_two, router_full, preferred_element_type=jnp.float32), axis=-1
    )
    pick_hot = (
        expert_ids[:, :, None] == jnp.arange(experts, dtype=jnp.int32)[None, None, :]
    ).astype(jnp.float32)
    chosen = jnp.sum(pick_hot * router_prob[:, None, :], axis=2)
    chosen_total = jnp.sum(chosen, axis=1, keepdims=True)
    gate_shares = chosen / chosen_total
    hot_int = pick_hot.astype(jnp.int32).reshape(row_count * 2, experts)
    earlier = jnp.cumsum(hot_int, axis=0) - hot_int
    slot_number = jnp.sum(earlier * hot_int, axis=1).reshape(row_count, 2)
    kept_copy = slot_number < capacity
    kept_float = kept_copy.astype(jnp.float32)
    target = jnp.where(kept_copy, expert_ids * capacity + slot_number, experts * capacity)
    copy_ids = jnp.arange(row_count * 2, dtype=jnp.int32)
    slot_copy = (
        jnp.full((experts * capacity + 1,), row_count * 2, jnp.int32)
        .at[target.reshape(-1)]
        .set(copy_ids)[: experts * capacity]
    )
    fetch_index = jnp.minimum(target, experts * capacity - 1).reshape(-1)
    token_of_slot = jnp.where(slot_copy < row_count * 2, slot_copy // 2, row_count)
    padded = jnp.concatenate([normed_two, jnp.zeros((1, D), jnp.bfloat16)], axis=0)
    send_rows = padded[token_of_slot].reshape(experts, capacity, D)
    expert_in = lax.all_to_all(send_rows, EXPERT, split_axis=0, concat_axis=1, tiled=True)[0]
    gate_piece = lax.all_gather(gate_weight, SEQ, axis=1, tiled=True)
    up_piece = lax.all_gather(up_weight, SEQ, axis=1, tiled=True)
    down_piece = lax.all_gather(down_weight, SEQ, axis=1, tiled=True)
    gate_pre = jnp.einsum(SPEC_3, expert_in, gate_piece[0], preferred_element_type=jnp.float32)
    up_pre = jnp.einsum(SPEC_3, expert_in, up_piece[0], preferred_element_type=jnp.float32)
    active = (gelu_tanh(gate_pre) * up_pre).astype(jnp.bfloat16)
    expert_sum = jnp.dot(active, down_piece[0], preferred_element_type=jnp.float32)
    returned = lax.all_to_all(
        expert_sum.astype(jnp.bfloat16)[None], EXPERT, split_axis=1, concat_axis=0, tiled=True
    )
    picked = (
        returned.reshape(experts * capacity, D)[fetch_index]
        .reshape(row_count, 2, D)
        .astype(jnp.float32)
    )
    weighted = gate_shares * kept_float
    mixture = jnp.sum(weighted[:, :, None] * picked, axis=1)
    layer_out = (residual + mixture).astype(jnp.bfloat16)
    local_sums = jnp.stack([jnp.sum(residual * residual), jnp.sum(mixture * mixture)])
    again = (
        lax.all_gather(attention_gain, BOTH, axis=0, tiled=True),
        lax.all_gather(query_weight, BOTH, axis=0, tiled=True),
        lax.all_gather(key_weight, BOTH, axis=0, tiled=True),
        lax.all_gather(value_weight, BOTH, axis=0, tiled=True),
        lax.all_gather(output_weight, BOTH, axis=0, tiled=True),
        lax.all_gather(bias_table, BOTH, axis=0, tiled=True),
        lax.all_gather(feedforward_gain, BOTH, axis=0, tiled=True),
        lax.all_gather(router_weight, BOTH, axis=0, tiled=True),
    )
    gain_one, query_full, key_full, value_full, output_full, bias_flat, gain_two, router_full = (
        again
    )
    bias_grid = bias_flat.reshape(BUCKETS, HEADS)
    grad_out = cotangent.astype(jnp.float32)
    copy_grad = (
        (weighted[:, :, None] * grad_out[:, None, :]).astype(jnp.bfloat16).reshape(row_count * 2, D)
    )
    copy_padded = jnp.concatenate([copy_grad, jnp.zeros((1, D), jnp.bfloat16)], axis=0)
    grad_send = copy_padded[slot_copy].reshape(experts, capacity, D)
    grad_in = lax.all_to_all(grad_send, EXPERT, split_axis=0, concat_axis=1, tiled=True)[0]
    gate_piece = lax.all_gather(gate_weight, SEQ, axis=1, tiled=True)
    up_piece = lax.all_gather(up_weight, SEQ, axis=1, tiled=True)
    down_piece = lax.all_gather(down_weight, SEQ, axis=1, tiled=True)
    gate_pre = jnp.einsum(SPEC_3, expert_in, gate_piece[0], preferred_element_type=jnp.float32)
    up_pre = jnp.einsum(SPEC_3, expert_in, up_piece[0], preferred_element_type=jnp.float32)
    gelu_out, gelu_pull = jax.vjp(gelu_tanh, gate_pre)
    act_grad = jnp.einsum(SPEC_3, grad_in, down_piece[0], preferred_element_type=jnp.float32)
    gate_back = gelu_pull(act_grad * up_pre)[0].astype(jnp.bfloat16)
    up_back = (act_grad * gelu_out).astype(jnp.bfloat16)
    input_grad = jnp.dot(gate_back, gate_piece[0], preferred_element_type=jnp.float32) + jnp.dot(
        up_back, up_piece[0], preferred_element_type=jnp.float32
    )
    active = (gelu_out * up_pre).astype(jnp.bfloat16)
    input_grad, gate_backs, up_backs, actives = (input_grad, gate_back, up_back, active)
    grad_back = lax.all_to_all(
        input_grad.astype(jnp.bfloat16)[None], EXPERT, split_axis=1, concat_axis=0, tiled=True
    )
    expert_back = (
        grad_back.reshape(experts * capacity, D)[fetch_index]
        .reshape(row_count, 2, D)
        .astype(jnp.float32)
    )
    normed_two_grad = jnp.sum(expert_back * kept_float[:, :, None], axis=1)
    expert_grads = lax.psum_scatter(
        jnp.stack(
            [
                jnp.einsum(SPEC_4, gate_backs, expert_in, preferred_element_type=jnp.float32),
                jnp.einsum(SPEC_4, up_backs, expert_in, preferred_element_type=jnp.float32),
                jnp.einsum(SPEC_4, actives, grad_in, preferred_element_type=jnp.float32),
            ],
            axis=1,
        ).astype(jnp.bfloat16),
        SEQ,
        scatter_dimension=0,
        tiled=True,
    ).astype(jnp.float32)
    share_grad = jnp.sum(grad_out[:, None, :] * picked, axis=2) * kept_float
    chosen_grad = (
        share_grad - jnp.sum(gate_shares * share_grad, axis=1, keepdims=True)
    ) / chosen_total
    prob_grad = jnp.sum(pick_hot * chosen_grad[:, :, None], axis=1)
    logit_grad = router_prob * (prob_grad - jnp.sum(router_prob * prob_grad, axis=1, keepdims=True))
    router_float = router_full.astype(jnp.float32)
    router_term = jnp.einsum(
        SPEC_5, normed_two.astype(jnp.float32), logit_grad, precision=lax.Precision.HIGHEST
    )
    normed_two_grad = normed_two_grad + jnp.einsum(
        SPEC_6, logit_grad, router_float, precision=lax.Precision.HIGHEST
    )
    gain_two_term = jnp.sum(normed_two_grad * unit_two, axis=0)
    unit_grad_two = normed_two_grad * gain_two.astype(jnp.float32)
    residual_grad = grad_out + scale_two * (
        unit_grad_two - unit_two * jnp.mean(unit_grad_two * unit_two, axis=-1, keepdims=True)
    )
    attention_out_grad = residual_grad.astype(jnp.bfloat16)
    output_term = jnp.einsum(
        SPEC_5, attended, attention_out_grad, preferred_element_type=jnp.float32
    )
    attended_grad = (
        jnp.einsum(SPEC_6, attention_out_grad, output_full, preferred_element_type=jnp.float32)
        .astype(jnp.bfloat16)
        .reshape(row_count, HEADS, HDIM)
    )
    row_delta = jnp.transpose(jnp.sum(attended_grad.astype(jnp.float32) * attended_float, axis=-1))
    total_all, delta_all = (
        lax.all_gather(log_total, SEQ, axis=1, tiled=True),
        lax.all_gather(row_delta, SEQ, axis=1, tiled=True),
    )
    key_piece = lax.all_gather(keys_own, SEQ, axis=0, tiled=True)
    value_piece = lax.all_gather(values_own, SEQ, axis=0, tiled=True)
    key_rows = jnp.arange(key_piece.shape[0], dtype=jnp.int32)
    visible, onehot, pair_bias = pair_terms(
        own_meta, token_info(key_rows, starts, before, reaches), own_rows, key_rows, bias_grid
    )
    scores = masked_scores(queries, key_piece, visible, pair_bias)
    soft_weights = jnp.exp(scores - log_total[:, :, None])
    dprob = jnp.einsum(
        SPEC_1, attended_grad, value_piece, preferred_element_type=jnp.float32
    )
    score_grad = (soft_weights * (dprob - row_delta[:, :, None])).astype(jnp.bfloat16)
    query_acc = jnp.einsum(
        SPEC_2, score_grad, key_piece, preferred_element_type=jnp.float32
    )
    bias_acc = jnp.einsum(SPEC_7, onehot, score_grad, preferred_element_type=jnp.float32)
    query_acc, bias_acc = (query_acc, bias_acc)
    query_piece = lax.all_gather(queries, SEQ, axis=0, tiled=True)
    grad_piece = lax.all_gather(attended_grad, SEQ, axis=0, tiled=True)
    piece_rows = query_piece.shape[0]
    query_rows = jnp.arange(piece_rows, dtype=jnp.int32)
    visible, onehot, pair_bias = pair_terms(
        token_info(query_rows, starts, before, reaches), own_meta, query_rows, own_rows, bias_grid
    )
    scores = masked_scores(query_piece, keys_own, visible, pair_bias)
    soft_weights = jnp.exp(scores - total_all[:, :, None])
    value_acc = jnp.einsum(
        SPEC_8,
        soft_weights.astype(jnp.bfloat16),
        grad_piece,
        preferred_element_type=jnp.float32,
    )
    dprob = jnp.einsum(SPEC_1, grad_piece, values_own, preferred_element_type=jnp.float32)
    score_grad = (soft_weights * (dprob - delta_all[:, :, None])).astype(jnp.bfloat16)
    key_acc = jnp.einsum(
        SPEC_8, score_grad, query_piece, preferred_element_type=jnp.float32
    )
    key_acc, value_acc = (key_acc, value_acc)
    query_back = (query_acc * score_scale).astype(jnp.bfloat16).reshape(row_count, D)
    key_back = (key_acc * score_scale).astype(jnp.bfloat16).reshape(row_count, D)
    value_back = value_acc.astype(jnp.bfloat16).reshape(row_count, D)
    query_term = jnp.einsum(SPEC_5, normed_one, query_back, preferred_element_type=jnp.float32)
    key_term = jnp.einsum(SPEC_5, normed_one, key_back, preferred_element_type=jnp.float32)
    value_term = jnp.einsum(SPEC_5, normed_one, value_back, preferred_element_type=jnp.float32)
    normed_one_grad = jnp.einsum(
        SPEC_6, query_back, query_full, preferred_element_type=jnp.float32
    )
    normed_one_grad = normed_one_grad + jnp.einsum(
        SPEC_6, key_back, key_full, preferred_element_type=jnp.float32
    )
    normed_one_grad = normed_one_grad + jnp.einsum(
        SPEC_6, value_back, value_full, preferred_element_type=jnp.float32
    )
    gain_one_term = jnp.sum(normed_one_grad * unit_one, axis=0)
    unit_grad_one = normed_one_grad * gain_one.astype(jnp.float32)
    tokens_grad = residual_grad + scale_one * (
        unit_grad_one - unit_one * jnp.mean(unit_grad_one * unit_one, axis=-1, keepdims=True)
    )
    stats_term = jnp.broadcast_to(local_sums[None, :], (all_count, 2))
    reduced = (
        lax.psum_scatter(gain_one_term, BOTH, scatter_dimension=0, tiled=True),
        lax.psum_scatter(query_term, BOTH, scatter_dimension=0, tiled=True),
        lax.psum_scatter(key_term, BOTH, scatter_dimension=0, tiled=True),
        lax.psum_scatter(value_term, BOTH, scatter_dimension=0, tiled=True),
        lax.psum_scatter(output_term, BOTH, scatter_dimension=0, tiled=True),
        lax.psum_scatter(
            bias_acc.reshape(BUCKETS * HEADS), BOTH, scatter_dimension=0, tiled=True
        ),
        lax.psum_scatter(gain_two_term, BOTH, scatter_dimension=0, tiled=True),
        lax.psum_scatter(router_term, BOTH, scatter_dimension=0, tiled=True),
        lax.psum_scatter(stats_term, BOTH, scatter_dimension=0, tiled=True),
    )
    roots = jnp.sqrt(reduced[8][0] / (row_count * all_count * D))
    return (
        layer_out,
        tokens_grad,
        reduced[0],
        reduced[1],
        reduced[2],
        reduced[3],
        reduced[4],
        reduced[5],
        reduced[6],
        reduced[7],
        expert_grads[None, :, 0, :],
        expert_grads[None, :, 1, :],
        expert_grads[None, :, 2, :],
        roots,
    )


def solution(mesh):
    kernels_fit = mesh.shape[EXPERT] == len(ORDER) and mesh.shape[SEQ] == 4
    return jax.shard_map(
        per_device_kernels if kernels_fit else per_device_general,
        mesh=mesh,
        in_specs=(
            P(BOTH, None),
            P(BOTH, None),
            P(BOTH, None),
            P(EXPERT, None),
            P(EXPERT, None),
            P(BOTH),
            P(BOTH, None),
            P(BOTH, None),
            P(BOTH, None),
            P(BOTH, None),
            P(BOTH),
            P(BOTH),
            P(BOTH, None),
            P(EXPERT, SEQ, None),
            P(EXPERT, SEQ, None),
            P(EXPERT, SEQ, None),
        ),
        out_specs=(
            P(BOTH, None),
            P(BOTH, None),
            P(BOTH),
            P(BOTH, None),
            P(BOTH, None),
            P(BOTH, None),
            P(BOTH, None),
            P(BOTH),
            P(BOTH),
            P(BOTH, None),
            P(EXPERT, SEQ, None),
            P(EXPERT, SEQ, None),
            P(EXPERT, SEQ, None),
            P(),
        ),
        check_vma=False,
    )
```

```python
import math

import jax
import jax.numpy as jnp
from jax import lax
from jax.experimental import pallas as pl
from jax.experimental.pallas import tpu as pltpu
from jax.sharding import PartitionSpec as P

SPEC_0 = "qkb,bh->hqk"
SPEC_1 = "qhd,khd->hqk"
SPEC_2 = "hqk,khd->qhd"
SPEC_3 = "rd,fd->rf"
SPEC_4 = "rf,rd->fd"
SPEC_5 = "rd,re->de"
SPEC_6 = "re,de->rd"
SPEC_7 = "qkb,hqk->bh"
SPEC_8 = "hqk,qhd->khd"
MESH = pl.DeviceIdType.MESH
VMEM_LIMIT = 62 << 20
EXPERT, SEQ = "expert", "seq"
BOTH = (EXPERT, SEQ)

D = 1024
HEADS = 16
HDIM = 64
BUCKETS = 32
MAXDIST = 128


EPSILON = 1e-06
NEGATIVE = -1e30


def norm_factor(values):
    return lax.rsqrt(jnp.mean(values * values, axis=-1, keepdims=True) + EPSILON)


def gelu_tanh(values):
    return jax.nn.gelu(values, approximate=True)


def bucket_of(distance):
    exact_span = BUCKETS // 2
    above = jnp.zeros(distance.shape, jnp.int32)
    for number in range(exact_span):
        threshold = int(math.ceil(exact_span * (MAXDIST / exact_span) ** (number / exact_span)))
        above = above + (distance >= threshold).astype(jnp.int32)
    return jnp.where(distance < exact_span, distance, exact_span - 1 + above)


def tree_tables(lengths, parents):
    ordinal = jnp.arange(lengths.shape[0], dtype=jnp.int32)
    starts = jnp.cumsum(lengths) - lengths

    def chase(number, running):
        current, reaches = running
        current = jnp.sum(
            jnp.where(current[:, None] == ordinal[None, :], parents[None, :], 0), axis=1
        )
        reaches = jnp.maximum(reaches, (current[:, None] == ordinal[None, :]).astype(jnp.int32))
        return (current, reaches)

    begin = (ordinal, (ordinal[:, None] == ordinal[None, :]).astype(jnp.int32))
    unused, reaches = lax.fori_loop(0, lengths.shape[0], chase, begin)
    before = jnp.sum(reaches * lengths[None, :], axis=1) - lengths
    return (starts, before, reaches)


def token_info(token_rows, starts, before, reaches):
    ordinal = jnp.arange(starts.shape[0], dtype=jnp.int32)
    segment = jnp.sum((token_rows[:, None] >= starts[None, :]).astype(jnp.int32), axis=1) - 1
    member = segment[:, None] == ordinal[None, :]
    position = token_rows + jnp.sum(jnp.where(member, (before - starts)[None, :], 0), axis=1)
    lineage = jnp.sum(jnp.where(member[:, :, None], reaches[None, :, :], 0), axis=1)
    return (member.astype(jnp.float32), position, lineage.astype(jnp.float32))


def pair_terms(query_meta, key_meta, query_rows, key_rows, bias_grid):
    visible = jnp.dot(query_meta[2], key_meta[0].T, preferred_element_type=jnp.float32) > 0.5
    visible = visible & (key_rows[None, :] <= query_rows[:, None])
    distance = jnp.maximum(query_meta[1][:, None] - key_meta[1][None, :], 0)
    onehot = (
        bucket_of(distance)[:, :, None] == jnp.arange(BUCKETS, dtype=jnp.int32)[None, None, :]
    ).astype(jnp.bfloat16)
    pair_bias = jnp.einsum(SPEC_0, onehot, bias_grid, preferred_element_type=jnp.float32)
    return (visible, onehot, pair_bias)


def masked_scores(query_block, key_block, visible, pair_bias):
    scores = (
        jnp.einsum(SPEC_1, query_block, key_block, preferred_element_type=jnp.float32)
        * HDIM ** (-0.5)
        + pair_bias
    )
    return jnp.where(visible[None], scores, NEGATIVE)


def remote(src, dst, send, recv, peer):
    return pltpu.make_async_remote_copy(
        src_ref=src, dst_ref=dst, send_sem=send, recv_sem=recv,
        device_id=peer, device_id_type=MESH,
    )


def contract(left, right, dims):
    return lax.dot_general(left, right, (dims, ((), ())), preferred_element_type=jnp.float32)


def gelu_parts(values):
    root = 0.7978845608028654
    square = values * values
    swing = jnp.tanh(root * values * (1.0 + 0.044715 * square))
    half = 0.5 * (1.0 + swing)
    slope = half + 0.5 * values * (1.0 - swing * swing) * (root * (1.0 + 3 * 0.044715 * square))
    return values * half, slope


ORDER = (0, 1, 2, 3, 4, 5, 6, 7)
UNITS = (
    (0, 0), (1, 0), (2, 0), (0, 1), (3, 0), (1, 1), (2, 1), (0, 2),
    (3, 1), (1, 2), (2, 2), (0, 3), (3, 2), (1, 3), (2, 3), (3, 3),
)


def expert_kernel(
    xs, gs, wg_far, wu_far, wd_far, ret_o, ret_b, dwg, dwu, dwd,
    xr, gr, act, gb, ub, po, pb, ro, rb, ro2, rb2, stage, wg, wu, wd,
    in_send, in_recv, hop_send, hop_recv, rs_send, rs_recv, out_send, out_recv, stage_sem, load_sem,
):
    e = lax.axis_index(EXPERT)
    s = lax.axis_index(SEQ)
    cap = xs.shape[0] // 8
    near_x, near_y = (e, s ^ 1), (e, s ^ 2)
    loads = [
        pltpu.make_async_copy(src, dst, load_sem.at[k])
        for k, (src, dst) in enumerate(((wg_far, wg), (wu_far, wu), (wd_far, wd)))
    ]
    for load in loads:
        load.start()
    barrier = pltpu.get_barrier_semaphore()
    peers = [near_x, near_y] + [(e ^ d, s) for d in range(1, 8)]
    for peer in peers:
        pl.semaphore_signal(barrier, inc=1, device_id=peer, device_id_type=MESH)
    pl.semaphore_wait(barrier, len(peers))

    def block(index):
        return pl.ds(pl.multiple_of(index * cap, 16), cap)

    tensors = ((xs, xr), (gs, gr))

    def entry(kind, place):
        src, dst = tensors[kind]
        d = ORDER[place]
        return remote(src.at[block(e ^ d)], dst.at[0, place], in_send.at[kind, place],
                      in_recv.at[kind, place], (e ^ d, s))

    def hop(kind, which, pair):
        buf = tensors[kind][1]
        two = pl.ds(2 * pair, 2)
        if which == 0:
            src, dst, peer = buf.at[0, two], buf.at[1, two], near_x
        elif which == 1:
            src, dst, peer = buf.at[0, two], buf.at[2, two], near_y
        elif kind == 0:
            src, dst, peer = buf.at[1, two], buf.at[3, two], near_y
        else:
            src, dst, peer = buf.at[2, two], buf.at[3, two], near_x
        return remote(src, dst, hop_send.at[kind, which, pair], hop_recv.at[kind, which, pair], peer)

    def rs(kind, which, c):
        part, one, two = ((po, ro, ro2), (pb, rb, rb2))[kind]
        first, second = ((near_x, near_y), (near_y, near_x))[kind]
        mine = 1 + kind
        if which == 0:
            src, dst, peer = part.at[mine, c], one.at[0, c], first
        elif which == 1:
            src, dst, peer = part.at[3, c], one.at[1, c], first
        else:
            src, dst, peer = part.at[2 - kind, c], two.at[c], second
        return remote(src, dst, rs_send.at[kind, which, c], rs_recv.at[kind, which, c], peer)

    def back(kind, place):
        part = (po, pb)[kind]
        ret = (ret_o, ret_b)[kind]
        c, i = place // 2, place % 2
        return remote(part.at[0, c, pl.ds(i * cap, cap)], ret.at[block(e)],
                      out_send.at[kind, place], out_recv.at[kind, place], (e ^ ORDER[place], s))

    def start_entries(pair):
        for kind in range(2):
            for place in (2 * pair, 2 * pair + 1):
                if ORDER[place]:
                    entry(kind, place).start()

    def forward_pair(pair):
        for kind in range(2):
            for place in (2 * pair, 2 * pair + 1):
                if ORDER[place]:
                    entry(kind, place).wait_recv()
            hop(kind, 0, pair).start()
            hop(kind, 1, pair).start()

    def forward_corner(pair):
        hop(0, 0, pair).wait_recv()
        hop(0, 2, pair).start()
        hop(1, 1, pair).wait_recv()
        hop(1, 2, pair).start()

    def start_sums(pair):
        for which in (1, 0):
            for kind in range(2):
                rs(kind, which, pair).start()

    def add_second(pair):
        for kind in range(2):
            rs(kind, 1, pair).wait_recv()
            part, one = ((po, ro), (pb, rb))[kind]
            group = 2 - kind
            part[group, pair] = (
                part[group, pair].astype(jnp.float32) + one[1, pair].astype(jnp.float32)
            ).astype(jnp.bfloat16)
            rs(kind, 2, pair).start()

    def finish(pair):
        for kind in range(2):
            rs(kind, 0, pair).wait_recv()
            rs(kind, 2, pair).wait_recv()
            part, one, two = ((po, ro, ro2), (pb, rb, rb2))[kind]
            part[0, pair] = (
                part[0, pair].astype(jnp.float32) + one[0, pair].astype(jnp.float32) + two[pair].astype(jnp.float32)
            ).astype(jnp.bfloat16)
            for i in range(2):
                if ORDER[2 * pair + i]:
                    back(kind, 2 * pair + i).start()
                else:
                    (ret_o, ret_b)[kind][block(e), :] = part[0, pair, i * cap:(i + 1) * cap]

    start_entries(0)
    start_entries(1)
    start_entries(2)
    for src, dst in tensors:
        dst[0, 0] = src[block(e), :]

    rows = 2 * cap

    def unit(u, carry):
        q, c = jnp.int32(0), jnp.int32(0)
        for k, (whose, pair) in enumerate(UNITS):
            q, c = jnp.where(u == k, whose, q), jnp.where(u == k, pair, c)

        for k, (whose, pair) in enumerate(UNITS):
            @pl.when(u == k)
            def _():
                if k == 0:
                    forward_pair(0)
                    for load in loads:
                        load.wait()
                if (whose, pair) in ((1, 0), (3, 0), (3, 1)):
                    ahead = {(1, 0): 1, (3, 0): 2, (3, 1): 3}[whose, pair]
                    forward_pair(ahead)
                    if ahead == 1:
                        start_entries(3)
                    forward_corner(ahead - 1)
                if (whose, pair) == (3, 2):
                    forward_corner(3)
                if whose == 1:
                    hop(1, 0, pair).wait_recv()
                if whose == 2:
                    hop(0, 1, pair).wait_recv()
                if whose == 3:
                    hop(0, 2, pair).wait_recv()
                    hop(1, 2, pair).wait_recv()

        x = xr[q, pl.ds(2 * c, 2)].reshape(rows, xs.shape[1])
        g = gr[q, pl.ds(2 * c, 2)].reshape(rows, xs.shape[1])
        gate = contract(x, wg[...], ((1,), (1,)))
        up = contract(x, wu[...], ((1,), (1,)))
        ag = contract(g, wd[...], ((1,), (1,)))
        value, slope = gelu_parts(gate)
        active = (value * up).astype(jnp.bfloat16)
        gate_back = (ag * up * slope).astype(jnp.bfloat16)
        up_back = (ag * value).astype(jnp.bfloat16)
        act[q, c] = active
        gb[q, c] = gate_back
        ub[q, c] = up_back
        po[q, c] = contract(active, wd[...], ((1,), (0,))).astype(jnp.bfloat16)
        pb[q, c] = (
            contract(gate_back, wg[...], ((1,), (0,))) + contract(up_back, wu[...], ((1,), (0,)))
        ).astype(jnp.bfloat16)

        for k, (whose, pair) in enumerate(UNITS):
            if whose == 3 and pair >= 2:
                @pl.when(u == k)
                def _():
                    start_sums(pair)
        return carry

    lax.fori_loop(0, len(UNITS), unit, 0)

    def grads(left, right, dst):
        def part(u):
            q, c = lax.rem(u, 4), u // 4
            return contract(left[q, pl.ds(2 * c, 2)].reshape(2 * rows, wg.shape[0]),
                            right[q, pl.ds(4 * c, 4)].reshape(2 * rows, xs.shape[1]), ((0,), (0,)))

        def more(u, carry):
            stage[...] += part(u)
            return carry

        stage[...] = part(0)
        lax.fori_loop(1, 8, more, 0)
        done = pltpu.make_async_copy(stage, dst, stage_sem)
        done.start()
        return done

    add_second(2)
    start_sums(1)
    done = grads(gb, xr, dwg)
    add_second(3)
    start_sums(0)
    finish(2)
    done.wait()
    done = grads(ub, xr, dwu)
    add_second(1)
    finish(3)
    done.wait()
    done = grads(act, gr, dwd)
    add_second(0)
    finish(1)
    finish(0)
    done.wait()

    for kind in range(2):
        for place in range(8):
            if ORDER[place]:
                entry(kind, place).wait_send()
                back(kind, place).wait()
        for which in range(3):
            for pair in range(4):
                hop(kind, which, pair).wait_send()
                rs(kind, which, pair).wait_send()


def experts(send_rows, grad_rows, gate_weight, up_weight, down_weight):
    rows, width = send_rows.shape
    units = gate_weight.shape[0]
    cap = rows // 8
    low, full = jnp.bfloat16, jnp.float32
    vmem = pl.BlockSpec(memory_space=pltpu.VMEM)
    hbm = pl.BlockSpec(memory_space=pl.ANY)
    dma = pltpu.SemaphoreType.DMA
    return pl.pallas_call(
        expert_kernel,
        out_shape=(
            jax.ShapeDtypeStruct((rows, width), low),
            jax.ShapeDtypeStruct((rows, width), low),
        ) + (jax.ShapeDtypeStruct((units, width), full),) * 3,
        in_specs=[vmem] * 2 + [hbm] * 3,
        out_specs=(vmem, vmem, hbm, hbm, hbm),
        scratch_shapes=[
            pltpu.VMEM((4, 8, cap, width), low),
            pltpu.VMEM((4, 8, cap, width), low),
            pltpu.VMEM((4, 4, 2 * cap, units), low),
            pltpu.VMEM((4, 4, 2 * cap, units), low),
            pltpu.VMEM((4, 4, 2 * cap, units), low),
            pltpu.VMEM((4, 4, 2 * cap, width), low),
            pltpu.VMEM((4, 4, 2 * cap, width), low),
            pltpu.VMEM((2, 4, 2 * cap, width), low),
            pltpu.VMEM((2, 4, 2 * cap, width), low),
            pltpu.VMEM((4, 2 * cap, width), low),
            pltpu.VMEM((4, 2 * cap, width), low),
            pltpu.VMEM((units, width), full),
            pltpu.VMEM((units, width), low),
            pltpu.VMEM((units, width), low),
            pltpu.VMEM((units, width), low),
            dma((2, 8)), dma((2, 8)),
            dma((2, 3, 4)), dma((2, 3, 4)),
            dma((2, 3, 4)), dma((2, 3, 4)),
            dma((2, 8)), dma((2, 8)),
            dma, dma((3,)),
        ],
        compiler_params=pltpu.CompilerParams(
            collective_id=1, has_side_effects=True, vmem_limit_bytes=VMEM_LIMIT
        ),
        cost_estimate=pl.CostEstimate(flops=2 * 9 * 4 * rows * units * width, bytes_accessed=20 << 20, transcendentals=4 * rows * units),
        name="experts",
    )(send_rows, grad_rows, gate_weight, up_weight, down_weight)


def greet(peers):
    barrier = pltpu.get_barrier_semaphore()
    for peer in peers:
        pl.semaphore_signal(barrier, inc=1, device_id=peer, device_id_type=MESH)
    pl.semaphore_wait(barrier, len(peers))


def aligned(index, size):
    return pl.ds(pl.multiple_of(index * size, size), size)


ZHOPS = (2, 4, 6)


def segment_scalars(lengths, parents, before_mem, reach_mem):
    count = lengths.shape[1]
    start = jnp.int32(0)
    found = []
    for k in range(count):
        length = lengths[0, k]
        if k == 0:
            before, reach = jnp.int32(0), jnp.int32(1)
        else:
            parent = parents[0, k]
            before = before_mem[parent] + lengths[0, parent]
            reach = reach_mem[parent] | (1 << k)
        before_mem[k] = before
        reach_mem[k] = reach
        found.append((start, before, reach, length))
        start = start + length
    return found


def token_columns(found, ids):
    offset = jnp.zeros(ids.shape, jnp.int32)
    reach = jnp.full(ids.shape, 1, jnp.int32)
    own = jnp.full(ids.shape, 1, jnp.int32)
    for k, (start, before, bits, _) in enumerate(found):
        if k:
            after = ids >= start
            offset = jnp.where(after, before - start, offset)
            reach = jnp.where(after, bits, reach)
            own = jnp.where(after, 1 << k, own)
    return ids + offset, reach, own


LAST = 127


def bias_tables(params, s):
    flat = params[2:3, 0:BUCKETS * HEADS]
    lane = lax.broadcasted_iota(jnp.int32, (8, BUCKETS * HEADS), 1)
    head = lax.broadcasted_iota(jnp.int32, (8, BUCKETS * HEADS), 0)
    heads_here = HEADS // 4
    chosen = jnp.where((lane % HEADS) == s * heads_here + head, jnp.broadcast_to(flat, lane.shape), 0.0)
    entry = lax.broadcasted_iota(jnp.int32, (BUCKETS * HEADS, LAST + 1), 0) // HEADS
    distance = lax.broadcasted_iota(jnp.int32, (BUCKETS * HEADS, LAST + 1), 1)
    hot = jnp.where(entry == bucket_of(distance), 1.0, 0.0)
    table = contract(chosen.astype(jnp.bfloat16), hot.astype(jnp.bfloat16), ((1,), (0,)))
    spot = lax.broadcasted_iota(jnp.int32, table.shape, 1)
    return jnp.where(spot == LAST, NEGATIVE, table)


def pair_index(found, first, rows, count):
    ids = first + lax.broadcasted_iota(jnp.int32, (rows, 1), 0)
    keys = lax.broadcasted_iota(jnp.int32, (1, count), 1)
    place, reach, _ = token_columns(found, ids)
    key_place, _, key_own = token_columns(found, keys)
    seen = ((reach & key_own) != 0) & (keys <= ids)
    return jnp.where(seen, jnp.minimum(place - key_place, LAST - 1), LAST), place, reach


def looked_up(row, index):
    rows, count = index.shape
    table = jnp.broadcast_to(row, (rows, LAST + 1))
    pieces = [
        jnp.take_along_axis(table, index[:, k * 128:(k + 1) * 128], axis=1)
        for k in range(count // 128)
    ]
    return jnp.concatenate(pieces, axis=1)


def routing(residual, params, ids_row, cap):
    rows = residual.shape[0]
    full, low = jnp.float32, jnp.bfloat16
    scale = norm_factor(residual)
    unit = residual * scale
    normed = (unit * params[1:2]).astype(low)
    router = params[8:16]
    logits = contract(normed, router.astype(low), ((1,), (1,)))
    expo = jnp.exp(logits - jnp.max(logits, axis=1, keepdims=True))
    prob = expo / jnp.sum(expo, axis=1, keepdims=True)
    level = lax.broadcasted_iota(jnp.int32, (8, rows), 0)
    hot_row = [jnp.where(ids_row[k:k + 1] == level, 1.0, 0.0).astype(full) for k in range(2)]
    down = lax.broadcasted_iota(jnp.int32, (rows, rows), 0)
    across = lax.broadcasted_iota(jnp.int32, (rows, rows), 1)
    after = jnp.where(down < across, 1.0, 0.0).astype(low)
    earlier = contract((hot_row[0] + hot_row[1]).astype(low), after, ((1,), (0,)))
    slot_row = [jnp.sum(h * earlier, axis=0, keepdims=True) for h in hot_row]
    kept_row = [jnp.where(slot < cap, 1.0, 0.0) for slot in slot_row]
    spot_row = [
        jnp.where(slot_row[k] < cap, ids_row[k:k + 1].astype(full) * cap + slot_row[k], -1.0) for k in range(2)
    ]
    target_row = [spot.astype(jnp.int32) for spot in spot_row]
    columns = jnp.transpose(jnp.concatenate(spot_row + kept_row + [jnp.zeros((4, rows), full)], axis=0))
    target = [columns[:, k:k + 1].astype(jnp.int32) for k in range(2)]
    kept = [columns[:, 2 + k:3 + k] for k in range(2)]
    hot = [jnp.transpose(h) for h in hot_row]
    chosen = [jnp.sum(h * prob, axis=1, keepdims=True) for h in hot]
    chosen_sum = chosen[0] + chosen[1]
    shares = [c / chosen_sum for c in chosen]
    return scale, unit, normed, router, prob, hot, chosen_sum, shares, kept, target, target_row


def front_kernel(
    lengths, parents, tokens, cotangent, ids_row, wq, wk, wv, wo, gains, bias, router_row,
    xs, gs, residual, all_tokens_far, qkv_far, cols_far, params, att_far, stats_far, wo_far,
    all_tokens, qkv, cols, wo_full, att, stats, part, misc, tags, tag_sum, all_tags, index, table, landed,
    before_mem, reach_mem,
    t_send, t_recv, w_send, w_recv, m_send, m_recv, c_send, c_recv, n_send, n_recv,
    o_send, o_recv, g_send, g_recv, a_send, a_recv, far_sem,
):
    e, s = lax.axis_index(EXPERT), lax.axis_index(SEQ)
    near_x, near_y, corner = (e, s ^ 1), (e, s ^ 2), (e, s ^ 3)
    around = (near_x, near_y, corner)
    hops = (1,) + ZHOPS
    low, full = jnp.bfloat16, jnp.float32
    rows, width = tokens.shape
    slim = wq.shape[0]
    shard = width // 4
    weights = (wq, wk, wv)
    place = e * 4 + s

    at_gain = lax.broadcasted_iota(jnp.int32, (slim, width), 1) == place * slim + lax.broadcasted_iota(
        jnp.int32, (slim, width), 0)
    gain_spot = jnp.where(at_gain, 1.0, 0.0).astype(low)
    few = bias.shape[1]
    at_bias = lax.broadcasted_iota(jnp.int32, (few, width), 1) == place * few + lax.broadcasted_iota(
        jnp.int32, (few, width), 0)
    bias_spot = jnp.where(at_bias, 1.0, 0.0).astype(low)
    two_gains = contract(gains[...], gain_spot, ((1,), (0,)))
    one_bias = contract(bias[...], bias_spot, ((1,), (0,)))
    misc[...] = jnp.concatenate(
        [two_gains, one_bias, jnp.zeros((5, width), full), contract(router_row[...], gain_spot, ((1,), (0,)))], axis=0
    ).astype(low)

    greet(list(around) + [(e ^ d, s) for d in hops])

    def send_tokens(k):
        return remote(tokens, all_tokens.at[aligned(s, rows)], t_send.at[k], t_recv.at[k], around[k])

    def pass_tokens(k):
        piece = pl.ds(pl.multiple_of((s ^ (1 + k)) * rows + k * (rows // 2), rows // 2), rows // 2)
        view = all_tokens.at[piece]
        return remote(view, view, t_send.at[2 + k], t_recv.at[2 + k], around[1 - k])

    def send_cols(k, m):
        return remote(
            weights[m].at[:, aligned(s ^ (k + 1), shard)], part.at[m, aligned(s, slim)],
            w_send.at[k, m], w_recv.at[k, m], around[k],
        )

    def send_tags(k):
        return remote(misc, tags.at[k], m_send.at[k], m_recv.at[k], around[k])

    def share(k):
        return remote(part, cols.at[:, aligned(e, 4 * slim)], c_send.at[k], c_recv.at[k], (e ^ hops[k], s))

    def share_tags(k):
        return remote(tag_sum, all_tags.at[k], n_send.at[k], n_recv.at[k], (e ^ hops[k], s))

    def relay(k):
        view = cols.at[:, aligned(e ^ hops[k], 4 * slim)]
        return remote(view, view, c_send.at[3 + k], c_recv.at[3 + k], (e ^ 1, s))

    def relay_tags(k):
        return remote(all_tags.at[k], all_tags.at[3 + k], n_send.at[3 + k], n_recv.at[3 + k], (e ^ 1, s))

    def share_out(k):
        return remote(wo, wo_full.at[e, s], o_send.at[k], o_recv.at[k], (e ^ hops[k], s))

    def relay_out(k):
        view = wo_full.at[e ^ hops[k], s]
        return remote(view, view, o_send.at[3 + k], o_recv.at[3 + k], (e ^ 1, s))

    def spread_out(k):
        view = wo_full.at[:, s]
        return remote(view, view, g_send.at[k], g_recv.at[k], around[k])

    def pass_out(k):
        view = wo_full.at[pl.ds(4 * k, 4), s ^ (1 + k)]
        return remote(view, view, g_send.at[2 + k], g_recv.at[2 + k], around[1 - k])

    def give(r):
        return remote(att.at[pl.ds(r * rows, rows)], landed.at[s], a_send.at[r], a_recv.at[s ^ r], (e, r))

    far = []

    def keep(src, dst):
        copy = pltpu.make_async_copy(src, dst, far_sem.at[len(far)])
        copy.start()
        far.append(copy)

    for k in range(3):
        for m in range(3):
            send_cols(k, m).start()
        send_tags(k).start()
    for k in range(2):
        send_tokens(k).start()
    for m in range(3):
        part[m, aligned(s, slim), :] = weights[m][:, aligned(s, shard)]
    all_tokens[aligned(s, rows), :] = tokens[...]
    wo_full[e, s] = wo[...]
    stats[...] = jnp.zeros_like(stats)
    found = segment_scalars(lengths, parents, before_mem, reach_mem)
    total = misc[...].astype(full)
    for k in range(3):
        send_tags(k).wait_recv()
        total += tags[k].astype(full)
    tag_sum[...] = total.astype(low)
    for k in range(3):
        for m in range(3):
            send_cols(k, m).wait_recv()
    for k in range(4):
        share_tags(k).start()
        share(k).start()
    for k in range(4):
        share_out(k).start()
    cols[:, aligned(e, 4 * slim), :] = part[...]
    for r in range(4):
        index[r, :, :(r + 1) * rows] = pair_index(found, r * rows, rows, (r + 1) * rows)[0]
    for k in range(2):
        send_tokens(k).wait_recv()
        pass_tokens(k).start()
    for k in range(1, 4):
        share_tags(k).wait_recv()
        relay_tags(k).start()
        share(k).wait_recv()
        relay(k).start()
    for k in range(1, 4):
        share_out(k).wait_recv()
        relay_out(k).start()
    share_tags(0).wait_recv()
    share(0).wait_recv()
    for k in range(1, 4):
        relay_tags(k).wait_recv()
        relay(k).wait_recv()
    for k in range(7):
        total += all_tags[k].astype(full)
    params[...] = total
    gain = total[0:1]
    table[...] = bias_tables(params, s)

    def group(q, carry):
        @pl.when(q == 3)
        def _():
            for k in range(2):
                pass_tokens(k).wait_recv()
        spot = aligned(s ^ q, rows)
        values = all_tokens[spot, :].astype(full)
        normed = (values * norm_factor(values) * gain).astype(low)
        for m in range(3):
            out = contract(normed, cols[m], ((1,), (0,)))
            if m == 0:
                out = out.astype(low).astype(full) * HDIM ** (-0.5)
            qkv[spot, m * shard:(m + 1) * shard] = out.astype(low)
        return carry

    lax.fori_loop(0, 4, group, 0)
    keep(all_tokens, all_tokens_far)
    keep(qkv, qkv_far)
    keep(cols, cols_far)
    share_out(0).wait_recv()
    for k in range(1, 4):
        relay_out(k).wait_recv()
    for k in range(2):
        spread_out(k).start()

    for r in (3, 2, 1, 0):
        first, count = r * rows, (r + 1) * rows

        def pair(h, carry):
            lanes = aligned(h, 128)
            q = qkv[first:count, lanes]
            k = qkv[0:count, aligned(h + shard // 128, 128)]
            v = qkv[0:count, aligned(h + 2 * shard // 128, 128)]
            lane = lax.broadcasted_iota(jnp.int32, (rows, 128), 1)
            results = []
            noted = stats[first:count, :]
            for side in range(2):
                mine = (lane // HDIM) == side
                scores = contract(jnp.where(mine, q, jnp.zeros_like(q)), k, ((1,), (1,)))
                scores = scores + looked_up(table[pl.ds(2 * h + side, 1), :], index[r, :, :count])
                peak = jnp.max(scores, axis=1, keepdims=True)
                expo = jnp.exp(scores - peak)
                mass = jnp.sum(expo, axis=1, keepdims=True)
                results.append(contract(expo.astype(low), v, ((1,), (0,))) * (1.0 / mass))
                noted = jnp.where(lane == 2 * h + side, peak + jnp.log(mass), noted)
            stats[first:count, :] = noted
            att[first:count, lanes] = jnp.where((lane // HDIM) == 0, results[0], results[1]).astype(low)
            return carry

        lax.fori_loop(0, shard // 128, pair, 0)

        @pl.when(s != r)
        def _():
            give(r).start()

        if r == 3:
            for k in range(2):
                spread_out(k).wait_recv()
                pass_out(k).start()

    keep(att, att_far)
    keep(stats, stats_far)
    for k in range(2):
        pass_out(k).wait_recv()
    keep(wo_full, wo_far)
    landed[s] = att[aligned(s, rows), :]
    total = tokens[...].astype(full)

    def out_rows(index):
        return wo_full[pl.ds(2 * index, 2)].reshape(shard, width)

    total += contract(landed[s], out_rows(s), ((1,), (0,)))
    for k in range(1, 4):
        remote(landed.at[s], landed.at[s ^ k], a_send.at[0], a_recv.at[k], (e, s ^ k)).wait_recv()
        total += contract(landed[s ^ k], out_rows(s ^ k), ((1,), (0,)))
    residual[...] = total
    cap = xs.shape[0] // 8
    _, _, normed, _, _, _, _, shares, kept, _, target_row = routing(total, params[...], ids_row[...], cap)
    spot = lax.broadcasted_iota(jnp.int32, (8 * cap, rows), 0)
    hot = [jnp.where(spot == target_row[k], 1.0, 0.0).astype(low) for k in range(2)]
    xs[...] = contract(hot[0] + hot[1], normed, ((1,), (0,))).astype(low)
    grad = cotangent[...].astype(full)
    weighted = [((shares[k] * kept[k]) * grad).astype(low) for k in range(2)]
    gs[...] = (
        contract(hot[0], weighted[0], ((1,), (0,))) + contract(hot[1], weighted[1], ((1,), (0,)))
    ).astype(low)

    for k in range(2):
        send_tokens(k).wait_send()
        pass_tokens(k).wait_send()
        spread_out(k).wait_send()
        pass_out(k).wait_send()
    for k in range(3):
        for m in range(3):
            send_cols(k, m).wait_send()
        send_tags(k).wait_send()
    for k in range(4):
        share(k).wait_send()
        share_tags(k).wait_send()
        share_out(k).wait_send()
    for k in range(1, 4):
        relay(k).wait_send()
        relay_tags(k).wait_send()
        relay_out(k).wait_send()
    for r in range(4):
        @pl.when(s != r)
        def _():
            give(r).wait_send()
    for copy in far:
        copy.wait()


def front(lengths, parents, tokens, cotangent, ids_row, wq, wk, wv, wo, gains, bias, router_row):
    rows, width = tokens.shape
    slim, shard = wq.shape[0], width // 4
    cap = 10 * rows // 32
    low, full = jnp.bfloat16, jnp.float32
    vmem, smem, hbm = (pl.BlockSpec(memory_space=m) for m in (pltpu.VMEM, pltpu.SMEM, pl.ANY))
    dma = pltpu.SemaphoreType.DMA
    kept = (
        jax.ShapeDtypeStruct((4 * rows, width), low),
        jax.ShapeDtypeStruct((4 * rows, 3 * shard), low),
        jax.ShapeDtypeStruct((3, width, shard), low),
        jax.ShapeDtypeStruct((16, width), full),
        jax.ShapeDtypeStruct((4 * rows, shard), low),
        jax.ShapeDtypeStruct((4 * rows, 128), full),
        jax.ShapeDtypeStruct((8, 4, slim, width), low),
    )
    return pl.pallas_call(
        front_kernel,
        out_shape=(
            jax.ShapeDtypeStruct((8 * cap, width), low),
            jax.ShapeDtypeStruct((8 * cap, width), low),
            jax.ShapeDtypeStruct((rows, width), full),
        ) + kept,
        in_specs=[smem, smem] + [vmem] * 10,
        out_specs=(vmem, vmem, vmem, hbm, hbm, hbm, vmem, hbm, hbm, hbm),
        scratch_shapes=[
            pltpu.VMEM(kept[0].shape, low), pltpu.VMEM(kept[1].shape, low), pltpu.VMEM(kept[2].shape, low),
            pltpu.VMEM(kept[6].shape, low), pltpu.VMEM(kept[4].shape, low), pltpu.VMEM(kept[5].shape, full),
            pltpu.VMEM((3, 4 * slim, shard), low),
            pltpu.VMEM((16, width), low), pltpu.VMEM((3, 16, width), low), pltpu.VMEM((16, width), low),
            pltpu.VMEM((7, 16, width), low),
            pltpu.VMEM((4, rows, 4 * rows), jnp.int32), pltpu.VMEM((8, 128), full),
            pltpu.VMEM((4, rows, shard), low),
            pltpu.SMEM((16,), jnp.int32), pltpu.SMEM((16,), jnp.int32),
            dma((4,)), dma((4,)), dma((3, 3)), dma((3, 3)), dma((3,)), dma((3,)),
            dma((7,)), dma((7,)), dma((7,)), dma((7,)), dma((7,)), dma((7,)), dma((4,)), dma((4,)),
            dma((4,)), dma((4,)), dma((6,)),
        ],
        compiler_params=pltpu.CompilerParams(
            collective_id=2, has_side_effects=True, vmem_limit_bytes=VMEM_LIMIT
        ),
        cost_estimate=pl.CostEstimate(flops=40 * rows * width * shard, bytes_accessed=24 << 20, transcendentals=8 * rows * rows * 16),
        name="front",
    )(lengths, parents, tokens, cotangent, ids_row, wq, wk, wv, wo, gains, bias, router_row)


def pair_index_across(found, first, rows, count):
    ids = first + lax.broadcasted_iota(jnp.int32, (1, rows), 1)
    keys = lax.broadcasted_iota(jnp.int32, (count, 1), 0)
    place, reach, _ = token_columns(found, ids)
    key_place, _, key_own = token_columns(found, keys)
    seen = ((reach & key_own) != 0) & (keys <= ids)
    return jnp.where(seen, jnp.minimum(place - key_place, LAST - 1), LAST)


def near_keys(found, first, rows):
    ids = first + lax.broadcasted_iota(jnp.int32, (rows, 1), 0)
    place, reach, _ = token_columns(found, ids)
    step = lax.broadcasted_iota(jnp.int32, (rows, LAST + 1), 1)
    wanted = place - step
    spot = jnp.full((rows, LAST + 1), -1, jnp.int32)
    for k, (start, before, _, length) in enumerate(found):
        inside = ((reach & (1 << k)) != 0) & (wanted >= before) & (wanted < before + length)
        spot = jnp.where(inside, wanted + (start - before), spot)
    return jnp.where(step == LAST, -1, spot)


GROUPS = ((0, 3), (6, 2), (3, 3))


def back_kernel(
    lengths, parents, ids_row, ret_o, ret_b, residual, cotangent, params,
    wo_far, qkv_far, cols_far, all_tokens_far, att_far, stats_far,
    layer_out, tokens_grad, dwq, dwk, dwv, dwo, small_sum,
    wo, qkv, cols, all_tokens, att, stats, datt, datt_own, aog_cols, aog_own, residual_grad,
    att_all, index, spots, lse, table, near, dk, dv, dqkv, normed,
    halves, core_got, sums, z_got, final, final_got, parts, first_got, second_got, mine, tally, tally_got,
    before_mem, reach_mem,
    load_sem, d_send, d_recv, g_send, g_recv, core_send, core_recv, z_send, z_recv, a_send, a_recv,
    n_send, n_recv, m_send, m_recv,
):
    e, s = lax.axis_index(EXPERT), lax.axis_index(SEQ)
    z, c = e // 2, lax.rem(e, 2)
    near_x, near_y = (e, s ^ 1), (e, s ^ 2)
    around = [(e, s ^ k) for k in range(1, 4)]
    hops = (1,) + ZHOPS
    full, low = jnp.float32, jnp.bfloat16
    high = lax.Precision.HIGHEST
    rows, width = residual.shape
    shard = cols.shape[2]
    slim = dwq.shape[0]
    cap = ret_o.shape[0] // 8
    half = shard // 2
    loads = [
        pltpu.make_async_copy(src, dst, load_sem.at[k])
        for k, (src, dst) in enumerate((
            (wo_far, wo), (att_far, att), (stats_far, stats), (qkv_far, qkv), (all_tokens_far, all_tokens),
            (cols_far, cols),
        ))
    ]
    for load in loads:
        load.start()
    greet(around + [(e ^ d, s) for d in hops])

    held = residual[...]
    scale, unit, unrouted, router, prob, hot, chosen_sum, shares, kept, target, _ = routing(
        held, params[...], ids_row[...], cap
    )
    place = lax.broadcasted_iota(jnp.int32, (rows, 8 * cap), 1)
    pick = [jnp.where(place == target[k], 1.0, 0.0).astype(low) for k in range(2)]
    grad = cotangent[...].astype(full)
    mixture = jnp.zeros((rows, width), full)
    share_grad = []
    for k in range(2):
        picked = contract(pick[k], ret_o[...], ((1,), (0,)))
        mixture += (shares[k] * kept[k]) * picked
        share_grad.append(jnp.sum(grad * picked, axis=1, keepdims=True) * kept[k])
    layer_out[...] = (held + mixture).astype(low)
    inner = shares[0] * share_grad[0] + shares[1] * share_grad[1]
    prob_grad = sum(hot[k] * ((share_grad[k] - inner) / chosen_sum) for k in range(2))
    logit_grad = prob * (prob_grad - jnp.sum(prob * prob_grad, axis=1, keepdims=True))
    normed_grad = contract(pick[0] + pick[1], ret_b[...], ((1,), (0,))) + lax.dot_general(
        logit_grad, router, (((1,), (0,)), ((), ())), precision=high, preferred_element_type=full
    )
    unit_grad = normed_grad * params[1:2]
    passed = grad + scale * (unit_grad - unit * jnp.mean(unit_grad * unit, axis=1, keepdims=True))
    residual_grad[...] = passed
    aog_own[...] = passed.astype(low)
    for load in loads[:1]:
        load.wait()
    datt_own[...] = contract(aog_own[...], wo[...], ((1,), (1,))).astype(low)

    def give(kind, k):
        src, dst = ((datt_own, datt), (aog_own, aog_cols))[kind]
        return remote(src.at[:, aligned(s ^ (k + 1), shard)], dst.at[aligned(s, rows)],
                      d_send.at[kind, k], d_recv.at[kind, k], around[k])

    for kind in range(2):
        for k in (2, 0, 1):
            give(kind, k).start()

    def spread_att(k):
        return remote(att, att_all.at[s], g_send.at[k], g_recv.at[k], around[k])

    def pass_att(k):
        view = att_all.at[s ^ (1 + k), pl.ds(2 * rows * k, 2 * rows)]
        return remote(view, view, g_send.at[2 + k], g_recv.at[2 + k], around[1 - k])

    for load in loads[1:3]:
        load.wait()
    for k in range(2):
        spread_att(k).start()
    att_all[s] = att[...]
    datt[aligned(s, rows), :] = datt_own[:, aligned(s, shard)]
    aog_cols[aligned(s, rows), :] = aog_own[:, aligned(s, shard)]
    tally[0] = jnp.zeros((16, width), full)
    tally[0, 1:2] = jnp.sum(normed_grad * unit, axis=0, keepdims=True)
    lane = lax.broadcasted_iota(jnp.int32, (1, width), 1)
    tally[0, 3:4] = jnp.where(lane == 0, jnp.sum(held * held), jnp.where(lane == 1, jnp.sum(mixture * mixture), 0.0))
    tally[0, 8:16] = lax.dot_general(logit_grad, unrouted.astype(full), (((0,), (0,)), ((), ())),
                                     precision=high, preferred_element_type=full)
    found = segment_scalars(lengths, parents, before_mem, reach_mem)
    table[...] = bias_tables(params, s)
    near[...] = jnp.zeros_like(near)
    for r in range(4):
        index[r, :(r + 1) * rows] = pair_index_across(found, r * rows, rows, (r + 1) * rows)
        spots[r] = near_keys(found, r * rows, rows)
        turned = jnp.transpose(stats[r * rows:(r + 1) * rows, :])
        for h in range(4):
            lse[h, r] = turned[h:h + 1]
    for load in loads[3:]:
        load.wait()
    gain = params[0:1]

    def units(q):
        values = all_tokens[aligned(s ^ q, rows), :].astype(full)
        factor = norm_factor(values)
        return values * factor, factor

    def norm_block(q, carry):
        normed[aligned(s ^ q, rows), :] = (units(q)[0] * gain).astype(low)
        return carry

    lax.fori_loop(0, 4, norm_block, 0)

    def core_copy(g):
        slots = pl.ds(*GROUPS[g])
        return remote(halves.at[1 - c, slots], core_got.at[slots], core_send.at[g], core_recv.at[g], (e ^ 1, s))

    def z_copy(g, k):
        slots = pl.ds(*GROUPS[g])
        return remote(sums.at[slots, z ^ k], z_got.at[k - 1, slots], z_send.at[g, k - 1], z_recv.at[g, k - 1],
                      (e ^ (2 * k), s))

    def a_copy(g, k):
        slots = pl.ds(*GROUPS[g])
        return remote(final.at[slots, aligned(s ^ (k + 1), slim)], final_got.at[s, slots],
                      a_send.at[g, k], a_recv.at[g, k], around[k])

    def store_halves(slot, zone, block):
        for i in range(2):
            halves[i, slot, zone] = block[i * half:(i + 1) * half].astype(low)

    def add_core(g):
        core_copy(g).wait_recv()
        first, amount = GROUPS[g]
        for slot in range(first, first + amount):
            for j in range(4):
                sums[slot, j] = (halves[c, slot, j].astype(full) + core_got[slot, j].astype(full)).astype(low)
        for k in range(1, 4):
            z_copy(g, k).start()

    def finish_grad(g):
        first, amount = GROUPS[g]
        for k in range(1, 4):
            z_copy(g, k).wait_recv()
        for slot in range(first, first + amount):
            block = sums[slot, z].astype(full)
            for k in range(1, 4):
                block += z_got[k - 1, slot].astype(full)
            final[slot] = block
        for k in range(3):
            a_copy(g, k).start()
        for slot in range(first, first + amount):
            final_got[s, slot] = final[slot, aligned(s, slim)]

    for k in range(3):
        give(0, k).wait_recv()

    def pair(p, carry):
        lanes = aligned(p, 128)
        dk[...] = jnp.zeros_like(dk)
        dv[...] = jnp.zeros_like(dv)
        for r in (3, 2, 1, 0):
            first, count = r * rows, (r + 1) * rows
            q = qkv[first:count, lanes]
            k = qkv[0:count, aligned(p + shard // 128, 128)]
            v = qkv[0:count, aligned(p + 2 * shard // 128, 128)]
            g = datt[first:count, lanes]
            lane = lax.broadcasted_iota(jnp.int32, (rows, 128), 1)
            lane_long = lax.broadcasted_iota(jnp.int32, (count, 128), 1)
            spot = spots[r]
            spot_lane, spot_block = spot & 127, jnp.where(spot < 0, -1, spot >> 7)
            dq = []
            key_sum, value_sum = 0.0, 0.0
            for side in range(2):
                mine_lanes = (lane // HDIM) == side
                q_side = jnp.where(mine_lanes, q, jnp.zeros_like(q))
                g_side = jnp.where(mine_lanes, g, jnp.zeros_like(g))
                scores = contract(k, q_side, ((1,), (1,)))
                scores = scores + looked_up(table[pl.ds(2 * p + side, 1), :], index[r, :count])
                soft = jnp.exp(scores - lse[2 * p + side, r])
                dprob = contract(v, g_side, ((1,), (1,)))
                delta = jnp.sum(soft * dprob, axis=0, keepdims=True)
                turned = soft * (dprob - delta)
                score_grad = turned.astype(low)
                key_sum = key_sum + contract(score_grad, q_side, ((1,), (0,)))
                value_sum = value_sum + contract(soft.astype(low), g_side, ((1,), (0,)))
                wide = jnp.transpose(turned)
                with_ones = jnp.where((lane_long // HDIM) == side, k, jnp.ones_like(k))
                part = contract(wide.astype(low), with_ones, ((1,), (0,)))
                dq.append(part)
                close = jnp.zeros((rows, 128), full)
                for b in range(count // 128):
                    taken = jnp.take_along_axis(wide[:, b * 128:(b + 1) * 128], spot_lane, axis=1)
                    close = jnp.where(spot_block == b, taken, close)
                near[0, 2 * p + side] += jnp.sum(close.reshape(rows // 8, 8, 128), axis=0)
                rest = jnp.where(mine_lanes, 0.0, part)
                near[1, 2 * p + side] += jnp.sum(rest.reshape(rows // 8, 8, 128), axis=0)
            dqkv[first:count, lanes] = (jnp.where((lane // HDIM) == 0, dq[0], dq[1]) * HDIM ** (-0.5)).astype(low)
            dk[0:count] += key_sum
            dv[0:count] += value_sum

            if r == 3:
                @pl.when(p == 0)
                def _():
                    for i in range(2):
                        spread_att(i).wait_recv()
                        pass_att(i).start()

                @pl.when(p == 1)
                def _():
                    add_core(0)
                    for i in range(2):
                        pass_att(i).wait_recv()
                    for i in range(3):
                        give(1, i).wait_recv()

                    def output_zone(j, carry):
                        block = contract(att_all[j], aog_cols[...], ((0,), (0,)))
                        for i in range(2):
                            store_halves(6 + i, j, block[:, i * 128:(i + 1) * 128])
                        return carry

                    lax.fori_loop(0, 4, output_zone, 0)
                    core_copy(1).start()
            if r == 2:
                @pl.when(p == 1)
                def _():
                    add_core(1)
        dqkv[:, aligned(p + shard // 128, 128)] = dk[...].astype(low)
        dqkv[:, aligned(p + 2 * shard // 128, 128)] = dv[...].astype(low)

        def qkv_zone(j, carry):
            right = jnp.concatenate([dqkv[:, aligned(p + m * shard // 128, 128)] for m in range(3)], axis=1)
            block = contract(normed[:, aligned(j, shard)], right, ((0,), (0,)))
            for m in range(3):
                for i in range(2):
                    halves[i, 3 * p + m, j] = block[i * half:(i + 1) * half, m * 128:(m + 1) * 128].astype(low)
            return carry

        lax.fori_loop(0, 4, qkv_zone, 0)

        @pl.when(p == 0)
        def _():
            core_copy(0).start()

        @pl.when(p == 1)
        def _():
            core_copy(2).start()
        return carry

    lax.fori_loop(0, 2, pair, 0)

    def n_copy(kind, which):
        one, two = ((near_x, near_y), (near_y, near_x))[kind]
        if which < 2:
            src = parts.at[(1 + kind, 3)[which], kind]
            return remote(src, first_got.at[kind, which], n_send.at[kind, which], n_recv.at[kind, which], one)
        return remote(parts.at[2 - kind, kind], second_got.at[kind], n_send.at[kind, 2], n_recv.at[kind, 2], two)

    def back_block(i, carry):
        q = 3 - i
        d = dqkv[aligned(s ^ q, rows), :]
        total = jnp.zeros((rows, width), full)
        for m in range(3):
            total += contract(d[:, m * shard:(m + 1) * shard], cols[m], ((1,), (1,)))
        tally[0, 0:1] += jnp.sum(total * units(q)[0], axis=0, keepdims=True)
        mine[...] = total
        for kind in range(2):
            parts[q, kind] = total[:, kind * (width // 2):(kind + 1) * (width // 2)].astype(low)

        @pl.when(i == 0)
        def _():
            n_copy(0, 1).start()
            n_copy(1, 1).start()
            add_core(2)

        @pl.when(i == 1)
        def _():
            n_copy(1, 0).start()

        @pl.when(i == 2)
        def _():
            n_copy(0, 0).start()
        return carry

    lax.fori_loop(0, 4, back_block, 0)

    close, rest = (
        jnp.concatenate([jnp.sum(near[kind, h], axis=0, keepdims=True) for h in range(8)], axis=0) for kind in range(2)
    )
    far = jnp.sum(rest, axis=1, keepdims=True) / HDIM - jnp.sum(close, axis=1, keepdims=True)
    spot = lax.broadcasted_iota(jnp.int32, close.shape, 1)
    by_distance = jnp.where(spot == LAST, far, close)
    lane = lax.broadcasted_iota(jnp.int32, (128, BUCKETS * HEADS), 1)
    distance = lax.broadcasted_iota(jnp.int32, (128, BUCKETS * HEADS), 0)
    hot_bucket = jnp.where((lane // HEADS) == bucket_of(distance), 1.0, 0.0)
    spread = lax.dot_general(by_distance, hot_bucket, (((1,), (0,)), ((), ())), precision=high, preferred_element_type=full)
    head = lax.broadcasted_iota(jnp.int32, spread.shape, 0)
    lane = lax.broadcasted_iota(jnp.int32, spread.shape, 1)
    here = ((lane % HEADS) == s * (HEADS // 4) + head) & (head < HEADS // 4)
    tally[0, 2:3, 0:BUCKETS * HEADS] = jnp.sum(jnp.where(here, spread, 0.0), axis=0, keepdims=True)

    def m_copy(stage, k):
        slot = (0, 3, 4)[stage] + k
        peer = (around[k], (e ^ 1, s), (e ^ (2 * (k + 1)), s))[stage]
        return remote(tally.at[stage], tally_got.at[slot], m_send.at[slot], m_recv.at[slot], peer)

    for k in range(3):
        m_copy(0, k).start()
    for kind in range(2):
        n_copy(kind, 1).wait_recv()
        group = 2 - kind
        parts[group, kind] = (parts[group, kind].astype(full) + first_got[kind, 1].astype(full)).astype(low)
        n_copy(kind, 2).start()
    finish_grad(0)
    finish_grad(1)
    total = tally[0]
    for k in range(3):
        m_copy(0, k).wait_recv()
        total += tally_got[k]
    tally[1] = total
    m_copy(1, 0).start()
    finish_grad(2)
    m_copy(1, 0).wait_recv()
    total = total + tally_got[3]
    tally[2] = total
    for k in range(3):
        m_copy(2, k).start()
    for kind in range(2):
        n_copy(kind, 0).wait_recv()
        n_copy(kind, 2).wait_recv()
        lanes = slice(kind * (width // 2), (kind + 1) * (width // 2))
        mine[:, lanes] += first_got[kind, 0].astype(full) + second_got[kind].astype(full)
    unit, scale = units(0)
    unit_grad = mine[...] * gain
    tokens_grad[...] = residual_grad[...] + scale * (
        unit_grad - unit * jnp.mean(unit_grad * unit, axis=1, keepdims=True)
    )
    for g in range(3):
        for k in range(3):
            a_copy(g, k).wait_recv()
    for m, out in enumerate((dwq, dwk, dwv, dwo)):
        for i in range(2):
            slot = (m + 3 * i) if m < 3 else 6 + i
            for j in range(4):
                out[:, j * shard + i * 128:j * shard + (i + 1) * 128] = final_got[j, slot]
    for k in range(3):
        m_copy(2, k).wait_recv()
        total += tally_got[4 + k]
    small_sum[...] = total
    for k in range(3):
        for kind in range(2):
            give(kind, k).wait_send()
        for g in range(3):
            z_copy(g, k + 1).wait_send()
            a_copy(g, k).wait_send()
        core_copy(k).wait_send()
    for k in range(2):
        spread_att(k).wait_send()
        pass_att(k).wait_send()
    for kind in range(2):
        for which in range(3):
            n_copy(kind, which).wait_send()
    for stage, amount in ((0, 3), (1, 1), (2, 3)):
        for k in range(amount):
            m_copy(stage, k).wait_send()


def back(lengths, parents, ids_row, ret_o, ret_b, residual, cotangent, params, wo, qkv, cols, all_tokens, att, stats):
    rows, width = residual.shape
    shard = cols.shape[2]
    slim = width // 32
    low, full = jnp.bfloat16, jnp.float32
    vmem, smem, hbm = (pl.BlockSpec(memory_space=m) for m in (pltpu.VMEM, pltpu.SMEM, pl.ANY))
    dma = pltpu.SemaphoreType.DMA
    half = shard // 2
    return pl.pallas_call(
        back_kernel,
        out_shape=(
            jax.ShapeDtypeStruct((rows, width), low),
            jax.ShapeDtypeStruct((rows, width), full),
        ) + (jax.ShapeDtypeStruct((slim, width), full),) * 4 + (jax.ShapeDtypeStruct((16, width), full),),
        in_specs=[smem, smem] + [vmem] * 6 + [hbm] * 6,
        out_specs=(vmem,) * 7,
        scratch_shapes=[
            pltpu.VMEM((width, width), low), pltpu.VMEM(qkv.shape, low), pltpu.VMEM(cols.shape, low),
            pltpu.VMEM(all_tokens.shape, low), pltpu.VMEM(att.shape, low), pltpu.VMEM(stats.shape, full),
            pltpu.VMEM((4 * rows, shard), low), pltpu.VMEM((rows, width), low),
            pltpu.VMEM((4 * rows, shard), low), pltpu.VMEM((rows, width), low), pltpu.VMEM((rows, width), full),
            pltpu.VMEM((4, 4 * rows, shard), low),
            pltpu.VMEM((4, 4 * rows, rows), jnp.int32), pltpu.VMEM((4, rows, 128), jnp.int32),
            pltpu.VMEM((4, 4, 1, rows), full), pltpu.VMEM((8, 128), full), pltpu.VMEM((2, 8, 8, 128), full),
            pltpu.VMEM((4 * rows, 128), full), pltpu.VMEM((4 * rows, 128), full),
            pltpu.VMEM((4 * rows, 3 * shard), low), pltpu.VMEM((4 * rows, width), low),
            pltpu.VMEM((2, 8, 4, half, half), low), pltpu.VMEM((8, 4, half, half), low),
            pltpu.VMEM((8, 4, half, half), low), pltpu.VMEM((3, 8, half, half), low),
            pltpu.VMEM((8, half, half), full), pltpu.VMEM((4, 8, slim, half), full),
            pltpu.VMEM((4, 2, rows, width // 2), low), pltpu.VMEM((2, 2, rows, width // 2), low),
            pltpu.VMEM((2, rows, width // 2), low), pltpu.VMEM((rows, width), full),
            pltpu.VMEM((3, 16, width), full), pltpu.VMEM((7, 16, width), full),
            pltpu.SMEM((16,), jnp.int32), pltpu.SMEM((16,), jnp.int32),
            dma((6,)), dma((2, 3)), dma((2, 3)), dma((4,)), dma((4,)), dma((3,)), dma((3,)),
            dma((3, 3)), dma((3, 3)), dma((3, 3)), dma((3, 3)), dma((2, 3)), dma((2, 3)), dma((7,)), dma((7,)),
        ],
        compiler_params=pltpu.CompilerParams(
            collective_id=5, has_side_effects=True, vmem_limit_bytes=VMEM_LIMIT
        ),
        cost_estimate=pl.CostEstimate(flops=120 * rows * width * shard, bytes_accessed=20 << 20, transcendentals=8 * rows * rows * 16),
        name="back",
    )(lengths, parents, ids_row, ret_o, ret_b, residual, cotangent, params, wo, qkv, cols, all_tokens, att, stats)


def emit_kernel(*refs):
    large, small = refs[:9], refs[9]
    out, (gain_one, gain_two, bias, router, roots) = refs[10:19], refs[19:24]
    held, in_sem, out_sem = refs[24:33], refs[33], refs[34]
    comes = [pltpu.make_async_copy(src, mid, in_sem.at[k]) for k, (src, mid) in enumerate(zip(large, held))]
    goes = [pltpu.make_async_copy(mid, dst, out_sem.at[k]) for k, (mid, dst) in enumerate(zip(held, out))]
    for copy in comes:
        copy.start()
    place = lax.axis_index(EXPERT) * 4 + lax.axis_index(SEQ)
    width = small.shape[1]

    def own(length):
        lane = lax.broadcasted_iota(jnp.int32, (length, width), 1)
        down = lax.broadcasted_iota(jnp.int32, (length, width), 0)
        return jnp.where(lane == place * length + down, 1.0, 0.0)

    def picked(left, right):
        return lax.dot_general(left, right, (((1,), (1,)), ((), ())),
                               precision=lax.Precision.HIGHEST, preferred_element_type=jnp.float32)

    slim = gain_one.shape[1]
    ours = own(slim)
    gains = picked(small[0:8], ours)
    gain_one[...] = gains[0:1]
    gain_two[...] = gains[1:2]
    bias[...] = picked(small[0:8], own(bias.shape[1]))[2:3]
    router[...] = picked(ours, small[8:16])
    roots[...] = jnp.sqrt(small[3:4, 0:2] / (32 * large[0].shape[0] * width))
    for come, go in zip(comes, goes):
        come.wait()
        go.start()
    for copy in goes:
        copy.wait()


def emit(large, small):
    full = jnp.float32
    width = small.shape[1]
    vmem, hbm = pl.BlockSpec(memory_space=pltpu.VMEM), pl.BlockSpec(memory_space=pl.ANY)
    slim = width // 32
    shapes = ((1, slim), (1, slim), (1, BUCKETS * HEADS // 32), (slim, 8), (1, 2))
    return pl.pallas_call(
        emit_kernel,
        out_shape=tuple(jax.ShapeDtypeStruct(x.shape, x.dtype) for x in large)
        + tuple(jax.ShapeDtypeStruct(shape, full) for shape in shapes),
        in_specs=[hbm] * 9 + [vmem],
        out_specs=(hbm,) * 9 + (vmem,) * 5,
        scratch_shapes=[pltpu.VMEM(x.shape, x.dtype) for x in large]
        + [pltpu.SemaphoreType.DMA((9,)), pltpu.SemaphoreType.DMA((9,))],
        compiler_params=pltpu.CompilerParams(vmem_limit_bytes=VMEM_LIMIT),
        name="emit",
    )(*large, small)


def per_device_kernels(
    tokens, cotangent, expert_ids, segment_lengths, segment_parents, attention_gain,
    query_weight, key_weight, value_weight, output_weight, bias_table, feedforward_gain,
    router_weight, gate_weight, up_weight, down_weight,
):
    ids_row = expert_ids.T
    gains = jnp.stack([attention_gain, feedforward_gain])
    send_rows, grad_rows, residual, all_tokens, qkv, cols, params, att, stats, wo = front(
        segment_lengths, segment_parents, tokens, cotangent, ids_row, query_weight, key_weight, value_weight,
        output_weight, gains, bias_table[None], router_weight.T,
    )
    returned, grad_back, gate_term, up_term, down_term = experts(
        send_rows, grad_rows, gate_weight[0], up_weight[0], down_weight[0]
    )
    layer_out, tokens_grad, dwq, dwk, dwv, dwo, totals = back(
        segment_lengths, segment_parents, ids_row, returned, grad_back, residual, cotangent, params,
        wo.reshape(D, D), qkv, cols, all_tokens, att, stats,
    )
    large = (layer_out, tokens_grad, dwq, dwk, dwv, dwo, gate_term, up_term, down_term)
    *large, gain_one, gain_two, bias, router, roots = emit(large, totals)
    layer_out, tokens_grad, dwq, dwk, dwv, dwo, gate_term, up_term, down_term = large
    return (
        layer_out, tokens_grad, gain_one[0], dwq, dwk, dwv, dwo, bias[0], gain_two[0], router,
        gate_term[None], up_term[None], down_term[None], roots[0],
    )


def per_device_general(
    tokens,
    cotangent,
    expert_ids,
    segment_lengths,
    segment_parents,
    attention_gain,
    query_weight,
    key_weight,
    value_weight,
    output_weight,
    bias_table,
    feedforward_gain,
    router_weight,
    gate_weight,
    up_weight,
    down_weight,
):
    seq_count = lax.axis_size(SEQ)
    seq_place = lax.axis_index(SEQ)
    all_count = lax.axis_size(EXPERT) * seq_count
    row_count = tokens.shape[0]
    experts = lax.axis_size(EXPERT) * gate_weight.shape[0]
    capacity = 10 * row_count // (4 * experts)
    score_scale = HDIM ** (-0.5)
    gathered = (
        lax.all_gather(attention_gain, BOTH, axis=0, tiled=True),
        lax.all_gather(query_weight, BOTH, axis=0, tiled=True),
        lax.all_gather(key_weight, BOTH, axis=0, tiled=True),
        lax.all_gather(value_weight, BOTH, axis=0, tiled=True),
        lax.all_gather(output_weight, BOTH, axis=0, tiled=True),
        lax.all_gather(bias_table, BOTH, axis=0, tiled=True),
        lax.all_gather(feedforward_gain, BOTH, axis=0, tiled=True),
        lax.all_gather(router_weight, BOTH, axis=0, tiled=True),
    )
    gain_one, query_full, key_full, value_full, output_full, bias_flat, gain_two, router_full = (
        gathered
    )
    bias_grid = bias_flat.reshape(BUCKETS, HEADS)
    starts, before, reaches = tree_tables(segment_lengths[0], segment_parents[0])
    own_rows = seq_place * row_count + jnp.arange(row_count, dtype=jnp.int32)
    own_meta = token_info(own_rows, starts, before, reaches)
    tokens_float = tokens.astype(jnp.float32)
    scale_one = norm_factor(tokens_float)
    unit_one = tokens_float * scale_one
    normed_one = (unit_one * gain_one.astype(jnp.float32)).astype(jnp.bfloat16)
    queries = (
        jnp.dot(normed_one, query_full, preferred_element_type=jnp.float32)
        .astype(jnp.bfloat16)
        .reshape(row_count, HEADS, HDIM)
    )
    keys_own = (
        jnp.dot(normed_one, key_full, preferred_element_type=jnp.float32)
        .astype(jnp.bfloat16)
        .reshape(row_count, HEADS, HDIM)
    )
    values_own = (
        jnp.dot(normed_one, value_full, preferred_element_type=jnp.float32)
        .astype(jnp.bfloat16)
        .reshape(row_count, HEADS, HDIM)
    )
    row_peak = jnp.full((HEADS, row_count), NEGATIVE, jnp.float32)
    key_piece = lax.all_gather(keys_own, SEQ, axis=0, tiled=True)
    value_piece = lax.all_gather(values_own, SEQ, axis=0, tiled=True)
    key_rows = jnp.arange(key_piece.shape[0], dtype=jnp.int32)
    visible, onehot, pair_bias = pair_terms(
        own_meta, token_info(key_rows, starts, before, reaches), own_rows, key_rows, bias_grid
    )
    scores = masked_scores(queries, key_piece, visible, pair_bias)
    new_peak = jnp.maximum(row_peak, jnp.max(scores, axis=-1))
    expo = jnp.exp(scores - new_peak[:, :, None])
    row_total = jnp.sum(expo, axis=-1)
    summed = jnp.einsum(
        SPEC_2, expo.astype(jnp.bfloat16), value_piece, preferred_element_type=jnp.float32
    )
    row_peak, row_total, summed = (new_peak, row_total, summed)
    log_total = row_peak + jnp.log(row_total)
    attended_float = summed / jnp.transpose(row_total)[:, :, None]
    attended = attended_float.astype(jnp.bfloat16).reshape(row_count, D)
    residual = tokens_float + jnp.dot(attended, output_full, preferred_element_type=jnp.float32)
    scale_two = norm_factor(residual)
    unit_two = residual * scale_two
    normed_two = (unit_two * gain_two.astype(jnp.float32)).astype(jnp.bfloat16)
    router_prob = jax.nn.softmax(
        jnp.dot(normed_two, router_full, preferred_element_type=jnp.float32), axis=-1
    )
    pick_hot = (
        expert_ids[:, :, None] == jnp.arange(experts, dtype=jnp.int32)[None, None, :]
    ).astype(jnp.float32)
    chosen = jnp.sum(pick_hot * router_prob[:, None, :], axis=2)
    chosen_total = jnp.sum(chosen, axis=1, keepdims=True)
    gate_shares = chosen / chosen_total
    hot_int = pick_hot.astype(jnp.int32).reshape(row_count * 2, experts)
    earlier = jnp.cumsum(hot_int, axis=0) - hot_int
    slot_number = jnp.sum(earlier * hot_int, axis=1).reshape(row_count, 2)
    kept_copy = slot_number < capacity
    kept_float = kept_copy.astype(jnp.float32)
    target = jnp.where(kept_copy, expert_ids * capacity + slot_number, experts * capacity)
    copy_ids = jnp.arange(row_count * 2, dtype=jnp.int32)
    slot_copy = (
        jnp.full((experts * capacity + 1,), row_count * 2, jnp.int32)
        .at[target.reshape(-1)]
        .set(copy_ids)[: experts * capacity]
    )
    fetch_index = jnp.minimum(target, experts * capacity - 1).reshape(-1)
    token_of_slot = jnp.where(slot_copy < row_count * 2, slot_copy // 2, row_count)
    padded = jnp.concatenate([normed_two, jnp.zeros((1, D), jnp.bfloat16)], axis=0)
    send_rows = padded[token_of_slot].reshape(experts, capacity, D)
    expert_in = lax.all_to_all(send_rows, EXPERT, split_axis=0, concat_axis=1, tiled=True)[0]
    gate_piece = lax.all_gather(gate_weight, SEQ, axis=1, tiled=True)
    up_piece = lax.all_gather(up_weight, SEQ, axis=1, tiled=True)
    down_piece = lax.all_gather(down_weight, SEQ, axis=1, tiled=True)
    gate_pre = jnp.einsum(SPEC_3, expert_in, gate_piece[0], preferred_element_type=jnp.float32)
    up_pre = jnp.einsum(SPEC_3, expert_in, up_piece[0], preferred_element_type=jnp.float32)
    active = (gelu_tanh(gate_pre) * up_pre).astype(jnp.bfloat16)
    expert_sum = jnp.dot(active, down_piece[0], preferred_element_type=jnp.float32)
    returned = lax.all_to_all(
        expert_sum.astype(jnp.bfloat16)[None], EXPERT, split_axis=1, concat_axis=0, tiled=True
    )
    picked = (
        returned.reshape(experts * capacity, D)[fetch_index]
        .reshape(row_count, 2, D)
        .astype(jnp.float32)
    )
    weighted = gate_shares * kept_float
    mixture = jnp.sum(weighted[:, :, None] * picked, axis=1)
    layer_out = (residual + mixture).astype(jnp.bfloat16)
    local_sums = jnp.stack([jnp.sum(residual * residual), jnp.sum(mixture * mixture)])
    again = (
        lax.all_gather(attention_gain, BOTH, axis=0, tiled=True),
        lax.all_gather(query_weight, BOTH, axis=0, tiled=True),
        lax.all_gather(key_weight, BOTH, axis=0, tiled=True),
        lax.all_gather(value_weight, BOTH, axis=0, tiled=True),
        lax.all_gather(output_weight, BOTH, axis=0, tiled=True),
        lax.all_gather(bias_table, BOTH, axis=0, tiled=True),
        lax.all_gather(feedforward_gain, BOTH, axis=0, tiled=True),
        lax.all_gather(router_weight, BOTH, axis=0, tiled=True),
    )
    gain_one, query_full, key_full, value_full, output_full, bias_flat, gain_two, router_full = (
        again
    )
    bias_grid = bias_flat.reshape(BUCKETS, HEADS)
    grad_out = cotangent.astype(jnp.float32)
    copy_grad = (
        (weighted[:, :, None] * grad_out[:, None, :]).astype(jnp.bfloat16).reshape(row_count * 2, D)
    )
    copy_padded = jnp.concatenate([copy_grad, jnp.zeros((1, D), jnp.bfloat16)], axis=0)
    grad_send = copy_padded[slot_copy].reshape(experts, capacity, D)
    grad_in = lax.all_to_all(grad_send, EXPERT, split_axis=0, concat_axis=1, tiled=True)[0]
    gate_piece = lax.all_gather(gate_weight, SEQ, axis=1, tiled=True)
    up_piece = lax.all_gather(up_weight, SEQ, axis=1, tiled=True)
    down_piece = lax.all_gather(down_weight, SEQ, axis=1, tiled=True)
    gate_pre = jnp.einsum(SPEC_3, expert_in, gate_piece[0], preferred_element_type=jnp.float32)
    up_pre = jnp.einsum(SPEC_3, expert_in, up_piece[0], preferred_element_type=jnp.float32)
    gelu_out, gelu_pull = jax.vjp(gelu_tanh, gate_pre)
    act_grad = jnp.einsum(SPEC_3, grad_in, down_piece[0], preferred_element_type=jnp.float32)
    gate_back = gelu_pull(act_grad * up_pre)[0].astype(jnp.bfloat16)
    up_back = (act_grad * gelu_out).astype(jnp.bfloat16)
    input_grad = jnp.dot(gate_back, gate_piece[0], preferred_element_type=jnp.float32) + jnp.dot(
        up_back, up_piece[0], preferred_element_type=jnp.float32
    )
    active = (gelu_out * up_pre).astype(jnp.bfloat16)
    input_grad, gate_backs, up_backs, actives = (input_grad, gate_back, up_back, active)
    grad_back = lax.all_to_all(
        input_grad.astype(jnp.bfloat16)[None], EXPERT, split_axis=1, concat_axis=0, tiled=True
    )
    expert_back = (
        grad_back.reshape(experts * capacity, D)[fetch_index]
        .reshape(row_count, 2, D)
        .astype(jnp.float32)
    )
    normed_two_grad = jnp.sum(expert_back * kept_float[:, :, None], axis=1)
    expert_grads = lax.psum_scatter(
        jnp.stack(
            [
                jnp.einsum(SPEC_4, gate_backs, expert_in, preferred_element_type=jnp.float32),
                jnp.einsum(SPEC_4, up_backs, expert_in, preferred_element_type=jnp.float32),
                jnp.einsum(SPEC_4, actives, grad_in, preferred_element_type=jnp.float32),
            ],
            axis=1,
        ).astype(jnp.bfloat16),
        SEQ,
        scatter_dimension=0,
        tiled=True,
    ).astype(jnp.float32)
    share_grad = jnp.sum(grad_out[:, None, :] * picked, axis=2) * kept_float
    chosen_grad = (
        share_grad - jnp.sum(gate_shares * share_grad, axis=1, keepdims=True)
    ) / chosen_total
    prob_grad = jnp.sum(pick_hot * chosen_grad[:, :, None], axis=1)
    logit_grad = router_prob * (prob_grad - jnp.sum(router_prob * prob_grad, axis=1, keepdims=True))
    router_float = router_full.astype(jnp.float32)
    router_term = jnp.einsum(
        SPEC_5, normed_two.astype(jnp.float32), logit_grad, precision=lax.Precision.HIGHEST
    )
    normed_two_grad = normed_two_grad + jnp.einsum(
        SPEC_6, logit_grad, router_float, precision=lax.Precision.HIGHEST
    )
    gain_two_term = jnp.sum(normed_two_grad * unit_two, axis=0)
    unit_grad_two = normed_two_grad * gain_two.astype(jnp.float32)
    residual_grad = grad_out + scale_two * (
        unit_grad_two - unit_two * jnp.mean(unit_grad_two * unit_two, axis=-1, keepdims=True)
    )
    attention_out_grad = residual_grad.astype(jnp.bfloat16)
    output_term = jnp.einsum(
        SPEC_5, attended, attention_out_grad, preferred_element_type=jnp.float32
    )
    attended_grad = (
        jnp.einsum(SPEC_6, attention_out_grad, output_full, preferred_element_type=jnp.float32)
        .astype(jnp.bfloat16)
        .reshape(row_count, HEADS, HDIM)
    )
    row_delta = jnp.transpose(jnp.sum(attended_grad.astype(jnp.float32) * attended_float, axis=-1))
    total_all, delta_all = (
        lax.all_gather(log_total, SEQ, axis=1, tiled=True),
        lax.all_gather(row_delta, SEQ, axis=1, tiled=True),
    )
    key_piece = lax.all_gather(keys_own, SEQ, axis=0, tiled=True)
    value_piece = lax.all_gather(values_own, SEQ, axis=0, tiled=True)
    key_rows = jnp.arange(key_piece.shape[0], dtype=jnp.int32)
    visible, onehot, pair_bias = pair_terms(
        own_meta, token_info(key_rows, starts, before, reaches), own_rows, key_rows, bias_grid
    )
    scores = masked_scores(queries, key_piece, visible, pair_bias)
    soft_weights = jnp.exp(scores - log_total[:, :, None])
    dprob = jnp.einsum(
        SPEC_1, attended_grad, value_piece, preferred_element_type=jnp.float32
    )
    score_grad = (soft_weights * (dprob - row_delta[:, :, None])).astype(jnp.bfloat16)
    query_acc = jnp.einsum(
        SPEC_2, score_grad, key_piece, preferred_element_type=jnp.float32
    )
    bias_acc = jnp.einsum(SPEC_7, onehot, score_grad, preferred_element_type=jnp.float32)
    query_acc, bias_acc = (query_acc, bias_acc)
    query_piece = lax.all_gather(queries, SEQ, axis=0, tiled=True)
    grad_piece = lax.all_gather(attended_grad, SEQ, axis=0, tiled=True)
    piece_rows = query_piece.shape[0]
    query_rows = jnp.arange(piece_rows, dtype=jnp.int32)
    visible, onehot, pair_bias = pair_terms(
        token_info(query_rows, starts, before, reaches), own_meta, query_rows, own_rows, bias_grid
    )
    scores = masked_scores(query_piece, keys_own, visible, pair_bias)
    soft_weights = jnp.exp(scores - total_all[:, :, None])
    value_acc = jnp.einsum(
        SPEC_8,
        soft_weights.astype(jnp.bfloat16),
        grad_piece,
        preferred_element_type=jnp.float32,
    )
    dprob = jnp.einsum(SPEC_1, grad_piece, values_own, preferred_element_type=jnp.float32)
    score_grad = (soft_weights * (dprob - delta_all[:, :, None])).astype(jnp.bfloat16)
    key_acc = jnp.einsum(
        SPEC_8, score_grad, query_piece, preferred_element_type=jnp.float32
    )
    key_acc, value_acc = (key_acc, value_acc)
    query_back = (query_acc * score_scale).astype(jnp.bfloat16).reshape(row_count, D)
    key_back = (key_acc * score_scale).astype(jnp.bfloat16).reshape(row_count, D)
    value_back = value_acc.astype(jnp.bfloat16).reshape(row_count, D)
    query_term = jnp.einsum(SPEC_5, normed_one, query_back, preferred_element_type=jnp.float32)
    key_term = jnp.einsum(SPEC_5, normed_one, key_back, preferred_element_type=jnp.float32)
    value_term = jnp.einsum(SPEC_5, normed_one, value_back, preferred_element_type=jnp.float32)
    normed_one_grad = jnp.einsum(
        SPEC_6, query_back, query_full, preferred_element_type=jnp.float32
    )
    normed_one_grad = normed_one_grad + jnp.einsum(
        SPEC_6, key_back, key_full, preferred_element_type=jnp.float32
    )
    normed_one_grad = normed_one_grad + jnp.einsum(
        SPEC_6, value_back, value_full, preferred_element_type=jnp.float32
    )
    gain_one_term = jnp.sum(normed_one_grad * unit_one, axis=0)
    unit_grad_one = normed_one_grad * gain_one.astype(jnp.float32)
    tokens_grad = residual_grad + scale_one * (
        unit_grad_one - unit_one * jnp.mean(unit_grad_one * unit_one, axis=-1, keepdims=True)
    )
    stats_term = jnp.broadcast_to(local_sums[None, :], (all_count, 2))
    reduced = (
        lax.psum_scatter(gain_one_term, BOTH, scatter_dimension=0, tiled=True),
        lax.psum_scatter(query_term, BOTH, scatter_dimension=0, tiled=True),
        lax.psum_scatter(key_term, BOTH, scatter_dimension=0, tiled=True),
        lax.psum_scatter(value_term, BOTH, scatter_dimension=0, tiled=True),
        lax.psum_scatter(output_term, BOTH, scatter_dimension=0, tiled=True),
        lax.psum_scatter(
            bias_acc.reshape(BUCKETS * HEADS), BOTH, scatter_dimension=0, tiled=True
        ),
        lax.psum_scatter(gain_two_term, BOTH, scatter_dimension=0, tiled=True),
        lax.psum_scatter(router_term, BOTH, scatter_dimension=0, tiled=True),
        lax.psum_scatter(stats_term, BOTH, scatter_dimension=0, tiled=True),
    )
    roots = jnp.sqrt(reduced[8][0] / (row_count * all_count * D))
    return (
        layer_out,
        tokens_grad,
        reduced[0],
        reduced[1],
        reduced[2],
        reduced[3],
        reduced[4],
        reduced[5],
        reduced[6],
        reduced[7],
        expert_grads[None, :, 0, :],
        expert_grads[None, :, 1, :],
        expert_grads[None, :, 2, :],
        roots,
    )


def solution(mesh):
    kernels_fit = mesh.shape[EXPERT] == len(ORDER) and mesh.shape[SEQ] == 4
    return jax.shard_map(
        per_device_kernels if kernels_fit else per_device_general,
        mesh=mesh,
        in_specs=(
            P(BOTH, None),
            P(BOTH, None),
            P(BOTH, None),
            P(EXPERT, None),
            P(EXPERT, None),
            P(BOTH),
            P(BOTH, None),
            P(BOTH, None),
            P(BOTH, None),
            P(BOTH, None),
            P(BOTH),
            P(BOTH),
            P(BOTH, None),
            P(EXPERT, SEQ, None),
            P(EXPERT, SEQ, None),
            P(EXPERT, SEQ, None),
        ),
        out_specs=(
            P(BOTH, None),
            P(BOTH, None),
            P(BOTH),
            P(BOTH, None),
            P(BOTH, None),
            P(BOTH, None),
            P(BOTH, None),
            P(BOTH),
            P(BOTH),
            P(BOTH, None),
            P(EXPERT, SEQ, None),
            P(EXPERT, SEQ, None),
            P(EXPERT, SEQ, None),
            P(),
        ),
        check_vma=False,
    )
```

```python
import math

import jax
import jax.numpy as jnp
from jax import lax
from jax.experimental import pallas as pl
from jax.experimental.pallas import tpu as pltpu
from jax.sharding import PartitionSpec as P

SPEC_0 = "qkb,bh->hqk"
SPEC_1 = "qhd,khd->hqk"
SPEC_2 = "hqk,khd->qhd"
SPEC_3 = "rd,fd->rf"
SPEC_4 = "rf,rd->fd"
SPEC_5 = "rd,re->de"
SPEC_6 = "re,de->rd"
SPEC_7 = "qkb,hqk->bh"
SPEC_8 = "hqk,qhd->khd"
MESH = pl.DeviceIdType.MESH
VMEM_LIMIT = 62 << 20
EXPERT, SEQ = "expert", "seq"
BOTH = (EXPERT, SEQ)

D = 1024
HEADS = 16
HDIM = 64
BUCKETS = 32
MAXDIST = 128


EPSILON = 1e-06
NEGATIVE = -1e30


def norm_factor(values):
    return lax.rsqrt(jnp.mean(values * values, axis=-1, keepdims=True) + EPSILON)


def gelu_tanh(values):
    return jax.nn.gelu(values, approximate=True)


def bucket_of(distance):
    exact_span = BUCKETS // 2
    above = jnp.zeros(distance.shape, jnp.int32)
    for number in range(exact_span):
        threshold = int(math.ceil(exact_span * (MAXDIST / exact_span) ** (number / exact_span)))
        above = above + (distance >= threshold).astype(jnp.int32)
    return jnp.where(distance < exact_span, distance, exact_span - 1 + above)


def tree_tables(lengths, parents):
    ordinal = jnp.arange(lengths.shape[0], dtype=jnp.int32)
    starts = jnp.cumsum(lengths) - lengths

    def chase(number, running):
        current, reaches = running
        current = jnp.sum(
            jnp.where(current[:, None] == ordinal[None, :], parents[None, :], 0), axis=1
        )
        reaches = jnp.maximum(reaches, (current[:, None] == ordinal[None, :]).astype(jnp.int32))
        return (current, reaches)

    begin = (ordinal, (ordinal[:, None] == ordinal[None, :]).astype(jnp.int32))
    unused, reaches = lax.fori_loop(0, lengths.shape[0], chase, begin)
    before = jnp.sum(reaches * lengths[None, :], axis=1) - lengths
    return (starts, before, reaches)


def token_info(token_rows, starts, before, reaches):
    ordinal = jnp.arange(starts.shape[0], dtype=jnp.int32)
    segment = jnp.sum((token_rows[:, None] >= starts[None, :]).astype(jnp.int32), axis=1) - 1
    member = segment[:, None] == ordinal[None, :]
    position = token_rows + jnp.sum(jnp.where(member, (before - starts)[None, :], 0), axis=1)
    lineage = jnp.sum(jnp.where(member[:, :, None], reaches[None, :, :], 0), axis=1)
    return (member.astype(jnp.float32), position, lineage.astype(jnp.float32))


def pair_terms(query_meta, key_meta, query_rows, key_rows, bias_grid):
    visible = jnp.dot(query_meta[2], key_meta[0].T, preferred_element_type=jnp.float32) > 0.5
    visible = visible & (key_rows[None, :] <= query_rows[:, None])
    distance = jnp.maximum(query_meta[1][:, None] - key_meta[1][None, :], 0)
    onehot = (
        bucket_of(distance)[:, :, None] == jnp.arange(BUCKETS, dtype=jnp.int32)[None, None, :]
    ).astype(jnp.bfloat16)
    pair_bias = jnp.einsum(SPEC_0, onehot, bias_grid, preferred_element_type=jnp.float32)
    return (visible, onehot, pair_bias)


def masked_scores(query_block, key_block, visible, pair_bias):
    scores = (
        jnp.einsum(SPEC_1, query_block, key_block, preferred_element_type=jnp.float32)
        * HDIM ** (-0.5)
        + pair_bias
    )
    return jnp.where(visible[None], scores, NEGATIVE)


def remote(src, dst, send, recv, peer):
    return pltpu.make_async_remote_copy(
        src_ref=src, dst_ref=dst, send_sem=send, recv_sem=recv,
        device_id=peer, device_id_type=MESH,
    )


def contract(left, right, dims):
    return lax.dot_general(left, right, (dims, ((), ())), preferred_element_type=jnp.float32)


def gelu_parts(values):
    root = 0.7978845608028654
    square = values * values
    swing = jnp.tanh(root * values * (1.0 + 0.044715 * square))
    half = 0.5 * (1.0 + swing)
    slope = half + 0.5 * values * (1.0 - swing * swing) * (root * (1.0 + 3 * 0.044715 * square))
    return values * half, slope


ORDER = (0, 1, 2, 3, 4, 5, 6, 7)
UNITS = (
    (0, 0), (1, 0), (2, 0), (0, 1), (3, 0), (1, 1), (2, 1), (0, 2),
    (3, 1), (1, 2), (2, 2), (0, 3), (3, 2), (1, 3), (2, 3), (3, 3),
)


def expert_kernel(
    xs, gs, wg_far, wu_far, wd_far, ret_o, ret_b, dwg, dwu, dwd,
    xr, gr, act, gb, ub, po, pb, ro, rb, ro2, rb2, stage, rounded, wg, wu, wd,
    in_send, in_recv, hop_send, hop_recv, rs_send, rs_recv, out_send, out_recv, stage_sem, load_sem, own_sem,
):
    e = lax.axis_index(EXPERT)
    s = lax.axis_index(SEQ)
    cap = xs.shape[0] // 8
    near_x, near_y = (e, s ^ 1), (e, s ^ 2)
    loads = [
        pltpu.make_async_copy(src, dst, load_sem.at[k])
        for k, (src, dst) in enumerate(((wg_far, wg), (wu_far, wu), (wd_far, wd)))
    ]
    for load in loads:
        load.start()
    barrier = pltpu.get_barrier_semaphore()
    peers = [near_x, near_y] + [(e ^ d, s) for d in range(1, 8)]
    for peer in peers:
        pl.semaphore_signal(barrier, inc=1, device_id=peer, device_id_type=MESH)
    pl.semaphore_wait(barrier, len(peers))

    def block(index):
        return pl.ds(pl.multiple_of(index * cap, 16), cap)

    tensors = ((xs, xr), (gs, gr))

    def entry(kind, place):
        src, dst = tensors[kind]
        d = ORDER[place]
        return remote(src.at[block(e ^ d)], dst.at[0, place], in_send.at[kind, place],
                      in_recv.at[kind, place], (e ^ d, s))

    def hop(kind, which, pair):
        buf = tensors[kind][1]
        two = pl.ds(2 * pair, 2)
        if which == 0:
            src, dst, peer = buf.at[0, two], buf.at[1, two], near_x
        elif which == 1:
            src, dst, peer = buf.at[0, two], buf.at[2, two], near_y
        elif kind == 0:
            src, dst, peer = buf.at[1, two], buf.at[3, two], near_y
        else:
            src, dst, peer = buf.at[2, two], buf.at[3, two], near_x
        return remote(src, dst, hop_send.at[kind, which, pair], hop_recv.at[kind, which, pair], peer)

    def rs(kind, which, c):
        part, one, two = ((po, ro, ro2), (pb, rb, rb2))[kind]
        first, second = ((near_x, near_y), (near_y, near_x))[kind]
        mine = 1 + kind
        if which == 0:
            src, dst, peer = part.at[mine, c], one.at[0, c], first
        elif which == 1:
            src, dst, peer = part.at[3, c], one.at[1, c], first
        else:
            src, dst, peer = part.at[2 - kind, c], two.at[c], second
        return remote(src, dst, rs_send.at[kind, which, c], rs_recv.at[kind, which, c], peer)

    def back(kind, place):
        part = (po, pb)[kind]
        ret = (ret_o, ret_b)[kind]
        c, i = place // 2, place % 2
        return remote(part.at[0, c, pl.ds(i * cap, cap)], ret.at[block(e)],
                      out_send.at[kind, place], out_recv.at[kind, place], (e ^ ORDER[place], s))

    def own_back(kind):
        return pltpu.make_async_copy((po, pb)[kind].at[0, 0, pl.ds(0, cap)], (ret_o, ret_b)[kind].at[block(e)],
                                     own_sem.at[2 + kind])

    def start_entries(pair):
        for kind in range(2):
            for place in (2 * pair, 2 * pair + 1):
                if ORDER[place]:
                    entry(kind, place).start()

    def forward_pair(pair):
        for kind in range(2):
            for place in (2 * pair, 2 * pair + 1):
                if ORDER[place]:
                    entry(kind, place).wait_recv()
            hop(kind, 0, pair).start()
            hop(kind, 1, pair).start()

    def forward_corner(pair):
        hop(0, 0, pair).wait_recv()
        hop(0, 2, pair).start()
        hop(1, 1, pair).wait_recv()
        hop(1, 2, pair).start()

    def start_sums(pair):
        for which in (1, 0):
            for kind in range(2):
                rs(kind, which, pair).start()

    def add_second(pair):
        for kind in range(2):
            rs(kind, 1, pair).wait_recv()
            part, one = ((po, ro), (pb, rb))[kind]
            group = 2 - kind
            part[group, pair] = (
                part[group, pair].astype(jnp.float32) + one[1, pair].astype(jnp.float32)
            ).astype(jnp.bfloat16)
            rs(kind, 2, pair).start()

    def finish(pair):
        for kind in range(2):
            rs(kind, 0, pair).wait_recv()
            rs(kind, 2, pair).wait_recv()
            part, one, two = ((po, ro, ro2), (pb, rb, rb2))[kind]
            part[0, pair] = (
                part[0, pair].astype(jnp.float32) + one[0, pair].astype(jnp.float32) + two[pair].astype(jnp.float32)
            ).astype(jnp.bfloat16)
            for i in range(2):
                if ORDER[2 * pair + i]:
                    back(kind, 2 * pair + i).start()
                else:
                    own_back(kind).start()

    own_rows = [
        pltpu.make_async_copy(src.at[block(e)], dst.at[0, 0], own_sem.at[kind])
        for kind, (src, dst) in enumerate(tensors)
    ]
    for copy in own_rows:
        copy.start()
    start_entries(0)
    start_entries(1)

    rows = 2 * cap

    def unit(u, carry):
        q, c = jnp.int32(0), jnp.int32(0)
        for k, (whose, pair) in enumerate(UNITS):
            q, c = jnp.where(u == k, whose, q), jnp.where(u == k, pair, c)

        for k, (whose, pair) in enumerate(UNITS):
            @pl.when(u == k)
            def _():
                if k == 0:
                    for copy in own_rows:
                        copy.wait()
                    forward_pair(0)
                    start_entries(2)
                    for load in loads:
                        load.wait()
                if (whose, pair) in ((1, 0), (3, 0), (3, 1)):
                    ahead = {(1, 0): 1, (3, 0): 2, (3, 1): 3}[whose, pair]
                    forward_corner(ahead - 1)
                    forward_pair(ahead)
                    if ahead == 1:
                        start_entries(3)
                if (whose, pair) == (3, 2):
                    forward_corner(3)
                if whose == 1:
                    hop(1, 0, pair).wait_recv()
                if whose == 2:
                    hop(0, 1, pair).wait_recv()
                if whose == 3:
                    hop(0, 2, pair).wait_recv()
                    hop(1, 2, pair).wait_recv()

        x = xr[q, pl.ds(2 * c, 2)].reshape(rows, xs.shape[1])
        g = gr[q, pl.ds(2 * c, 2)].reshape(rows, xs.shape[1])
        gate = contract(x, wg[...], ((1,), (1,)))
        up = contract(x, wu[...], ((1,), (1,)))
        ag = contract(g, wd[...], ((1,), (1,)))
        value, slope = gelu_parts(gate)
        active = (value * up).astype(jnp.bfloat16)
        gate_back = (ag * up * slope).astype(jnp.bfloat16)
        up_back = (ag * value).astype(jnp.bfloat16)
        act[q, c] = active
        gb[q, c] = gate_back
        ub[q, c] = up_back
        po[q, c] = contract(active, wd[...], ((1,), (0,))).astype(jnp.bfloat16)
        pb[q, c] = (
            contract(gate_back, wg[...], ((1,), (0,))) + contract(up_back, wu[...], ((1,), (0,)))
        ).astype(jnp.bfloat16)

        for k, (whose, pair) in enumerate(UNITS):
            if whose == 3 and pair == 2:
                @pl.when(u == k)
                def _():
                    start_sums(pair)
        return carry

    lax.fori_loop(0, len(UNITS), unit, 0)

    def grads(left, right, dst):
        def part(u):
            q, c = lax.rem(u, 4), u // 4
            return contract(left[q, pl.ds(2 * c, 2)].reshape(2 * rows, wg.shape[0]),
                            right[q, pl.ds(4 * c, 4)].reshape(2 * rows, xs.shape[1]), ((0,), (0,)))

        def more(u, carry):
            stage[...] += part(u)
            return carry

        stage[...] = part(0)
        lax.fori_loop(1, 8, more, 0)
        rounded[...] = stage[...].astype(jnp.bfloat16)
        done = pltpu.make_async_copy(rounded, dst, stage_sem)
        done.start()
        return done

    add_second(2)
    start_sums(3)
    done = grads(gb, xr, dwg)
    finish(2)
    add_second(3)
    start_sums(1)
    done.wait()
    done = grads(ub, xr, dwu)
    finish(3)
    add_second(1)
    start_sums(0)
    done.wait()
    done = grads(act, gr, dwd)
    finish(1)
    add_second(0)
    finish(0)
    done.wait()

    for kind in range(2):
        own_back(kind).wait()
        for place in range(8):
            if ORDER[place]:
                entry(kind, place).wait_send()
                back(kind, place).wait()
        for which in range(3):
            for pair in range(4):
                hop(kind, which, pair).wait_send()
                rs(kind, which, pair).wait_send()


def experts(send_rows, grad_rows, gate_weight, up_weight, down_weight):
    rows, width = send_rows.shape
    units = gate_weight.shape[0]
    cap = rows // 8
    low, full = jnp.bfloat16, jnp.float32
    vmem = pl.BlockSpec(memory_space=pltpu.VMEM)
    hbm = pl.BlockSpec(memory_space=pl.ANY)
    dma = pltpu.SemaphoreType.DMA
    return pl.pallas_call(
        expert_kernel,
        out_shape=(
            jax.ShapeDtypeStruct((rows, width), low),
            jax.ShapeDtypeStruct((rows, width), low),
        ) + (jax.ShapeDtypeStruct((units, width), low),) * 3,
        in_specs=[hbm] * 5,
        out_specs=(hbm,) * 5,
        scratch_shapes=[
            pltpu.VMEM((4, 8, cap, width), low),
            pltpu.VMEM((4, 8, cap, width), low),
            pltpu.VMEM((4, 4, 2 * cap, units), low),
            pltpu.VMEM((4, 4, 2 * cap, units), low),
            pltpu.VMEM((4, 4, 2 * cap, units), low),
            pltpu.VMEM((4, 4, 2 * cap, width), low),
            pltpu.VMEM((4, 4, 2 * cap, width), low),
            pltpu.VMEM((2, 4, 2 * cap, width), low),
            pltpu.VMEM((2, 4, 2 * cap, width), low),
            pltpu.VMEM((4, 2 * cap, width), low),
            pltpu.VMEM((4, 2 * cap, width), low),
            pltpu.VMEM((units, width), full),
            pltpu.VMEM((units, width), low),
            pltpu.VMEM((units, width), low),
            pltpu.VMEM((units, width), low),
            pltpu.VMEM((units, width), low),
            dma((2, 8)), dma((2, 8)),
            dma((2, 3, 4)), dma((2, 3, 4)),
            dma((2, 3, 4)), dma((2, 3, 4)),
            dma((2, 8)), dma((2, 8)),
            dma, dma((3,)), dma((4,)),
        ],
        compiler_params=pltpu.CompilerParams(
            collective_id=1, has_side_effects=True, vmem_limit_bytes=VMEM_LIMIT
        ),
        cost_estimate=pl.CostEstimate(flops=2 * 9 * 4 * rows * units * width, bytes_accessed=20 << 20, transcendentals=4 * rows * units),
        name="experts",
    )(send_rows, grad_rows, gate_weight, up_weight, down_weight)


def greet(peers):
    barrier = pltpu.get_barrier_semaphore()
    for peer in peers:
        pl.semaphore_signal(barrier, inc=1, device_id=peer, device_id_type=MESH)
    pl.semaphore_wait(barrier, len(peers))


def aligned(index, size):
    return pl.ds(pl.multiple_of(index * size, size), size)


ZHOPS = (2, 4, 6)


def segment_scalars(lengths, parents, before_mem, reach_mem):
    count = lengths.shape[1]
    start = jnp.int32(0)
    found = []
    for k in range(count):
        length = lengths[0, k]
        if k == 0:
            before, reach = jnp.int32(0), jnp.int32(1)
        else:
            parent = parents[0, k]
            before = before_mem[parent] + lengths[0, parent]
            reach = reach_mem[parent] | (1 << k)
        before_mem[k] = before
        reach_mem[k] = reach
        found.append((start, before, reach, length))
        start = start + length
    return found


def token_columns(found, ids):
    offset = jnp.zeros(ids.shape, jnp.int32)
    reach = jnp.full(ids.shape, 1, jnp.int32)
    own = jnp.full(ids.shape, 1, jnp.int32)
    for k, (start, before, bits, _) in enumerate(found):
        if k:
            after = ids >= start
            offset = jnp.where(after, before - start, offset)
            reach = jnp.where(after, bits, reach)
            own = jnp.where(after, 1 << k, own)
    return ids + offset, reach, own


LAST = 127


def bias_tables(params, s):
    flat = params[2:3, 0:BUCKETS * HEADS]
    lane = lax.broadcasted_iota(jnp.int32, (8, BUCKETS * HEADS), 1)
    head = lax.broadcasted_iota(jnp.int32, (8, BUCKETS * HEADS), 0)
    heads_here = HEADS // 4
    chosen = jnp.where((lane % HEADS) == s * heads_here + head, jnp.broadcast_to(flat, lane.shape), 0.0)
    entry = lax.broadcasted_iota(jnp.int32, (BUCKETS * HEADS, LAST + 1), 0) // HEADS
    distance = lax.broadcasted_iota(jnp.int32, (BUCKETS * HEADS, LAST + 1), 1)
    hot = jnp.where(entry == bucket_of(distance), 1.0, 0.0)
    table = contract(chosen.astype(jnp.bfloat16), hot.astype(jnp.bfloat16), ((1,), (0,)))
    spot = lax.broadcasted_iota(jnp.int32, table.shape, 1)
    return jnp.where(spot == LAST, NEGATIVE, table)


def pair_index(found, first, rows, count):
    ids = first + lax.broadcasted_iota(jnp.int32, (rows, 1), 0)
    keys = lax.broadcasted_iota(jnp.int32, (1, count), 1)
    place, reach, _ = token_columns(found, ids)
    key_place, _, key_own = token_columns(found, keys)
    seen = ((reach & key_own) != 0) & (keys <= ids)
    return jnp.where(seen, jnp.minimum(place - key_place, LAST - 1), LAST), place, reach


def looked_up(row, index):
    rows, count = index.shape
    table = jnp.broadcast_to(row, (rows, LAST + 1))
    pieces = [
        jnp.take_along_axis(table, index[:, k * 128:(k + 1) * 128], axis=1)
        for k in range(count // 128)
    ]
    return jnp.concatenate(pieces, axis=1)


def routing(residual, params, ids_row, cap):
    rows = residual.shape[0]
    full, low = jnp.float32, jnp.bfloat16
    scale = norm_factor(residual)
    unit = residual * scale
    normed = (unit * params[1:2]).astype(low)
    router = params[8:16]
    logits = contract(normed, router.astype(low), ((1,), (1,)))
    expo = jnp.exp(logits - jnp.max(logits, axis=1, keepdims=True))
    prob = expo / jnp.sum(expo, axis=1, keepdims=True)
    level = lax.broadcasted_iota(jnp.int32, (8, rows), 0)
    hot_row = [jnp.where(ids_row[k:k + 1] == level, 1.0, 0.0).astype(full) for k in range(2)]
    down = lax.broadcasted_iota(jnp.int32, (rows, rows), 0)
    across = lax.broadcasted_iota(jnp.int32, (rows, rows), 1)
    after = jnp.where(down < across, 1.0, 0.0).astype(low)
    earlier = contract((hot_row[0] + hot_row[1]).astype(low), after, ((1,), (0,)))
    slot_row = [jnp.sum(h * earlier, axis=0, keepdims=True) for h in hot_row]
    kept_row = [jnp.where(slot < cap, 1.0, 0.0) for slot in slot_row]
    spot_row = [
        jnp.where(slot_row[k] < cap, ids_row[k:k + 1].astype(full) * cap + slot_row[k], -1.0) for k in range(2)
    ]
    target_row = [spot.astype(jnp.int32) for spot in spot_row]
    columns = jnp.transpose(jnp.concatenate(spot_row + kept_row + [jnp.zeros((4, rows), full)], axis=0))
    target = [columns[:, k:k + 1].astype(jnp.int32) for k in range(2)]
    kept = [columns[:, 2 + k:3 + k] for k in range(2)]
    hot = [jnp.transpose(h) for h in hot_row]
    chosen = [jnp.sum(h * prob, axis=1, keepdims=True) for h in hot]
    chosen_sum = chosen[0] + chosen[1]
    shares = [c / chosen_sum for c in chosen]
    return scale, unit, normed, router, prob, hot, chosen_sum, shares, kept, target, target_row


def front_kernel(
    lengths, parents, tokens, cotangent, ids_row, wq, wk, wv, wo, gain_one, gain_two, bias, router_row,
    xs, gs, residual, all_tokens_far, qkv_far, cols_far, params, att_far, stats_far, wo_far,
    all_tokens, qkv, cols, wo_full, att, stats, got, part, normed, misc, tags, tag_sum, all_tags, index, table, landed,
    before_mem, reach_mem,
    t_send, t_recv, w_send, w_recv, m_send, m_recv, c_send, c_recv, n_send, n_recv,
    o_send, o_recv, g_send, g_recv, h_send, h_recv, a_send, a_recv, far_sem,
):
    e, s = lax.axis_index(EXPERT), lax.axis_index(SEQ)
    near_x, near_y, corner = (e, s ^ 1), (e, s ^ 2), (e, s ^ 3)
    around = (near_x, near_y, corner)
    hops = (1,) + ZHOPS
    low, full = jnp.bfloat16, jnp.float32
    rows, width = tokens.shape
    slim = wq.shape[0]
    shard = width // 4
    weights = (wq, wk, wv)
    place = e * 4 + s

    at_gain = lax.broadcasted_iota(jnp.int32, (slim, width), 1) == place * slim + lax.broadcasted_iota(
        jnp.int32, (slim, width), 0)
    gain_spot = jnp.where(at_gain, 1.0, 0.0).astype(low)
    few = bias.shape[1]
    at_bias = lax.broadcasted_iota(jnp.int32, (few, width), 1) == place * few + lax.broadcasted_iota(
        jnp.int32, (few, width), 0)
    bias_spot = jnp.where(at_bias, 1.0, 0.0).astype(low)
    two_gains = [contract(one[...], gain_spot, ((1,), (0,))) for one in (gain_one, gain_two)]
    one_bias = contract(bias[...], bias_spot, ((1,), (0,)))
    misc[...] = jnp.concatenate(
        two_gains + [one_bias, jnp.zeros((5, width), full), contract(router_row[...], gain_spot, ((1,), (0,)))], axis=0
    ).astype(low)

    greet(list(around) + [(e ^ d, s) for d in hops])

    def send_tokens(k):
        return remote(tokens, all_tokens.at[aligned(s, rows)], t_send.at[k], t_recv.at[k], around[k])

    def pass_tokens(k):
        piece = pl.ds(pl.multiple_of((s ^ (1 + k)) * rows + k * (rows // 2), rows // 2), rows // 2)
        view = all_tokens.at[piece]
        return remote(view, view, t_send.at[2 + k], t_recv.at[2 + k], around[1 - k])

    def send_cols(k, m):
        return remote(
            weights[m].at[:, aligned(s ^ (k + 1), shard)], got.at[m, aligned(s, slim)],
            w_send.at[k, m], w_recv.at[k, m], around[k],
        )

    def send_tags(k):
        return remote(misc, tags.at[k], m_send.at[k], m_recv.at[k], around[k])

    def share(k, p):
        return remote(part.at[p], cols.at[p, aligned(e, 4 * slim)], c_send.at[p, k], c_recv.at[p, k], (e ^ hops[k], s))

    def share_tags(k):
        return remote(tag_sum, all_tags.at[k], n_send.at[k], n_recv.at[k], (e ^ hops[k], s))

    def relay(k, p):
        view = cols.at[p, aligned(e ^ hops[k], 4 * slim)]
        return remote(view, view, c_send.at[p, 3 + k], c_recv.at[p, 3 + k], (e ^ 1, s))

    def relay_tags(k):
        return remote(all_tags.at[k], all_tags.at[3 + k], n_send.at[3 + k], n_recv.at[3 + k], (e ^ 1, s))

    few_rows = slim // 2

    def share_out(k):
        return remote(wo.at[pl.ds(0, few_rows)], wo_full.at[e, s, 0], o_send.at[k], o_recv.at[k], (e ^ hops[k], s))

    def relay_out(k):
        view = wo_full.at[e ^ hops[k], s, 0]
        return remote(view, view, o_send.at[3 + k], o_recv.at[3 + k], (e ^ 1, s))

    def spread_out(k):
        view = wo_full.at[:, s, 0]
        return remote(view, view, g_send.at[k], g_recv.at[k], around[k])

    def pass_out(k):
        view = wo_full.at[pl.ds(4 * k, 4), s ^ (1 + k), 0]
        return remote(view, view, g_send.at[2 + k], g_recv.at[2 + k], around[1 - k])

    def early_out(k):
        return remote(wo.at[pl.ds(few_rows, few_rows)], wo_full.at[e, s, 1], h_send.at[k], h_recv.at[k], around[k])

    def along_out(k):
        view = wo_full.at[e, :, 1]
        return remote(view, view, h_send.at[3 + k], h_recv.at[3 + k], (e ^ hops[k], s))

    def relay_along(k):
        view = wo_full.at[e ^ hops[k], :, 1]
        return remote(view, view, h_send.at[6 + k], h_recv.at[6 + k], (e ^ 1, s))

    def give(r):
        return remote(att.at[pl.ds(r * rows, rows)], landed.at[s], a_send.at[r], a_recv.at[s ^ r], (e, r))

    far = []

    def keep(src, dst):
        copy = pltpu.make_async_copy(src, dst, far_sem.at[len(far)])
        copy.start()
        far.append(copy)

    for k in range(3):
        for m in range(3):
            send_cols(k, m).start()
        send_tags(k).start()
    for k in range(2):
        send_tokens(k).start()
    for k in range(3):
        early_out(k).start()
    for m in range(3):
        got[m, aligned(s, slim), :] = weights[m][:, aligned(s, shard)]
    all_tokens[aligned(s, rows), :] = tokens[...]
    wo_full[e, s] = wo[...].reshape(2, few_rows, width)
    found = segment_scalars(lengths, parents, before_mem, reach_mem)
    total = misc[...].astype(full)
    for k in range(3):
        send_tags(k).wait_recv()
        total += tags[k].astype(full)
    tag_sum[...] = total.astype(low)
    for k in range(4):
        share_tags(k).start()
    for k in range(3):
        for m in range(3):
            send_cols(k, m).wait_recv()
    for p in range(2):
        for m in range(3):
            part[p, :, m * 128:(m + 1) * 128] = got[m, :, p * 128:(p + 1) * 128]
    for k in (3, 2, 1, 0):
        share(k, 0).start()
    for k in range(4):
        share_out(k).start()
    for p in range(2):
        cols[p, aligned(e, 4 * slim), :] = part[p]
    stats[...] = jnp.zeros_like(stats)
    for r in range(4):
        index[r, :, :(r + 1) * rows] = pair_index(found, r * rows, rows, (r + 1) * rows)[0]
    for k in range(1, 4):
        share_tags(k).wait_recv()
        relay_tags(k).start()
    for k in range(2):
        send_tokens(k).wait_recv()
        pass_tokens(k).start()
    for k in range(1, 4):
        share(k, 0).wait_recv()
        relay(k, 0).start()
    for k in (3, 2, 1, 0):
        share(k, 1).start()
    share_tags(0).wait_recv()
    for k in range(1, 4):
        relay_tags(k).wait_recv()
    for k in range(7):
        total += all_tags[k].astype(full)
    params[...] = total
    gain = total[0:1]
    table[...] = bias_tables(params, s)

    def norm_block(q, carry):
        spot = aligned(s ^ q, rows)
        values = all_tokens[spot, :].astype(full)
        normed[spot, :] = (values * norm_factor(values) * gain).astype(low)
        return carry

    lax.fori_loop(0, 3, norm_block, 0)
    for k in range(1, 4):
        share_out(k).wait_recv()
        relay_out(k).start()
    for k in range(2):
        pass_tokens(k).wait_recv()
    lax.fori_loop(3, 4, norm_block, 0)
    share_out(0).wait_recv()
    for k in range(1, 4):
        relay_out(k).wait_recv()
    for k in range(2):
        spread_out(k).start()
    keep(all_tokens, all_tokens_far)

    def pair(p, carry):
        for which in range(2):
            @pl.when(p == which)
            def _():
                share(0, which).wait_recv()
                for k in range(1, 4):
                    relay(k, which).wait_recv()

        for r in range(4):
            out = contract(normed[r * rows:(r + 1) * rows, :], cols[p], ((1,), (0,)))
            first_part = out[:, 0:128].astype(low).astype(full) * HDIM ** (-0.5)
            qkv[p, r * rows:(r + 1) * rows, :] = jnp.concatenate([first_part, out[:, 128:]], axis=1).astype(low)

        for r in (3, 2, 1, 0):
            first, count = r * rows, (r + 1) * rows
            q = qkv[p, first:count, 0:128]
            k = qkv[p, 0:count, 128:256]
            v = qkv[p, 0:count, 256:384]
            lane = lax.broadcasted_iota(jnp.int32, (rows, 128), 1)
            results = []
            noted = stats[first:count, :]
            for side in range(2):
                mine = (lane // HDIM) == side
                scores = contract(jnp.where(mine, q, jnp.zeros_like(q)), k, ((1,), (1,)))
                scores = scores + looked_up(table[pl.ds(2 * p + side, 1), :], index[r, :, :count])
                peak = jnp.max(scores, axis=1, keepdims=True)
                expo = jnp.exp(scores - peak)
                mass = jnp.sum(expo, axis=1, keepdims=True)
                results.append(contract(expo.astype(low), v, ((1,), (0,))) * (1.0 / mass))
                noted = jnp.where(lane == 2 * p + side, peak + jnp.log(mass), noted)
            stats[first:count, :] = noted
            att[first:count, aligned(p, 128)] = jnp.where((lane // HDIM) == 0, results[0], results[1]).astype(low)

            @pl.when((p == 1) & (s != r))
            def _():
                give(r).start()

            if r == 3:
                @pl.when(p == 0)
                def _():
                    for i in range(3):
                        early_out(i).wait_recv()
                    for i in range(4):
                        along_out(i).start()

                @pl.when(p == 1)
                def _():
                    for i in range(2):
                        spread_out(i).wait_recv()
                        pass_out(i).start()
                    for i in range(1, 4):
                        along_out(i).wait_recv()
                        relay_along(i).start()
            if r == 1:
                @pl.when(p == 0)
                def _():
                    for i in range(1, 4):
                        share(i, 1).wait_recv()
                        relay(i, 1).start()
        return carry

    lax.fori_loop(0, 2, pair, 0)
    keep(qkv, qkv_far)
    keep(cols, cols_far)
    keep(att, att_far)
    keep(stats, stats_far)
    for k in range(2):
        pass_out(k).wait_recv()
    along_out(0).wait_recv()
    for k in range(1, 4):
        relay_along(k).wait_recv()
    keep(wo_full, wo_far)
    landed[s] = att[aligned(s, rows), :]
    total = tokens[...].astype(full)

    def out_rows(index):
        return wo_full[pl.ds(2 * index, 2)].reshape(shard, width)

    total += contract(landed[s], out_rows(s), ((1,), (0,)))
    for k in range(1, 4):
        remote(landed.at[s], landed.at[s ^ k], a_send.at[0], a_recv.at[k], (e, s ^ k)).wait_recv()
        total += contract(landed[s ^ k], out_rows(s ^ k), ((1,), (0,)))
    residual[...] = total
    cap = xs.shape[0] // 8
    _, _, normed, _, _, _, _, shares, kept, _, target_row = routing(total, params[...], ids_row[...], cap)
    spot = lax.broadcasted_iota(jnp.int32, (8 * cap, rows), 0)
    hot = [jnp.where(spot == target_row[k], 1.0, 0.0).astype(low) for k in range(2)]
    xs[...] = contract(hot[0] + hot[1], normed, ((1,), (0,))).astype(low)
    grad = cotangent[...].astype(full)
    weighted = [((shares[k] * kept[k]) * grad).astype(low) for k in range(2)]
    gs[...] = (
        contract(hot[0], weighted[0], ((1,), (0,))) + contract(hot[1], weighted[1], ((1,), (0,)))
    ).astype(low)

    for k in range(2):
        send_tokens(k).wait_send()
        pass_tokens(k).wait_send()
        spread_out(k).wait_send()
        pass_out(k).wait_send()
    for k in range(3):
        for m in range(3):
            send_cols(k, m).wait_send()
        send_tags(k).wait_send()
        early_out(k).wait_send()
    for k in range(4):
        share_tags(k).wait_send()
        share_out(k).wait_send()
        along_out(k).wait_send()
        for p in range(2):
            share(k, p).wait_send()
    for k in range(1, 4):
        relay_tags(k).wait_send()
        relay_out(k).wait_send()
        relay_along(k).wait_send()
        for p in range(2):
            relay(k, p).wait_send()
    for r in range(4):
        @pl.when(s != r)
        def _():
            give(r).wait_send()
    for copy in far:
        copy.wait()


def front(lengths, parents, tokens, cotangent, ids_row, wq, wk, wv, wo, gain_one, gain_two, bias, router_row):
    rows, width = tokens.shape
    slim, shard = wq.shape[0], width // 4
    cap = 10 * rows // 32
    low, full = jnp.bfloat16, jnp.float32
    vmem, smem, hbm = (pl.BlockSpec(memory_space=m) for m in (pltpu.VMEM, pltpu.SMEM, pl.ANY))
    dma = pltpu.SemaphoreType.DMA
    kept = (
        jax.ShapeDtypeStruct((4 * rows, width), low),
        jax.ShapeDtypeStruct((2, 4 * rows, 3 * shard // 2), low),
        jax.ShapeDtypeStruct((2, width, 3 * shard // 2), low),
        jax.ShapeDtypeStruct((16, width), full),
        jax.ShapeDtypeStruct((4 * rows, shard), low),
        jax.ShapeDtypeStruct((4 * rows, 128), full),
        jax.ShapeDtypeStruct((8, 4, 2, slim // 2, width), low),
    )
    return pl.pallas_call(
        front_kernel,
        out_shape=(
            jax.ShapeDtypeStruct((8 * cap, width), low),
            jax.ShapeDtypeStruct((8 * cap, width), low),
            jax.ShapeDtypeStruct((rows, width), full),
        ) + kept,
        in_specs=[smem, smem] + [vmem] * 11,
        out_specs=(vmem, vmem, vmem, hbm, hbm, hbm, vmem, hbm, hbm, hbm),
        scratch_shapes=[
            pltpu.VMEM(kept[0].shape, low), pltpu.VMEM(kept[1].shape, low), pltpu.VMEM(kept[2].shape, low),
            pltpu.VMEM(kept[6].shape, low), pltpu.VMEM(kept[4].shape, low), pltpu.VMEM(kept[5].shape, full),
            pltpu.VMEM((3, 4 * slim, shard), low), pltpu.VMEM((2, 4 * slim, 3 * shard // 2), low),
            pltpu.VMEM((4 * rows, width), low),
            pltpu.VMEM((16, width), low), pltpu.VMEM((3, 16, width), low), pltpu.VMEM((16, width), low),
            pltpu.VMEM((7, 16, width), low),
            pltpu.VMEM((4, rows, 4 * rows), jnp.int32), pltpu.VMEM((8, 128), full),
            pltpu.VMEM((4, rows, shard), low),
            pltpu.SMEM((16,), jnp.int32), pltpu.SMEM((16,), jnp.int32),
            dma((4,)), dma((4,)), dma((3, 3)), dma((3, 3)), dma((3,)), dma((3,)),
            dma((2, 7)), dma((2, 7)), dma((7,)), dma((7,)), dma((7,)), dma((7,)), dma((4,)), dma((4,)),
            dma((10,)), dma((10,)), dma((4,)), dma((4,)), dma((6,)),
        ],
        compiler_params=pltpu.CompilerParams(
            collective_id=2, has_side_effects=True, vmem_limit_bytes=VMEM_LIMIT
        ),
        cost_estimate=pl.CostEstimate(flops=40 * rows * width * shard, bytes_accessed=24 << 20, transcendentals=8 * rows * rows * 16),
        name="front",
    )(lengths, parents, tokens, cotangent, ids_row, wq, wk, wv, wo, gain_one, gain_two, bias, router_row)


def pair_index_across(found, first, rows, count):
    ids = first + lax.broadcasted_iota(jnp.int32, (1, rows), 1)
    keys = lax.broadcasted_iota(jnp.int32, (count, 1), 0)
    place, reach, _ = token_columns(found, ids)
    key_place, _, key_own = token_columns(found, keys)
    seen = ((reach & key_own) != 0) & (keys <= ids)
    return jnp.where(seen, jnp.minimum(place - key_place, LAST - 1), LAST)


def near_keys(found, first, rows):
    ids = first + lax.broadcasted_iota(jnp.int32, (rows, 1), 0)
    place, reach, _ = token_columns(found, ids)
    step = lax.broadcasted_iota(jnp.int32, (rows, LAST + 1), 1)
    wanted = place - step
    spot = jnp.full((rows, LAST + 1), -1, jnp.int32)
    for k, (start, before, _, length) in enumerate(found):
        inside = ((reach & (1 << k)) != 0) & (wanted >= before) & (wanted < before + length)
        spot = jnp.where(inside, wanted + (start - before), spot)
    return jnp.where(step == LAST, -1, spot)


GROUPS = ((0, 3), (6, 2), (3, 3))


def back_kernel(
    lengths, parents, ids_row, params, ret_o_far, ret_b_far, residual_far, cotangent_far,
    wo_far, qkv_far, cols_far, all_tokens_far, att_far, stats_far,
    layer_out_far, tokens_grad, dwq, dwk, dwv, dwo, small_sum,
    ret_o, ret_b, residual, cotangent, layer_out, wo, qkv, cols, all_tokens, att, stats, datt, datt_own, aog_cols, aog_own, residual_grad,
    att_all, index, spots, lse, table, near, dk, dv, dqkv, normed,
    halves, core_got, sums, z_got, final, final_got, parts, first_got, second_got, mine, tally, tally_got,
    before_mem, reach_mem,
    load_sem, d_send, d_recv, g_send, g_recv, core_send, core_recv, z_send, z_recv, a_send, a_recv,
    n_send, n_recv, m_send, m_recv,
):
    e, s = lax.axis_index(EXPERT), lax.axis_index(SEQ)
    z, c = e // 2, lax.rem(e, 2)
    near_x, near_y = (e, s ^ 1), (e, s ^ 2)
    around = [(e, s ^ k) for k in range(1, 4)]
    hops = (1,) + ZHOPS
    full, low = jnp.float32, jnp.bfloat16
    high = lax.Precision.HIGHEST
    rows, width = residual.shape
    shard = att.shape[1]
    slim = dwq.shape[0]
    cap = ret_o.shape[0] // 8
    half = shard // 2
    pairs = (
        (residual_far, residual), (ret_o_far, ret_o), (cotangent_far, cotangent), (ret_b_far, ret_b), (wo_far, wo),
        (att_far, att), (stats_far, stats), (qkv_far, qkv), (all_tokens_far, all_tokens), (cols_far, cols),
    )
    loads = [pltpu.make_async_copy(src, dst, load_sem.at[k]) for k, (src, dst) in enumerate(pairs)]
    for load in loads:
        load.start()
    greet(around + [(e ^ d, s) for d in hops])

    def spread_att(k):
        return remote(att, att_all.at[s], g_send.at[k], g_recv.at[k], around[k])

    def pass_att(k):
        view = att_all.at[s ^ (1 + k), pl.ds(2 * rows * k, 2 * rows)]
        return remote(view, view, g_send.at[2 + k], g_recv.at[2 + k], around[1 - k])

    loads[5].wait()
    for k in range(2):
        spread_att(k).start()
    loads[0].wait()

    held = residual[...]
    scale, unit, unrouted, router, prob, hot, chosen_sum, shares, kept, target, _ = routing(
        held, params[...], ids_row[...], cap
    )
    place = lax.broadcasted_iota(jnp.int32, (rows, 8 * cap), 1)
    pick = [jnp.where(place == target[k], 1.0, 0.0).astype(low) for k in range(2)]
    for load in loads[1:5]:
        load.wait()
    grad = cotangent[...].astype(full)
    mixture = jnp.zeros((rows, width), full)
    share_grad = []
    for k in range(2):
        picked = contract(pick[k], ret_o[...], ((1,), (0,)))
        mixture += (shares[k] * kept[k]) * picked
        share_grad.append(jnp.sum(grad * picked, axis=1, keepdims=True) * kept[k])
    layer_out[...] = (held + mixture).astype(low)
    layer_done = pltpu.make_async_copy(layer_out, layer_out_far, load_sem.at[0])
    layer_done.start()
    inner = shares[0] * share_grad[0] + shares[1] * share_grad[1]
    prob_grad = sum(hot[k] * ((share_grad[k] - inner) / chosen_sum) for k in range(2))
    logit_grad = prob * (prob_grad - jnp.sum(prob * prob_grad, axis=1, keepdims=True))
    normed_grad = contract(pick[0] + pick[1], ret_b[...], ((1,), (0,))) + lax.dot_general(
        logit_grad, router, (((1,), (0,)), ((), ())), precision=high, preferred_element_type=full
    )
    unit_grad = normed_grad * params[1:2]
    passed = grad + scale * (unit_grad - unit * jnp.mean(unit_grad * unit, axis=1, keepdims=True))
    residual_grad[...] = passed
    aog_own[...] = passed.astype(low)
    datt_own[...] = contract(aog_own[...], wo[...], ((1,), (1,))).astype(low)

    def give(kind, k):
        src, dst = ((datt_own, datt), (aog_own, aog_cols))[kind]
        return remote(src.at[:, aligned(s ^ (k + 1), shard)], dst.at[aligned(s, rows)],
                      d_send.at[kind, k], d_recv.at[kind, k], around[k])

    for k in (2, 0, 1):
        give(0, k).start()

    for load in loads[6:]:
        load.wait()
    att_all[s] = att[...]
    datt[aligned(s, rows), :] = datt_own[:, aligned(s, shard)]
    aog_cols[aligned(s, rows), :] = aog_own[:, aligned(s, shard)]
    tally[0] = jnp.zeros((16, width), full)
    tally[0, 1:2] = jnp.sum(normed_grad * unit, axis=0, keepdims=True)
    lane = lax.broadcasted_iota(jnp.int32, (1, width), 1)
    tally[0, 3:4] = jnp.where(lane == 0, jnp.sum(held * held), jnp.where(lane == 1, jnp.sum(mixture * mixture), 0.0))
    tally[0, 8:16] = lax.dot_general(logit_grad, unrouted.astype(full), (((0,), (0,)), ((), ())),
                                     precision=high, preferred_element_type=full)
    found = segment_scalars(lengths, parents, before_mem, reach_mem)
    table[...] = bias_tables(params, s)
    near[...] = jnp.zeros_like(near)
    for r in range(4):
        index[r, :(r + 1) * rows] = pair_index_across(found, r * rows, rows, (r + 1) * rows)
        spots[r] = near_keys(found, r * rows, rows)
        turned = jnp.transpose(stats[r * rows:(r + 1) * rows, :])
        for h in range(4):
            lse[h, r] = turned[h:h + 1]
    gain = params[0:1]

    def units(q):
        values = all_tokens[aligned(s ^ q, rows), :].astype(full)
        factor = norm_factor(values)
        return values * factor, factor

    def norm_block(q, carry):
        normed[aligned(s ^ q, rows), :] = (units(q)[0] * gain).astype(low)
        return carry

    lax.fori_loop(0, 4, norm_block, 0)

    def core_copy(g):
        slots = pl.ds(*GROUPS[g])
        return remote(halves.at[1 - c, slots], core_got.at[slots], core_send.at[g], core_recv.at[g], (e ^ 1, s))

    def z_copy(g, k):
        slots = pl.ds(*GROUPS[g])
        return remote(sums.at[slots, z ^ k], z_got.at[k - 1, slots], z_send.at[g, k - 1], z_recv.at[g, k - 1],
                      (e ^ (2 * k), s))

    def a_copy(g, k):
        slots = pl.ds(*GROUPS[g])
        return remote(final.at[slots, aligned(s ^ (k + 1), slim)], final_got.at[s, slots],
                      a_send.at[g, k], a_recv.at[g, k], around[k])

    def store_halves(slot, zone, block):
        for i in range(2):
            halves[i, slot, zone] = block[i * half:(i + 1) * half].astype(low)

    def add_core(g):
        core_copy(g).wait_recv()
        first, amount = GROUPS[g]
        for slot in range(first, first + amount):
            for j in range(4):
                sums[slot, j] = (halves[c, slot, j].astype(full) + core_got[slot, j].astype(full)).astype(low)
        for k in range(1, 4):
            z_copy(g, k).start()

    def finish_grad(g):
        first, amount = GROUPS[g]
        for k in range(1, 4):
            z_copy(g, k).wait_recv()
        for slot in range(first, first + amount):
            block = sums[slot, z].astype(full)
            for k in range(1, 4):
                block += z_got[k - 1, slot].astype(full)
            final[slot] = block
        for k in range(3):
            a_copy(g, k).start()
        for slot in range(first, first + amount):
            final_got[s, slot] = final[slot, aligned(s, slim)]

    for k in range(3):
        give(0, k).wait_recv()
    for k in (2, 0, 1):
        give(1, k).start()
    for k in range(2):
        spread_att(k).wait_recv()
        pass_att(k).start()

    def pair(p, carry):
        lanes = aligned(p, 128)
        dk[...] = jnp.zeros_like(dk)
        dv[...] = jnp.zeros_like(dv)
        for r in (3, 2, 1, 0):
            first, count = r * rows, (r + 1) * rows
            q = qkv[p, first:count, 0:128]
            k = qkv[p, 0:count, 128:256]
            v = qkv[p, 0:count, 256:384]
            g = datt[first:count, lanes]
            lane = lax.broadcasted_iota(jnp.int32, (rows, 128), 1)
            lane_long = lax.broadcasted_iota(jnp.int32, (count, 128), 1)
            spot = spots[r]
            spot_lane, spot_block = spot & 127, jnp.where(spot < 0, -1, spot >> 7)
            dq = []
            key_sum, value_sum = 0.0, 0.0
            for side in range(2):
                mine_lanes = (lane // HDIM) == side
                q_side = jnp.where(mine_lanes, q, jnp.zeros_like(q))
                g_side = jnp.where(mine_lanes, g, jnp.zeros_like(g))
                scores = contract(k, q_side, ((1,), (1,)))
                scores = scores + looked_up(table[pl.ds(2 * p + side, 1), :], index[r, :count])
                soft = jnp.exp(scores - lse[2 * p + side, r])
                dprob = contract(v, g_side, ((1,), (1,)))
                delta = jnp.sum(soft * dprob, axis=0, keepdims=True)
                turned = soft * (dprob - delta)
                score_grad = turned.astype(low)
                key_sum = key_sum + contract(score_grad, q_side, ((1,), (0,)))
                value_sum = value_sum + contract(soft.astype(low), g_side, ((1,), (0,)))
                wide = jnp.transpose(turned)
                with_ones = jnp.where((lane_long // HDIM) == side, k, jnp.ones_like(k))
                part = contract(wide.astype(low), with_ones, ((1,), (0,)))
                dq.append(part)
                close = jnp.zeros((rows, 128), full)
                for b in range(count // 128):
                    taken = jnp.take_along_axis(wide[:, b * 128:(b + 1) * 128], spot_lane, axis=1)
                    close = jnp.where(spot_block == b, taken, close)
                near[0, 2 * p + side] += jnp.sum(close.reshape(rows // 8, 8, 128), axis=0)
                rest = jnp.where(mine_lanes, 0.0, part)
                near[1, 2 * p + side] += jnp.sum(rest.reshape(rows // 8, 8, 128), axis=0)
            dqkv[p, first:count, 0:128] = (jnp.where((lane // HDIM) == 0, dq[0], dq[1]) * HDIM ** (-0.5)).astype(low)
            dk[0:count] += key_sum
            dv[0:count] += value_sum

            if r == 3:
                @pl.when(p == 1)
                def _():
                    add_core(0)
                    for i in range(2):
                        pass_att(i).wait_recv()
                    for i in range(3):
                        give(1, i).wait_recv()

                    def output_zone(j, carry):
                        block = contract(att_all[j], aog_cols[...], ((0,), (0,)))
                        for i in range(2):
                            store_halves(6 + i, j, block[:, i * 128:(i + 1) * 128])
                        return carry

                    lax.fori_loop(0, 4, output_zone, 0)
                    core_copy(1).start()
            if r == 2:
                @pl.when(p == 1)
                def _():
                    add_core(1)
        dqkv[p, :, 128:256] = dk[...].astype(low)
        dqkv[p, :, 256:384] = dv[...].astype(low)

        def qkv_zone(j, carry):
            block = contract(normed[:, aligned(j, shard)], dqkv[p], ((0,), (0,)))
            for m in range(3):
                for i in range(2):
                    halves[i, 3 * p + m, j] = block[i * half:(i + 1) * half, m * 128:(m + 1) * 128].astype(low)
            return carry

        lax.fori_loop(0, 4, qkv_zone, 0)

        @pl.when(p == 0)
        def _():
            core_copy(0).start()

        @pl.when(p == 1)
        def _():
            core_copy(2).start()
        return carry

    lax.fori_loop(0, 2, pair, 0)

    def n_copy(kind, which):
        one, two = ((near_x, near_y), (near_y, near_x))[kind]
        if which < 2:
            src = parts.at[(1 + kind, 3)[which], kind]
            return remote(src, first_got.at[kind, which], n_send.at[kind, which], n_recv.at[kind, which], one)
        return remote(parts.at[2 - kind, kind], second_got.at[kind], n_send.at[kind, 2], n_recv.at[kind, 2], two)

    def back_block(i, carry):
        q = 3 - i
        total = jnp.zeros((rows, width), full)
        for p in range(2):
            total += contract(dqkv[p, aligned(s ^ q, rows), :], cols[p], ((1,), (1,)))
        tally[0, 0:1] += jnp.sum(total * units(q)[0], axis=0, keepdims=True)
        mine[...] = total
        for kind in range(2):
            parts[q, kind] = total[:, kind * (width // 2):(kind + 1) * (width // 2)].astype(low)

        @pl.when(i == 0)
        def _():
            n_copy(0, 1).start()
            n_copy(1, 1).start()
            add_core(2)

        @pl.when(i == 1)
        def _():
            n_copy(1, 0).start()

        @pl.when(i == 2)
        def _():
            n_copy(0, 0).start()
        return carry

    lax.fori_loop(0, 4, back_block, 0)

    close, rest = (
        jnp.concatenate([jnp.sum(near[kind, h], axis=0, keepdims=True) for h in range(8)], axis=0) for kind in range(2)
    )
    far = jnp.sum(rest, axis=1, keepdims=True) / HDIM - jnp.sum(close, axis=1, keepdims=True)
    spot = lax.broadcasted_iota(jnp.int32, close.shape, 1)
    by_distance = jnp.where(spot == LAST, far, close)
    lane = lax.broadcasted_iota(jnp.int32, (128, BUCKETS * HEADS), 1)
    distance = lax.broadcasted_iota(jnp.int32, (128, BUCKETS * HEADS), 0)
    hot_bucket = jnp.where((lane // HEADS) == bucket_of(distance), 1.0, 0.0)
    spread = lax.dot_general(by_distance, hot_bucket, (((1,), (0,)), ((), ())), precision=high, preferred_element_type=full)
    head = lax.broadcasted_iota(jnp.int32, spread.shape, 0)
    lane = lax.broadcasted_iota(jnp.int32, spread.shape, 1)
    here = ((lane % HEADS) == s * (HEADS // 4) + head) & (head < HEADS // 4)
    tally[0, 2:3, 0:BUCKETS * HEADS] = jnp.sum(jnp.where(here, spread, 0.0), axis=0, keepdims=True)

    def m_copy(stage, k):
        slot = (0, 3, 4)[stage] + k
        peer = (around[k], (e ^ 1, s), (e ^ (2 * (k + 1)), s))[stage]
        return remote(tally.at[stage], tally_got.at[slot], m_send.at[slot], m_recv.at[slot], peer)

    for k in range(3):
        m_copy(0, k).start()
    for kind in range(2):
        n_copy(kind, 1).wait_recv()
        group = 2 - kind
        parts[group, kind] = (parts[group, kind].astype(full) + first_got[kind, 1].astype(full)).astype(low)
        n_copy(kind, 2).start()
    finish_grad(0)
    finish_grad(1)
    total = tally[0]
    for k in range(3):
        m_copy(0, k).wait_recv()
        total += tally_got[k]
    tally[1] = total
    m_copy(1, 0).start()
    finish_grad(2)
    m_copy(1, 0).wait_recv()
    total = total + tally_got[3]
    tally[2] = total
    for k in range(3):
        m_copy(2, k).start()
    for kind in range(2):
        n_copy(kind, 0).wait_recv()
        n_copy(kind, 2).wait_recv()
        lanes = slice(kind * (width // 2), (kind + 1) * (width // 2))
        mine[:, lanes] += first_got[kind, 0].astype(full) + second_got[kind].astype(full)
    unit, scale = units(0)
    unit_grad = mine[...] * gain
    tokens_grad[...] = residual_grad[...] + scale * (
        unit_grad - unit * jnp.mean(unit_grad * unit, axis=1, keepdims=True)
    )
    for g in range(3):
        for k in range(3):
            a_copy(g, k).wait_recv()
    for m, out in enumerate((dwq, dwk, dwv, dwo)):
        for i in range(2):
            slot = (m + 3 * i) if m < 3 else 6 + i
            for j in range(4):
                out[:, j * shard + i * 128:j * shard + (i + 1) * 128] = final_got[j, slot]
    for k in range(3):
        m_copy(2, k).wait_recv()
        total += tally_got[4 + k]
    small_sum[...] = total
    layer_done.wait()
    for k in range(3):
        for kind in range(2):
            give(kind, k).wait_send()
        for g in range(3):
            z_copy(g, k + 1).wait_send()
            a_copy(g, k).wait_send()
        core_copy(k).wait_send()
    for k in range(2):
        spread_att(k).wait_send()
        pass_att(k).wait_send()
    for kind in range(2):
        for which in range(3):
            n_copy(kind, which).wait_send()
    for stage, amount in ((0, 3), (1, 1), (2, 3)):
        for k in range(amount):
            m_copy(stage, k).wait_send()


def back(lengths, parents, ids_row, params, ret_o, ret_b, residual, cotangent, wo, qkv, cols, all_tokens, att, stats):
    rows, width = residual.shape
    shard = att.shape[1]
    slim = width // 32
    low, full = jnp.bfloat16, jnp.float32
    vmem, smem, hbm = (pl.BlockSpec(memory_space=m) for m in (pltpu.VMEM, pltpu.SMEM, pl.ANY))
    dma = pltpu.SemaphoreType.DMA
    half = shard // 2
    return pl.pallas_call(
        back_kernel,
        out_shape=(
            jax.ShapeDtypeStruct((rows, width), low),
            jax.ShapeDtypeStruct((rows, width), full),
        ) + (jax.ShapeDtypeStruct((slim, width), full),) * 4 + (jax.ShapeDtypeStruct((16, width), full),),
        in_specs=[smem, smem] + [vmem] * 2 + [hbm] * 10,
        out_specs=(hbm,) + (vmem,) * 6,
        scratch_shapes=[
            pltpu.VMEM(ret_o.shape, low), pltpu.VMEM(ret_b.shape, low), pltpu.VMEM((rows, width), full),
            pltpu.VMEM((rows, width), low), pltpu.VMEM((rows, width), low),
            pltpu.VMEM((width, width), low), pltpu.VMEM(qkv.shape, low), pltpu.VMEM(cols.shape, low),
            pltpu.VMEM(all_tokens.shape, low), pltpu.VMEM(att.shape, low), pltpu.VMEM(stats.shape, full),
            pltpu.VMEM((4 * rows, shard), low), pltpu.VMEM((rows, width), low),
            pltpu.VMEM((4 * rows, shard), low), pltpu.VMEM((rows, width), low), pltpu.VMEM((rows, width), full),
            pltpu.VMEM((4, 4 * rows, shard), low),
            pltpu.VMEM((4, 4 * rows, rows), jnp.int32), pltpu.VMEM((4, rows, 128), jnp.int32),
            pltpu.VMEM((4, 4, 1, rows), full), pltpu.VMEM((8, 128), full), pltpu.VMEM((2, 8, 8, 128), full),
            pltpu.VMEM((4 * rows, 128), full), pltpu.VMEM((4 * rows, 128), full),
            pltpu.VMEM((2, 4 * rows, 3 * shard // 2), low), pltpu.VMEM((4 * rows, width), low),
            pltpu.VMEM((2, 8, 4, half, half), low), pltpu.VMEM((8, 4, half, half), low),
            pltpu.VMEM((8, 4, half, half), low), pltpu.VMEM((3, 8, half, half), low),
            pltpu.VMEM((8, half, half), full), pltpu.VMEM((4, 8, slim, half), full),
            pltpu.VMEM((4, 2, rows, width // 2), low), pltpu.VMEM((2, 2, rows, width // 2), low),
            pltpu.VMEM((2, rows, width // 2), low), pltpu.VMEM((rows, width), full),
            pltpu.VMEM((3, 16, width), full), pltpu.VMEM((7, 16, width), full),
            pltpu.SMEM((16,), jnp.int32), pltpu.SMEM((16,), jnp.int32),
            dma((10,)), dma((2, 3)), dma((2, 3)), dma((4,)), dma((4,)), dma((3,)), dma((3,)),
            dma((3, 3)), dma((3, 3)), dma((3, 3)), dma((3, 3)), dma((2, 3)), dma((2, 3)), dma((7,)), dma((7,)),
        ],
        compiler_params=pltpu.CompilerParams(
            collective_id=5, has_side_effects=True, vmem_limit_bytes=VMEM_LIMIT
        ),
        cost_estimate=pl.CostEstimate(flops=120 * rows * width * shard, bytes_accessed=20 << 20, transcendentals=8 * rows * rows * 16),
        name="back",
    )(lengths, parents, ids_row, params, ret_o, ret_b, residual, cotangent, wo, qkv, cols, all_tokens, att, stats)


def emit_kernel(*refs):
    large, small = refs[:9], refs[9]
    out, (gain_one, gain_two, bias, router, roots) = refs[10:19], refs[19:24]
    held, wide, in_sem, out_sem = refs[24:33], refs[33:36], refs[36], refs[37]
    comes, goes = [], []
    for k, (src, mid, dst) in enumerate(zip(large, held, out)):
        pieces = 4 if k >= 6 else 1
        amount = src.shape[0] // pieces
        for i in range(pieces):
            part = pl.ds(i * amount, amount)
            comes.append(pltpu.make_async_copy(src.at[part], mid.at[part], in_sem.at[len(comes)]))
            last = wide[k - 6] if k >= 6 else mid
            goes.append(pltpu.make_async_copy(last.at[part], dst.at[part], out_sem.at[len(goes)]))
    order = list(range(6, 18)) + list(range(6))
    for k in order:
        comes[k].start()
    place = lax.axis_index(EXPERT) * 4 + lax.axis_index(SEQ)
    width = small.shape[1]

    def own(length):
        lane = lax.broadcasted_iota(jnp.int32, (length, width), 1)
        down = lax.broadcasted_iota(jnp.int32, (length, width), 0)
        return jnp.where(lane == place * length + down, 1.0, 0.0)

    def picked(left, right):
        return lax.dot_general(left, right, (((1,), (1,)), ((), ())),
                               precision=lax.Precision.HIGHEST, preferred_element_type=jnp.float32)

    for k in order:
        comes[k].wait()
        if k >= 6:
            which, i = (k - 6) // 4, (k - 6) % 4
            amount = held[6].shape[0] // 4
            part = slice(i * amount, (i + 1) * amount)
            wide[which][part] = held[6 + which][part].astype(jnp.float32)
        goes[k].start()
    slim = gain_one.shape[1]
    ours = own(slim)
    gains = picked(small[0:8], ours)
    gain_one[...] = gains[0:1]
    gain_two[...] = gains[1:2]
    bias[...] = picked(small[0:8], own(bias.shape[1]))[2:3]
    router[...] = picked(small[8:16], ours)
    roots[...] = jnp.sqrt(small[3:4, 0:2] / (32 * large[0].shape[0] * width))
    for copy in goes:
        copy.wait()


def emit(large, small):
    full = jnp.float32
    width = small.shape[1]
    vmem, hbm = pl.BlockSpec(memory_space=pltpu.VMEM), pl.BlockSpec(memory_space=pl.ANY)
    slim = width // 32
    shapes = ((1, slim), (1, slim), (1, BUCKETS * HEADS // 32), (8, slim), (1, 2))
    return pl.pallas_call(
        emit_kernel,
        out_shape=tuple(jax.ShapeDtypeStruct(x.shape, x.dtype) for x in large[:6])
        + tuple(jax.ShapeDtypeStruct(x.shape, full) for x in large[6:])
        + tuple(jax.ShapeDtypeStruct(shape, full) for shape in shapes),
        in_specs=[hbm] * 9 + [vmem],
        out_specs=(hbm,) * 9 + (vmem,) * 5,
        scratch_shapes=[pltpu.VMEM(x.shape, x.dtype) for x in large]
        + [pltpu.VMEM(x.shape, full) for x in large[6:]]
        + [pltpu.SemaphoreType.DMA((18,)), pltpu.SemaphoreType.DMA((18,))],
        compiler_params=pltpu.CompilerParams(vmem_limit_bytes=VMEM_LIMIT),
        name="emit",
    )(*large, small)


def per_device_kernels(
    tokens, cotangent, expert_ids, segment_lengths, segment_parents, attention_gain,
    query_weight, key_weight, value_weight, output_weight, bias_table, feedforward_gain,
    router_weight, gate_weight, up_weight, down_weight,
):
    ids_row = expert_ids.T
    send_rows, grad_rows, residual, all_tokens, qkv, cols, params, att, stats, wo = front(
        segment_lengths, segment_parents, tokens, cotangent, ids_row, query_weight, key_weight, value_weight,
        output_weight, attention_gain[None], feedforward_gain[None], bias_table[None], router_weight.T,
    )
    returned, grad_back, gate_term, up_term, down_term = experts(
        send_rows, grad_rows, gate_weight[0], up_weight[0], down_weight[0]
    )
    layer_out, tokens_grad, dwq, dwk, dwv, dwo, totals = back(
        segment_lengths, segment_parents, ids_row, params, returned, grad_back, residual, cotangent,
        wo.reshape(D, D), qkv, cols, all_tokens, att, stats,
    )
    large = (layer_out, tokens_grad, dwq, dwk, dwv, dwo, gate_term, up_term, down_term)
    *large, gain_one, gain_two, bias, router, roots = emit(large, totals)
    layer_out, tokens_grad, dwq, dwk, dwv, dwo, gate_term, up_term, down_term = large
    return (
        layer_out, tokens_grad, gain_one[0], dwq, dwk, dwv, dwo, bias[0], gain_two[0], router.T,
        gate_term[None], up_term[None], down_term[None], roots[0],
    )


def per_device_general(
    tokens,
    cotangent,
    expert_ids,
    segment_lengths,
    segment_parents,
    attention_gain,
    query_weight,
    key_weight,
    value_weight,
    output_weight,
    bias_table,
    feedforward_gain,
    router_weight,
    gate_weight,
    up_weight,
    down_weight,
):
    seq_count = lax.axis_size(SEQ)
    seq_place = lax.axis_index(SEQ)
    all_count = lax.axis_size(EXPERT) * seq_count
    row_count = tokens.shape[0]
    experts = lax.axis_size(EXPERT) * gate_weight.shape[0]
    capacity = 10 * row_count // (4 * experts)
    score_scale = HDIM ** (-0.5)
    gathered = (
        lax.all_gather(attention_gain, BOTH, axis=0, tiled=True),
        lax.all_gather(query_weight, BOTH, axis=0, tiled=True),
        lax.all_gather(key_weight, BOTH, axis=0, tiled=True),
        lax.all_gather(value_weight, BOTH, axis=0, tiled=True),
        lax.all_gather(output_weight, BOTH, axis=0, tiled=True),
        lax.all_gather(bias_table, BOTH, axis=0, tiled=True),
        lax.all_gather(feedforward_gain, BOTH, axis=0, tiled=True),
        lax.all_gather(router_weight, BOTH, axis=0, tiled=True),
    )
    gain_one, query_full, key_full, value_full, output_full, bias_flat, gain_two, router_full = (
        gathered
    )
    bias_grid = bias_flat.reshape(BUCKETS, HEADS)
    starts, before, reaches = tree_tables(segment_lengths[0], segment_parents[0])
    own_rows = seq_place * row_count + jnp.arange(row_count, dtype=jnp.int32)
    own_meta = token_info(own_rows, starts, before, reaches)
    tokens_float = tokens.astype(jnp.float32)
    scale_one = norm_factor(tokens_float)
    unit_one = tokens_float * scale_one
    normed_one = (unit_one * gain_one.astype(jnp.float32)).astype(jnp.bfloat16)
    queries = (
        jnp.dot(normed_one, query_full, preferred_element_type=jnp.float32)
        .astype(jnp.bfloat16)
        .reshape(row_count, HEADS, HDIM)
    )
    keys_own = (
        jnp.dot(normed_one, key_full, preferred_element_type=jnp.float32)
        .astype(jnp.bfloat16)
        .reshape(row_count, HEADS, HDIM)
    )
    values_own = (
        jnp.dot(normed_one, value_full, preferred_element_type=jnp.float32)
        .astype(jnp.bfloat16)
        .reshape(row_count, HEADS, HDIM)
    )
    row_peak = jnp.full((HEADS, row_count), NEGATIVE, jnp.float32)
    key_piece = lax.all_gather(keys_own, SEQ, axis=0, tiled=True)
    value_piece = lax.all_gather(values_own, SEQ, axis=0, tiled=True)
    key_rows = jnp.arange(key_piece.shape[0], dtype=jnp.int32)
    visible, onehot, pair_bias = pair_terms(
        own_meta, token_info(key_rows, starts, before, reaches), own_rows, key_rows, bias_grid
    )
    scores = masked_scores(queries, key_piece, visible, pair_bias)
    new_peak = jnp.maximum(row_peak, jnp.max(scores, axis=-1))
    expo = jnp.exp(scores - new_peak[:, :, None])
    row_total = jnp.sum(expo, axis=-1)
    summed = jnp.einsum(
        SPEC_2, expo.astype(jnp.bfloat16), value_piece, preferred_element_type=jnp.float32
    )
    row_peak, row_total, summed = (new_peak, row_total, summed)
    log_total = row_peak + jnp.log(row_total)
    attended_float = summed / jnp.transpose(row_total)[:, :, None]
    attended = attended_float.astype(jnp.bfloat16).reshape(row_count, D)
    residual = tokens_float + jnp.dot(attended, output_full, preferred_element_type=jnp.float32)
    scale_two = norm_factor(residual)
    unit_two = residual * scale_two
    normed_two = (unit_two * gain_two.astype(jnp.float32)).astype(jnp.bfloat16)
    router_prob = jax.nn.softmax(
        jnp.dot(normed_two, router_full, preferred_element_type=jnp.float32), axis=-1
    )
    pick_hot = (
        expert_ids[:, :, None] == jnp.arange(experts, dtype=jnp.int32)[None, None, :]
    ).astype(jnp.float32)
    chosen = jnp.sum(pick_hot * router_prob[:, None, :], axis=2)
    chosen_total = jnp.sum(chosen, axis=1, keepdims=True)
    gate_shares = chosen / chosen_total
    hot_int = pick_hot.astype(jnp.int32).reshape(row_count * 2, experts)
    earlier = jnp.cumsum(hot_int, axis=0) - hot_int
    slot_number = jnp.sum(earlier * hot_int, axis=1).reshape(row_count, 2)
    kept_copy = slot_number < capacity
    kept_float = kept_copy.astype(jnp.float32)
    target = jnp.where(kept_copy, expert_ids * capacity + slot_number, experts * capacity)
    copy_ids = jnp.arange(row_count * 2, dtype=jnp.int32)
    slot_copy = (
        jnp.full((experts * capacity + 1,), row_count * 2, jnp.int32)
        .at[target.reshape(-1)]
        .set(copy_ids)[: experts * capacity]
    )
    fetch_index = jnp.minimum(target, experts * capacity - 1).reshape(-1)
    token_of_slot = jnp.where(slot_copy < row_count * 2, slot_copy // 2, row_count)
    padded = jnp.concatenate([normed_two, jnp.zeros((1, D), jnp.bfloat16)], axis=0)
    send_rows = padded[token_of_slot].reshape(experts, capacity, D)
    expert_in = lax.all_to_all(send_rows, EXPERT, split_axis=0, concat_axis=1, tiled=True)[0]
    gate_piece = lax.all_gather(gate_weight, SEQ, axis=1, tiled=True)
    up_piece = lax.all_gather(up_weight, SEQ, axis=1, tiled=True)
    down_piece = lax.all_gather(down_weight, SEQ, axis=1, tiled=True)
    gate_pre = jnp.einsum(SPEC_3, expert_in, gate_piece[0], preferred_element_type=jnp.float32)
    up_pre = jnp.einsum(SPEC_3, expert_in, up_piece[0], preferred_element_type=jnp.float32)
    active = (gelu_tanh(gate_pre) * up_pre).astype(jnp.bfloat16)
    expert_sum = jnp.dot(active, down_piece[0], preferred_element_type=jnp.float32)
    returned = lax.all_to_all(
        expert_sum.astype(jnp.bfloat16)[None], EXPERT, split_axis=1, concat_axis=0, tiled=True
    )
    picked = (
        returned.reshape(experts * capacity, D)[fetch_index]
        .reshape(row_count, 2, D)
        .astype(jnp.float32)
    )
    weighted = gate_shares * kept_float
    mixture = jnp.sum(weighted[:, :, None] * picked, axis=1)
    layer_out = (residual + mixture).astype(jnp.bfloat16)
    local_sums = jnp.stack([jnp.sum(residual * residual), jnp.sum(mixture * mixture)])
    again = (
        lax.all_gather(attention_gain, BOTH, axis=0, tiled=True),
        lax.all_gather(query_weight, BOTH, axis=0, tiled=True),
        lax.all_gather(key_weight, BOTH, axis=0, tiled=True),
        lax.all_gather(value_weight, BOTH, axis=0, tiled=True),
        lax.all_gather(output_weight, BOTH, axis=0, tiled=True),
        lax.all_gather(bias_table, BOTH, axis=0, tiled=True),
        lax.all_gather(feedforward_gain, BOTH, axis=0, tiled=True),
        lax.all_gather(router_weight, BOTH, axis=0, tiled=True),
    )
    gain_one, query_full, key_full, value_full, output_full, bias_flat, gain_two, router_full = (
        again
    )
    bias_grid = bias_flat.reshape(BUCKETS, HEADS)
    grad_out = cotangent.astype(jnp.float32)
    copy_grad = (
        (weighted[:, :, None] * grad_out[:, None, :]).astype(jnp.bfloat16).reshape(row_count * 2, D)
    )
    copy_padded = jnp.concatenate([copy_grad, jnp.zeros((1, D), jnp.bfloat16)], axis=0)
    grad_send = copy_padded[slot_copy].reshape(experts, capacity, D)
    grad_in = lax.all_to_all(grad_send, EXPERT, split_axis=0, concat_axis=1, tiled=True)[0]
    gate_piece = lax.all_gather(gate_weight, SEQ, axis=1, tiled=True)
    up_piece = lax.all_gather(up_weight, SEQ, axis=1, tiled=True)
    down_piece = lax.all_gather(down_weight, SEQ, axis=1, tiled=True)
    gate_pre = jnp.einsum(SPEC_3, expert_in, gate_piece[0], preferred_element_type=jnp.float32)
    up_pre = jnp.einsum(SPEC_3, expert_in, up_piece[0], preferred_element_type=jnp.float32)
    gelu_out, gelu_pull = jax.vjp(gelu_tanh, gate_pre)
    act_grad = jnp.einsum(SPEC_3, grad_in, down_piece[0], preferred_element_type=jnp.float32)
    gate_back = gelu_pull(act_grad * up_pre)[0].astype(jnp.bfloat16)
    up_back = (act_grad * gelu_out).astype(jnp.bfloat16)
    input_grad = jnp.dot(gate_back, gate_piece[0], preferred_element_type=jnp.float32) + jnp.dot(
        up_back, up_piece[0], preferred_element_type=jnp.float32
    )
    active = (gelu_out * up_pre).astype(jnp.bfloat16)
    input_grad, gate_backs, up_backs, actives = (input_grad, gate_back, up_back, active)
    grad_back = lax.all_to_all(
        input_grad.astype(jnp.bfloat16)[None], EXPERT, split_axis=1, concat_axis=0, tiled=True
    )
    expert_back = (
        grad_back.reshape(experts * capacity, D)[fetch_index]
        .reshape(row_count, 2, D)
        .astype(jnp.float32)
    )
    normed_two_grad = jnp.sum(expert_back * kept_float[:, :, None], axis=1)
    expert_grads = lax.psum_scatter(
        jnp.stack(
            [
                jnp.einsum(SPEC_4, gate_backs, expert_in, preferred_element_type=jnp.float32),
                jnp.einsum(SPEC_4, up_backs, expert_in, preferred_element_type=jnp.float32),
                jnp.einsum(SPEC_4, actives, grad_in, preferred_element_type=jnp.float32),
            ],
            axis=1,
        ).astype(jnp.bfloat16),
        SEQ,
        scatter_dimension=0,
        tiled=True,
    ).astype(jnp.float32)
    share_grad = jnp.sum(grad_out[:, None, :] * picked, axis=2) * kept_float
    chosen_grad = (
        share_grad - jnp.sum(gate_shares * share_grad, axis=1, keepdims=True)
    ) / chosen_total
    prob_grad = jnp.sum(pick_hot * chosen_grad[:, :, None], axis=1)
    logit_grad = router_prob * (prob_grad - jnp.sum(router_prob * prob_grad, axis=1, keepdims=True))
    router_float = router_full.astype(jnp.float32)
    router_term = jnp.einsum(
        SPEC_5, normed_two.astype(jnp.float32), logit_grad, precision=lax.Precision.HIGHEST
    )
    normed_two_grad = normed_two_grad + jnp.einsum(
        SPEC_6, logit_grad, router_float, precision=lax.Precision.HIGHEST
    )
    gain_two_term = jnp.sum(normed_two_grad * unit_two, axis=0)
    unit_grad_two = normed_two_grad * gain_two.astype(jnp.float32)
    residual_grad = grad_out + scale_two * (
        unit_grad_two - unit_two * jnp.mean(unit_grad_two * unit_two, axis=-1, keepdims=True)
    )
    attention_out_grad = residual_grad.astype(jnp.bfloat16)
    output_term = jnp.einsum(
        SPEC_5, attended, attention_out_grad, preferred_element_type=jnp.float32
    )
    attended_grad = (
        jnp.einsum(SPEC_6, attention_out_grad, output_full, preferred_element_type=jnp.float32)
        .astype(jnp.bfloat16)
        .reshape(row_count, HEADS, HDIM)
    )
    row_delta = jnp.transpose(jnp.sum(attended_grad.astype(jnp.float32) * attended_float, axis=-1))
    total_all, delta_all = (
        lax.all_gather(log_total, SEQ, axis=1, tiled=True),
        lax.all_gather(row_delta, SEQ, axis=1, tiled=True),
    )
    key_piece = lax.all_gather(keys_own, SEQ, axis=0, tiled=True)
    value_piece = lax.all_gather(values_own, SEQ, axis=0, tiled=True)
    key_rows = jnp.arange(key_piece.shape[0], dtype=jnp.int32)
    visible, onehot, pair_bias = pair_terms(
        own_meta, token_info(key_rows, starts, before, reaches), own_rows, key_rows, bias_grid
    )
    scores = masked_scores(queries, key_piece, visible, pair_bias)
    soft_weights = jnp.exp(scores - log_total[:, :, None])
    dprob = jnp.einsum(
        SPEC_1, attended_grad, value_piece, preferred_element_type=jnp.float32
    )
    score_grad = (soft_weights * (dprob - row_delta[:, :, None])).astype(jnp.bfloat16)
    query_acc = jnp.einsum(
        SPEC_2, score_grad, key_piece, preferred_element_type=jnp.float32
    )
    bias_acc = jnp.einsum(SPEC_7, onehot, score_grad, preferred_element_type=jnp.float32)
    query_acc, bias_acc = (query_acc, bias_acc)
    query_piece = lax.all_gather(queries, SEQ, axis=0, tiled=True)
    grad_piece = lax.all_gather(attended_grad, SEQ, axis=0, tiled=True)
    piece_rows = query_piece.shape[0]
    query_rows = jnp.arange(piece_rows, dtype=jnp.int32)
    visible, onehot, pair_bias = pair_terms(
        token_info(query_rows, starts, before, reaches), own_meta, query_rows, own_rows, bias_grid
    )
    scores = masked_scores(query_piece, keys_own, visible, pair_bias)
    soft_weights = jnp.exp(scores - total_all[:, :, None])
    value_acc = jnp.einsum(
        SPEC_8,
        soft_weights.astype(jnp.bfloat16),
        grad_piece,
        preferred_element_type=jnp.float32,
    )
    dprob = jnp.einsum(SPEC_1, grad_piece, values_own, preferred_element_type=jnp.float32)
    score_grad = (soft_weights * (dprob - delta_all[:, :, None])).astype(jnp.bfloat16)
    key_acc = jnp.einsum(
        SPEC_8, score_grad, query_piece, preferred_element_type=jnp.float32
    )
    key_acc, value_acc = (key_acc, value_acc)
    query_back = (query_acc * score_scale).astype(jnp.bfloat16).reshape(row_count, D)
    key_back = (key_acc * score_scale).astype(jnp.bfloat16).reshape(row_count, D)
    value_back = value_acc.astype(jnp.bfloat16).reshape(row_count, D)
    query_term = jnp.einsum(SPEC_5, normed_one, query_back, preferred_element_type=jnp.float32)
    key_term = jnp.einsum(SPEC_5, normed_one, key_back, preferred_element_type=jnp.float32)
    value_term = jnp.einsum(SPEC_5, normed_one, value_back, preferred_element_type=jnp.float32)
    normed_one_grad = jnp.einsum(
        SPEC_6, query_back, query_full, preferred_element_type=jnp.float32
    )
    normed_one_grad = normed_one_grad + jnp.einsum(
        SPEC_6, key_back, key_full, preferred_element_type=jnp.float32
    )
    normed_one_grad = normed_one_grad + jnp.einsum(
        SPEC_6, value_back, value_full, preferred_element_type=jnp.float32
    )
    gain_one_term = jnp.sum(normed_one_grad * unit_one, axis=0)
    unit_grad_one = normed_one_grad * gain_one.astype(jnp.float32)
    tokens_grad = residual_grad + scale_one * (
        unit_grad_one - unit_one * jnp.mean(unit_grad_one * unit_one, axis=-1, keepdims=True)
    )
    stats_term = jnp.broadcast_to(local_sums[None, :], (all_count, 2))
    reduced = (
        lax.psum_scatter(gain_one_term, BOTH, scatter_dimension=0, tiled=True),
        lax.psum_scatter(query_term, BOTH, scatter_dimension=0, tiled=True),
        lax.psum_scatter(key_term, BOTH, scatter_dimension=0, tiled=True),
        lax.psum_scatter(value_term, BOTH, scatter_dimension=0, tiled=True),
        lax.psum_scatter(output_term, BOTH, scatter_dimension=0, tiled=True),
        lax.psum_scatter(
            bias_acc.reshape(BUCKETS * HEADS), BOTH, scatter_dimension=0, tiled=True
        ),
        lax.psum_scatter(gain_two_term, BOTH, scatter_dimension=0, tiled=True),
        lax.psum_scatter(router_term, BOTH, scatter_dimension=0, tiled=True),
        lax.psum_scatter(stats_term, BOTH, scatter_dimension=0, tiled=True),
    )
    roots = jnp.sqrt(reduced[8][0] / (row_count * all_count * D))
    return (
        layer_out,
        tokens_grad,
        reduced[0],
        reduced[1],
        reduced[2],
        reduced[3],
        reduced[4],
        reduced[5],
        reduced[6],
        reduced[7],
        expert_grads[None, :, 0, :],
        expert_grads[None, :, 1, :],
        expert_grads[None, :, 2, :],
        roots,
    )


def solution(mesh):
    kernels_fit = mesh.shape[EXPERT] == len(ORDER) and mesh.shape[SEQ] == 4
    return jax.shard_map(
        per_device_kernels if kernels_fit else per_device_general,
        mesh=mesh,
        in_specs=(
            P(BOTH, None),
            P(BOTH, None),
            P(BOTH, None),
            P(EXPERT, None),
            P(EXPERT, None),
            P(BOTH),
            P(BOTH, None),
            P(BOTH, None),
            P(BOTH, None),
            P(BOTH, None),
            P(BOTH),
            P(BOTH),
            P(BOTH, None),
            P(EXPERT, SEQ, None),
            P(EXPERT, SEQ, None),
            P(EXPERT, SEQ, None),
        ),
        out_specs=(
            P(BOTH, None),
            P(BOTH, None),
            P(BOTH),
            P(BOTH, None),
            P(BOTH, None),
            P(BOTH, None),
            P(BOTH, None),
            P(BOTH),
            P(BOTH),
            P(BOTH, None),
            P(EXPERT, SEQ, None),
            P(EXPERT, SEQ, None),
            P(EXPERT, SEQ, None),
            P(),
        ),
        check_vma=False,
    )
```

```python
import math

import jax
import jax.numpy as jnp
from jax import lax
from jax.experimental import pallas as pl
from jax.experimental.pallas import tpu as pltpu
from jax.sharding import PartitionSpec as P

SPEC_0 = "qkb,bh->hqk"
SPEC_1 = "qhd,khd->hqk"
SPEC_2 = "hqk,khd->qhd"
SPEC_3 = "rd,fd->rf"
SPEC_4 = "rf,rd->fd"
SPEC_5 = "rd,re->de"
SPEC_6 = "re,de->rd"
SPEC_7 = "qkb,hqk->bh"
SPEC_8 = "hqk,qhd->khd"
MESH = pl.DeviceIdType.MESH
VMEM_LIMIT = 62 << 20
EXPERT, SEQ = "expert", "seq"
BOTH = (EXPERT, SEQ)

D = 1024
HEADS = 16
HDIM = 64
BUCKETS = 32
MAXDIST = 128


EPSILON = 1e-06
NEGATIVE = -1e30


def norm_factor(values):
    return lax.rsqrt(jnp.mean(values * values, axis=-1, keepdims=True) + EPSILON)


def gelu_tanh(values):
    return jax.nn.gelu(values, approximate=True)


def bucket_of(distance):
    exact_span = BUCKETS // 2
    above = jnp.zeros(distance.shape, jnp.int32)
    for number in range(exact_span):
        threshold = int(math.ceil(exact_span * (MAXDIST / exact_span) ** (number / exact_span)))
        above = above + (distance >= threshold).astype(jnp.int32)
    return jnp.where(distance < exact_span, distance, exact_span - 1 + above)


def tree_tables(lengths, parents):
    ordinal = jnp.arange(lengths.shape[0], dtype=jnp.int32)
    starts = jnp.cumsum(lengths) - lengths

    def chase(number, running):
        current, reaches = running
        current = jnp.sum(
            jnp.where(current[:, None] == ordinal[None, :], parents[None, :], 0), axis=1
        )
        reaches = jnp.maximum(reaches, (current[:, None] == ordinal[None, :]).astype(jnp.int32))
        return (current, reaches)

    begin = (ordinal, (ordinal[:, None] == ordinal[None, :]).astype(jnp.int32))
    unused, reaches = lax.fori_loop(0, lengths.shape[0], chase, begin)
    before = jnp.sum(reaches * lengths[None, :], axis=1) - lengths
    return (starts, before, reaches)


def token_info(token_rows, starts, before, reaches):
    ordinal = jnp.arange(starts.shape[0], dtype=jnp.int32)
    segment = jnp.sum((token_rows[:, None] >= starts[None, :]).astype(jnp.int32), axis=1) - 1
    member = segment[:, None] == ordinal[None, :]
    position = token_rows + jnp.sum(jnp.where(member, (before - starts)[None, :], 0), axis=1)
    lineage = jnp.sum(jnp.where(member[:, :, None], reaches[None, :, :], 0), axis=1)
    return (member.astype(jnp.float32), position, lineage.astype(jnp.float32))


def pair_terms(query_meta, key_meta, query_rows, key_rows, bias_grid):
    visible = jnp.dot(query_meta[2], key_meta[0].T, preferred_element_type=jnp.float32) > 0.5
    visible = visible & (key_rows[None, :] <= query_rows[:, None])
    distance = jnp.maximum(query_meta[1][:, None] - key_meta[1][None, :], 0)
    onehot = (
        bucket_of(distance)[:, :, None] == jnp.arange(BUCKETS, dtype=jnp.int32)[None, None, :]
    ).astype(jnp.bfloat16)
    pair_bias = jnp.einsum(SPEC_0, onehot, bias_grid, preferred_element_type=jnp.float32)
    return (visible, onehot, pair_bias)


def masked_scores(query_block, key_block, visible, pair_bias):
    scores = (
        jnp.einsum(SPEC_1, query_block, key_block, preferred_element_type=jnp.float32)
        * HDIM ** (-0.5)
        + pair_bias
    )
    return jnp.where(visible[None], scores, NEGATIVE)


def remote(src, dst, send, recv, peer):
    return pltpu.make_async_remote_copy(
        src_ref=src, dst_ref=dst, send_sem=send, recv_sem=recv,
        device_id=peer, device_id_type=MESH,
    )


def contract(left, right, dims):
    return lax.dot_general(left, right, (dims, ((), ())), preferred_element_type=jnp.float32)


def gelu_parts(values):
    root = 0.7978845608028654
    square = values * values
    swing = jnp.tanh(root * values * (1.0 + 0.044715 * square))
    half = 0.5 * (1.0 + swing)
    slope = half + 0.5 * values * (1.0 - swing * swing) * (root * (1.0 + 3 * 0.044715 * square))
    return values * half, slope


ORDER = (0, 1, 2, 3, 4, 5, 6, 7)
UNITS = (
    (0, 0), (0, 1), (1, 0), (2, 0), (3, 0), (1, 1), (2, 1), (3, 1),
    (0, 2), (1, 2), (2, 2), (0, 3), (3, 2), (1, 3), (2, 3), (3, 3),
)


def greet(peers):
    barrier = pltpu.get_barrier_semaphore()
    for peer in peers:
        pl.semaphore_signal(barrier, inc=1, device_id=peer, device_id_type=MESH)
    pl.semaphore_wait(barrier, len(peers))


def aligned(index, size):
    return pl.ds(pl.multiple_of(index * size, size), size)


ZHOPS = (2, 4, 6)


def expert_kernel(
    xs, gs, shares, g_early, wg_far, wu_far, wd_far, po_far, ret_b, ret_s, dwg, dwu, dwd,
    xr, gr, sh, act, gb, ub, po, pb, rb, rb2, sd, sd_got, sd_out, stage, rounded, wg, wu, wd,
    in_send, in_recv, hop_send, hop_recv, sh_send, sh_recv, rs_send, rs_recv, out_send, out_recv,
    sd_send, sd_recv, sr_send, sr_recv, po_sem, stage_sem, load_sem, own_sem,
):
    e = lax.axis_index(EXPERT)
    s = lax.axis_index(SEQ)
    cap = xs.shape[0] // 8
    width = xs.shape[1]
    full, low = jnp.float32, jnp.bfloat16
    near_x, near_y = (e, s ^ 1), (e, s ^ 2)
    around = (near_x, near_y, (e, s ^ 3))
    loads = [
        pltpu.make_async_copy(src, dst, load_sem.at[k])
        for k, (src, dst) in enumerate(((wg_far, wg), (wu_far, wu), (wd_far, wd), (g_early, gr.at[:, pl.ds(0, 4)])))
    ]
    for load in loads:
        load.start()
    greet(list(around) + [(e ^ d, s) for d in range(1, 8)])

    def block(index):
        return pl.ds(pl.multiple_of(index * cap, 16), cap)

    tensors = ((xs, xr), (gs, gr))

    def entry(kind, place):
        src, dst = tensors[kind]
        d = ORDER[place]
        return remote(src.at[block(e ^ d)], dst.at[0, place], in_send.at[kind, place],
                      in_recv.at[kind, place], (e ^ d, s))

    def hop(kind, which, pair):
        buf = tensors[kind][1]
        places = pl.ds(2 * pair, 2) if which < 2 else pl.ds(2 * pair + which - 2, 1)
        src = buf.at[(0, 0, 1, 2)[which], places]
        dst = buf.at[(1, 2, 3, 3)[which], places]
        peer = (near_x, near_y, near_y, near_x)[which]
        return remote(src, dst, hop_send.at[kind, which, pair], hop_recv.at[kind, which, pair], peer)

    def share_entry(place):
        d = ORDER[place]
        return remote(shares.at[e ^ d], sh.at[0, place], sh_send.at[place], sh_recv.at[place], (e ^ d, s))

    def share_hop(which):
        return remote(sh.at[(0, 0, 1)[which]], sh.at[1 + which], sh_send.at[8 + which], sh_recv.at[8 + which],
                      (near_x, near_y, near_y)[which])

    def rs(half, which, pair):
        first, second = ((near_x, near_y), (near_y, near_x))[half]
        src = pb.at[(1 + half, 3, 2 - half)[which], half, pair]
        dst = rb2.at[half, pair] if which == 2 else rb.at[which, half, pair]
        return remote(src, dst, rs_send.at[half, which, pair], rs_recv.at[half, which, pair],
                      second if which == 2 else first)

    def back(place):
        return remote(pb.at[0, place % 2, place // 2], ret_b.at[block(e)],
                      out_send.at[place], out_recv.at[place], (e ^ ORDER[place], s))

    def own_back():
        return pltpu.make_async_copy(pb.at[0, 0, 0], ret_b.at[block(e)], own_sem.at[2])

    def start_entries(kind, pair):
        for place in (2 * pair, 2 * pair + 1):
            if ORDER[place]:
                entry(kind, place).start()

    def forward_pair(kind, pair):
        for place in (2 * pair, 2 * pair + 1):
            if ORDER[place]:
                entry(kind, place).wait_recv()
        hop(kind, 0, pair).start()
        hop(kind, 1, pair).start()

    def forward_corner(kind, pair):
        for which in range(2):
            hop(kind, which, pair).wait_recv()
            hop(kind, 2 + which, pair).start()

    def wait_corner(pair):
        for kind in range(2 if pair >= 2 else 1):
            for which in (2, 3):
                hop(kind, which, pair).wait_recv()

    def start_sums(pair):
        for which in (1, 0):
            for half in range(2):
                rs(half, which, pair).start()

    def add_second(pair):
        for half in range(2):
            rs(half, 1, pair).wait_recv()
            group = 2 - half
            pb[group, half, pair] = (pb[group, half, pair].astype(full) + rb[1, half, pair].astype(full)).astype(low)
            rs(half, 2, pair).start()

    def finish(pair):
        for half in range(2):
            rs(half, 0, pair).wait_recv()
            rs(half, 2, pair).wait_recv()
            pb[0, half, pair] = (
                pb[0, half, pair].astype(full) + rb[0, half, pair].astype(full) + rb2[half, pair].astype(full)
            ).astype(low)
            if ORDER[2 * pair + half]:
                back(2 * pair + half).start()
            else:
                own_back().start()

    own_rows = [
        pltpu.make_async_copy(xs.at[block(e)], xr.at[0, 0], own_sem.at[0]),
        pltpu.make_async_copy(shares.at[e], sh.at[0, 0], own_sem.at[1]),
    ]
    for copy in own_rows:
        copy.start()
    start_entries(0, 0)
    for place in range(1, 8):
        share_entry(place).start()
    start_entries(0, 1)
    start_entries(1, 2)

    rows = 2 * cap

    def put_out(u, q, c):
        return pltpu.make_async_copy(po.at[q, :, c], po_far.at[q, :, c], po_sem.at[u])

    def unit(u, carry):
        q, c = jnp.int32(0), jnp.int32(0)
        for k, (whose, pair) in enumerate(UNITS):
            q, c = jnp.where(u == k, whose, q), jnp.where(u == k, pair, c)

        for k, (whose, pair) in enumerate(UNITS):
            @pl.when(u == k)
            def _():
                if k == 0:
                    for copy in own_rows:
                        copy.wait()
                    forward_pair(0, 0)
                    for place in range(1, 8):
                        share_entry(place).wait_recv()
                    share_hop(0).start()
                    share_hop(1).start()
                    for load in loads:
                        load.wait()
                if k == 1:
                    forward_corner(0, 0)
                    forward_pair(0, 1)
                    start_entries(1, 3)
                if k == 2:
                    share_hop(0).wait_recv()
                    share_hop(2).start()
                    share_hop(1).wait_recv()
                if k == 3:
                    forward_corner(0, 1)
                    forward_pair(1, 2)
                    start_entries(0, 2)
                if k == 4:
                    share_hop(2).wait_recv()
                if k == 6:
                    forward_corner(1, 2)
                    forward_pair(1, 3)
                    start_entries(0, 3)
                if k == 8:
                    forward_corner(1, 3)
                    forward_pair(0, 2)
                if k == 9:
                    forward_corner(0, 2)
                if k == 10:
                    add_second(1)
                if k == 11:
                    forward_pair(0, 3)
                if k == 13:
                    forward_corner(0, 3)
                    finish(1)
                if k == 15:
                    add_second(2)
                if whose == 3:
                    wait_corner(pair)

        x = xr[q, pl.ds(2 * c, 2)].reshape(rows, width)
        g = gr[q, pl.ds(2 * c, 2)].reshape(rows, width)
        share = jnp.concatenate([jnp.transpose(sh[q, 2 * c + i])[0:cap, 0:1] for i in range(2)], axis=0)
        gate = contract(x, wg[...], ((1,), (1,)))
        up = contract(x, wu[...], ((1,), (1,)))
        ag = contract(g, wd[...], ((1,), (1,))) * share
        value, slope = gelu_parts(gate)
        active = value * up
        gate_back = (ag * up * slope).astype(low)
        up_back = (ag * value).astype(low)
        act[q, c] = (active * share).astype(low)
        gb[q, c] = gate_back
        ub[q, c] = up_back
        out = contract(active.astype(low), wd[...], ((1,), (0,)))
        dots = lax.dot_general(jnp.ones((8, width), full), out * g.astype(full), (((1,), (1,)), ((), ())),
                               precision=lax.Precision.HIGHEST, preferred_element_type=full)
        sd[q, c, :, 0:rows] = dots
        weighted = (out * share).astype(low)
        into = contract(gate_back, wg[...], ((1,), (0,))) + contract(up_back, wu[...], ((1,), (0,)))
        for half in range(2):
            po[q, half, c] = weighted[half * cap:(half + 1) * cap]
            pb[q, half, c] = into[half * cap:(half + 1) * cap].astype(low)
        put_out(u, q, c).start()

        for k, (whose, pair) in enumerate(UNITS):
            if whose == 3 and pair:
                @pl.when(u == k)
                def _():
                    start_sums(pair)
            elif pair == 3 and whose:
                @pl.when(u == k)
                def _():
                    give_dots(whose).start()
        return carry

    def give_dots(q):
        return remote(sd.at[q], sd_got.at[q - 1], sd_send.at[q - 1], sd_recv.at[q - 1], around[q - 1])

    def return_dots(place):
        return remote(sd_out.at[place], ret_s.at[e], sr_send.at[place], sr_recv.at[place], (e ^ ORDER[place], s))

    def own_dots():
        return pltpu.make_async_copy(sd_out.at[0], ret_s.at[e], own_sem.at[3])

    sd[...] = jnp.zeros_like(sd)
    lax.fori_loop(0, len(UNITS), unit, 0)
    give_dots(3).start()

    def grads(left, right, dst):
        def part(u):
            q, c = lax.rem(u, 4), u // 4
            return contract(left[q, pl.ds(2 * c, 2)].reshape(2 * rows, wg.shape[0]),
                            right[q, pl.ds(4 * c, 4)].reshape(2 * rows, width), ((0,), (0,)))

        def more(u, carry):
            stage[...] += part(u)
            return carry

        stage[...] = part(0)
        lax.fori_loop(1, 8, more, 0)
        rounded[...] = stage[...].astype(low)
        done = pltpu.make_async_copy(rounded, dst, stage_sem)
        done.start()
        return done

    done = grads(gb, xr, dwg)
    finish(2)
    add_second(3)
    start_sums(0)
    for q in range(1, 4):
        give_dots(q).wait_recv()
    for c in range(4):
        dots = sd[0, c] + sd_got[0, c] + sd_got[1, c] + sd_got[2, c]
        for i in range(2):
            sd_out[2 * c + i] = jnp.zeros((8, 128), full)
            sd_out[2 * c + i, :, 0:cap] = dots[:, i * cap:(i + 1) * cap]
    for place in range(1, 8):
        return_dots(place).start()
    own_dots().start()
    done.wait()
    done = grads(ub, xr, dwu)
    finish(3)
    add_second(0)
    done.wait()
    done = grads(act, gr, dwd)
    finish(0)
    done.wait()

    own_back().wait()
    own_dots().wait()
    for place in range(1, 8):
        back(place).wait()
        return_dots(place).wait()
        share_entry(place).wait_send()
        for kind in range(2 if place >= 4 else 1):
            entry(kind, place).wait_send()
    for which in range(3):
        share_hop(which).wait_send()
        give_dots(1 + which).wait_send()
    for pair in range(4):
        for kind in range(2 if pair >= 2 else 1):
            for which in range(4):
                hop(kind, which, pair).wait_send()
        for half in range(2):
            for which in range(3):
                rs(half, which, pair).wait_send()
    for k, (whose, pair) in enumerate(UNITS):
        put_out(k, whose, pair).wait()


def experts(send_rows, grad_rows, shares, g_early, gate_weight, up_weight, down_weight):
    rows, width = send_rows.shape
    units = gate_weight.shape[0]
    cap = rows // 8
    low, full = jnp.bfloat16, jnp.float32
    hbm = pl.BlockSpec(memory_space=pl.ANY)
    dma = pltpu.SemaphoreType.DMA
    part = (4, 2, 4, cap, width)
    return pl.pallas_call(
        expert_kernel,
        out_shape=(
            jax.ShapeDtypeStruct(part, low),
            jax.ShapeDtypeStruct((rows, width), low),
            jax.ShapeDtypeStruct((8, 8, 128), full),
        ) + (jax.ShapeDtypeStruct((units, width), low),) * 3,
        in_specs=[hbm] * 7,
        out_specs=(hbm,) * 6,
        scratch_shapes=[
            pltpu.VMEM((4, 8, cap, width), low),
            pltpu.VMEM((4, 8, cap, width), low),
            pltpu.VMEM((4, 8, 8, 128), full),
            pltpu.VMEM((4, 4, 2 * cap, units), low),
            pltpu.VMEM((4, 4, 2 * cap, units), low),
            pltpu.VMEM((4, 4, 2 * cap, units), low),
            pltpu.VMEM(part, low),
            pltpu.VMEM(part, low),
            pltpu.VMEM((2, 2, 4, cap, width), low),
            pltpu.VMEM((2, 4, cap, width), low),
            pltpu.VMEM((4, 4, 8, 256), full),
            pltpu.VMEM((3, 4, 8, 256), full),
            pltpu.VMEM((8, 8, 128), full),
            pltpu.VMEM((units, width), full),
            pltpu.VMEM((units, width), low),
            pltpu.VMEM((units, width), low),
            pltpu.VMEM((units, width), low),
            pltpu.VMEM((units, width), low),
            dma((2, 8)), dma((2, 8)),
            dma((2, 4, 4)), dma((2, 4, 4)),
            dma((11,)), dma((11,)),
            dma((2, 3, 4)), dma((2, 3, 4)),
            dma((8,)), dma((8,)),
            dma((3,)), dma((3,)),
            dma((8,)), dma((8,)),
            dma((len(UNITS),)), dma, dma((4,)), dma((4,)),
        ],
        compiler_params=pltpu.CompilerParams(
            collective_id=1, has_side_effects=True, vmem_limit_bytes=VMEM_LIMIT
        ),
        cost_estimate=pl.CostEstimate(flops=2 * 9 * 4 * rows * units * width, bytes_accessed=20 << 20, transcendentals=4 * rows * units),
        name="experts",
    )(send_rows, grad_rows, shares, g_early, gate_weight, up_weight, down_weight)


def segment_scalars(lengths, parents, before_mem, reach_mem):
    count = lengths.shape[1]
    start = jnp.int32(0)
    found = []
    for k in range(count):
        length = lengths[0, k]
        if k == 0:
            before, reach = jnp.int32(0), jnp.int32(1)
        else:
            parent = parents[0, k]
            before = before_mem[parent] + lengths[0, parent]
            reach = reach_mem[parent] | (1 << k)
        before_mem[k] = before
        reach_mem[k] = reach
        found.append((start, before, reach, length))
        start = start + length
    return found


def token_columns(found, ids):
    offset = jnp.zeros(ids.shape, jnp.int32)
    reach = jnp.full(ids.shape, 1, jnp.int32)
    own = jnp.full(ids.shape, 1, jnp.int32)
    for k, (start, before, bits, _) in enumerate(found):
        if k:
            after = ids >= start
            offset = jnp.where(after, before - start, offset)
            reach = jnp.where(after, bits, reach)
            own = jnp.where(after, 1 << k, own)
    return ids + offset, reach, own


LAST = 127


def bias_tables(params, s):
    flat = params[2:3, 0:BUCKETS * HEADS]
    lane = lax.broadcasted_iota(jnp.int32, (8, BUCKETS * HEADS), 1)
    head = lax.broadcasted_iota(jnp.int32, (8, BUCKETS * HEADS), 0)
    heads_here = HEADS // 4
    chosen = jnp.where((lane % HEADS) == s * heads_here + head, jnp.broadcast_to(flat, lane.shape), 0.0)
    entry = lax.broadcasted_iota(jnp.int32, (BUCKETS * HEADS, LAST + 1), 0) // HEADS
    distance = lax.broadcasted_iota(jnp.int32, (BUCKETS * HEADS, LAST + 1), 1)
    hot = jnp.where(entry == bucket_of(distance), 1.0, 0.0)
    table = contract(chosen.astype(jnp.bfloat16), hot.astype(jnp.bfloat16), ((1,), (0,)))
    spot = lax.broadcasted_iota(jnp.int32, table.shape, 1)
    return jnp.where(spot == LAST, NEGATIVE, table)


def pair_index(found, first, rows, count):
    ids = first + lax.broadcasted_iota(jnp.int32, (rows, 1), 0)
    keys = lax.broadcasted_iota(jnp.int32, (1, count), 1)
    place, reach, _ = token_columns(found, ids)
    key_place, _, key_own = token_columns(found, keys)
    seen = ((reach & key_own) != 0) & (keys <= ids)
    return jnp.where(seen, jnp.minimum(place - key_place, LAST - 1), LAST), place, reach


def looked_up(row, index):
    rows, count = index.shape
    table = jnp.broadcast_to(row, (rows, LAST + 1))
    pieces = [
        jnp.take_along_axis(table, index[:, k * 128:(k + 1) * 128], axis=1)
        for k in range(count // 128)
    ]
    return jnp.concatenate(pieces, axis=1)


def slots_of(ids_row, cap):
    rows = ids_row.shape[1]
    full, low = jnp.float32, jnp.bfloat16
    level = lax.broadcasted_iota(jnp.int32, (8, rows), 0)
    hot_row = [jnp.where(ids_row[k:k + 1] == level, 1.0, 0.0).astype(full) for k in range(2)]
    down = lax.broadcasted_iota(jnp.int32, (rows, rows), 0)
    across = lax.broadcasted_iota(jnp.int32, (rows, rows), 1)
    after = jnp.where(down < across, 1.0, 0.0).astype(low)
    earlier = contract((hot_row[0] + hot_row[1]).astype(low), after, ((1,), (0,)))
    slot_row = [jnp.sum(h * earlier, axis=0, keepdims=True) for h in hot_row]
    spot_row = [
        jnp.where(slot_row[k] < cap, ids_row[k:k + 1].astype(full) * cap + slot_row[k], -1.0) for k in range(2)
    ]
    columns = jnp.transpose(jnp.concatenate(spot_row + slot_row + [jnp.zeros((4, rows), full)], axis=0))
    target = [columns[:, k:k + 1].astype(jnp.int32) for k in range(2)]
    slot = [columns[:, 2 + k:3 + k].astype(jnp.int32) for k in range(2)]
    hot = [jnp.transpose(h) for h in hot_row]
    target_row = [spot.astype(jnp.int32) for spot in spot_row]
    return hot_row, hot, slot, target, target_row


def router_of(residual, params, hot):
    low = jnp.bfloat16
    scale = norm_factor(residual)
    unit = residual * scale
    normed = (unit * params[1:2]).astype(low)
    router = params[8:16]
    logits = contract(normed, router.astype(low), ((1,), (1,)))
    expo = jnp.exp(logits - jnp.max(logits, axis=1, keepdims=True))
    prob = expo / jnp.sum(expo, axis=1, keepdims=True)
    chosen = [jnp.sum(h * prob, axis=1, keepdims=True) for h in hot]
    chosen_sum = chosen[0] + chosen[1]
    shares = [c / chosen_sum for c in chosen]
    return scale, unit, normed, router, prob, chosen_sum, shares


def front_kernel(
    lengths, parents, tokens, cotangent, ids_row, wq, wk, wv, wo, gain_one, gain_two, bias, router_row,
    xs, gs_far, shares, residual, all_tokens_far, qkv_far, cols_far, params, att_far, stats_far, wo_far, g_far,
    all_tokens, qkv, cols, wo_full, att, stats, got, part, normed, misc, tags, tag_sum, all_tags, index, table, landed, gs, g_early,
    before_mem, reach_mem,
    t_send, t_recv, w_send, w_recv, m_send, m_recv, c_send, c_recv, n_send, n_recv,
    h_send, h_recv, a_send, a_recv,
    e_send, e_recv, j_send, j_recv, far_sem,
):
    e, s = lax.axis_index(EXPERT), lax.axis_index(SEQ)
    near_x, near_y, corner = (e, s ^ 1), (e, s ^ 2), (e, s ^ 3)
    around = (near_x, near_y, corner)
    hops = (1,) + ZHOPS
    low, full = jnp.bfloat16, jnp.float32
    rows, width = tokens.shape
    slim = wq.shape[0]
    shard = width // 4
    weights = (wq, wk, wv)
    place = e * 4 + s

    at_gain = lax.broadcasted_iota(jnp.int32, (slim, width), 1) == place * slim + lax.broadcasted_iota(
        jnp.int32, (slim, width), 0)
    gain_spot = jnp.where(at_gain, 1.0, 0.0).astype(low)
    few = bias.shape[1]
    at_bias = lax.broadcasted_iota(jnp.int32, (few, width), 1) == place * few + lax.broadcasted_iota(
        jnp.int32, (few, width), 0)
    bias_spot = jnp.where(at_bias, 1.0, 0.0).astype(low)
    two_gains = [contract(one[...], gain_spot, ((1,), (0,))) for one in (gain_one, gain_two)]
    one_bias = contract(bias[...], bias_spot, ((1,), (0,)))
    misc[...] = jnp.concatenate(
        two_gains + [one_bias, jnp.zeros((5, width), full), contract(router_row[...], gain_spot, ((1,), (0,)))], axis=0
    ).astype(low)

    greet(list(around) + [(e ^ d, s) for d in (1, 2, 3, 4, 6)])

    def send_tokens(k):
        return remote(tokens, all_tokens.at[aligned(s, rows)], t_send.at[k], t_recv.at[k], around[k])

    def pass_tokens(k):
        piece = pl.ds(pl.multiple_of((s ^ (1 + k)) * rows + k * (rows // 2), rows // 2), rows // 2)
        view = all_tokens.at[piece]
        return remote(view, view, t_send.at[2 + k], t_recv.at[2 + k], around[1 - k])

    def send_cols(k, m):
        return remote(
            weights[m].at[:, aligned(s ^ (k + 1), shard)], got.at[m, aligned(s, slim)],
            w_send.at[k, m], w_recv.at[k, m], around[k],
        )

    def send_tags(k):
        return remote(misc, tags.at[k], m_send.at[k], m_recv.at[k], around[k])

    def share(k, p):
        return remote(part.at[p], cols.at[p, aligned(e, 4 * slim)], c_send.at[p, k], c_recv.at[p, k], (e ^ hops[k], s))

    def share_tags(k):
        return remote(tag_sum, all_tags.at[k], n_send.at[k], n_recv.at[k], (e ^ hops[k], s))

    def relay(k, p):
        view = cols.at[p, aligned(e ^ hops[k], 4 * slim)]
        return remote(view, view, c_send.at[p, 3 + k], c_recv.at[p, 3 + k], (e ^ 1, s))

    def relay_tags(k):
        return remote(all_tags.at[k], all_tags.at[3 + k], n_send.at[3 + k], n_recv.at[3 + k], (e ^ 1, s))

    def early_out(k):
        return remote(wo, wo_full.at[e, s], h_send.at[k], h_recv.at[k], around[k])

    def along_out(k):
        view = wo_full.at[e]
        return remote(view, view, h_send.at[3 + k], h_recv.at[3 + k], (e ^ hops[k], s))

    def relay_along(k):
        view = wo_full.at[e ^ hops[k]]
        return remote(view, view, h_send.at[6 + k], h_recv.at[6 + k], (e ^ 1, s))

    def give(r):
        return remote(att.at[pl.ds(r * rows, rows)], landed.at[s], a_send.at[r], a_recv.at[s ^ r], (e, r))

    cap = xs.shape[0] // 8

    def g_entry(place):
        return remote(gs.at[pl.ds(pl.multiple_of((e ^ ORDER[place]) * cap, 16), cap)], g_early.at[0, place],
                      e_send.at[place], e_recv.at[place], (e ^ ORDER[place], s))

    def g_hop(which, pair):
        places = pl.ds(2 * pair, 2) if which < 2 else pl.ds(2 * pair + which - 2, 1)
        return remote(g_early.at[(0, 0, 1, 2)[which], places], g_early.at[(1, 2, 3, 3)[which], places],
                      j_send.at[which, pair], j_recv.at[which, pair], (near_x, near_y, near_y, near_x)[which])

    def g_corner(pair):
        for which in range(2):
            g_hop(which, pair).wait_recv()
            g_hop(2 + which, pair).start()

    far = []

    def keep(src, dst):
        copy = pltpu.make_async_copy(src, dst, far_sem.at[len(far)])
        copy.start()
        far.append(copy)

    for k in range(3):
        for m in range(3):
            send_cols(k, m).start()
        send_tags(k).start()
    for k in range(2):
        send_tokens(k).start()
    for k in range(3):
        early_out(k).start()
    for m in range(3):
        got[m, aligned(s, slim), :] = weights[m][:, aligned(s, shard)]
    all_tokens[aligned(s, rows), :] = tokens[...]
    wo_full[e, s] = wo[...]
    hot_row, hot, slot, _, target_row = slots_of(ids_row[...], cap)
    level = lax.broadcasted_iota(jnp.int32, (8 * cap, rows), 0)
    takes = jnp.where((level == target_row[0]) | (level == target_row[1]), 1.0, 0.0).astype(low)
    total = misc[...].astype(full)
    for k in range(3):
        send_tags(k).wait_recv()
        total += tags[k].astype(full)
    tag_sum[...] = total.astype(low)
    for k in range(4):
        share_tags(k).start()
    for k in range(3):
        for m in range(3):
            send_cols(k, m).wait_recv()
    for p in range(2):
        for m in range(3):
            part[p, :, m * 128:(m + 1) * 128] = got[m, :, p * 128:(p + 1) * 128]
    for k in (3, 2, 1, 0):
        share(k, 0).start()
    for p in range(2):
        cols[p, aligned(e, 4 * slim), :] = part[p]
    gs[...] = contract(takes, cotangent[...], ((1,), (0,))).astype(low)
    for place in range(1, 4):
        g_entry(place).start()
    g_early[0, 0] = gs[pl.ds(pl.multiple_of(e * cap, 16), cap), :]
    keep(gs, gs_far)
    found = segment_scalars(lengths, parents, before_mem, reach_mem)
    stats[...] = jnp.zeros_like(stats)
    for r in range(4):
        index[r, :, :(r + 1) * rows] = pair_index(found, r * rows, rows, (r + 1) * rows)[0]
    for k in range(1, 4):
        share_tags(k).wait_recv()
        relay_tags(k).start()
    for k in range(2):
        send_tokens(k).wait_recv()
        pass_tokens(k).start()
    g_entry(1).wait_recv()
    for which in range(2):
        g_hop(which, 0).start()
    for k in range(1, 4):
        share(k, 0).wait_recv()
        relay(k, 0).start()
    for k in (3, 2, 1, 0):
        share(k, 1).start()
    for k in range(3):
        early_out(k).wait_recv()
    for k in (3, 2, 1, 0):
        along_out(k).start()
    share_tags(0).wait_recv()
    for k in range(1, 4):
        relay_tags(k).wait_recv()
    for k in range(7):
        total += all_tags[k].astype(full)
    params[...] = total
    gain = total[0:1]
    table[...] = bias_tables(params, s)

    def norm_block(q, carry):
        spot = aligned(s ^ q, rows)
        values = all_tokens[spot, :].astype(full)
        normed[spot, :] = (values * norm_factor(values) * gain).astype(low)
        return carry

    lax.fori_loop(0, 3, norm_block, 0)
    for k in range(2):
        pass_tokens(k).wait_recv()
    lax.fori_loop(3, 4, norm_block, 0)
    keep(all_tokens, all_tokens_far)

    def pair(p, carry):
        for which in range(2):
            @pl.when(p == which)
            def _():
                share(0, which).wait_recv()
                for k in range(1, 4):
                    relay(k, which).wait_recv()

        for r in range(4):
            out = contract(normed[r * rows:(r + 1) * rows, :], cols[p], ((1,), (0,)))
            first_part = out[:, 0:128].astype(low).astype(full) * HDIM ** (-0.5)
            qkv[p, r * rows:(r + 1) * rows, :] = jnp.concatenate([first_part, out[:, 128:]], axis=1).astype(low)

        for r in (3, 2, 1, 0):
            first, count = r * rows, (r + 1) * rows
            q = qkv[p, first:count, 0:128]
            k = qkv[p, 0:count, 128:256]
            v = qkv[p, 0:count, 256:384]
            lane = lax.broadcasted_iota(jnp.int32, (rows, 128), 1)
            results = []
            noted = stats[first:count, :]
            for side in range(2):
                mine = (lane // HDIM) == side
                scores = contract(jnp.where(mine, q, jnp.zeros_like(q)), k, ((1,), (1,)))
                scores = scores + looked_up(table[pl.ds(2 * p + side, 1), :], index[r, :, :count])
                peak = jnp.max(scores, axis=1, keepdims=True)
                expo = jnp.exp(scores - peak)
                mass = jnp.sum(expo, axis=1, keepdims=True)
                results.append(contract(expo.astype(low), v, ((1,), (0,))) * (1.0 / mass))
                noted = jnp.where(lane == 2 * p + side, peak + jnp.log(mass), noted)
            stats[first:count, :] = noted
            att[first:count, aligned(p, 128)] = jnp.where((lane // HDIM) == 0, results[0], results[1]).astype(low)

            @pl.when((p == 1) & (s != r))
            def _():
                give(r).start()

            if r == 3:
                @pl.when(p == 0)
                def _():
                    g_corner(0)
                    for i in (2, 3):
                        g_entry(i).wait_recv()
                    for which in range(2):
                        g_hop(which, 1).start()

                @pl.when(p == 1)
                def _():
                    g_corner(1)
            if r == 1:
                @pl.when(p == 1)
                def _():
                    for i in range(1, 4):
                        along_out(i).wait_recv()
                        relay_along(i).start()
            if r == 1:
                @pl.when(p == 0)
                def _():
                    for i in range(1, 4):
                        share(i, 1).wait_recv()
                        relay(i, 1).start()
        return carry

    lax.fori_loop(0, 2, pair, 0)
    keep(qkv, qkv_far)
    keep(cols, cols_far)
    keep(stats, stats_far)
    along_out(0).wait_recv()
    for k in range(1, 4):
        relay_along(k).wait_recv()
    keep(wo_full, wo_far)
    landed[s] = att[aligned(s, rows), :]
    total = tokens[...].astype(full)

    def out_rows(index):
        return wo_full[pl.ds(2 * index, 2)].reshape(shard, width)

    total += contract(landed[s], out_rows(s), ((1,), (0,)))
    for k in range(1, 4):
        remote(landed.at[s], landed.at[s ^ k], a_send.at[0], a_recv.at[k], (e, s ^ k)).wait_recv()
        total += contract(landed[s ^ k], out_rows(s ^ k), ((1,), (0,)))
    residual[...] = total
    keep(landed, att_far)
    _, _, normed, _, _, _, given = router_of(total, params[...], hot)
    xs[...] = contract(takes, normed, ((1,), (0,))).astype(low)
    at_slot = lax.broadcasted_iota(jnp.int32, (rows, 128), 1)
    by_slot = jnp.zeros((8, 128), full)
    for k in range(2):
        placed = jnp.where((at_slot == slot[k]) & (slot[k] < cap), given[k], 0.0)
        by_slot += lax.dot_general(hot_row[k], placed, (((1,), (0,)), ((), ())),
                                   precision=lax.Precision.HIGHEST, preferred_element_type=full)
    shares[...] = jnp.zeros_like(shares)
    for k in range(8):
        shares[k, 0:1, :] = by_slot[k:k + 1]
    for pair in range(2):
        for which in range(2):
            g_hop(2 + which, pair).wait_recv()
    keep(g_early, g_far)

    for place in range(1, 4):
        g_entry(place).wait_send()
    for pair in range(2):
        for which in range(4):
            g_hop(which, pair).wait_send()
    for k in range(2):
        send_tokens(k).wait_send()
        pass_tokens(k).wait_send()
    for k in range(3):
        for m in range(3):
            send_cols(k, m).wait_send()
        send_tags(k).wait_send()
        early_out(k).wait_send()
    for k in range(4):
        share_tags(k).wait_send()
        along_out(k).wait_send()
        for p in range(2):
            share(k, p).wait_send()
    for k in range(1, 4):
        relay_tags(k).wait_send()
        relay_along(k).wait_send()
        for p in range(2):
            relay(k, p).wait_send()
    for r in range(4):
        @pl.when(s != r)
        def _():
            give(r).wait_send()
    for copy in far:
        copy.wait()


def front(lengths, parents, tokens, cotangent, ids_row, wq, wk, wv, wo, gain_one, gain_two, bias, router_row):
    rows, width = tokens.shape
    slim, shard = wq.shape[0], width // 4
    cap = 10 * rows // 32
    low, full = jnp.bfloat16, jnp.float32
    vmem, smem, hbm = (pl.BlockSpec(memory_space=m) for m in (pltpu.VMEM, pltpu.SMEM, pl.ANY))
    dma = pltpu.SemaphoreType.DMA
    kept = (
        jax.ShapeDtypeStruct((4 * rows, width), low),
        jax.ShapeDtypeStruct((2, 4 * rows, 3 * shard // 2), low),
        jax.ShapeDtypeStruct((2, width, 3 * shard // 2), low),
        jax.ShapeDtypeStruct((16, width), full),
        jax.ShapeDtypeStruct((4, rows, shard), low),
        jax.ShapeDtypeStruct((4 * rows, 128), full),
        jax.ShapeDtypeStruct((8, 4, slim, width), low),
    )
    return pl.pallas_call(
        front_kernel,
        out_shape=(
            jax.ShapeDtypeStruct((8 * cap, width), low),
            jax.ShapeDtypeStruct((8 * cap, width), low),
            jax.ShapeDtypeStruct((8, 8, 128), full),
            jax.ShapeDtypeStruct((rows, width), full),
        ) + kept + (jax.ShapeDtypeStruct((4, 4, cap, width), low),),
        in_specs=[smem, smem] + [vmem] * 11,
        out_specs=(vmem, hbm, vmem, vmem, hbm, hbm, hbm, vmem, hbm, hbm, hbm, hbm),
        scratch_shapes=[
            pltpu.VMEM(kept[0].shape, low), pltpu.VMEM(kept[1].shape, low), pltpu.VMEM(kept[2].shape, low),
            pltpu.VMEM(kept[6].shape, low), pltpu.VMEM((4 * rows, shard), low), pltpu.VMEM(kept[5].shape, full),
            pltpu.VMEM((3, 4 * slim, shard), low), pltpu.VMEM((2, 4 * slim, 3 * shard // 2), low),
            pltpu.VMEM((4 * rows, width), low),
            pltpu.VMEM((16, width), low), pltpu.VMEM((3, 16, width), low), pltpu.VMEM((16, width), low),
            pltpu.VMEM((7, 16, width), low),
            pltpu.VMEM((4, rows, 4 * rows), jnp.int32), pltpu.VMEM((8, 128), full),
            pltpu.VMEM((4, rows, shard), low),
            pltpu.VMEM((8 * cap, width), low), pltpu.VMEM((4, 4, cap, width), low),
            pltpu.SMEM((16,), jnp.int32), pltpu.SMEM((16,), jnp.int32),
            dma((4,)), dma((4,)), dma((3, 3)), dma((3, 3)), dma((3,)), dma((3,)),
            dma((2, 7)), dma((2, 7)), dma((7,)), dma((7,)),
            dma((10,)), dma((10,)), dma((4,)), dma((4,)),
            dma((4,)), dma((4,)), dma((4, 2)), dma((4, 2)), dma((8,)),
        ],
        compiler_params=pltpu.CompilerParams(
            collective_id=2, has_side_effects=True, vmem_limit_bytes=VMEM_LIMIT
        ),
        cost_estimate=pl.CostEstimate(flops=40 * rows * width * shard, bytes_accessed=24 << 20, transcendentals=8 * rows * rows * 16),
        name="front",
    )(lengths, parents, tokens, cotangent, ids_row, wq, wk, wv, wo, gain_one, gain_two, bias, router_row)


def pair_index_across(found, first, rows, count):
    ids = first + lax.broadcasted_iota(jnp.int32, (1, rows), 1)
    keys = lax.broadcasted_iota(jnp.int32, (count, 1), 0)
    place, reach, _ = token_columns(found, ids)
    key_place, _, key_own = token_columns(found, keys)
    seen = ((reach & key_own) != 0) & (keys <= ids)
    return jnp.where(seen, jnp.minimum(place - key_place, LAST - 1), LAST)


def near_keys(found, first, rows):
    ids = first + lax.broadcasted_iota(jnp.int32, (rows, 1), 0)
    place, reach, _ = token_columns(found, ids)
    step = lax.broadcasted_iota(jnp.int32, (rows, LAST + 1), 1)
    wanted = place - step
    spot = jnp.full((rows, LAST + 1), -1, jnp.int32)
    for k, (start, before, _, length) in enumerate(found):
        inside = ((reach & (1 << k)) != 0) & (wanted >= before) & (wanted < before + length)
        spot = jnp.where(inside, wanted + (start - before), spot)
    return jnp.where(step == LAST, -1, spot)


GROUPS = ((0, 3), (3, 3))


def back_kernel(
    lengths, parents, ids_row, params, ret_s, po_far, ret_b_far, residual_far, cotangent_far,
    wo_far, qkv_far, cols_far, all_tokens_far, att_far, stats_far,
    layer_out_far, tokens_grad, dwq, dwk, dwv, dwo, small_sum,
    po0, po2, ro, ro2, ret_o, ret_b, residual, cotangent, layer_out, wo, qkv, cols, all_tokens, att, stats, datt, datt_own, aog_own, residual_grad,
    o_halves, o_core, o_sums, o_z, o_final, o_seq, index, spots, lse, table, near, dk, dv, dqkv, normed,
    halves, core_got, sums, z_got, final, final_got, parts, first_got, second_got, mine, tally, tally_got, square, square_got,
    before_mem, reach_mem,
    load_sem, d_send, d_recv, w_send, w_recv, core_send, core_recv, z_send, z_recv, a_send, a_recv,
    n_send, n_recv, m_send, m_recv, o_send, o_recv, r_send, r_recv, q_send, q_recv, own_sem,
):
    e, s = lax.axis_index(EXPERT), lax.axis_index(SEQ)
    z, c = e // 2, lax.rem(e, 2)
    near_x, near_y = (e, s ^ 1), (e, s ^ 2)
    around = [(e, s ^ k) for k in range(1, 4)]
    hops = (1,) + ZHOPS
    full, low = jnp.float32, jnp.bfloat16
    high = lax.Precision.HIGHEST
    rows, width = residual.shape
    shard = att.shape[2]
    slim = dwq.shape[0]
    cap = ret_b.shape[0] // 8
    half = shard // 2
    pairs = (
        (residual_far, residual), (cotangent_far, cotangent), (ret_b_far, ret_b), (wo_far, wo), (po_far.at[0], po0),
        (att_far, att), (stats_far, stats), (qkv_far, qkv), (all_tokens_far, all_tokens), (cols_far, cols),
        (po_far.at[2, 0], po2.at[0]), (po_far.at[1, 1], po2.at[1]),
    )
    loads = [pltpu.make_async_copy(src, dst, load_sem.at[k]) for k, (src, dst) in enumerate(pairs)]
    for load in loads:
        load.start()
    greet(around + [(e ^ d, s) for d in range(1, 8)])

    def o_copy(side, which, zone):
        first, second = ((near_x, near_y), (near_y, near_x))[side]
        two = pl.ds(2 * zone, 2)
        if which == 2:
            src, dst = po2.at[side, two], ro2.at[side, two]
        else:
            src, dst = po_far.at[(1 + side, 3)[which], side, two], ro.at[which, side, two]
        return remote(src, dst, o_send.at[side, which, zone], o_recv.at[side, which, zone], second if which == 2 else first)

    def block(index):
        return pl.ds(pl.multiple_of(index * cap, 16), cap)

    def return_rows(place):
        return remote(po0.at[place % 2, place // 2], ret_o.at[block(e)], r_send.at[place], r_recv.at[place],
                      (e ^ ORDER[place], s))

    def start_outs(zone):
        for which in (1, 0):
            for side in range(2):
                o_copy(side, which, zone).start()

    def add_outs(zone):
        for side in range(2):
            o_copy(side, 1, zone).wait_recv()
            for i in (2 * zone, 2 * zone + 1):
                po2[side, i] = (po2[side, i].astype(full) + ro[1, side, i].astype(full)).astype(low)
            o_copy(side, 2, zone).start()

    def finish_outs(zone):
        for side in range(2):
            o_copy(side, 0, zone).wait_recv()
            o_copy(side, 2, zone).wait_recv()
            for i in (2 * zone, 2 * zone + 1):
                po0[side, i] = (
                    po0[side, i].astype(full) + ro[0, side, i].astype(full) + ro2[side, i].astype(full)
                ).astype(low)
                if 2 * i + side:
                    return_rows(2 * i + side).start()
                else:
                    ret_o[block(e), :] = po0[0, 0]

    start_outs(1)
    loads[0].wait()

    held = residual[...]
    _, hot, slot, target, _ = slots_of(ids_row[...], cap)
    scale, unit, unrouted, router, prob, chosen_sum, shares = router_of(held, params[...], hot)
    place = lax.broadcasted_iota(jnp.int32, (rows, 8 * cap), 1)
    takes = jnp.where((place == target[0]) | (place == target[1]), 1.0, 0.0).astype(low)
    at_slot = lax.broadcasted_iota(jnp.int32, (rows, 128), 1)
    dots = jnp.concatenate([ret_s[k, 0:1, :] for k in range(8)], axis=0)
    share_grad = []
    for k in range(2):
        mine_dots = lax.dot_general(hot[k], dots, (((1,), (0,)), ((), ())), precision=high, preferred_element_type=full)
        share_grad.append(jnp.sum(
            jnp.where((at_slot == slot[k]) & (slot[k] < cap), mine_dots, 0.0), axis=1, keepdims=True))
    for load in loads[1:4]:
        load.wait()
    grad = cotangent[...].astype(full)
    inner = shares[0] * share_grad[0] + shares[1] * share_grad[1]
    prob_grad = sum(hot[k] * ((share_grad[k] - inner) / chosen_sum) for k in range(2))
    logit_grad = prob * (prob_grad - jnp.sum(prob * prob_grad, axis=1, keepdims=True))
    normed_grad = contract(takes, ret_b[...], ((1,), (0,))) + lax.dot_general(
        logit_grad, router, (((1,), (0,)), ((), ())), precision=high, preferred_element_type=full
    )
    unit_grad = normed_grad * params[1:2]
    passed = grad + scale * (unit_grad - unit * jnp.mean(unit_grad * unit, axis=1, keepdims=True))
    residual_grad[...] = passed
    aog_own[...] = passed.astype(low)
    datt_own[...] = contract(aog_own[...], wo[...], ((1,), (1,))).astype(low)

    def give(k):
        return remote(datt_own.at[:, aligned(s ^ (k + 1), shard)], datt.at[aligned(s, rows)],
                      d_send.at[k], d_recv.at[k], around[k])

    for k in (2, 0, 1):
        give(k).start()

    def wide_core():
        return remote(o_halves.at[1 - c], o_core, w_send.at[0], w_recv.at[0], (e ^ 1, s))

    def wide_z(k):
        return remote(o_sums.at[z ^ k], o_z.at[k - 1], w_send.at[k], w_recv.at[k], (e ^ (2 * k), s))

    def wide_seq(k):
        return remote(o_final.at[aligned(s ^ (k + 1), slim)], o_seq.at[k], w_send.at[4 + k], w_recv.at[4 + k], around[k])

    for load in loads[4:]:
        load.wait()

    def output_zone(j, carry):
        part = contract(att[j], aog_own[...], ((0,), (0,)))
        for i in range(2):
            o_halves[i, j] = part[i * half:(i + 1) * half].astype(low)
        return carry

    lax.fori_loop(0, 4, output_zone, 0)
    wide_core().start()
    datt[aligned(s, rows), :] = datt_own[:, aligned(s, shard)]
    tally[0] = jnp.zeros((16, width), full)
    tally[0, 1:2] = jnp.sum(normed_grad * unit, axis=0, keepdims=True)
    lane = lax.broadcasted_iota(jnp.int32, (1, width), 1)
    tally[0, 3:4] = jnp.where(lane == 0, jnp.sum(held * held), 0.0)
    tally[0, 8:16] = lax.dot_general(logit_grad, unrouted.astype(full), (((0,), (0,)), ((), ())),
                                     precision=high, preferred_element_type=full)
    wide_core().wait_recv()
    for j in range(4):
        o_sums[j] = (o_halves[c, j].astype(full) + o_core[j].astype(full)).astype(low)
    for k in range(1, 4):
        wide_z(k).start()
    found = segment_scalars(lengths, parents, before_mem, reach_mem)
    table[...] = bias_tables(params, s)
    near[...] = jnp.zeros_like(near)
    for r in range(4):
        index[r, :(r + 1) * rows] = pair_index_across(found, r * rows, rows, (r + 1) * rows)
        spots[r] = near_keys(found, r * rows, rows)
        turned = jnp.transpose(stats[r * rows:(r + 1) * rows, :])
        for h in range(4):
            lse[h, r] = turned[h:h + 1]
    gain = params[0:1]

    def units(q):
        values = all_tokens[aligned(s ^ q, rows), :].astype(full)
        factor = norm_factor(values)
        return values * factor, factor

    def norm_block(q, carry):
        normed[aligned(s ^ q, rows), :] = (units(q)[0] * gain).astype(low)
        return carry

    lax.fori_loop(0, 4, norm_block, 0)

    def core_copy(g):
        slots = pl.ds(*GROUPS[g])
        return remote(halves.at[1 - c, slots], core_got.at[slots], core_send.at[g], core_recv.at[g], (e ^ 1, s))

    def z_copy(g, k):
        slots = pl.ds(*GROUPS[g])
        return remote(sums.at[slots, z ^ k], z_got.at[k - 1, slots], z_send.at[g, k - 1], z_recv.at[g, k - 1],
                      (e ^ (2 * k), s))

    def a_copy(g, k):
        slots = pl.ds(*GROUPS[g])
        return remote(final.at[slots, aligned(s ^ (k + 1), slim)], final_got.at[s, slots],
                      a_send.at[g, k], a_recv.at[g, k], around[k])

    def add_core(g):
        core_copy(g).wait_recv()
        first, amount = GROUPS[g]
        for slot in range(first, first + amount):
            for j in range(4):
                sums[slot, j] = (halves[c, slot, j].astype(full) + core_got[slot, j].astype(full)).astype(low)
        for k in range(1, 4):
            z_copy(g, k).start()

    def finish_grad(g):
        first, amount = GROUPS[g]
        for k in range(1, 4):
            z_copy(g, k).wait_recv()
        for slot in range(first, first + amount):
            block = sums[slot, z].astype(full)
            for k in range(1, 4):
                block += z_got[k - 1, slot].astype(full)
            final[slot] = block
        for k in range(3):
            a_copy(g, k).start()
        for slot in range(first, first + amount):
            final_got[s, slot] = final[slot, aligned(s, slim)]

    for k in range(3):
        give(k).wait_recv()
    add_outs(1)

    def pair(p, carry):
        lanes = aligned(p, 128)
        dk[...] = jnp.zeros_like(dk)
        dv[...] = jnp.zeros_like(dv)
        for r in (3, 2, 1, 0):
            first, count = r * rows, (r + 1) * rows
            q = qkv[p, first:count, 0:128]
            k = qkv[p, 0:count, 128:256]
            v = qkv[p, 0:count, 256:384]
            g = datt[first:count, lanes]
            lane = lax.broadcasted_iota(jnp.int32, (rows, 128), 1)
            lane_long = lax.broadcasted_iota(jnp.int32, (count, 128), 1)
            spot = spots[r]
            spot_lane, spot_block = spot & 127, jnp.where(spot < 0, -1, spot >> 7)
            dq = []
            key_sum, value_sum = 0.0, 0.0
            for side in range(2):
                mine_lanes = (lane // HDIM) == side
                q_side = jnp.where(mine_lanes, q, jnp.zeros_like(q))
                g_side = jnp.where(mine_lanes, g, jnp.zeros_like(g))
                scores = contract(k, q_side, ((1,), (1,)))
                scores = scores + looked_up(table[pl.ds(2 * p + side, 1), :], index[r, :count])
                soft = jnp.exp(scores - lse[2 * p + side, r])
                dprob = contract(v, g_side, ((1,), (1,)))
                delta = jnp.sum(soft * dprob, axis=0, keepdims=True)
                turned = soft * (dprob - delta)
                score_grad = turned.astype(low)
                key_sum = key_sum + contract(score_grad, q_side, ((1,), (0,)))
                value_sum = value_sum + contract(soft.astype(low), g_side, ((1,), (0,)))
                wide = jnp.transpose(turned)
                with_ones = jnp.where((lane_long // HDIM) == side, k, jnp.ones_like(k))
                part = contract(wide.astype(low), with_ones, ((1,), (0,)))
                dq.append(part)
                close = jnp.zeros((rows, 128), full)
                for b in range(count // 128):
                    taken = jnp.take_along_axis(wide[:, b * 128:(b + 1) * 128], spot_lane, axis=1)
                    close = jnp.where(spot_block == b, taken, close)
                near[0, 2 * p + side] += jnp.sum(close.reshape(rows // 8, 8, 128), axis=0)
                rest = jnp.where(mine_lanes, 0.0, part)
                near[1, 2 * p + side] += jnp.sum(rest.reshape(rows // 8, 8, 128), axis=0)
            dqkv[p, first:count, 0:128] = (jnp.where((lane // HDIM) == 0, dq[0], dq[1]) * HDIM ** (-0.5)).astype(low)
            dk[0:count] += key_sum
            dv[0:count] += value_sum

            if r == 3:
                @pl.when(p == 0)
                def _():
                    finish_outs(1)
                    start_outs(0)

                @pl.when(p == 1)
                def _():
                    add_core(0)
            if r == 1:
                @pl.when(p == 1)
                def _():
                    add_outs(0)
        dqkv[p, :, 128:256] = dk[...].astype(low)
        dqkv[p, :, 256:384] = dv[...].astype(low)

        def qkv_zone(j, carry):
            block = contract(normed[:, aligned(j, shard)], dqkv[p], ((0,), (0,)))
            for m in range(3):
                for i in range(2):
                    halves[i, 3 * p + m, j] = block[i * half:(i + 1) * half, m * 128:(m + 1) * 128].astype(low)
            return carry

        lax.fori_loop(0, 4, qkv_zone, 0)

        @pl.when(p == 0)
        def _():
            core_copy(0).start()

        @pl.when(p == 1)
        def _():
            core_copy(1).start()
        return carry

    lax.fori_loop(0, 2, pair, 0)

    def n_copy(kind, which):
        one, two = ((near_x, near_y), (near_y, near_x))[kind]
        if which < 2:
            src = parts.at[(1 + kind, 3)[which], kind]
            return remote(src, first_got.at[kind, which], n_send.at[kind, which], n_recv.at[kind, which], one)
        return remote(parts.at[2 - kind, kind], second_got.at[kind], n_send.at[kind, 2], n_recv.at[kind, 2], two)

    def back_block(i, carry):
        q = 3 - i
        total = jnp.zeros((rows, width), full)
        for p in range(2):
            total += contract(dqkv[p, aligned(s ^ q, rows), :], cols[p], ((1,), (1,)))
        tally[0, 0:1] += jnp.sum(total * units(q)[0], axis=0, keepdims=True)
        mine[...] = total
        for kind in range(2):
            parts[q, kind] = total[:, kind * (width // 2):(kind + 1) * (width // 2)].astype(low)

        @pl.when(i == 0)
        def _():
            n_copy(0, 1).start()
            n_copy(1, 1).start()
            add_core(1)

        @pl.when(i == 1)
        def _():
            n_copy(1, 0).start()

        @pl.when(i == 2)
        def _():
            n_copy(0, 0).start()
        return carry

    lax.fori_loop(0, 4, back_block, 0)
    finish_outs(0)
    for k in range(1, 4):
        wide_z(k).wait_recv()
    whole = o_sums[z].astype(full)
    for k in range(3):
        whole += o_z[k].astype(full)
    o_final[...] = whole.astype(low)
    for k in range(3):
        wide_seq(k).start()

    close, rest = (
        jnp.concatenate([jnp.sum(near[kind, h], axis=0, keepdims=True) for h in range(8)], axis=0) for kind in range(2)
    )
    far = jnp.sum(rest, axis=1, keepdims=True) / HDIM - jnp.sum(close, axis=1, keepdims=True)
    spot = lax.broadcasted_iota(jnp.int32, close.shape, 1)
    by_distance = jnp.where(spot == LAST, far, close)
    lane = lax.broadcasted_iota(jnp.int32, (128, BUCKETS * HEADS), 1)
    distance = lax.broadcasted_iota(jnp.int32, (128, BUCKETS * HEADS), 0)
    hot_bucket = jnp.where((lane // HEADS) == bucket_of(distance), 1.0, 0.0)
    spread = lax.dot_general(by_distance, hot_bucket, (((1,), (0,)), ((), ())), precision=high, preferred_element_type=full)
    head = lax.broadcasted_iota(jnp.int32, spread.shape, 0)
    lane = lax.broadcasted_iota(jnp.int32, spread.shape, 1)
    here = ((lane % HEADS) == s * (HEADS // 4) + head) & (head < HEADS // 4)
    tally[0, 2:3, 0:BUCKETS * HEADS] = jnp.sum(jnp.where(here, spread, 0.0), axis=0, keepdims=True)

    def m_copy(stage, k):
        slot = (0, 3, 4)[stage] + k
        peer = (around[k], (e ^ 1, s), (e ^ (2 * (k + 1)), s))[stage]
        return remote(tally.at[stage], tally_got.at[slot], m_send.at[slot], m_recv.at[slot], peer)

    for k in range(3):
        m_copy(0, k).start()
    for kind in range(2):
        n_copy(kind, 1).wait_recv()
        group = 2 - kind
        parts[group, kind] = (parts[group, kind].astype(full) + first_got[kind, 1].astype(full)).astype(low)
        n_copy(kind, 2).start()
    finish_grad(0)
    total = tally[0]
    for k in range(3):
        m_copy(0, k).wait_recv()
        total += tally_got[k]
    tally[1] = total
    m_copy(1, 0).start()

    for place in range(1, 8):
        return_rows(place).wait_recv()
    mixture = contract(takes, ret_o[...], ((1,), (0,)))
    layer_out[...] = (residual[...] + mixture).astype(low)
    layer_done = pltpu.make_async_copy(layer_out, layer_out_far, own_sem)
    layer_done.start()
    squares = jnp.full((8, 128), jnp.sum(mixture * mixture), full)

    def q_copy(stage, k):
        slot = (0, 3, 4)[stage] + k
        peer = (around[k], (e ^ 1, s), (e ^ (2 * (k + 1)), s))[stage]
        return remote(square.at[stage], square_got.at[slot], q_send.at[slot], q_recv.at[slot], peer)

    square[0] = squares
    for k in range(3):
        q_copy(0, k).start()
    finish_grad(1)
    m_copy(1, 0).wait_recv()
    total = total + tally_got[3]
    tally[2] = total
    for k in range(3):
        m_copy(2, k).start()
    for k in range(3):
        q_copy(0, k).wait_recv()
        squares += square_got[k]
    square[1] = squares
    q_copy(1, 0).start()
    for kind in range(2):
        n_copy(kind, 0).wait_recv()
        n_copy(kind, 2).wait_recv()
        lanes = slice(kind * (width // 2), (kind + 1) * (width // 2))
        mine[:, lanes] += first_got[kind, 0].astype(full) + second_got[kind].astype(full)
    unit, scale = units(0)
    unit_grad = mine[...] * gain
    tokens_grad[...] = residual_grad[...] + scale * (
        unit_grad - unit * jnp.mean(unit_grad * unit, axis=1, keepdims=True)
    )
    q_copy(1, 0).wait_recv()
    squares += square_got[3]
    square[2] = squares
    for k in range(3):
        q_copy(2, k).start()
    for g in range(2):
        for k in range(3):
            a_copy(g, k).wait_recv()
    for m, out in enumerate((dwq, dwk, dwv)):
        for i in range(2):
            for j in range(4):
                out[:, j * shard + i * 128:j * shard + (i + 1) * 128] = final_got[j, m + 3 * i]
    whole = o_final[aligned(s, slim), :].astype(full)
    for k in range(3):
        wide_seq(k).wait_recv()
        whole += o_seq[k].astype(full)
    dwo[...] = whole
    for k in range(3):
        m_copy(2, k).wait_recv()
        total += tally_got[4 + k]
    for k in range(3):
        q_copy(2, k).wait_recv()
        squares += square_got[4 + k]
    lane = lax.broadcasted_iota(jnp.int32, (1, 128), 1)
    small_sum[...] = total
    small_sum[3:4, 0:128] = jnp.where(lane == 1, squares[0:1], total[3:4, 0:128])
    layer_done.wait()
    wide_core().wait_send()
    for k in range(3):
        give(k).wait_send()
        wide_z(k + 1).wait_send()
        wide_seq(k).wait_send()
        for g in range(2):
            z_copy(g, k + 1).wait_send()
            a_copy(g, k).wait_send()
    for g in range(2):
        core_copy(g).wait_send()
    for kind in range(2):
        for which in range(3):
            n_copy(kind, which).wait_send()
    for stage, amount in ((0, 3), (1, 1), (2, 3)):
        for k in range(amount):
            m_copy(stage, k).wait_send()
            q_copy(stage, k).wait_send()
    for place in range(1, 8):
        return_rows(place).wait_send()
    for side in range(2):
        for which in range(3):
            for zone in range(2):
                o_copy(side, which, zone).wait_send()


def back(lengths, parents, ids_row, params, ret_s, part_o, ret_b, residual, cotangent, wo, qkv, cols, all_tokens, att, stats):
    rows, width = residual.shape
    shard = att.shape[2]
    slim = width // 32
    low, full = jnp.bfloat16, jnp.float32
    vmem, smem, hbm = (pl.BlockSpec(memory_space=m) for m in (pltpu.VMEM, pltpu.SMEM, pl.ANY))
    dma = pltpu.SemaphoreType.DMA
    half = shard // 2
    return pl.pallas_call(
        back_kernel,
        out_shape=(
            jax.ShapeDtypeStruct((rows, width), low),
            jax.ShapeDtypeStruct((rows, width), full),
        ) + (jax.ShapeDtypeStruct((slim, width), full),) * 4 + (jax.ShapeDtypeStruct((16, width), full),),
        in_specs=[smem, smem] + [vmem] * 3 + [hbm] * 10,
        out_specs=(hbm,) + (vmem,) * 6,
        scratch_shapes=[
            pltpu.VMEM(part_o.shape[1:], low), pltpu.VMEM(part_o.shape[1:], low), pltpu.VMEM((2,) + part_o.shape[1:], low),
            pltpu.VMEM(part_o.shape[1:], low),
            pltpu.VMEM(ret_b.shape, low), pltpu.VMEM(ret_b.shape, low), pltpu.VMEM((rows, width), full),
            pltpu.VMEM((rows, width), low), pltpu.VMEM((rows, width), low),
            pltpu.VMEM((width, width), low), pltpu.VMEM(qkv.shape, low), pltpu.VMEM(cols.shape, low),
            pltpu.VMEM(all_tokens.shape, low), pltpu.VMEM(att.shape, low), pltpu.VMEM(stats.shape, full),
            pltpu.VMEM((4 * rows, shard), low), pltpu.VMEM((rows, width), low),
            pltpu.VMEM((rows, width), low), pltpu.VMEM((rows, width), full),
            pltpu.VMEM((2, 4, half, width), low), pltpu.VMEM((4, half, width), low),
            pltpu.VMEM((4, half, width), low), pltpu.VMEM((3, half, width), low),
            pltpu.VMEM((half, width), low), pltpu.VMEM((3, slim, width), low),
            pltpu.VMEM((4, 4 * rows, rows), jnp.int32), pltpu.VMEM((4, rows, 128), jnp.int32),
            pltpu.VMEM((4, 4, 1, rows), full), pltpu.VMEM((8, 128), full), pltpu.VMEM((2, 8, 8, 128), full),
            pltpu.VMEM((4 * rows, 128), full), pltpu.VMEM((4 * rows, 128), full),
            pltpu.VMEM((2, 4 * rows, 3 * shard // 2), low), pltpu.VMEM((4 * rows, width), low),
            pltpu.VMEM((2, 6, 4, half, half), low), pltpu.VMEM((6, 4, half, half), low),
            pltpu.VMEM((6, 4, half, half), low), pltpu.VMEM((3, 6, half, half), low),
            pltpu.VMEM((6, half, half), full), pltpu.VMEM((4, 6, slim, half), full),
            pltpu.VMEM((4, 2, rows, width // 2), low), pltpu.VMEM((2, 2, rows, width // 2), low),
            pltpu.VMEM((2, rows, width // 2), low), pltpu.VMEM((rows, width), full),
            pltpu.VMEM((3, 16, width), full), pltpu.VMEM((7, 16, width), full),
            pltpu.VMEM((3, 8, 128), full), pltpu.VMEM((7, 8, 128), full),
            pltpu.SMEM((16,), jnp.int32), pltpu.SMEM((16,), jnp.int32),
            dma((12,)), dma((3,)), dma((3,)), dma((7,)), dma((7,)), dma((2,)), dma((2,)),
            dma((2, 3)), dma((2, 3)), dma((2, 3)), dma((2, 3)), dma((2, 3)), dma((2, 3)), dma((7,)), dma((7,)),
            dma((2, 3, 2)), dma((2, 3, 2)), dma((8,)), dma((8,)), dma((7,)), dma((7,)), dma,
        ],
        compiler_params=pltpu.CompilerParams(
            collective_id=5, has_side_effects=True, vmem_limit_bytes=VMEM_LIMIT
        ),
        cost_estimate=pl.CostEstimate(flops=120 * rows * width * shard, bytes_accessed=20 << 20, transcendentals=8 * rows * rows * 16),
        name="back",
    )(lengths, parents, ids_row, params, ret_s, part_o, ret_b, residual, cotangent, wo, qkv, cols, all_tokens, att, stats)


def emit_kernel(*refs):
    large, small = refs[:9], refs[9]
    out, (gain_one, gain_two, bias, router, roots) = refs[10:19], refs[19:24]
    held, wide, in_sem, out_sem = refs[24:33], refs[33:36], refs[36], refs[37]
    comes, goes = [], []
    for k, (src, mid, dst) in enumerate(zip(large, held, out)):
        pieces = 4 if k >= 6 else 1
        amount = src.shape[0] // pieces
        for i in range(pieces):
            part = pl.ds(i * amount, amount)
            comes.append(pltpu.make_async_copy(src.at[part], mid.at[part], in_sem.at[len(comes)]))
            last = wide[k - 6] if k >= 6 else mid
            goes.append(pltpu.make_async_copy(last.at[part], dst.at[part], out_sem.at[len(goes)]))
    order = list(range(6, 18)) + list(range(6))
    for k in order:
        comes[k].start()
    place = lax.axis_index(EXPERT) * 4 + lax.axis_index(SEQ)
    width = small.shape[1]

    def own(length):
        lane = lax.broadcasted_iota(jnp.int32, (length, width), 1)
        down = lax.broadcasted_iota(jnp.int32, (length, width), 0)
        return jnp.where(lane == place * length + down, 1.0, 0.0)

    def picked(left, right):
        return lax.dot_general(left, right, (((1,), (1,)), ((), ())),
                               precision=lax.Precision.HIGHEST, preferred_element_type=jnp.float32)

    for k in order:
        comes[k].wait()
        if k >= 6:
            which, i = (k - 6) // 4, (k - 6) % 4
            amount = held[6].shape[0] // 4
            part = slice(i * amount, (i + 1) * amount)
            wide[which][part] = held[6 + which][part].astype(jnp.float32)
        goes[k].start()
    slim = gain_one.shape[1]
    ours = own(slim)
    gains = picked(small[0:8], ours)
    gain_one[...] = gains[0:1]
    gain_two[...] = gains[1:2]
    bias[...] = picked(small[0:8], own(bias.shape[1]))[2:3]
    router[...] = picked(small[8:16], ours)
    roots[...] = jnp.sqrt(small[3:4, 0:2] / (32 * large[0].shape[0] * width))
    for copy in goes:
        copy.wait()


def emit(large, small):
    full = jnp.float32
    width = small.shape[1]
    vmem, hbm = pl.BlockSpec(memory_space=pltpu.VMEM), pl.BlockSpec(memory_space=pl.ANY)
    slim = width // 32
    shapes = ((1, slim), (1, slim), (1, BUCKETS * HEADS // 32), (8, slim), (1, 2))
    return pl.pallas_call(
        emit_kernel,
        out_shape=tuple(jax.ShapeDtypeStruct(x.shape, x.dtype) for x in large[:6])
        + tuple(jax.ShapeDtypeStruct(x.shape, full) for x in large[6:])
        + tuple(jax.ShapeDtypeStruct(shape, full) for shape in shapes),
        in_specs=[hbm] * 9 + [vmem],
        out_specs=(hbm,) * 9 + (vmem,) * 5,
        scratch_shapes=[pltpu.VMEM(x.shape, x.dtype) for x in large]
        + [pltpu.VMEM(x.shape, full) for x in large[6:]]
        + [pltpu.SemaphoreType.DMA((18,)), pltpu.SemaphoreType.DMA((18,))],
        compiler_params=pltpu.CompilerParams(vmem_limit_bytes=VMEM_LIMIT),
        name="emit",
    )(*large, small)


def per_device_kernels(
    tokens, cotangent, expert_ids, segment_lengths, segment_parents, attention_gain,
    query_weight, key_weight, value_weight, output_weight, bias_table, feedforward_gain,
    router_weight, gate_weight, up_weight, down_weight,
):
    ids_row = expert_ids.T
    send_rows, grad_rows, shares, residual, all_tokens, qkv, cols, params, att, stats, wo, g_early = front(
        segment_lengths, segment_parents, tokens, cotangent, ids_row, query_weight, key_weight, value_weight,
        output_weight, attention_gain[None], feedforward_gain[None], bias_table[None], router_weight.T,
    )
    part_out, grad_back, dots, gate_term, up_term, down_term = experts(
        send_rows, grad_rows, shares, g_early, gate_weight[0], up_weight[0], down_weight[0]
    )
    layer_out, tokens_grad, dwq, dwk, dwv, dwo, totals = back(
        segment_lengths, segment_parents, ids_row, params, dots, part_out, grad_back, residual, cotangent,
        wo.reshape(D, D), qkv, cols, all_tokens, att, stats,
    )
    large = (layer_out, tokens_grad, dwq, dwk, dwv, dwo, gate_term, up_term, down_term)
    *large, gain_one, gain_two, bias, router, roots = emit(large, totals)
    layer_out, tokens_grad, dwq, dwk, dwv, dwo, gate_term, up_term, down_term = large
    return (
        layer_out, tokens_grad, gain_one[0], dwq, dwk, dwv, dwo, bias[0], gain_two[0], router.T,
        gate_term[None], up_term[None], down_term[None], roots[0],
    )


def per_device_general(
    tokens,
    cotangent,
    expert_ids,
    segment_lengths,
    segment_parents,
    attention_gain,
    query_weight,
    key_weight,
    value_weight,
    output_weight,
    bias_table,
    feedforward_gain,
    router_weight,
    gate_weight,
    up_weight,
    down_weight,
):
    seq_count = lax.axis_size(SEQ)
    seq_place = lax.axis_index(SEQ)
    all_count = lax.axis_size(EXPERT) * seq_count
    row_count = tokens.shape[0]
    experts = lax.axis_size(EXPERT) * gate_weight.shape[0]
    capacity = 10 * row_count // (4 * experts)
    score_scale = HDIM ** (-0.5)
    gathered = (
        lax.all_gather(attention_gain, BOTH, axis=0, tiled=True),
        lax.all_gather(query_weight, BOTH, axis=0, tiled=True),
        lax.all_gather(key_weight, BOTH, axis=0, tiled=True),
        lax.all_gather(value_weight, BOTH, axis=0, tiled=True),
        lax.all_gather(output_weight, BOTH, axis=0, tiled=True),
        lax.all_gather(bias_table, BOTH, axis=0, tiled=True),
        lax.all_gather(feedforward_gain, BOTH, axis=0, tiled=True),
        lax.all_gather(router_weight, BOTH, axis=0, tiled=True),
    )
    gain_one, query_full, key_full, value_full, output_full, bias_flat, gain_two, router_full = (
        gathered
    )
    bias_grid = bias_flat.reshape(BUCKETS, HEADS)
    starts, before, reaches = tree_tables(segment_lengths[0], segment_parents[0])
    own_rows = seq_place * row_count + jnp.arange(row_count, dtype=jnp.int32)
    own_meta = token_info(own_rows, starts, before, reaches)
    tokens_float = tokens.astype(jnp.float32)
    scale_one = norm_factor(tokens_float)
    unit_one = tokens_float * scale_one
    normed_one = (unit_one * gain_one.astype(jnp.float32)).astype(jnp.bfloat16)
    queries = (
        jnp.dot(normed_one, query_full, preferred_element_type=jnp.float32)
        .astype(jnp.bfloat16)
        .reshape(row_count, HEADS, HDIM)
    )
    keys_own = (
        jnp.dot(normed_one, key_full, preferred_element_type=jnp.float32)
        .astype(jnp.bfloat16)
        .reshape(row_count, HEADS, HDIM)
    )
    values_own = (
        jnp.dot(normed_one, value_full, preferred_element_type=jnp.float32)
        .astype(jnp.bfloat16)
        .reshape(row_count, HEADS, HDIM)
    )
    row_peak = jnp.full((HEADS, row_count), NEGATIVE, jnp.float32)
    key_piece = lax.all_gather(keys_own, SEQ, axis=0, tiled=True)
    value_piece = lax.all_gather(values_own, SEQ, axis=0, tiled=True)
    key_rows = jnp.arange(key_piece.shape[0], dtype=jnp.int32)
    visible, onehot, pair_bias = pair_terms(
        own_meta, token_info(key_rows, starts, before, reaches), own_rows, key_rows, bias_grid
    )
    scores = masked_scores(queries, key_piece, visible, pair_bias)
    new_peak = jnp.maximum(row_peak, jnp.max(scores, axis=-1))
    expo = jnp.exp(scores - new_peak[:, :, None])
    row_total = jnp.sum(expo, axis=-1)
    summed = jnp.einsum(
        SPEC_2, expo.astype(jnp.bfloat16), value_piece, preferred_element_type=jnp.float32
    )
    row_peak, row_total, summed = (new_peak, row_total, summed)
    log_total = row_peak + jnp.log(row_total)
    attended_float = summed / jnp.transpose(row_total)[:, :, None]
    attended = attended_float.astype(jnp.bfloat16).reshape(row_count, D)
    residual = tokens_float + jnp.dot(attended, output_full, preferred_element_type=jnp.float32)
    scale_two = norm_factor(residual)
    unit_two = residual * scale_two
    normed_two = (unit_two * gain_two.astype(jnp.float32)).astype(jnp.bfloat16)
    router_prob = jax.nn.softmax(
        jnp.dot(normed_two, router_full, preferred_element_type=jnp.float32), axis=-1
    )
    pick_hot = (
        expert_ids[:, :, None] == jnp.arange(experts, dtype=jnp.int32)[None, None, :]
    ).astype(jnp.float32)
    chosen = jnp.sum(pick_hot * router_prob[:, None, :], axis=2)
    chosen_total = jnp.sum(chosen, axis=1, keepdims=True)
    gate_shares = chosen / chosen_total
    hot_int = pick_hot.astype(jnp.int32).reshape(row_count * 2, experts)
    earlier = jnp.cumsum(hot_int, axis=0) - hot_int
    slot_number = jnp.sum(earlier * hot_int, axis=1).reshape(row_count, 2)
    kept_copy = slot_number < capacity
    kept_float = kept_copy.astype(jnp.float32)
    target = jnp.where(kept_copy, expert_ids * capacity + slot_number, experts * capacity)
    copy_ids = jnp.arange(row_count * 2, dtype=jnp.int32)
    slot_copy = (
        jnp.full((experts * capacity + 1,), row_count * 2, jnp.int32)
        .at[target.reshape(-1)]
        .set(copy_ids)[: experts * capacity]
    )
    fetch_index = jnp.minimum(target, experts * capacity - 1).reshape(-1)
    token_of_slot = jnp.where(slot_copy < row_count * 2, slot_copy // 2, row_count)
    padded = jnp.concatenate([normed_two, jnp.zeros((1, D), jnp.bfloat16)], axis=0)
    send_rows = padded[token_of_slot].reshape(experts, capacity, D)
    expert_in = lax.all_to_all(send_rows, EXPERT, split_axis=0, concat_axis=1, tiled=True)[0]
    gate_piece = lax.all_gather(gate_weight, SEQ, axis=1, tiled=True)
    up_piece = lax.all_gather(up_weight, SEQ, axis=1, tiled=True)
    down_piece = lax.all_gather(down_weight, SEQ, axis=1, tiled=True)
    gate_pre = jnp.einsum(SPEC_3, expert_in, gate_piece[0], preferred_element_type=jnp.float32)
    up_pre = jnp.einsum(SPEC_3, expert_in, up_piece[0], preferred_element_type=jnp.float32)
    active = (gelu_tanh(gate_pre) * up_pre).astype(jnp.bfloat16)
    expert_sum = jnp.dot(active, down_piece[0], preferred_element_type=jnp.float32)
    returned = lax.all_to_all(
        expert_sum.astype(jnp.bfloat16)[None], EXPERT, split_axis=1, concat_axis=0, tiled=True
    )
    picked = (
        returned.reshape(experts * capacity, D)[fetch_index]
        .reshape(row_count, 2, D)
        .astype(jnp.float32)
    )
    weighted = gate_shares * kept_float
    mixture = jnp.sum(weighted[:, :, None] * picked, axis=1)
    layer_out = (residual + mixture).astype(jnp.bfloat16)
    local_sums = jnp.stack([jnp.sum(residual * residual), jnp.sum(mixture * mixture)])
    again = (
        lax.all_gather(attention_gain, BOTH, axis=0, tiled=True),
        lax.all_gather(query_weight, BOTH, axis=0, tiled=True),
        lax.all_gather(key_weight, BOTH, axis=0, tiled=True),
        lax.all_gather(value_weight, BOTH, axis=0, tiled=True),
        lax.all_gather(output_weight, BOTH, axis=0, tiled=True),
        lax.all_gather(bias_table, BOTH, axis=0, tiled=True),
        lax.all_gather(feedforward_gain, BOTH, axis=0, tiled=True),
        lax.all_gather(router_weight, BOTH, axis=0, tiled=True),
    )
    gain_one, query_full, key_full, value_full, output_full, bias_flat, gain_two, router_full = (
        again
    )
    bias_grid = bias_flat.reshape(BUCKETS, HEADS)
    grad_out = cotangent.astype(jnp.float32)
    copy_grad = (
        (weighted[:, :, None] * grad_out[:, None, :]).astype(jnp.bfloat16).reshape(row_count * 2, D)
    )
    copy_padded = jnp.concatenate([copy_grad, jnp.zeros((1, D), jnp.bfloat16)], axis=0)
    grad_send = copy_padded[slot_copy].reshape(experts, capacity, D)
    grad_in = lax.all_to_all(grad_send, EXPERT, split_axis=0, concat_axis=1, tiled=True)[0]
    gate_piece = lax.all_gather(gate_weight, SEQ, axis=1, tiled=True)
    up_piece = lax.all_gather(up_weight, SEQ, axis=1, tiled=True)
    down_piece = lax.all_gather(down_weight, SEQ, axis=1, tiled=True)
    gate_pre = jnp.einsum(SPEC_3, expert_in, gate_piece[0], preferred_element_type=jnp.float32)
    up_pre = jnp.einsum(SPEC_3, expert_in, up_piece[0], preferred_element_type=jnp.float32)
    gelu_out, gelu_pull = jax.vjp(gelu_tanh, gate_pre)
    act_grad = jnp.einsum(SPEC_3, grad_in, down_piece[0], preferred_element_type=jnp.float32)
    gate_back = gelu_pull(act_grad * up_pre)[0].astype(jnp.bfloat16)
    up_back = (act_grad * gelu_out).astype(jnp.bfloat16)
    input_grad = jnp.dot(gate_back, gate_piece[0], preferred_element_type=jnp.float32) + jnp.dot(
        up_back, up_piece[0], preferred_element_type=jnp.float32
    )
    active = (gelu_out * up_pre).astype(jnp.bfloat16)
    input_grad, gate_backs, up_backs, actives = (input_grad, gate_back, up_back, active)
    grad_back = lax.all_to_all(
        input_grad.astype(jnp.bfloat16)[None], EXPERT, split_axis=1, concat_axis=0, tiled=True
    )
    expert_back = (
        grad_back.reshape(experts * capacity, D)[fetch_index]
        .reshape(row_count, 2, D)
        .astype(jnp.float32)
    )
    normed_two_grad = jnp.sum(expert_back * kept_float[:, :, None], axis=1)
    expert_grads = lax.psum_scatter(
        jnp.stack(
            [
                jnp.einsum(SPEC_4, gate_backs, expert_in, preferred_element_type=jnp.float32),
                jnp.einsum(SPEC_4, up_backs, expert_in, preferred_element_type=jnp.float32),
                jnp.einsum(SPEC_4, actives, grad_in, preferred_element_type=jnp.float32),
            ],
            axis=1,
        ).astype(jnp.bfloat16),
        SEQ,
        scatter_dimension=0,
        tiled=True,
    ).astype(jnp.float32)
    share_grad = jnp.sum(grad_out[:, None, :] * picked, axis=2) * kept_float
    chosen_grad = (
        share_grad - jnp.sum(gate_shares * share_grad, axis=1, keepdims=True)
    ) / chosen_total
    prob_grad = jnp.sum(pick_hot * chosen_grad[:, :, None], axis=1)
    logit_grad = router_prob * (prob_grad - jnp.sum(router_prob * prob_grad, axis=1, keepdims=True))
    router_float = router_full.astype(jnp.float32)
    router_term = jnp.einsum(
        SPEC_5, normed_two.astype(jnp.float32), logit_grad, precision=lax.Precision.HIGHEST
    )
    normed_two_grad = normed_two_grad + jnp.einsum(
        SPEC_6, logit_grad, router_float, precision=lax.Precision.HIGHEST
    )
    gain_two_term = jnp.sum(normed_two_grad * unit_two, axis=0)
    unit_grad_two = normed_two_grad * gain_two.astype(jnp.float32)
    residual_grad = grad_out + scale_two * (
        unit_grad_two - unit_two * jnp.mean(unit_grad_two * unit_two, axis=-1, keepdims=True)
    )
    attention_out_grad = residual_grad.astype(jnp.bfloat16)
    output_term = jnp.einsum(
        SPEC_5, attended, attention_out_grad, preferred_element_type=jnp.float32
    )
    attended_grad = (
        jnp.einsum(SPEC_6, attention_out_grad, output_full, preferred_element_type=jnp.float32)
        .astype(jnp.bfloat16)
        .reshape(row_count, HEADS, HDIM)
    )
    row_delta = jnp.transpose(jnp.sum(attended_grad.astype(jnp.float32) * attended_float, axis=-1))
    total_all, delta_all = (
        lax.all_gather(log_total, SEQ, axis=1, tiled=True),
        lax.all_gather(row_delta, SEQ, axis=1, tiled=True),
    )
    key_piece = lax.all_gather(keys_own, SEQ, axis=0, tiled=True)
    value_piece = lax.all_gather(values_own, SEQ, axis=0, tiled=True)
    key_rows = jnp.arange(key_piece.shape[0], dtype=jnp.int32)
    visible, onehot, pair_bias = pair_terms(
        own_meta, token_info(key_rows, starts, before, reaches), own_rows, key_rows, bias_grid
    )
    scores = masked_scores(queries, key_piece, visible, pair_bias)
    soft_weights = jnp.exp(scores - log_total[:, :, None])
    dprob = jnp.einsum(
        SPEC_1, attended_grad, value_piece, preferred_element_type=jnp.float32
    )
    score_grad = (soft_weights * (dprob - row_delta[:, :, None])).astype(jnp.bfloat16)
    query_acc = jnp.einsum(
        SPEC_2, score_grad, key_piece, preferred_element_type=jnp.float32
    )
    bias_acc = jnp.einsum(SPEC_7, onehot, score_grad, preferred_element_type=jnp.float32)
    query_acc, bias_acc = (query_acc, bias_acc)
    query_piece = lax.all_gather(queries, SEQ, axis=0, tiled=True)
    grad_piece = lax.all_gather(attended_grad, SEQ, axis=0, tiled=True)
    piece_rows = query_piece.shape[0]
    query_rows = jnp.arange(piece_rows, dtype=jnp.int32)
    visible, onehot, pair_bias = pair_terms(
        token_info(query_rows, starts, before, reaches), own_meta, query_rows, own_rows, bias_grid
    )
    scores = masked_scores(query_piece, keys_own, visible, pair_bias)
    soft_weights = jnp.exp(scores - total_all[:, :, None])
    value_acc = jnp.einsum(
        SPEC_8,
        soft_weights.astype(jnp.bfloat16),
        grad_piece,
        preferred_element_type=jnp.float32,
    )
    dprob = jnp.einsum(SPEC_1, grad_piece, values_own, preferred_element_type=jnp.float32)
    score_grad = (soft_weights * (dprob - delta_all[:, :, None])).astype(jnp.bfloat16)
    key_acc = jnp.einsum(
        SPEC_8, score_grad, query_piece, preferred_element_type=jnp.float32
    )
    key_acc, value_acc = (key_acc, value_acc)
    query_back = (query_acc * score_scale).astype(jnp.bfloat16).reshape(row_count, D)
    key_back = (key_acc * score_scale).astype(jnp.bfloat16).reshape(row_count, D)
    value_back = value_acc.astype(jnp.bfloat16).reshape(row_count, D)
    query_term = jnp.einsum(SPEC_5, normed_one, query_back, preferred_element_type=jnp.float32)
    key_term = jnp.einsum(SPEC_5, normed_one, key_back, preferred_element_type=jnp.float32)
    value_term = jnp.einsum(SPEC_5, normed_one, value_back, preferred_element_type=jnp.float32)
    normed_one_grad = jnp.einsum(
        SPEC_6, query_back, query_full, preferred_element_type=jnp.float32
    )
    normed_one_grad = normed_one_grad + jnp.einsum(
        SPEC_6, key_back, key_full, preferred_element_type=jnp.float32
    )
    normed_one_grad = normed_one_grad + jnp.einsum(
        SPEC_6, value_back, value_full, preferred_element_type=jnp.float32
    )
    gain_one_term = jnp.sum(normed_one_grad * unit_one, axis=0)
    unit_grad_one = normed_one_grad * gain_one.astype(jnp.float32)
    tokens_grad = residual_grad + scale_one * (
        unit_grad_one - unit_one * jnp.mean(unit_grad_one * unit_one, axis=-1, keepdims=True)
    )
    stats_term = jnp.broadcast_to(local_sums[None, :], (all_count, 2))
    reduced = (
        lax.psum_scatter(gain_one_term, BOTH, scatter_dimension=0, tiled=True),
        lax.psum_scatter(query_term, BOTH, scatter_dimension=0, tiled=True),
        lax.psum_scatter(key_term, BOTH, scatter_dimension=0, tiled=True),
        lax.psum_scatter(value_term, BOTH, scatter_dimension=0, tiled=True),
        lax.psum_scatter(output_term, BOTH, scatter_dimension=0, tiled=True),
        lax.psum_scatter(
            bias_acc.reshape(BUCKETS * HEADS), BOTH, scatter_dimension=0, tiled=True
        ),
        lax.psum_scatter(gain_two_term, BOTH, scatter_dimension=0, tiled=True),
        lax.psum_scatter(router_term, BOTH, scatter_dimension=0, tiled=True),
        lax.psum_scatter(stats_term, BOTH, scatter_dimension=0, tiled=True),
    )
    roots = jnp.sqrt(reduced[8][0] / (row_count * all_count * D))
    return (
        layer_out,
        tokens_grad,
        reduced[0],
        reduced[1],
        reduced[2],
        reduced[3],
        reduced[4],
        reduced[5],
        reduced[6],
        reduced[7],
        expert_grads[None, :, 0, :],
        expert_grads[None, :, 1, :],
        expert_grads[None, :, 2, :],
        roots,
    )


def solution(mesh):
    kernels_fit = mesh.shape[EXPERT] == len(ORDER) and mesh.shape[SEQ] == 4
    return jax.shard_map(
        per_device_kernels if kernels_fit else per_device_general,
        mesh=mesh,
        in_specs=(
            P(BOTH, None),
            P(BOTH, None),
            P(BOTH, None),
            P(EXPERT, None),
            P(EXPERT, None),
            P(BOTH),
            P(BOTH, None),
            P(BOTH, None),
            P(BOTH, None),
            P(BOTH, None),
            P(BOTH),
            P(BOTH),
            P(BOTH, None),
            P(EXPERT, SEQ, None),
            P(EXPERT, SEQ, None),
            P(EXPERT, SEQ, None),
        ),
        out_specs=(
            P(BOTH, None),
            P(BOTH, None),
            P(BOTH),
            P(BOTH, None),
            P(BOTH, None),
            P(BOTH, None),
            P(BOTH, None),
            P(BOTH),
            P(BOTH),
            P(BOTH, None),
            P(EXPERT, SEQ, None),
            P(EXPERT, SEQ, None),
            P(EXPERT, SEQ, None),
            P(),
        ),
        check_vma=False,
    )
```

```python
import math

import jax
import jax.numpy as jnp
from jax import lax
from jax.experimental import pallas as pl
from jax.experimental.pallas import tpu as pltpu
from jax.sharding import PartitionSpec as P

SPEC_0 = "qkb,bh->hqk"
SPEC_1 = "qhd,khd->hqk"
SPEC_2 = "hqk,khd->qhd"
SPEC_3 = "rd,fd->rf"
SPEC_4 = "rf,rd->fd"
SPEC_5 = "rd,re->de"
SPEC_6 = "re,de->rd"
SPEC_7 = "qkb,hqk->bh"
SPEC_8 = "hqk,qhd->khd"
MESH = pl.DeviceIdType.MESH
VMEM_LIMIT = 62 << 20
EXPERT, SEQ = "expert", "seq"
BOTH = (EXPERT, SEQ)

D = 1024
HEADS = 16
HDIM = 64
BUCKETS = 32
MAXDIST = 128


EPSILON = 1e-06
NEGATIVE = -1e30


def norm_factor(values):
    return lax.rsqrt(jnp.mean(values * values, axis=-1, keepdims=True) + EPSILON)


def gelu_tanh(values):
    return jax.nn.gelu(values, approximate=True)


def bucket_of(distance):
    exact_span = BUCKETS // 2
    above = jnp.zeros(distance.shape, jnp.int32)
    for number in range(exact_span):
        threshold = int(math.ceil(exact_span * (MAXDIST / exact_span) ** (number / exact_span)))
        above = above + (distance >= threshold).astype(jnp.int32)
    return jnp.where(distance < exact_span, distance, exact_span - 1 + above)


def tree_tables(lengths, parents):
    ordinal = jnp.arange(lengths.shape[0], dtype=jnp.int32)
    starts = jnp.cumsum(lengths) - lengths

    def chase(number, running):
        current, reaches = running
        current = jnp.sum(
            jnp.where(current[:, None] == ordinal[None, :], parents[None, :], 0), axis=1
        )
        reaches = jnp.maximum(reaches, (current[:, None] == ordinal[None, :]).astype(jnp.int32))
        return (current, reaches)

    begin = (ordinal, (ordinal[:, None] == ordinal[None, :]).astype(jnp.int32))
    unused, reaches = lax.fori_loop(0, lengths.shape[0], chase, begin)
    before = jnp.sum(reaches * lengths[None, :], axis=1) - lengths
    return (starts, before, reaches)


def token_info(token_rows, starts, before, reaches):
    ordinal = jnp.arange(starts.shape[0], dtype=jnp.int32)
    segment = jnp.sum((token_rows[:, None] >= starts[None, :]).astype(jnp.int32), axis=1) - 1
    member = segment[:, None] == ordinal[None, :]
    position = token_rows + jnp.sum(jnp.where(member, (before - starts)[None, :], 0), axis=1)
    lineage = jnp.sum(jnp.where(member[:, :, None], reaches[None, :, :], 0), axis=1)
    return (member.astype(jnp.float32), position, lineage.astype(jnp.float32))


def pair_terms(query_meta, key_meta, query_rows, key_rows, bias_grid):
    visible = jnp.dot(query_meta[2], key_meta[0].T, preferred_element_type=jnp.float32) > 0.5
    visible = visible & (key_rows[None, :] <= query_rows[:, None])
    distance = jnp.maximum(query_meta[1][:, None] - key_meta[1][None, :], 0)
    onehot = (
        bucket_of(distance)[:, :, None] == jnp.arange(BUCKETS, dtype=jnp.int32)[None, None, :]
    ).astype(jnp.bfloat16)
    pair_bias = jnp.einsum(SPEC_0, onehot, bias_grid, preferred_element_type=jnp.float32)
    return (visible, onehot, pair_bias)


def masked_scores(query_block, key_block, visible, pair_bias):
    scores = (
        jnp.einsum(SPEC_1, query_block, key_block, preferred_element_type=jnp.float32)
        * HDIM ** (-0.5)
        + pair_bias
    )
    return jnp.where(visible[None], scores, NEGATIVE)


def remote(src, dst, send, recv, peer):
    return pltpu.make_async_remote_copy(
        src_ref=src, dst_ref=dst, send_sem=send, recv_sem=recv,
        device_id=peer, device_id_type=MESH,
    )


def contract(left, right, dims):
    return lax.dot_general(left, right, (dims, ((), ())), preferred_element_type=jnp.float32)


def gelu_parts(values):
    root = 0.7978845608028654
    square = values * values
    swing = jnp.tanh(root * values * (1.0 + 0.044715 * square))
    half = 0.5 * (1.0 + swing)
    slope = half + 0.5 * values * (1.0 - swing * swing) * (root * (1.0 + 3 * 0.044715 * square))
    return values * half, slope


ORDER = (0, 1, 2, 3, 4, 5, 6, 7)
UNITS = (
    (0, 0), (0, 1), (1, 0), (2, 0), (3, 0), (1, 1), (2, 1), (3, 1),
    (0, 2), (1, 2), (2, 2), (0, 3), (3, 2), (1, 3), (2, 3), (3, 3),
)


def announce(peers):
    barrier = pltpu.get_barrier_semaphore()
    for peer in peers:
        pl.semaphore_signal(barrier, inc=1, device_id=peer, device_id_type=MESH)


def greet(peers):
    announce(peers)
    pl.semaphore_wait(pltpu.get_barrier_semaphore(), len(peers))


def aligned(index, size):
    return pl.ds(pl.multiple_of(index * size, size), size)


ZHOPS = (2, 4, 6)


def expert_kernel(
    xs, gs, shares, g_early, wg_far, wu_far, wd_far, po_far, ret_b, ret_s, dwg, dwu, dwd,
    xr, gr, sh, act, gb, ub, po, pb, rb, rb2, sd, sd_got, sd_out, stage, rounded, wg, wu, wd,
    in_send, in_recv, hop_send, hop_recv, sh_send, sh_recv, rs_send, rs_recv, out_send, out_recv,
    sd_send, sd_recv, sr_send, sr_recv, po_sem, stage_sem, load_sem, own_sem,
):
    e = lax.axis_index(EXPERT)
    s = lax.axis_index(SEQ)
    cap = xs.shape[0] // 8
    width = xs.shape[1]
    full, low = jnp.float32, jnp.bfloat16
    near_x, near_y = (e, s ^ 1), (e, s ^ 2)
    around = (near_x, near_y, (e, s ^ 3))
    loads = [
        pltpu.make_async_copy(src, dst, load_sem.at[k])
        for k, (src, dst) in enumerate(((wg_far, wg), (wu_far, wu), (wd_far, wd), (g_early, gr.at[:, pl.ds(0, 4)])))
    ]
    for load in loads:
        load.start()
    greet(list(around) + [(e ^ d, s) for d in range(1, 8)])

    def block(index):
        return pl.ds(pl.multiple_of(index * cap, 16), cap)

    tensors = ((xs, xr), (gs, gr))

    def entry(kind, place):
        src, dst = tensors[kind]
        d = ORDER[place]
        return remote(src.at[block(e ^ d)], dst.at[0, place], in_send.at[kind, place],
                      in_recv.at[kind, place], (e ^ d, s))

    def hop(kind, which, pair):
        buf = tensors[kind][1]
        places = pl.ds(2 * pair, 2) if which < 2 else pl.ds(2 * pair + which - 2, 1)
        src = buf.at[(0, 0, 1, 2)[which], places]
        dst = buf.at[(1, 2, 3, 3)[which], places]
        peer = (near_x, near_y, near_y, near_x)[which]
        return remote(src, dst, hop_send.at[kind, which, pair], hop_recv.at[kind, which, pair], peer)

    def share_entry(place):
        d = ORDER[place]
        return remote(shares.at[e ^ d], sh.at[0, place], sh_send.at[place], sh_recv.at[place], (e ^ d, s))

    def share_hop(which):
        return remote(sh.at[(0, 0, 1)[which]], sh.at[1 + which], sh_send.at[8 + which], sh_recv.at[8 + which],
                      (near_x, near_y, near_y)[which])

    def rs(half, which, pair):
        first, second = ((near_x, near_y), (near_y, near_x))[half]
        src = pb.at[(1 + half, 3, 2 - half)[which], half, pair]
        dst = rb2.at[half, pair] if which == 2 else rb.at[which, half, pair]
        return remote(src, dst, rs_send.at[half, which, pair], rs_recv.at[half, which, pair],
                      second if which == 2 else first)

    def back(place):
        return remote(pb.at[0, place % 2, place // 2], ret_b.at[block(e)],
                      out_send.at[place], out_recv.at[place], (e ^ ORDER[place], s))

    def own_back():
        return pltpu.make_async_copy(pb.at[0, 0, 0], ret_b.at[block(e)], own_sem.at[2])

    def start_entries(kind, pair):
        for place in (2 * pair, 2 * pair + 1):
            if ORDER[place]:
                entry(kind, place).start()

    def forward_pair(kind, pair):
        for place in (2 * pair, 2 * pair + 1):
            if ORDER[place]:
                entry(kind, place).wait_recv()
        hop(kind, 0, pair).start()
        hop(kind, 1, pair).start()

    def forward_corner(kind, pair):
        for which in range(2):
            hop(kind, which, pair).wait_recv()
            hop(kind, 2 + which, pair).start()

    def wait_corner(pair):
        for kind in range(2 if pair >= 2 else 1):
            for which in (2, 3):
                hop(kind, which, pair).wait_recv()

    def start_sums(pair):
        for which in (1, 0):
            for half in range(2):
                rs(half, which, pair).start()

    def add_second(pair):
        for half in range(2):
            rs(half, 1, pair).wait_recv()
            group = 2 - half
            pb[group, half, pair] = (pb[group, half, pair].astype(full) + rb[1, half, pair].astype(full)).astype(low)
            rs(half, 2, pair).start()

    def finish(pair):
        for half in range(2):
            rs(half, 0, pair).wait_recv()
            rs(half, 2, pair).wait_recv()
            pb[0, half, pair] = (
                pb[0, half, pair].astype(full) + rb[0, half, pair].astype(full) + rb2[half, pair].astype(full)
            ).astype(low)
            if ORDER[2 * pair + half]:
                back(2 * pair + half).start()
            else:
                own_back().start()

    own_rows = [
        pltpu.make_async_copy(xs.at[block(e)], xr.at[0, 0], own_sem.at[0]),
        pltpu.make_async_copy(shares.at[e], sh.at[0, 0], own_sem.at[1]),
    ]
    for copy in own_rows:
        copy.start()
    start_entries(0, 0)
    for place in range(1, 8):
        share_entry(place).start()
    start_entries(0, 1)
    start_entries(1, 2)

    rows = 2 * cap

    def put_out(u, q, c):
        return pltpu.make_async_copy(po.at[q, :, c], po_far.at[q, :, c], po_sem.at[u])

    def unit(u, carry):
        q, c = jnp.int32(0), jnp.int32(0)
        for k, (whose, pair) in enumerate(UNITS):
            q, c = jnp.where(u == k, whose, q), jnp.where(u == k, pair, c)

        for k, (whose, pair) in enumerate(UNITS):
            @pl.when(u == k)
            def _():
                if k == 0:
                    for copy in own_rows:
                        copy.wait()
                    forward_pair(0, 0)
                    for place in range(1, 8):
                        share_entry(place).wait_recv()
                    share_hop(0).start()
                    share_hop(1).start()
                    for load in loads:
                        load.wait()
                if k == 1:
                    forward_corner(0, 0)
                    forward_pair(0, 1)
                    start_entries(1, 3)
                if k == 2:
                    share_hop(0).wait_recv()
                    share_hop(2).start()
                    share_hop(1).wait_recv()
                if k == 3:
                    forward_corner(0, 1)
                    forward_pair(1, 2)
                    start_entries(0, 2)
                if k == 4:
                    share_hop(2).wait_recv()
                if k == 6:
                    forward_corner(1, 2)
                    forward_pair(1, 3)
                    start_entries(0, 3)
                if k == 8:
                    forward_corner(1, 3)
                    forward_pair(0, 2)
                if k == 9:
                    forward_corner(0, 2)
                if k == 10:
                    add_second(1)
                if k == 11:
                    forward_pair(0, 3)
                if k == 13:
                    forward_corner(0, 3)
                    finish(1)
                if k == 15:
                    add_second(2)
                if whose == 3:
                    wait_corner(pair)

        x = xr[q, pl.ds(2 * c, 2)].reshape(rows, width)
        g = gr[q, pl.ds(2 * c, 2)].reshape(rows, width)
        share = jnp.concatenate([jnp.transpose(sh[q, 2 * c + i])[0:cap, 0:1] for i in range(2)], axis=0)
        gate = contract(x, wg[...], ((1,), (1,)))
        up = contract(x, wu[...], ((1,), (1,)))
        ag = contract(g, wd[...], ((1,), (1,))) * share
        value, slope = gelu_parts(gate)
        active = value * up
        gate_back = (ag * up * slope).astype(low)
        up_back = (ag * value).astype(low)
        act[q, c] = (active * share).astype(low)
        gb[q, c] = gate_back
        ub[q, c] = up_back
        out = contract(active.astype(low), wd[...], ((1,), (0,)))
        dots = lax.dot_general(jnp.ones((8, width), full), out * g.astype(full), (((1,), (1,)), ((), ())),
                               precision=lax.Precision.HIGHEST, preferred_element_type=full)
        sd[q, c, :, 0:rows] = dots
        weighted = (out * share).astype(low)
        into = contract(gate_back, wg[...], ((1,), (0,))) + contract(up_back, wu[...], ((1,), (0,)))
        for half in range(2):
            po[q, half, c] = weighted[half * cap:(half + 1) * cap]
            pb[q, half, c] = into[half * cap:(half + 1) * cap].astype(low)
        put_out(u, q, c).start()

        for k, (whose, pair) in enumerate(UNITS):
            if whose == 3 and pair:
                @pl.when(u == k)
                def _():
                    start_sums(pair)
            elif pair == 3 and whose:
                @pl.when(u == k)
                def _():
                    give_dots(whose).start()
        return carry

    def give_dots(q):
        return remote(sd.at[q], sd_got.at[q - 1], sd_send.at[q - 1], sd_recv.at[q - 1], around[q - 1])

    def return_dots(place):
        return remote(sd_out.at[place], ret_s.at[e], sr_send.at[place], sr_recv.at[place], (e ^ ORDER[place], s))

    def own_dots():
        return pltpu.make_async_copy(sd_out.at[0], ret_s.at[e], own_sem.at[3])

    sd[...] = jnp.zeros_like(sd)
    lax.fori_loop(0, len(UNITS), unit, 0)
    give_dots(3).start()

    def grads(left, right, dst):
        def part(u):
            q, c = lax.rem(u, 4), u // 4
            return contract(left[q, pl.ds(2 * c, 2)].reshape(2 * rows, wg.shape[0]),
                            right[q, pl.ds(4 * c, 4)].reshape(2 * rows, width), ((0,), (0,)))

        def more(u, carry):
            stage[...] += part(u)
            return carry

        stage[...] = part(0)
        lax.fori_loop(1, 8, more, 0)
        rounded[...] = stage[...].astype(low)
        done = pltpu.make_async_copy(rounded, dst, stage_sem)
        done.start()
        return done

    done = grads(gb, xr, dwg)
    finish(2)
    add_second(3)
    start_sums(0)
    for q in range(1, 4):
        give_dots(q).wait_recv()
    for c in range(4):
        dots = sd[0, c] + sd_got[0, c] + sd_got[1, c] + sd_got[2, c]
        for i in range(2):
            sd_out[2 * c + i] = jnp.zeros((8, 128), full)
            sd_out[2 * c + i, :, 0:cap] = dots[:, i * cap:(i + 1) * cap]
    for place in range(1, 8):
        return_dots(place).start()
    own_dots().start()
    done.wait()
    done = grads(ub, xr, dwu)
    finish(3)
    add_second(0)
    done.wait()
    done = grads(act, gr, dwd)
    finish(0)
    done.wait()

    own_back().wait()
    own_dots().wait()
    for place in range(1, 8):
        back(place).wait()
        return_dots(place).wait()
        share_entry(place).wait_send()
        for kind in range(2 if place >= 4 else 1):
            entry(kind, place).wait_send()
    for which in range(3):
        share_hop(which).wait_send()
        give_dots(1 + which).wait_send()
    for pair in range(4):
        for kind in range(2 if pair >= 2 else 1):
            for which in range(4):
                hop(kind, which, pair).wait_send()
        for half in range(2):
            for which in range(3):
                rs(half, which, pair).wait_send()
    for k, (whose, pair) in enumerate(UNITS):
        put_out(k, whose, pair).wait()


def experts(send_rows, grad_rows, shares, g_early, gate_weight, up_weight, down_weight):
    rows, width = send_rows.shape
    units = gate_weight.shape[0]
    cap = rows // 8
    low, full = jnp.bfloat16, jnp.float32
    hbm = pl.BlockSpec(memory_space=pl.ANY)
    dma = pltpu.SemaphoreType.DMA
    part = (4, 2, 4, cap, width)
    return pl.pallas_call(
        expert_kernel,
        out_shape=(
            jax.ShapeDtypeStruct(part, low),
            jax.ShapeDtypeStruct((rows, width), low),
            jax.ShapeDtypeStruct((8, 8, 128), full),
        ) + (jax.ShapeDtypeStruct((units, width), low),) * 3,
        in_specs=[hbm] * 7,
        out_specs=(hbm,) * 6,
        scratch_shapes=[
            pltpu.VMEM((4, 8, cap, width), low),
            pltpu.VMEM((4, 8, cap, width), low),
            pltpu.VMEM((4, 8, 8, 128), full),
            pltpu.VMEM((4, 4, 2 * cap, units), low),
            pltpu.VMEM((4, 4, 2 * cap, units), low),
            pltpu.VMEM((4, 4, 2 * cap, units), low),
            pltpu.VMEM(part, low),
            pltpu.VMEM(part, low),
            pltpu.VMEM((2, 2, 4, cap, width), low),
            pltpu.VMEM((2, 4, cap, width), low),
            pltpu.VMEM((4, 4, 8, 256), full),
            pltpu.VMEM((3, 4, 8, 256), full),
            pltpu.VMEM((8, 8, 128), full),
            pltpu.VMEM((units, width), full),
            pltpu.VMEM((units, width), low),
            pltpu.VMEM((units, width), low),
            pltpu.VMEM((units, width), low),
            pltpu.VMEM((units, width), low),
            dma((2, 8)), dma((2, 8)),
            dma((2, 4, 4)), dma((2, 4, 4)),
            dma((11,)), dma((11,)),
            dma((2, 3, 4)), dma((2, 3, 4)),
            dma((8,)), dma((8,)),
            dma((3,)), dma((3,)),
            dma((8,)), dma((8,)),
            dma((len(UNITS),)), dma, dma((4,)), dma((4,)),
        ],
        compiler_params=pltpu.CompilerParams(
            collective_id=1, has_side_effects=True, vmem_limit_bytes=VMEM_LIMIT
        ),
        cost_estimate=pl.CostEstimate(flops=2 * 9 * 4 * rows * units * width, bytes_accessed=20 << 20, transcendentals=4 * rows * units),
        name="experts",
    )(send_rows, grad_rows, shares, g_early, gate_weight, up_weight, down_weight)


def segment_scalars(lengths, parents, before_mem, reach_mem):
    count = lengths.shape[1]
    start = jnp.int32(0)
    found = []
    for k in range(count):
        length = lengths[0, k]
        if k == 0:
            before, reach = jnp.int32(0), jnp.int32(1)
        else:
            parent = parents[0, k]
            before = before_mem[parent] + lengths[0, parent]
            reach = reach_mem[parent] | (1 << k)
        before_mem[k] = before
        reach_mem[k] = reach
        found.append((start, before, reach, length))
        start = start + length
    return found


def token_columns(found, ids):
    offset = jnp.zeros(ids.shape, jnp.int32)
    reach = jnp.full(ids.shape, 1, jnp.int32)
    own = jnp.full(ids.shape, 1, jnp.int32)
    for k, (start, before, bits, _) in enumerate(found):
        if k:
            after = ids >= start
            offset = jnp.where(after, before - start, offset)
            reach = jnp.where(after, bits, reach)
            own = jnp.where(after, 1 << k, own)
    return ids + offset, reach, own


LAST = 127


def bias_tables(params, s):
    flat = params[2:3, 0:BUCKETS * HEADS]
    lane = lax.broadcasted_iota(jnp.int32, (8, BUCKETS * HEADS), 1)
    head = lax.broadcasted_iota(jnp.int32, (8, BUCKETS * HEADS), 0)
    heads_here = HEADS // 4
    chosen = jnp.where((lane % HEADS) == s * heads_here + head, jnp.broadcast_to(flat, lane.shape), 0.0)
    entry = lax.broadcasted_iota(jnp.int32, (BUCKETS * HEADS, LAST + 1), 0) // HEADS
    distance = lax.broadcasted_iota(jnp.int32, (BUCKETS * HEADS, LAST + 1), 1)
    hot = jnp.where(entry == bucket_of(distance), 1.0, 0.0)
    table = contract(chosen.astype(jnp.bfloat16), hot.astype(jnp.bfloat16), ((1,), (0,)))
    spot = lax.broadcasted_iota(jnp.int32, table.shape, 1)
    return jnp.where(spot == LAST, NEGATIVE, table)


def pair_index(found, first, rows, count):
    ids = first + lax.broadcasted_iota(jnp.int32, (rows, 1), 0)
    keys = lax.broadcasted_iota(jnp.int32, (1, count), 1)
    place, reach, _ = token_columns(found, ids)
    key_place, _, key_own = token_columns(found, keys)
    seen = ((reach & key_own) != 0) & (keys <= ids)
    return jnp.where(seen, jnp.minimum(place - key_place, LAST - 1), LAST), place, reach


def looked_up(row, index):
    rows, count = index.shape
    table = jnp.broadcast_to(row, (rows, LAST + 1))
    pieces = [
        jnp.take_along_axis(table, index[:, k * 128:(k + 1) * 128], axis=1)
        for k in range(count // 128)
    ]
    return jnp.concatenate(pieces, axis=1)


def slots_of(ids_row, cap):
    rows = ids_row.shape[1]
    full, low = jnp.float32, jnp.bfloat16
    level = lax.broadcasted_iota(jnp.int32, (8, rows), 0)
    hot_row = [jnp.where(ids_row[k:k + 1] == level, 1.0, 0.0).astype(full) for k in range(2)]
    down = lax.broadcasted_iota(jnp.int32, (rows, rows), 0)
    across = lax.broadcasted_iota(jnp.int32, (rows, rows), 1)
    after = jnp.where(down < across, 1.0, 0.0).astype(low)
    earlier = contract((hot_row[0] + hot_row[1]).astype(low), after, ((1,), (0,)))
    slot_row = [jnp.sum(h * earlier, axis=0, keepdims=True) for h in hot_row]
    spot_row = [
        jnp.where(slot_row[k] < cap, ids_row[k:k + 1].astype(full) * cap + slot_row[k], -1.0) for k in range(2)
    ]
    columns = jnp.transpose(jnp.concatenate(spot_row + slot_row + [jnp.zeros((4, rows), full)], axis=0))
    target = [columns[:, k:k + 1].astype(jnp.int32) for k in range(2)]
    slot = [columns[:, 2 + k:3 + k].astype(jnp.int32) for k in range(2)]
    hot = [jnp.transpose(h) for h in hot_row]
    target_row = [spot.astype(jnp.int32) for spot in spot_row]
    return hot_row, hot, slot, target, target_row


def router_of(residual, params, hot):
    low = jnp.bfloat16
    scale = norm_factor(residual)
    unit = residual * scale
    normed = (unit * params[1:2]).astype(low)
    router = params[8:16]
    logits = contract(normed, router.astype(low), ((1,), (1,)))
    expo = jnp.exp(logits - jnp.max(logits, axis=1, keepdims=True))
    prob = expo / jnp.sum(expo, axis=1, keepdims=True)
    chosen = [jnp.sum(h * prob, axis=1, keepdims=True) for h in hot]
    chosen_sum = chosen[0] + chosen[1]
    shares = [c / chosen_sum for c in chosen]
    return scale, unit, normed, router, prob, chosen_sum, shares


def front_kernel(
    lengths, parents, tokens, cotangent, ids_row, wq, wk, wv, wo, gain_one, gain_two, bias, router_row,
    xs, gs_far, shares, residual, all_tokens_far, qkv_far, cols_far, params, att_far, probs_far, wo_far, g_far,
    all_tokens, qkv, cols, wo_full, att, probs, got, part, normed, misc, tags, tag_sum, all_tags, index, table, landed, gs, g_early,
    before_mem, reach_mem,
    t_send, t_recv, w_send, w_recv, m_send, m_recv, c_send, c_recv, n_send, n_recv,
    h_send, h_recv, a_send, a_recv,
    e_send, e_recv, j_send, j_recv, far_sem, save_sem,
):
    e, s = lax.axis_index(EXPERT), lax.axis_index(SEQ)
    near_x, near_y, corner = (e, s ^ 1), (e, s ^ 2), (e, s ^ 3)
    around = (near_x, near_y, corner)
    hops = (1,) + ZHOPS
    low, full = jnp.bfloat16, jnp.float32
    rows, width = tokens.shape
    slim = wq.shape[0]
    shard = width // 4
    weights = (wq, wk, wv)
    place = e * 4 + s

    at_gain = lax.broadcasted_iota(jnp.int32, (slim, width), 1) == place * slim + lax.broadcasted_iota(
        jnp.int32, (slim, width), 0)
    gain_spot = jnp.where(at_gain, 1.0, 0.0).astype(low)
    few = bias.shape[1]
    at_bias = lax.broadcasted_iota(jnp.int32, (few, width), 1) == place * few + lax.broadcasted_iota(
        jnp.int32, (few, width), 0)
    bias_spot = jnp.where(at_bias, 1.0, 0.0).astype(low)
    two_gains = [contract(one[...], gain_spot, ((1,), (0,))) for one in (gain_one, gain_two)]
    one_bias = contract(bias[...], bias_spot, ((1,), (0,)))
    misc[...] = jnp.concatenate(
        two_gains + [one_bias, jnp.zeros((5, width), full), contract(router_row[...], gain_spot, ((1,), (0,)))], axis=0
    ).astype(low)

    greet(list(around) + [(e ^ d, s) for d in (1, 2, 3, 4, 6)])

    def send_tokens(k):
        return remote(tokens, all_tokens.at[aligned(s, rows)], t_send.at[k], t_recv.at[k], around[k])

    def pass_tokens(k):
        piece = pl.ds(pl.multiple_of((s ^ (1 + k)) * rows + k * (rows // 2), rows // 2), rows // 2)
        view = all_tokens.at[piece]
        return remote(view, view, t_send.at[2 + k], t_recv.at[2 + k], around[1 - k])

    def send_cols(k, m):
        return remote(
            weights[m].at[:, aligned(s ^ (k + 1), shard)], got.at[m, aligned(s, slim)],
            w_send.at[k, m], w_recv.at[k, m], around[k],
        )

    def send_tags(k):
        return remote(misc, tags.at[k], m_send.at[k], m_recv.at[k], around[k])

    def share(k, p):
        return remote(part.at[p], cols.at[p, aligned(e, 4 * slim)], c_send.at[p, k], c_recv.at[p, k], (e ^ hops[k], s))

    def share_tags(k):
        return remote(tag_sum, all_tags.at[k], n_send.at[k], n_recv.at[k], (e ^ hops[k], s))

    def relay(k, p):
        view = cols.at[p, aligned(e ^ hops[k], 4 * slim)]
        return remote(view, view, c_send.at[p, 3 + k], c_recv.at[p, 3 + k], (e ^ 1, s))

    def relay_tags(k):
        return remote(all_tags.at[k], all_tags.at[3 + k], n_send.at[3 + k], n_recv.at[3 + k], (e ^ 1, s))

    def early_out(k):
        return remote(wo, wo_full.at[e, s], h_send.at[k], h_recv.at[k], around[k])

    def along_out(k):
        view = wo_full.at[e]
        return remote(view, view, h_send.at[3 + k], h_recv.at[3 + k], (e ^ hops[k], s))

    def relay_along(k):
        view = wo_full.at[e ^ hops[k]]
        return remote(view, view, h_send.at[6 + k], h_recv.at[6 + k], (e ^ 1, s))

    def give(r):
        return remote(att.at[pl.ds(r * rows, rows)], landed.at[s], a_send.at[r], a_recv.at[s ^ r], (e, r))

    cap = xs.shape[0] // 8

    def g_entry(place):
        return remote(gs.at[pl.ds(pl.multiple_of((e ^ ORDER[place]) * cap, 16), cap)], g_early.at[0, place],
                      e_send.at[place], e_recv.at[place], (e ^ ORDER[place], s))

    def g_hop(which, pair):
        places = pl.ds(2 * pair, 2) if which < 2 else pl.ds(2 * pair + which - 2, 1)
        return remote(g_early.at[(0, 0, 1, 2)[which], places], g_early.at[(1, 2, 3, 3)[which], places],
                      j_send.at[which, pair], j_recv.at[which, pair], (near_x, near_y, near_y, near_x)[which])

    def g_corner(pair):
        for which in range(2):
            g_hop(which, pair).wait_recv()
            g_hop(2 + which, pair).start()

    far = []

    def keep(src, dst):
        copy = pltpu.make_async_copy(src, dst, far_sem.at[len(far)])
        copy.start()
        far.append(copy)

    for k in range(3):
        for m in range(3):
            send_cols(k, m).start()
        send_tags(k).start()
    for k in range(2):
        send_tokens(k).start()
    for k in range(3):
        early_out(k).start()
    for m in range(3):
        got[m, aligned(s, slim), :] = weights[m][:, aligned(s, shard)]
    all_tokens[aligned(s, rows), :] = tokens[...]
    wo_full[e, s] = wo[...]
    hot_row, hot, slot, _, target_row = slots_of(ids_row[...], cap)
    level = lax.broadcasted_iota(jnp.int32, (8 * cap, rows), 0)
    takes = jnp.where((level == target_row[0]) | (level == target_row[1]), 1.0, 0.0).astype(low)
    total = misc[...].astype(full)
    for k in range(3):
        send_tags(k).wait_recv()
        total += tags[k].astype(full)
    tag_sum[...] = total.astype(low)
    for k in range(4):
        share_tags(k).start()
    for k in range(3):
        for m in range(3):
            send_cols(k, m).wait_recv()
    for p in range(2):
        for m in range(3):
            part[p, :, m * 128:(m + 1) * 128] = got[m, :, p * 128:(p + 1) * 128]
    for k in (3, 2, 1, 0):
        share(k, 0).start()
    for p in range(2):
        cols[p, aligned(e, 4 * slim), :] = part[p]
    gs[...] = contract(takes, cotangent[...], ((1,), (0,))).astype(low)
    for place in range(1, 4):
        g_entry(place).start()
    g_early[0, 0] = gs[pl.ds(pl.multiple_of(e * cap, 16), cap), :]
    keep(gs, gs_far)
    found = segment_scalars(lengths, parents, before_mem, reach_mem)
    for r in range(4):
        index[r, :, :(r + 1) * rows] = pair_index(found, r * rows, rows, (r + 1) * rows)[0]
    for k in range(1, 4):
        share_tags(k).wait_recv()
        relay_tags(k).start()
    for k in range(2):
        send_tokens(k).wait_recv()
        pass_tokens(k).start()
    g_entry(1).wait_recv()
    for which in range(2):
        g_hop(which, 0).start()
    for k in range(1, 4):
        share(k, 0).wait_recv()
        relay(k, 0).start()
    for k in (3, 2, 1, 0):
        share(k, 1).start()
    for k in range(3):
        early_out(k).wait_recv()
    for k in (3, 2, 1, 0):
        along_out(k).start()
    share_tags(0).wait_recv()
    for k in range(1, 4):
        relay_tags(k).wait_recv()
    for k in range(7):
        total += all_tags[k].astype(full)
    params[...] = total
    gain = total[0:1]
    table[...] = bias_tables(params, s)

    def norm_block(q, carry):
        spot = aligned(s ^ q, rows)
        values = all_tokens[spot, :].astype(full)
        normed[spot, :] = (values * norm_factor(values) * gain).astype(low)
        return carry

    lax.fori_loop(0, 3, norm_block, 0)
    for k in range(2):
        pass_tokens(k).wait_recv()
    lax.fori_loop(3, 4, norm_block, 0)
    keep(all_tokens, all_tokens_far)

    def save_probs(p, r):
        piece = probs.at[pl.ds(2 * p, 2), r, :, pl.ds(0, (r + 1) * rows)]
        return pltpu.make_async_copy(piece, probs_far.at[pl.ds(2 * p, 2), r, :, pl.ds(0, (r + 1) * rows)], save_sem.at[p, r])

    def pair(p, carry):
        for which in range(2):
            @pl.when(p == which)
            def _():
                share(0, which).wait_recv()
                for k in range(1, 4):
                    relay(k, which).wait_recv()

        for r in range(4):
            out = contract(normed[r * rows:(r + 1) * rows, :], cols[p], ((1,), (0,)))
            first_part = out[:, 0:128].astype(low).astype(full) * HDIM ** (-0.5)
            qkv[p, r * rows:(r + 1) * rows, :] = jnp.concatenate([first_part, out[:, 128:]], axis=1).astype(low)

        for r in (3, 2, 1, 0):
            first, count = r * rows, (r + 1) * rows
            q = qkv[p, first:count, 0:128]
            k = qkv[p, 0:count, 128:256]
            v = qkv[p, 0:count, 256:384]
            lane = lax.broadcasted_iota(jnp.int32, (rows, 128), 1)
            results = []
            for side in range(2):
                mine = (lane // HDIM) == side
                scores = contract(jnp.where(mine, q, jnp.zeros_like(q)), k, ((1,), (1,)))
                scores = scores + looked_up(table[pl.ds(2 * p + side, 1), :], index[r, :, :count])
                expo = jnp.exp(scores - jnp.max(scores, axis=1, keepdims=True))
                soft = (expo * (1.0 / jnp.sum(expo, axis=1, keepdims=True))).astype(low)
                probs[2 * p + side, r, :, :count] = soft
                results.append(contract(soft, v, ((1,), (0,))))
            att[first:count, aligned(p, 128)] = jnp.where((lane // HDIM) == 0, results[0], results[1]).astype(low)

            save_probs(p, r).start()

            @pl.when((p == 1) & (s != r))
            def _():
                give(r).start()

            if r == 2:
                @pl.when(p == 0)
                def _():
                    for i in (2, 3):
                        g_entry(i).wait_recv()
                    for which in range(2):
                        g_hop(which, 1).start()
            if r == 1:
                @pl.when(p == 0)
                def _():
                    g_corner(0)
                    for i in range(1, 4):
                        share(i, 1).wait_recv()
                        relay(i, 1).start()

                @pl.when(p == 1)
                def _():
                    for i in range(1, 4):
                        along_out(i).wait_recv()
                        relay_along(i).start()
            if r == 0:
                @pl.when(p == 1)
                def _():
                    g_corner(1)
        return carry

    lax.fori_loop(0, 2, pair, 0)
    keep(qkv, qkv_far)
    keep(cols, cols_far)
    along_out(0).wait_recv()
    for k in range(1, 4):
        relay_along(k).wait_recv()
    keep(wo_full, wo_far)
    landed[s] = att[aligned(s, rows), :]
    total = tokens[...].astype(full)

    def out_rows(index):
        return wo_full[pl.ds(2 * index, 2)].reshape(shard, width)

    total += contract(landed[s], out_rows(s), ((1,), (0,)))
    for k in range(1, 4):
        remote(landed.at[s], landed.at[s ^ k], a_send.at[0], a_recv.at[k], (e, s ^ k)).wait_recv()
        total += contract(landed[s ^ k], out_rows(s ^ k), ((1,), (0,)))
    residual[...] = total
    keep(landed, att_far)
    _, _, normed, _, _, _, given = router_of(total, params[...], hot)
    xs[...] = contract(takes, normed, ((1,), (0,))).astype(low)
    at_slot = lax.broadcasted_iota(jnp.int32, (rows, 128), 1)
    by_slot = jnp.zeros((8, 128), full)
    for k in range(2):
        placed = jnp.where((at_slot == slot[k]) & (slot[k] < cap), given[k], 0.0)
        by_slot += lax.dot_general(hot_row[k], placed, (((1,), (0,)), ((), ())),
                                   precision=lax.Precision.HIGHEST, preferred_element_type=full)
    shares[...] = jnp.zeros_like(shares)
    for k in range(8):
        shares[k, 0:1, :] = by_slot[k:k + 1]
    for pair in range(2):
        for which in range(2):
            g_hop(2 + which, pair).wait_recv()
    keep(g_early, g_far)

    for place in range(1, 4):
        g_entry(place).wait_send()
    for pair in range(2):
        for which in range(4):
            g_hop(which, pair).wait_send()
    for k in range(2):
        send_tokens(k).wait_send()
        pass_tokens(k).wait_send()
    for k in range(3):
        for m in range(3):
            send_cols(k, m).wait_send()
        send_tags(k).wait_send()
        early_out(k).wait_send()
    for k in range(4):
        share_tags(k).wait_send()
        along_out(k).wait_send()
        for p in range(2):
            share(k, p).wait_send()
    for k in range(1, 4):
        relay_tags(k).wait_send()
        relay_along(k).wait_send()
        for p in range(2):
            relay(k, p).wait_send()
    for r in range(4):
        @pl.when(s != r)
        def _():
            give(r).wait_send()
    for copy in far:
        copy.wait()
    for p in range(2):
        for r in range(4):
            save_probs(p, r).wait()


def front(lengths, parents, tokens, cotangent, ids_row, wq, wk, wv, wo, gain_one, gain_two, bias, router_row):
    rows, width = tokens.shape
    slim, shard = wq.shape[0], width // 4
    cap = 10 * rows // 32
    low, full = jnp.bfloat16, jnp.float32
    vmem, smem, hbm = (pl.BlockSpec(memory_space=m) for m in (pltpu.VMEM, pltpu.SMEM, pl.ANY))
    dma = pltpu.SemaphoreType.DMA
    kept = (
        jax.ShapeDtypeStruct((4 * rows, width), low),
        jax.ShapeDtypeStruct((2, 4 * rows, 3 * shard // 2), low),
        jax.ShapeDtypeStruct((2, width, 3 * shard // 2), low),
        jax.ShapeDtypeStruct((16, width), full),
        jax.ShapeDtypeStruct((4, rows, shard), low),
        jax.ShapeDtypeStruct((4, 4, rows, 4 * rows), low),
        jax.ShapeDtypeStruct((8, 4, slim, width), low),
    )
    return pl.pallas_call(
        front_kernel,
        out_shape=(
            jax.ShapeDtypeStruct((8 * cap, width), low),
            jax.ShapeDtypeStruct((8 * cap, width), low),
            jax.ShapeDtypeStruct((8, 8, 128), full),
            jax.ShapeDtypeStruct((rows, width), full),
        ) + kept + (jax.ShapeDtypeStruct((4, 4, cap, width), low),),
        in_specs=[smem, smem] + [vmem] * 11,
        out_specs=(vmem, hbm, vmem, vmem, hbm, hbm, hbm, vmem, hbm, hbm, hbm, hbm),
        scratch_shapes=[
            pltpu.VMEM(kept[0].shape, low), pltpu.VMEM(kept[1].shape, low), pltpu.VMEM(kept[2].shape, low),
            pltpu.VMEM(kept[6].shape, low), pltpu.VMEM((4 * rows, shard), low), pltpu.VMEM(kept[5].shape, low),
            pltpu.VMEM((3, 4 * slim, shard), low), pltpu.VMEM((2, 4 * slim, 3 * shard // 2), low),
            pltpu.VMEM((4 * rows, width), low),
            pltpu.VMEM((16, width), low), pltpu.VMEM((3, 16, width), low), pltpu.VMEM((16, width), low),
            pltpu.VMEM((7, 16, width), low),
            pltpu.VMEM((4, rows, 4 * rows), jnp.int32), pltpu.VMEM((8, 128), full),
            pltpu.VMEM((4, rows, shard), low),
            pltpu.VMEM((8 * cap, width), low), pltpu.VMEM((4, 4, cap, width), low),
            pltpu.SMEM((16,), jnp.int32), pltpu.SMEM((16,), jnp.int32),
            dma((4,)), dma((4,)), dma((3, 3)), dma((3, 3)), dma((3,)), dma((3,)),
            dma((2, 7)), dma((2, 7)), dma((7,)), dma((7,)),
            dma((10,)), dma((10,)), dma((4,)), dma((4,)),
            dma((4,)), dma((4,)), dma((4, 2)), dma((4, 2)), dma((8,)), dma((2, 4)),
        ],
        compiler_params=pltpu.CompilerParams(
            collective_id=2, has_side_effects=True, vmem_limit_bytes=VMEM_LIMIT
        ),
        cost_estimate=pl.CostEstimate(flops=40 * rows * width * shard, bytes_accessed=24 << 20, transcendentals=8 * rows * rows * 16),
        name="front",
    )(lengths, parents, tokens, cotangent, ids_row, wq, wk, wv, wo, gain_one, gain_two, bias, router_row)


def near_keys(found, first, rows):
    ids = first + lax.broadcasted_iota(jnp.int32, (rows, 1), 0)
    place, reach, _ = token_columns(found, ids)
    step = lax.broadcasted_iota(jnp.int32, (rows, LAST + 1), 1)
    wanted = place - step
    spot = jnp.full((rows, LAST + 1), -1, jnp.int32)
    for k, (start, before, _, length) in enumerate(found):
        inside = ((reach & (1 << k)) != 0) & (wanted >= before) & (wanted < before + length)
        spot = jnp.where(inside, wanted + (start - before), spot)
    return jnp.where(step == LAST, -1, spot)


GROUPS = ((0, 3), (3, 3))


def back_kernel(
    lengths, parents, ids_row, params, ret_s, po_far, ret_b_far, residual_far, cotangent_far,
    wo_far, qkv_far, cols_far, all_tokens_far, att_far, probs_far,
    layer_out_far, tokens_grad, dwq, dwk, dwv, dwo, small_sum,
    po0, po2, ro, ro2, ret_o, ret_b, residual, cotangent, layer_out, wo, qkv, cols, all_tokens, att, probs, datt, datt_own, aog_own, residual_grad,
    takes, o_halves, o_core, o_sums, o_z, o_final, o_seq, spots, near, dk, dv, dqkv, normed,
    halves, core_got, sums, z_got, final, final_got, parts, first_got, second_got, mine, tally, tally_got, square, square_got,
    before_mem, reach_mem,
    load_sem, d_send, d_recv, w_send, w_recv, core_send, core_recv, z_send, z_recv, a_send, a_recv,
    n_send, n_recv, m_send, m_recv, o_send, o_recv, r_send, r_recv, q_send, q_recv, own_sem, probs_sem,
):
    e, s = lax.axis_index(EXPERT), lax.axis_index(SEQ)
    z, c = e // 2, lax.rem(e, 2)
    near_x, near_y = (e, s ^ 1), (e, s ^ 2)
    around = [(e, s ^ k) for k in range(1, 4)]
    hops = (1,) + ZHOPS
    full, low = jnp.float32, jnp.bfloat16
    high = lax.Precision.HIGHEST
    rows, width = residual.shape
    shard = att.shape[2]
    slim = dwq.shape[0]
    cap = ret_b.shape[0] // 8
    half = shard // 2
    pairs = (
        (residual_far, residual), (cotangent_far, cotangent), (ret_b_far, ret_b), (wo_far, wo), (po_far.at[0], po0),
        (att_far, att), (qkv_far, qkv), (all_tokens_far, all_tokens), (cols_far, cols),
        (po_far.at[2, 0], po2.at[0]), (po_far.at[1, 1], po2.at[1]),
    )
    loads = [pltpu.make_async_copy(src, dst, load_sem.at[k]) for k, (src, dst) in enumerate(pairs)]
    for load in loads[:4]:
        load.start()
    peers = around + [(e ^ d, s) for d in range(1, 8)]
    announce(peers)
    early_probs = [
        pltpu.make_async_copy(probs_far.at[:, r, :, pl.ds(0, (r + 1) * rows)], probs.at[:, r, :, pl.ds(0, (r + 1) * rows)],
                              probs_sem.at[r])
        for r in range(4)
    ]
    _, hot, slot, target, _ = slots_of(ids_row[...], cap)
    place = lax.broadcasted_iota(jnp.int32, (rows, 8 * cap), 1)
    takes[...] = jnp.where((place == target[0]) | (place == target[1]), 1.0, 0.0).astype(low)
    pl.semaphore_wait(pltpu.get_barrier_semaphore(), len(peers))

    def o_copy(side, which, zone):
        first, second = ((near_x, near_y), (near_y, near_x))[side]
        two = pl.ds(2 * zone, 2)
        if which == 2:
            src, dst = po2.at[side, two], ro2.at[side, two]
        else:
            src, dst = po_far.at[(1 + side, 3)[which], side, two], ro.at[which, side, two]
        return remote(src, dst, o_send.at[side, which, zone], o_recv.at[side, which, zone], second if which == 2 else first)

    def block(index):
        return pl.ds(pl.multiple_of(index * cap, 16), cap)

    def return_rows(place):
        return remote(po0.at[place % 2, place // 2], ret_o.at[block(e)], r_send.at[place], r_recv.at[place],
                      (e ^ ORDER[place], s))

    def start_outs(zone, which):
        for side in range(2):
            o_copy(side, which, zone).start()

    def add_outs(zone):
        for side in range(2):
            o_copy(side, 1, zone).wait_recv()
            for i in (2 * zone, 2 * zone + 1):
                po2[side, i] = (po2[side, i].astype(full) + ro[1, side, i].astype(full)).astype(low)
            o_copy(side, 2, zone).start()

    def finish_outs(zone):
        for side in range(2):
            o_copy(side, 0, zone).wait_recv()
            o_copy(side, 2, zone).wait_recv()
            for i in (2 * zone, 2 * zone + 1):
                po0[side, i] = (
                    po0[side, i].astype(full) + ro[0, side, i].astype(full) + ro2[side, i].astype(full)
                ).astype(low)
                if 2 * i + side:
                    return_rows(2 * i + side).start()
                else:
                    ret_o[block(e), :] = po0[0, 0]

    start_outs(1, 1)
    loads[0].wait()

    held = residual[...]
    scale, unit, unrouted, router, prob, chosen_sum, shares = router_of(held, params[...], hot)
    at_slot = lax.broadcasted_iota(jnp.int32, (rows, 128), 1)
    dots = jnp.concatenate([ret_s[k, 0:1, :] for k in range(8)], axis=0)
    share_grad = []
    for k in range(2):
        mine_dots = lax.dot_general(hot[k], dots, (((1,), (0,)), ((), ())), precision=high, preferred_element_type=full)
        share_grad.append(jnp.sum(
            jnp.where((at_slot == slot[k]) & (slot[k] < cap), mine_dots, 0.0), axis=1, keepdims=True))
    for load in loads[1:4]:
        load.wait()
    for load in loads[4:] + early_probs:
        load.start()
    grad = cotangent[...].astype(full)
    inner = shares[0] * share_grad[0] + shares[1] * share_grad[1]
    prob_grad = sum(hot[k] * ((share_grad[k] - inner) / chosen_sum) for k in range(2))
    logit_grad = prob * (prob_grad - jnp.sum(prob * prob_grad, axis=1, keepdims=True))
    normed_grad = contract(takes[...], ret_b[...], ((1,), (0,))) + lax.dot_general(
        logit_grad, router, (((1,), (0,)), ((), ())), precision=high, preferred_element_type=full
    )
    unit_grad = normed_grad * params[1:2]
    passed = grad + scale * (unit_grad - unit * jnp.mean(unit_grad * unit, axis=1, keepdims=True))
    residual_grad[...] = passed
    aog_own[...] = passed.astype(low)
    datt_own[...] = contract(aog_own[...], wo[...], ((1,), (1,))).astype(low)

    def give(k):
        return remote(datt_own.at[:, aligned(s ^ (k + 1), shard)], datt.at[aligned(s, rows)],
                      d_send.at[k], d_recv.at[k], around[k])

    for k in (2, 0, 1):
        give(k).start()

    def wide_core():
        return remote(o_halves.at[1 - c], o_core, w_send.at[0], w_recv.at[0], (e ^ 1, s))

    def wide_z(k):
        return remote(o_sums.at[z ^ (1, 3, 2)[k - 1]], o_z.at[k - 1], w_send.at[k], w_recv.at[k],
                      (e ^ (2, 2, 4)[k - 1], s))

    def wide_on():
        wide_z(2).wait_recv()
        o_sums[z ^ 2] = (o_sums[z ^ 2].astype(full) + o_z[1].astype(full)).astype(low)
        wide_z(3).start()

    def wide_seq(k):
        return remote(o_final.at[aligned(s ^ (k + 1), slim)], o_seq.at[k], w_send.at[4 + k], w_recv.at[4 + k], around[k])

    for load in loads[4:]:
        load.wait()

    def output_zone(j, carry):
        part = contract(att[j], aog_own[...], ((0,), (0,)))
        for i in range(2):
            o_halves[i, j] = part[i * half:(i + 1) * half].astype(low)
        return carry

    lax.fori_loop(0, 4, output_zone, 0)
    wide_core().start()
    datt[aligned(s, rows), :] = datt_own[:, aligned(s, shard)]
    tally[0] = jnp.zeros((16, width), full)
    tally[0, 1:2] = jnp.sum(normed_grad * unit, axis=0, keepdims=True)
    lane = lax.broadcasted_iota(jnp.int32, (1, width), 1)
    tally[0, 3:4] = jnp.where(lane == 0, jnp.sum(held * held), 0.0)
    tally[0, 8:16] = lax.dot_general(logit_grad, unrouted.astype(full), (((0,), (0,)), ((), ())),
                                     precision=high, preferred_element_type=full)
    wide_core().wait_recv()
    for j in range(4):
        o_sums[j] = (o_halves[c, j].astype(full) + o_core[j].astype(full)).astype(low)
    for k in (2, 1):
        wide_z(k).start()
    found = segment_scalars(lengths, parents, before_mem, reach_mem)
    near[...] = jnp.zeros_like(near)
    for r in range(4):
        spots[r] = near_keys(found, r * rows, rows)
    gain = params[0:1]

    def units(q):
        values = all_tokens[aligned(s ^ q, rows), :].astype(full)
        factor = norm_factor(values)
        return values * factor, factor

    def norm_block(q, carry):
        normed[aligned(s ^ q, rows), :] = (units(q)[0] * gain).astype(low)
        return carry

    lax.fori_loop(0, 4, norm_block, 0)

    def core_copy(g):
        slots = pl.ds(*GROUPS[g])
        return remote(halves.at[1 - c, slots], core_got.at[slots], core_send.at[g], core_recv.at[g], (e ^ 1, s))

    def z_copy(g, k):
        slots = pl.ds(*GROUPS[g])
        return remote(sums.at[slots, z ^ k], z_got.at[k - 1, slots], z_send.at[g, k - 1], z_recv.at[g, k - 1],
                      (e ^ (2 * k), s))

    def a_copy(g, k):
        slots = pl.ds(*GROUPS[g])
        return remote(final.at[slots, aligned(s ^ (k + 1), slim)], final_got.at[s, slots],
                      a_send.at[g, k], a_recv.at[g, k], around[k])

    def add_core(g):
        core_copy(g).wait_recv()
        first, amount = GROUPS[g]
        for slot in range(first, first + amount):
            for j in range(4):
                sums[slot, j] = (halves[c, slot, j].astype(full) + core_got[slot, j].astype(full)).astype(low)
        for k in range(1, 4):
            z_copy(g, k).start()

    def finish_grad(g):
        first, amount = GROUPS[g]
        for k in range(1, 4):
            z_copy(g, k).wait_recv()
        for slot in range(first, first + amount):
            block = sums[slot, z].astype(full)
            for k in range(1, 4):
                block += z_got[k - 1, slot].astype(full)
            final[slot] = block
        for k in range(3):
            a_copy(g, k).start()
        for slot in range(first, first + amount):
            final_got[s, slot] = final[slot, aligned(s, slim)]

    for load in early_probs:
        load.wait()
    for k in range(3):
        give(k).wait_recv()
    add_outs(1)
    start_outs(1, 0)

    def pair(p, carry):
        lanes = aligned(p, 128)
        dk[...] = jnp.zeros_like(dk)
        dv[...] = jnp.zeros_like(dv)
        for r in (3, 2, 1, 0):
            first, count = r * rows, (r + 1) * rows
            q = qkv[p, first:count, 0:128]
            k = qkv[p, 0:count, 128:256]
            v = qkv[p, 0:count, 256:384]
            g = datt[first:count, lanes]
            lane = lax.broadcasted_iota(jnp.int32, (rows, 128), 1)
            lane_long = lax.broadcasted_iota(jnp.int32, (count, 128), 1)
            spot = spots[r]
            spot_lane, spot_block = spot & 127, jnp.where(spot < 0, -1, spot >> 7)
            dq = []
            key_sum, value_sum = 0.0, 0.0
            for side in range(2):
                mine_lanes = (lane // HDIM) == side
                q_side = jnp.where(mine_lanes, q, jnp.zeros_like(q))
                g_side = jnp.where(mine_lanes, g, jnp.zeros_like(g))
                soft = probs[2 * p + side, r, :, :count]
                wide_soft = soft.astype(full)
                dprob = contract(g_side, v, ((1,), (1,)))
                delta = jnp.sum(wide_soft * dprob, axis=1, keepdims=True)
                wide = wide_soft * (dprob - delta)
                score_grad = wide.astype(low)
                key_sum = key_sum + contract(score_grad, q_side, ((0,), (0,)))
                value_sum = value_sum + contract(soft, g_side, ((0,), (0,)))
                with_ones = jnp.where((lane_long // HDIM) == side, k, jnp.ones_like(k))
                part = contract(score_grad, with_ones, ((1,), (0,)))
                dq.append(part)
                close = jnp.zeros((rows, 128), full)
                for b in range(count // 128):
                    taken = jnp.take_along_axis(wide[:, b * 128:(b + 1) * 128], spot_lane, axis=1)
                    close = jnp.where(spot_block == b, taken, close)
                near[0, 2 * p + side] += jnp.sum(close.reshape(rows // 8, 8, 128), axis=0)
                rest = jnp.where(mine_lanes, 0.0, part)
                near[1, 2 * p + side] += jnp.sum(rest.reshape(rows // 8, 8, 128), axis=0)
            dqkv[p, first:count, 0:128] = (jnp.where((lane // HDIM) == 0, dq[0], dq[1]) * HDIM ** (-0.5)).astype(low)
            dk[0:count] += key_sum
            dv[0:count] += value_sum

            if r == 3:
                @pl.when(p == 0)
                def _():
                    start_outs(0, 1)
                    start_outs(0, 0)
                    wide_on()

                @pl.when(p == 1)
                def _():
                    add_core(0)
            if r == 2:
                @pl.when(p == 0)
                def _():
                    finish_outs(1)
            if r == 1:
                @pl.when(p == 1)
                def _():
                    add_outs(0)
        dqkv[p, :, 128:256] = dk[...].astype(low)
        dqkv[p, :, 256:384] = dv[...].astype(low)

        def qkv_zone(j, carry):
            block = contract(normed[:, aligned(j, shard)], dqkv[p], ((0,), (0,)))
            for m in range(3):
                for i in range(2):
                    halves[i, 3 * p + m, j] = block[i * half:(i + 1) * half, m * 128:(m + 1) * 128].astype(low)
            return carry

        lax.fori_loop(0, 4, qkv_zone, 0)

        @pl.when(p == 0)
        def _():
            core_copy(0).start()

        @pl.when(p == 1)
        def _():
            core_copy(1).start()
        return carry

    lax.fori_loop(0, 2, pair, 0)

    def n_copy(kind, which):
        one, two = ((near_x, near_y), (near_y, near_x))[kind]
        if which < 2:
            src = parts.at[(1 + kind, 3)[which], kind]
            return remote(src, first_got.at[kind, which], n_send.at[kind, which], n_recv.at[kind, which], one)
        return remote(parts.at[2 - kind, kind], second_got.at[kind], n_send.at[kind, 2], n_recv.at[kind, 2], two)

    def back_block(i, carry):
        q = 3 - i
        total = jnp.zeros((rows, width), full)
        for p in range(2):
            total += contract(dqkv[p, aligned(s ^ q, rows), :], cols[p], ((1,), (1,)))
        tally[0, 0:1] += jnp.sum(total * units(q)[0], axis=0, keepdims=True)
        mine[...] = total
        for kind in range(2):
            parts[q, kind] = total[:, kind * (width // 2):(kind + 1) * (width // 2)].astype(low)

        @pl.when(i == 0)
        def _():
            n_copy(0, 1).start()
            n_copy(1, 1).start()
            add_core(1)

        @pl.when(i == 1)
        def _():
            n_copy(1, 0).start()

        @pl.when(i == 2)
        def _():
            n_copy(0, 0).start()
        return carry

    lax.fori_loop(0, 4, back_block, 0)
    finish_outs(0)
    wide_z(1).wait_recv()
    wide_z(3).wait_recv()
    whole = o_sums[z].astype(full) + o_z[0].astype(full) + o_z[2].astype(full)
    o_final[...] = whole.astype(low)
    for k in range(3):
        wide_seq(k).start()

    close, rest = (
        jnp.concatenate([jnp.sum(near[kind, h], axis=0, keepdims=True) for h in range(8)], axis=0) for kind in range(2)
    )
    far = jnp.sum(rest, axis=1, keepdims=True) / HDIM - jnp.sum(close, axis=1, keepdims=True)
    spot = lax.broadcasted_iota(jnp.int32, close.shape, 1)
    by_distance = jnp.where(spot == LAST, far, close)
    lane = lax.broadcasted_iota(jnp.int32, (128, BUCKETS * HEADS), 1)
    distance = lax.broadcasted_iota(jnp.int32, (128, BUCKETS * HEADS), 0)
    hot_bucket = jnp.where((lane // HEADS) == bucket_of(distance), 1.0, 0.0)
    spread = lax.dot_general(by_distance, hot_bucket, (((1,), (0,)), ((), ())), precision=high, preferred_element_type=full)
    head = lax.broadcasted_iota(jnp.int32, spread.shape, 0)
    lane = lax.broadcasted_iota(jnp.int32, spread.shape, 1)
    here = ((lane % HEADS) == s * (HEADS // 4) + head) & (head < HEADS // 4)
    tally[0, 2:3, 0:BUCKETS * HEADS] = jnp.sum(jnp.where(here, spread, 0.0), axis=0, keepdims=True)

    def m_copy(stage, k):
        slot = (0, 3, 4)[stage] + k
        peer = (around[k], (e ^ 1, s), (e ^ (2 * (k + 1)), s))[stage]
        return remote(tally.at[stage], tally_got.at[slot], m_send.at[slot], m_recv.at[slot], peer)

    for k in range(3):
        m_copy(0, k).start()
    for kind in range(2):
        n_copy(kind, 1).wait_recv()
        group = 2 - kind
        parts[group, kind] = (parts[group, kind].astype(full) + first_got[kind, 1].astype(full)).astype(low)
        n_copy(kind, 2).start()
    finish_grad(0)
    total = tally[0]
    for k in range(3):
        m_copy(0, k).wait_recv()
        total += tally_got[k]
    tally[1] = total
    m_copy(1, 0).start()

    for place in range(1, 8):
        return_rows(place).wait_recv()
    mixture = contract(takes[...], ret_o[...], ((1,), (0,)))
    layer_out[...] = (residual[...] + mixture).astype(low)
    layer_done = pltpu.make_async_copy(layer_out, layer_out_far, own_sem)
    layer_done.start()
    squares = jnp.full((8, 128), jnp.sum(mixture * mixture), full)

    def q_copy(stage, k):
        slot = (0, 3, 4)[stage] + k
        peer = (around[k], (e ^ 1, s), (e ^ (2 * (k + 1)), s))[stage]
        return remote(square.at[stage], square_got.at[slot], q_send.at[slot], q_recv.at[slot], peer)

    square[0] = squares
    for k in range(3):
        q_copy(0, k).start()
    finish_grad(1)
    m_copy(1, 0).wait_recv()
    total = total + tally_got[3]
    tally[2] = total
    for k in range(3):
        m_copy(2, k).start()
    for k in range(3):
        q_copy(0, k).wait_recv()
        squares += square_got[k]
    square[1] = squares
    q_copy(1, 0).start()
    for kind in range(2):
        n_copy(kind, 0).wait_recv()
        n_copy(kind, 2).wait_recv()
        lanes = slice(kind * (width // 2), (kind + 1) * (width // 2))
        mine[:, lanes] += first_got[kind, 0].astype(full) + second_got[kind].astype(full)
    unit, scale = units(0)
    unit_grad = mine[...] * gain
    tokens_grad[...] = residual_grad[...] + scale * (
        unit_grad - unit * jnp.mean(unit_grad * unit, axis=1, keepdims=True)
    )
    q_copy(1, 0).wait_recv()
    squares += square_got[3]
    square[2] = squares
    for k in range(3):
        q_copy(2, k).start()
    for g in range(2):
        for k in range(3):
            a_copy(g, k).wait_recv()
    for m, out in enumerate((dwq, dwk, dwv)):
        for i in range(2):
            for j in range(4):
                out[:, j * shard + i * 128:j * shard + (i + 1) * 128] = final_got[j, m + 3 * i]
    whole = o_final[aligned(s, slim), :].astype(full)
    for k in range(3):
        wide_seq(k).wait_recv()
        whole += o_seq[k].astype(full)
    dwo[...] = whole
    for k in range(3):
        m_copy(2, k).wait_recv()
        total += tally_got[4 + k]
    for k in range(3):
        q_copy(2, k).wait_recv()
        squares += square_got[4 + k]
    lane = lax.broadcasted_iota(jnp.int32, (1, 128), 1)
    small_sum[...] = total
    small_sum[3:4, 0:128] = jnp.where(lane == 1, squares[0:1], total[3:4, 0:128])
    layer_done.wait()
    wide_core().wait_send()
    for k in range(3):
        give(k).wait_send()
        wide_z(k + 1).wait_send()
        wide_seq(k).wait_send()
        for g in range(2):
            z_copy(g, k + 1).wait_send()
            a_copy(g, k).wait_send()
    for g in range(2):
        core_copy(g).wait_send()
    for kind in range(2):
        for which in range(3):
            n_copy(kind, which).wait_send()
    for stage, amount in ((0, 3), (1, 1), (2, 3)):
        for k in range(amount):
            m_copy(stage, k).wait_send()
            q_copy(stage, k).wait_send()
    for place in range(1, 8):
        return_rows(place).wait_send()
    for side in range(2):
        for which in range(3):
            for zone in range(2):
                o_copy(side, which, zone).wait_send()


def back(lengths, parents, ids_row, params, ret_s, part_o, ret_b, residual, cotangent, wo, qkv, cols, all_tokens, att, probs):
    rows, width = residual.shape
    shard = att.shape[2]
    slim = width // 32
    low, full = jnp.bfloat16, jnp.float32
    vmem, smem, hbm = (pl.BlockSpec(memory_space=m) for m in (pltpu.VMEM, pltpu.SMEM, pl.ANY))
    dma = pltpu.SemaphoreType.DMA
    half = shard // 2
    return pl.pallas_call(
        back_kernel,
        out_shape=(
            jax.ShapeDtypeStruct((rows, width), low),
            jax.ShapeDtypeStruct((rows, width), full),
        ) + (jax.ShapeDtypeStruct((slim, width), full),) * 4 + (jax.ShapeDtypeStruct((16, width), full),),
        in_specs=[smem, smem] + [vmem] * 3 + [hbm] * 10,
        out_specs=(hbm,) + (vmem,) * 6,
        scratch_shapes=[
            pltpu.VMEM(part_o.shape[1:], low), pltpu.VMEM(part_o.shape[1:], low), pltpu.VMEM((2,) + part_o.shape[1:], low),
            pltpu.VMEM(part_o.shape[1:], low),
            pltpu.VMEM(ret_b.shape, low), pltpu.VMEM(ret_b.shape, low), pltpu.VMEM((rows, width), full),
            pltpu.VMEM((rows, width), low), pltpu.VMEM((rows, width), low),
            pltpu.VMEM((width, width), low), pltpu.VMEM(qkv.shape, low), pltpu.VMEM(cols.shape, low),
            pltpu.VMEM(all_tokens.shape, low), pltpu.VMEM(att.shape, low), pltpu.VMEM(probs.shape, low),
            pltpu.VMEM((4 * rows, shard), low), pltpu.VMEM((rows, width), low),
            pltpu.VMEM((rows, width), low), pltpu.VMEM((rows, width), full),
            pltpu.VMEM((rows, ret_b.shape[0]), low),
            pltpu.VMEM((2, 4, half, width), low), pltpu.VMEM((4, half, width), low),
            pltpu.VMEM((4, half, width), low), pltpu.VMEM((3, half, width), low),
            pltpu.VMEM((half, width), low), pltpu.VMEM((3, slim, width), low),
            pltpu.VMEM((4, rows, 128), jnp.int32), pltpu.VMEM((2, 8, 8, 128), full),
            pltpu.VMEM((4 * rows, 128), full), pltpu.VMEM((4 * rows, 128), full),
            pltpu.VMEM((2, 4 * rows, 3 * shard // 2), low), pltpu.VMEM((4 * rows, width), low),
            pltpu.VMEM((2, 6, 4, half, half), low), pltpu.VMEM((6, 4, half, half), low),
            pltpu.VMEM((6, 4, half, half), low), pltpu.VMEM((3, 6, half, half), low),
            pltpu.VMEM((6, half, half), full), pltpu.VMEM((4, 6, slim, half), full),
            pltpu.VMEM((4, 2, rows, width // 2), low), pltpu.VMEM((2, 2, rows, width // 2), low),
            pltpu.VMEM((2, rows, width // 2), low), pltpu.VMEM((rows, width), full),
            pltpu.VMEM((3, 16, width), full), pltpu.VMEM((7, 16, width), full),
            pltpu.VMEM((3, 8, 128), full), pltpu.VMEM((7, 8, 128), full),
            pltpu.SMEM((16,), jnp.int32), pltpu.SMEM((16,), jnp.int32),
            dma((12,)), dma((3,)), dma((3,)), dma((7,)), dma((7,)), dma((2,)), dma((2,)),
            dma((2, 3)), dma((2, 3)), dma((2, 3)), dma((2, 3)), dma((2, 3)), dma((2, 3)), dma((7,)), dma((7,)),
            dma((2, 3, 2)), dma((2, 3, 2)), dma((8,)), dma((8,)), dma((7,)), dma((7,)), dma, dma((4,)),
        ],
        compiler_params=pltpu.CompilerParams(
            collective_id=5, has_side_effects=True, vmem_limit_bytes=VMEM_LIMIT
        ),
        cost_estimate=pl.CostEstimate(flops=120 * rows * width * shard, bytes_accessed=20 << 20, transcendentals=8 * rows * rows * 16),
        name="back",
    )(lengths, parents, ids_row, params, ret_s, part_o, ret_b, residual, cotangent, wo, qkv, cols, all_tokens, att, probs)


def emit_kernel(*refs):
    large, small = refs[:9], refs[9]
    out, (gain_one, gain_two, bias, router, roots) = refs[10:19], refs[19:24]
    held, wide, in_sem, out_sem = refs[24:33], refs[33:36], refs[36], refs[37]
    comes, goes = [], []
    for k, (src, mid, dst) in enumerate(zip(large, held, out)):
        pieces = 4 if k >= 6 else 1
        amount = src.shape[0] // pieces
        for i in range(pieces):
            part = pl.ds(i * amount, amount)
            comes.append(pltpu.make_async_copy(src.at[part], mid.at[part], in_sem.at[len(comes)]))
            last = wide[k - 6] if k >= 6 else mid
            goes.append(pltpu.make_async_copy(last.at[part], dst.at[part], out_sem.at[len(goes)]))
    order = list(range(6, 18)) + list(range(6))
    for k in order:
        comes[k].start()
    place = lax.axis_index(EXPERT) * 4 + lax.axis_index(SEQ)
    width = small.shape[1]

    def own(length):
        lane = lax.broadcasted_iota(jnp.int32, (length, width), 1)
        down = lax.broadcasted_iota(jnp.int32, (length, width), 0)
        return jnp.where(lane == place * length + down, 1.0, 0.0)

    def picked(left, right):
        return lax.dot_general(left, right, (((1,), (1,)), ((), ())),
                               precision=lax.Precision.HIGHEST, preferred_element_type=jnp.float32)

    for k in order:
        comes[k].wait()
        if k >= 6:
            which, i = (k - 6) // 4, (k - 6) % 4
            amount = held[6].shape[0] // 4
            part = slice(i * amount, (i + 1) * amount)
            wide[which][part] = held[6 + which][part].astype(jnp.float32)
        goes[k].start()
    slim = gain_one.shape[1]
    ours = own(slim)
    gains = picked(small[0:8], ours)
    gain_one[...] = gains[0:1]
    gain_two[...] = gains[1:2]
    bias[...] = picked(small[0:8], own(bias.shape[1]))[2:3]
    router[...] = picked(small[8:16], ours)
    roots[...] = jnp.sqrt(small[3:4, 0:2] / (32 * large[0].shape[0] * width))
    for copy in goes:
        copy.wait()


def emit(large, small):
    full = jnp.float32
    width = small.shape[1]
    vmem, hbm = pl.BlockSpec(memory_space=pltpu.VMEM), pl.BlockSpec(memory_space=pl.ANY)
    slim = width // 32
    shapes = ((1, slim), (1, slim), (1, BUCKETS * HEADS // 32), (8, slim), (1, 2))
    return pl.pallas_call(
        emit_kernel,
        out_shape=tuple(jax.ShapeDtypeStruct(x.shape, x.dtype) for x in large[:6])
        + tuple(jax.ShapeDtypeStruct(x.shape, full) for x in large[6:])
        + tuple(jax.ShapeDtypeStruct(shape, full) for shape in shapes),
        in_specs=[hbm] * 9 + [vmem],
        out_specs=(hbm,) * 9 + (vmem,) * 5,
        scratch_shapes=[pltpu.VMEM(x.shape, x.dtype) for x in large]
        + [pltpu.VMEM(x.shape, full) for x in large[6:]]
        + [pltpu.SemaphoreType.DMA((18,)), pltpu.SemaphoreType.DMA((18,))],
        compiler_params=pltpu.CompilerParams(vmem_limit_bytes=VMEM_LIMIT),
        name="emit",
    )(*large, small)


def per_device_kernels(
    tokens, cotangent, expert_ids, segment_lengths, segment_parents, attention_gain,
    query_weight, key_weight, value_weight, output_weight, bias_table, feedforward_gain,
    router_weight, gate_weight, up_weight, down_weight,
):
    ids_row = expert_ids.T
    send_rows, grad_rows, shares, residual, all_tokens, qkv, cols, params, att, probs, wo, g_early = front(
        segment_lengths, segment_parents, tokens, cotangent, ids_row, query_weight, key_weight, value_weight,
        output_weight, attention_gain[None], feedforward_gain[None], bias_table[None], router_weight.T,
    )
    part_out, grad_back, dots, gate_term, up_term, down_term = experts(
        send_rows, grad_rows, shares, g_early, gate_weight[0], up_weight[0], down_weight[0]
    )
    layer_out, tokens_grad, dwq, dwk, dwv, dwo, totals = back(
        segment_lengths, segment_parents, ids_row, params, dots, part_out, grad_back, residual, cotangent,
        wo.reshape(D, D), qkv, cols, all_tokens, att, probs,
    )
    large = (layer_out, tokens_grad, dwq, dwk, dwv, dwo, gate_term, up_term, down_term)
    *large, gain_one, gain_two, bias, router, roots = emit(large, totals)
    layer_out, tokens_grad, dwq, dwk, dwv, dwo, gate_term, up_term, down_term = large
    return (
        layer_out, tokens_grad, gain_one[0], dwq, dwk, dwv, dwo, bias[0], gain_two[0], router.T,
        gate_term[None], up_term[None], down_term[None], roots[0],
    )


def per_device_general(
    tokens,
    cotangent,
    expert_ids,
    segment_lengths,
    segment_parents,
    attention_gain,
    query_weight,
    key_weight,
    value_weight,
    output_weight,
    bias_table,
    feedforward_gain,
    router_weight,
    gate_weight,
    up_weight,
    down_weight,
):
    seq_count = lax.axis_size(SEQ)
    seq_place = lax.axis_index(SEQ)
    all_count = lax.axis_size(EXPERT) * seq_count
    row_count = tokens.shape[0]
    experts = lax.axis_size(EXPERT) * gate_weight.shape[0]
    capacity = 10 * row_count // (4 * experts)
    score_scale = HDIM ** (-0.5)
    gathered = (
        lax.all_gather(attention_gain, BOTH, axis=0, tiled=True),
        lax.all_gather(query_weight, BOTH, axis=0, tiled=True),
        lax.all_gather(key_weight, BOTH, axis=0, tiled=True),
        lax.all_gather(value_weight, BOTH, axis=0, tiled=True),
        lax.all_gather(output_weight, BOTH, axis=0, tiled=True),
        lax.all_gather(bias_table, BOTH, axis=0, tiled=True),
        lax.all_gather(feedforward_gain, BOTH, axis=0, tiled=True),
        lax.all_gather(router_weight, BOTH, axis=0, tiled=True),
    )
    gain_one, query_full, key_full, value_full, output_full, bias_flat, gain_two, router_full = (
        gathered
    )
    bias_grid = bias_flat.reshape(BUCKETS, HEADS)
    starts, before, reaches = tree_tables(segment_lengths[0], segment_parents[0])
    own_rows = seq_place * row_count + jnp.arange(row_count, dtype=jnp.int32)
    own_meta = token_info(own_rows, starts, before, reaches)
    tokens_float = tokens.astype(jnp.float32)
    scale_one = norm_factor(tokens_float)
    unit_one = tokens_float * scale_one
    normed_one = (unit_one * gain_one.astype(jnp.float32)).astype(jnp.bfloat16)
    queries = (
        jnp.dot(normed_one, query_full, preferred_element_type=jnp.float32)
        .astype(jnp.bfloat16)
        .reshape(row_count, HEADS, HDIM)
    )
    keys_own = (
        jnp.dot(normed_one, key_full, preferred_element_type=jnp.float32)
        .astype(jnp.bfloat16)
        .reshape(row_count, HEADS, HDIM)
    )
    values_own = (
        jnp.dot(normed_one, value_full, preferred_element_type=jnp.float32)
        .astype(jnp.bfloat16)
        .reshape(row_count, HEADS, HDIM)
    )
    row_peak = jnp.full((HEADS, row_count), NEGATIVE, jnp.float32)
    key_piece = lax.all_gather(keys_own, SEQ, axis=0, tiled=True)
    value_piece = lax.all_gather(values_own, SEQ, axis=0, tiled=True)
    key_rows = jnp.arange(key_piece.shape[0], dtype=jnp.int32)
    visible, onehot, pair_bias = pair_terms(
        own_meta, token_info(key_rows, starts, before, reaches), own_rows, key_rows, bias_grid
    )
    scores = masked_scores(queries, key_piece, visible, pair_bias)
    new_peak = jnp.maximum(row_peak, jnp.max(scores, axis=-1))
    expo = jnp.exp(scores - new_peak[:, :, None])
    row_total = jnp.sum(expo, axis=-1)
    summed = jnp.einsum(
        SPEC_2, expo.astype(jnp.bfloat16), value_piece, preferred_element_type=jnp.float32
    )
    row_peak, row_total, summed = (new_peak, row_total, summed)
    log_total = row_peak + jnp.log(row_total)
    attended_float = summed / jnp.transpose(row_total)[:, :, None]
    attended = attended_float.astype(jnp.bfloat16).reshape(row_count, D)
    residual = tokens_float + jnp.dot(attended, output_full, preferred_element_type=jnp.float32)
    scale_two = norm_factor(residual)
    unit_two = residual * scale_two
    normed_two = (unit_two * gain_two.astype(jnp.float32)).astype(jnp.bfloat16)
    router_prob = jax.nn.softmax(
        jnp.dot(normed_two, router_full, preferred_element_type=jnp.float32), axis=-1
    )
    pick_hot = (
        expert_ids[:, :, None] == jnp.arange(experts, dtype=jnp.int32)[None, None, :]
    ).astype(jnp.float32)
    chosen = jnp.sum(pick_hot * router_prob[:, None, :], axis=2)
    chosen_total = jnp.sum(chosen, axis=1, keepdims=True)
    gate_shares = chosen / chosen_total
    hot_int = pick_hot.astype(jnp.int32).reshape(row_count * 2, experts)
    earlier = jnp.cumsum(hot_int, axis=0) - hot_int
    slot_number = jnp.sum(earlier * hot_int, axis=1).reshape(row_count, 2)
    kept_copy = slot_number < capacity
    kept_float = kept_copy.astype(jnp.float32)
    target = jnp.where(kept_copy, expert_ids * capacity + slot_number, experts * capacity)
    copy_ids = jnp.arange(row_count * 2, dtype=jnp.int32)
    slot_copy = (
        jnp.full((experts * capacity + 1,), row_count * 2, jnp.int32)
        .at[target.reshape(-1)]
        .set(copy_ids)[: experts * capacity]
    )
    fetch_index = jnp.minimum(target, experts * capacity - 1).reshape(-1)
    token_of_slot = jnp.where(slot_copy < row_count * 2, slot_copy // 2, row_count)
    padded = jnp.concatenate([normed_two, jnp.zeros((1, D), jnp.bfloat16)], axis=0)
    send_rows = padded[token_of_slot].reshape(experts, capacity, D)
    expert_in = lax.all_to_all(send_rows, EXPERT, split_axis=0, concat_axis=1, tiled=True)[0]
    gate_piece = lax.all_gather(gate_weight, SEQ, axis=1, tiled=True)
    up_piece = lax.all_gather(up_weight, SEQ, axis=1, tiled=True)
    down_piece = lax.all_gather(down_weight, SEQ, axis=1, tiled=True)
    gate_pre = jnp.einsum(SPEC_3, expert_in, gate_piece[0], preferred_element_type=jnp.float32)
    up_pre = jnp.einsum(SPEC_3, expert_in, up_piece[0], preferred_element_type=jnp.float32)
    active = (gelu_tanh(gate_pre) * up_pre).astype(jnp.bfloat16)
    expert_sum = jnp.dot(active, down_piece[0], preferred_element_type=jnp.float32)
    returned = lax.all_to_all(
        expert_sum.astype(jnp.bfloat16)[None], EXPERT, split_axis=1, concat_axis=0, tiled=True
    )
    picked = (
        returned.reshape(experts * capacity, D)[fetch_index]
        .reshape(row_count, 2, D)
        .astype(jnp.float32)
    )
    weighted = gate_shares * kept_float
    mixture = jnp.sum(weighted[:, :, None] * picked, axis=1)
    layer_out = (residual + mixture).astype(jnp.bfloat16)
    local_sums = jnp.stack([jnp.sum(residual * residual), jnp.sum(mixture * mixture)])
    again = (
        lax.all_gather(attention_gain, BOTH, axis=0, tiled=True),
        lax.all_gather(query_weight, BOTH, axis=0, tiled=True),
        lax.all_gather(key_weight, BOTH, axis=0, tiled=True),
        lax.all_gather(value_weight, BOTH, axis=0, tiled=True),
        lax.all_gather(output_weight, BOTH, axis=0, tiled=True),
        lax.all_gather(bias_table, BOTH, axis=0, tiled=True),
        lax.all_gather(feedforward_gain, BOTH, axis=0, tiled=True),
        lax.all_gather(router_weight, BOTH, axis=0, tiled=True),
    )
    gain_one, query_full, key_full, value_full, output_full, bias_flat, gain_two, router_full = (
        again
    )
    bias_grid = bias_flat.reshape(BUCKETS, HEADS)
    grad_out = cotangent.astype(jnp.float32)
    copy_grad = (
        (weighted[:, :, None] * grad_out[:, None, :]).astype(jnp.bfloat16).reshape(row_count * 2, D)
    )
    copy_padded = jnp.concatenate([copy_grad, jnp.zeros((1, D), jnp.bfloat16)], axis=0)
    grad_send = copy_padded[slot_copy].reshape(experts, capacity, D)
    grad_in = lax.all_to_all(grad_send, EXPERT, split_axis=0, concat_axis=1, tiled=True)[0]
    gate_piece = lax.all_gather(gate_weight, SEQ, axis=1, tiled=True)
    up_piece = lax.all_gather(up_weight, SEQ, axis=1, tiled=True)
    down_piece = lax.all_gather(down_weight, SEQ, axis=1, tiled=True)
    gate_pre = jnp.einsum(SPEC_3, expert_in, gate_piece[0], preferred_element_type=jnp.float32)
    up_pre = jnp.einsum(SPEC_3, expert_in, up_piece[0], preferred_element_type=jnp.float32)
    gelu_out, gelu_pull = jax.vjp(gelu_tanh, gate_pre)
    act_grad = jnp.einsum(SPEC_3, grad_in, down_piece[0], preferred_element_type=jnp.float32)
    gate_back = gelu_pull(act_grad * up_pre)[0].astype(jnp.bfloat16)
    up_back = (act_grad * gelu_out).astype(jnp.bfloat16)
    input_grad = jnp.dot(gate_back, gate_piece[0], preferred_element_type=jnp.float32) + jnp.dot(
        up_back, up_piece[0], preferred_element_type=jnp.float32
    )
    active = (gelu_out * up_pre).astype(jnp.bfloat16)
    input_grad, gate_backs, up_backs, actives = (input_grad, gate_back, up_back, active)
    grad_back = lax.all_to_all(
        input_grad.astype(jnp.bfloat16)[None], EXPERT, split_axis=1, concat_axis=0, tiled=True
    )
    expert_back = (
        grad_back.reshape(experts * capacity, D)[fetch_index]
        .reshape(row_count, 2, D)
        .astype(jnp.float32)
    )
    normed_two_grad = jnp.sum(expert_back * kept_float[:, :, None], axis=1)
    expert_grads = lax.psum_scatter(
        jnp.stack(
            [
                jnp.einsum(SPEC_4, gate_backs, expert_in, preferred_element_type=jnp.float32),
                jnp.einsum(SPEC_4, up_backs, expert_in, preferred_element_type=jnp.float32),
                jnp.einsum(SPEC_4, actives, grad_in, preferred_element_type=jnp.float32),
            ],
            axis=1,
        ).astype(jnp.bfloat16),
        SEQ,
        scatter_dimension=0,
        tiled=True,
    ).astype(jnp.float32)
    share_grad = jnp.sum(grad_out[:, None, :] * picked, axis=2) * kept_float
    chosen_grad = (
        share_grad - jnp.sum(gate_shares * share_grad, axis=1, keepdims=True)
    ) / chosen_total
    prob_grad = jnp.sum(pick_hot * chosen_grad[:, :, None], axis=1)
    logit_grad = router_prob * (prob_grad - jnp.sum(router_prob * prob_grad, axis=1, keepdims=True))
    router_float = router_full.astype(jnp.float32)
    router_term = jnp.einsum(
        SPEC_5, normed_two.astype(jnp.float32), logit_grad, precision=lax.Precision.HIGHEST
    )
    normed_two_grad = normed_two_grad + jnp.einsum(
        SPEC_6, logit_grad, router_float, precision=lax.Precision.HIGHEST
    )
    gain_two_term = jnp.sum(normed_two_grad * unit_two, axis=0)
    unit_grad_two = normed_two_grad * gain_two.astype(jnp.float32)
    residual_grad = grad_out + scale_two * (
        unit_grad_two - unit_two * jnp.mean(unit_grad_two * unit_two, axis=-1, keepdims=True)
    )
    attention_out_grad = residual_grad.astype(jnp.bfloat16)
    output_term = jnp.einsum(
        SPEC_5, attended, attention_out_grad, preferred_element_type=jnp.float32
    )
    attended_grad = (
        jnp.einsum(SPEC_6, attention_out_grad, output_full, preferred_element_type=jnp.float32)
        .astype(jnp.bfloat16)
        .reshape(row_count, HEADS, HDIM)
    )
    row_delta = jnp.transpose(jnp.sum(attended_grad.astype(jnp.float32) * attended_float, axis=-1))
    total_all, delta_all = (
        lax.all_gather(log_total, SEQ, axis=1, tiled=True),
        lax.all_gather(row_delta, SEQ, axis=1, tiled=True),
    )
    key_piece = lax.all_gather(keys_own, SEQ, axis=0, tiled=True)
    value_piece = lax.all_gather(values_own, SEQ, axis=0, tiled=True)
    key_rows = jnp.arange(key_piece.shape[0], dtype=jnp.int32)
    visible, onehot, pair_bias = pair_terms(
        own_meta, token_info(key_rows, starts, before, reaches), own_rows, key_rows, bias_grid
    )
    scores = masked_scores(queries, key_piece, visible, pair_bias)
    soft_weights = jnp.exp(scores - log_total[:, :, None])
    dprob = jnp.einsum(
        SPEC_1, attended_grad, value_piece, preferred_element_type=jnp.float32
    )
    score_grad = (soft_weights * (dprob - row_delta[:, :, None])).astype(jnp.bfloat16)
    query_acc = jnp.einsum(
        SPEC_2, score_grad, key_piece, preferred_element_type=jnp.float32
    )
    bias_acc = jnp.einsum(SPEC_7, onehot, score_grad, preferred_element_type=jnp.float32)
    query_acc, bias_acc = (query_acc, bias_acc)
    query_piece = lax.all_gather(queries, SEQ, axis=0, tiled=True)
    grad_piece = lax.all_gather(attended_grad, SEQ, axis=0, tiled=True)
    piece_rows = query_piece.shape[0]
    query_rows = jnp.arange(piece_rows, dtype=jnp.int32)
    visible, onehot, pair_bias = pair_terms(
        token_info(query_rows, starts, before, reaches), own_meta, query_rows, own_rows, bias_grid
    )
    scores = masked_scores(query_piece, keys_own, visible, pair_bias)
    soft_weights = jnp.exp(scores - total_all[:, :, None])
    value_acc = jnp.einsum(
        SPEC_8,
        soft_weights.astype(jnp.bfloat16),
        grad_piece,
        preferred_element_type=jnp.float32,
    )
    dprob = jnp.einsum(SPEC_1, grad_piece, values_own, preferred_element_type=jnp.float32)
    score_grad = (soft_weights * (dprob - delta_all[:, :, None])).astype(jnp.bfloat16)
    key_acc = jnp.einsum(
        SPEC_8, score_grad, query_piece, preferred_element_type=jnp.float32
    )
    key_acc, value_acc = (key_acc, value_acc)
    query_back = (query_acc * score_scale).astype(jnp.bfloat16).reshape(row_count, D)
    key_back = (key_acc * score_scale).astype(jnp.bfloat16).reshape(row_count, D)
    value_back = value_acc.astype(jnp.bfloat16).reshape(row_count, D)
    query_term = jnp.einsum(SPEC_5, normed_one, query_back, preferred_element_type=jnp.float32)
    key_term = jnp.einsum(SPEC_5, normed_one, key_back, preferred_element_type=jnp.float32)
    value_term = jnp.einsum(SPEC_5, normed_one, value_back, preferred_element_type=jnp.float32)
    normed_one_grad = jnp.einsum(
        SPEC_6, query_back, query_full, preferred_element_type=jnp.float32
    )
    normed_one_grad = normed_one_grad + jnp.einsum(
        SPEC_6, key_back, key_full, preferred_element_type=jnp.float32
    )
    normed_one_grad = normed_one_grad + jnp.einsum(
        SPEC_6, value_back, value_full, preferred_element_type=jnp.float32
    )
    gain_one_term = jnp.sum(normed_one_grad * unit_one, axis=0)
    unit_grad_one = normed_one_grad * gain_one.astype(jnp.float32)
    tokens_grad = residual_grad + scale_one * (
        unit_grad_one - unit_one * jnp.mean(unit_grad_one * unit_one, axis=-1, keepdims=True)
    )
    stats_term = jnp.broadcast_to(local_sums[None, :], (all_count, 2))
    reduced = (
        lax.psum_scatter(gain_one_term, BOTH, scatter_dimension=0, tiled=True),
        lax.psum_scatter(query_term, BOTH, scatter_dimension=0, tiled=True),
        lax.psum_scatter(key_term, BOTH, scatter_dimension=0, tiled=True),
        lax.psum_scatter(value_term, BOTH, scatter_dimension=0, tiled=True),
        lax.psum_scatter(output_term, BOTH, scatter_dimension=0, tiled=True),
        lax.psum_scatter(
            bias_acc.reshape(BUCKETS * HEADS), BOTH, scatter_dimension=0, tiled=True
        ),
        lax.psum_scatter(gain_two_term, BOTH, scatter_dimension=0, tiled=True),
        lax.psum_scatter(router_term, BOTH, scatter_dimension=0, tiled=True),
        lax.psum_scatter(stats_term, BOTH, scatter_dimension=0, tiled=True),
    )
    roots = jnp.sqrt(reduced[8][0] / (row_count * all_count * D))
    return (
        layer_out,
        tokens_grad,
        reduced[0],
        reduced[1],
        reduced[2],
        reduced[3],
        reduced[4],
        reduced[5],
        reduced[6],
        reduced[7],
        expert_grads[None, :, 0, :],
        expert_grads[None, :, 1, :],
        expert_grads[None, :, 2, :],
        roots,
    )


def solution(mesh):
    kernels_fit = mesh.shape[EXPERT] == len(ORDER) and mesh.shape[SEQ] == 4
    return jax.shard_map(
        per_device_kernels if kernels_fit else per_device_general,
        mesh=mesh,
        in_specs=(
            P(BOTH, None),
            P(BOTH, None),
            P(BOTH, None),
            P(EXPERT, None),
            P(EXPERT, None),
            P(BOTH),
            P(BOTH, None),
            P(BOTH, None),
            P(BOTH, None),
            P(BOTH, None),
            P(BOTH),
            P(BOTH),
            P(BOTH, None),
            P(EXPERT, SEQ, None),
            P(EXPERT, SEQ, None),
            P(EXPERT, SEQ, None),
        ),
        out_specs=(
            P(BOTH, None),
            P(BOTH, None),
            P(BOTH),
            P(BOTH, None),
            P(BOTH, None),
            P(BOTH, None),
            P(BOTH, None),
            P(BOTH),
            P(BOTH),
            P(BOTH, None),
            P(EXPERT, SEQ, None),
            P(EXPERT, SEQ, None),
            P(EXPERT, SEQ, None),
            P(),
        ),
        check_vma=False,
    )
```

```python
import math

import jax
import jax.numpy as jnp
from jax import lax
from jax.experimental import pallas as pl
from jax.experimental.pallas import tpu as pltpu
from jax.sharding import PartitionSpec as P

SPEC_0 = "qkb,bh->hqk"
SPEC_1 = "qhd,khd->hqk"
SPEC_2 = "hqk,khd->qhd"
SPEC_3 = "rd,fd->rf"
SPEC_4 = "rf,rd->fd"
SPEC_5 = "rd,re->de"
SPEC_6 = "re,de->rd"
SPEC_7 = "qkb,hqk->bh"
SPEC_8 = "hqk,qhd->khd"
MESH = pl.DeviceIdType.MESH
VMEM_LIMIT = 62 << 20
EXPERT, SEQ = "expert", "seq"
BOTH = (EXPERT, SEQ)

D = 1024
HEADS = 16
HDIM = 64
BUCKETS = 32
MAXDIST = 128


EPSILON = 1e-06
NEGATIVE = -1e30


def norm_factor(values):
    return lax.rsqrt(jnp.mean(values * values, axis=-1, keepdims=True) + EPSILON)


def gelu_tanh(values):
    return jax.nn.gelu(values, approximate=True)


def bucket_of(distance):
    exact_span = BUCKETS // 2
    above = jnp.zeros(distance.shape, jnp.int32)
    for number in range(exact_span):
        threshold = int(math.ceil(exact_span * (MAXDIST / exact_span) ** (number / exact_span)))
        above = above + (distance >= threshold).astype(jnp.int32)
    return jnp.where(distance < exact_span, distance, exact_span - 1 + above)


def tree_tables(lengths, parents):
    ordinal = jnp.arange(lengths.shape[0], dtype=jnp.int32)
    starts = jnp.cumsum(lengths) - lengths

    def chase(number, running):
        current, reaches = running
        current = jnp.sum(
            jnp.where(current[:, None] == ordinal[None, :], parents[None, :], 0), axis=1
        )
        reaches = jnp.maximum(reaches, (current[:, None] == ordinal[None, :]).astype(jnp.int32))
        return (current, reaches)

    begin = (ordinal, (ordinal[:, None] == ordinal[None, :]).astype(jnp.int32))
    unused, reaches = lax.fori_loop(0, lengths.shape[0], chase, begin)
    before = jnp.sum(reaches * lengths[None, :], axis=1) - lengths
    return (starts, before, reaches)


def token_info(token_rows, starts, before, reaches):
    ordinal = jnp.arange(starts.shape[0], dtype=jnp.int32)
    segment = jnp.sum((token_rows[:, None] >= starts[None, :]).astype(jnp.int32), axis=1) - 1
    member = segment[:, None] == ordinal[None, :]
    position = token_rows + jnp.sum(jnp.where(member, (before - starts)[None, :], 0), axis=1)
    lineage = jnp.sum(jnp.where(member[:, :, None], reaches[None, :, :], 0), axis=1)
    return (member.astype(jnp.float32), position, lineage.astype(jnp.float32))


def pair_terms(query_meta, key_meta, query_rows, key_rows, bias_grid):
    visible = jnp.dot(query_meta[2], key_meta[0].T, preferred_element_type=jnp.float32) > 0.5
    visible = visible & (key_rows[None, :] <= query_rows[:, None])
    distance = jnp.maximum(query_meta[1][:, None] - key_meta[1][None, :], 0)
    onehot = (
        bucket_of(distance)[:, :, None] == jnp.arange(BUCKETS, dtype=jnp.int32)[None, None, :]
    ).astype(jnp.bfloat16)
    pair_bias = jnp.einsum(SPEC_0, onehot, bias_grid, preferred_element_type=jnp.float32)
    return (visible, onehot, pair_bias)


def masked_scores(query_block, key_block, visible, pair_bias):
    scores = (
        jnp.einsum(SPEC_1, query_block, key_block, preferred_element_type=jnp.float32)
        * HDIM ** (-0.5)
        + pair_bias
    )
    return jnp.where(visible[None], scores, NEGATIVE)


def remote(src, dst, send, recv, peer):
    return pltpu.make_async_remote_copy(
        src_ref=src, dst_ref=dst, send_sem=send, recv_sem=recv,
        device_id=peer, device_id_type=MESH,
    )


def contract(left, right, dims):
    return lax.dot_general(left, right, (dims, ((), ())), preferred_element_type=jnp.float32)


def gelu_parts(values):
    root = 0.7978845608028654
    square = values * values
    swing = jnp.tanh(root * values * (1.0 + 0.044715 * square))
    half = 0.5 * (1.0 + swing)
    slope = half + 0.5 * values * (1.0 - swing * swing) * (root * (1.0 + 3 * 0.044715 * square))
    return values * half, slope


ORDER = (0, 1, 2, 3, 4, 5, 6, 7)
UNITS = (
    (0, 0), (0, 1), (1, 0), (2, 0), (3, 0), (1, 1), (2, 1), (3, 1),
    (0, 2), (1, 2), (2, 2), (0, 3), (3, 2), (1, 3), (2, 3), (3, 3),
)


def announce(peers):
    barrier = pltpu.get_barrier_semaphore()
    for peer in peers:
        pl.semaphore_signal(barrier, inc=1, device_id=peer, device_id_type=MESH)


def greet(peers):
    announce(peers)
    pl.semaphore_wait(pltpu.get_barrier_semaphore(), len(peers))


def aligned(index, size):
    return pl.ds(pl.multiple_of(index * size, size), size)


ZHOPS = (2, 4, 6)


def expert_kernel(
    xs, gs, shares, g_early, wg_far, wu_far, wd_far, po_far, ret_b, ret_s, dwg, dwu, dwd,
    xr, gr, sh, act, gb, ub, po, pb, rb, rb2, sd, sd_got, sd_out, stage, rounded, wg, wu, wd,
    in_send, in_recv, hop_send, hop_recv, sh_send, sh_recv, rs_send, rs_recv, out_send, out_recv,
    sd_send, sd_recv, sr_send, sr_recv, po_sem, stage_sem, load_sem, own_sem,
):
    e = lax.axis_index(EXPERT)
    s = lax.axis_index(SEQ)
    cap = xs.shape[0] // 8
    width = xs.shape[1]
    full, low = jnp.float32, jnp.bfloat16
    near_x, near_y = (e, s ^ 1), (e, s ^ 2)
    around = (near_x, near_y, (e, s ^ 3))
    loads = [
        pltpu.make_async_copy(src, dst, load_sem.at[k])
        for k, (src, dst) in enumerate(((wg_far, wg), (wu_far, wu), (wd_far, wd), (g_early, gr.at[:, pl.ds(0, 4)])))
    ]
    for load in loads:
        load.start()
    greet(list(around) + [(e ^ d, s) for d in range(1, 8)])

    def block(index):
        return pl.ds(pl.multiple_of(index * cap, 16), cap)

    tensors = ((xs, xr), (gs, gr))

    def entry(kind, place):
        src, dst = tensors[kind]
        d = ORDER[place]
        return remote(src.at[block(e ^ d)], dst.at[0, place], in_send.at[kind, place],
                      in_recv.at[kind, place], (e ^ d, s))

    def hop(kind, which, pair):
        buf = tensors[kind][1]
        places = pl.ds(2 * pair, 2) if which < 2 else pl.ds(2 * pair + which - 2, 1)
        src = buf.at[(0, 0, 1, 2)[which], places]
        dst = buf.at[(1, 2, 3, 3)[which], places]
        peer = (near_x, near_y, near_y, near_x)[which]
        return remote(src, dst, hop_send.at[kind, which, pair], hop_recv.at[kind, which, pair], peer)

    def share_entry(place):
        d = ORDER[place]
        return remote(shares.at[e ^ d], sh.at[0, place], sh_send.at[place], sh_recv.at[place], (e ^ d, s))

    def share_hop(which):
        return remote(sh.at[(0, 0, 1)[which]], sh.at[1 + which], sh_send.at[8 + which], sh_recv.at[8 + which],
                      (near_x, near_y, near_y)[which])

    def rs(half, which, pair):
        first, second = ((near_x, near_y), (near_y, near_x))[half]
        src = pb.at[(1 + half, 3, 2 - half)[which], half, pair]
        dst = rb2.at[half, pair] if which == 2 else rb.at[which, half, pair]
        return remote(src, dst, rs_send.at[half, which, pair], rs_recv.at[half, which, pair],
                      second if which == 2 else first)

    def back(place):
        return remote(pb.at[0, place % 2, place // 2], ret_b.at[block(e)],
                      out_send.at[place], out_recv.at[place], (e ^ ORDER[place], s))

    def own_back():
        return pltpu.make_async_copy(pb.at[0, 0, 0], ret_b.at[block(e)], own_sem.at[2])

    def start_entries(kind, pair):
        for place in (2 * pair, 2 * pair + 1):
            if ORDER[place]:
                entry(kind, place).start()

    def forward_pair(kind, pair):
        for place in (2 * pair, 2 * pair + 1):
            if ORDER[place]:
                entry(kind, place).wait_recv()
        hop(kind, 0, pair).start()
        hop(kind, 1, pair).start()

    def forward_corner(kind, pair):
        for which in range(2):
            hop(kind, which, pair).wait_recv()
            hop(kind, 2 + which, pair).start()

    def wait_corner(pair):
        for kind in range(2 if pair >= 2 else 1):
            for which in (2, 3):
                hop(kind, which, pair).wait_recv()

    def start_sums(pair):
        for which in (1, 0):
            for half in range(2):
                rs(half, which, pair).start()

    def add_second(pair):
        for half in range(2):
            rs(half, 1, pair).wait_recv()
            group = 2 - half
            pb[group, half, pair] = (pb[group, half, pair].astype(full) + rb[1, half, pair].astype(full)).astype(low)
            rs(half, 2, pair).start()

    def finish(pair):
        for half in range(2):
            rs(half, 0, pair).wait_recv()
            rs(half, 2, pair).wait_recv()
            pb[0, half, pair] = (
                pb[0, half, pair].astype(full) + rb[0, half, pair].astype(full) + rb2[half, pair].astype(full)
            ).astype(low)
            if ORDER[2 * pair + half]:
                back(2 * pair + half).start()
            else:
                own_back().start()

    own_rows = [
        pltpu.make_async_copy(xs.at[block(e)], xr.at[0, 0], own_sem.at[0]),
        pltpu.make_async_copy(shares.at[e], sh.at[0, 0], own_sem.at[1]),
    ]
    for copy in own_rows:
        copy.start()
    start_entries(0, 0)
    for place in range(1, 8):
        share_entry(place).start()
    start_entries(0, 1)
    start_entries(1, 2)

    rows = 2 * cap

    def put_out(u, q, c):
        return pltpu.make_async_copy(po.at[q, :, c], po_far.at[q, :, c], po_sem.at[u])

    def unit(u, carry):
        q, c = jnp.int32(0), jnp.int32(0)
        for k, (whose, pair) in enumerate(UNITS):
            q, c = jnp.where(u == k, whose, q), jnp.where(u == k, pair, c)

        for k, (whose, pair) in enumerate(UNITS):
            @pl.when(u == k)
            def _():
                if k == 0:
                    for copy in own_rows:
                        copy.wait()
                    forward_pair(0, 0)
                    for place in range(1, 8):
                        share_entry(place).wait_recv()
                    share_hop(0).start()
                    share_hop(1).start()
                    for load in loads:
                        load.wait()
                if k == 1:
                    forward_corner(0, 0)
                    forward_pair(0, 1)
                    start_entries(1, 3)
                if k == 2:
                    share_hop(0).wait_recv()
                    share_hop(2).start()
                    share_hop(1).wait_recv()
                if k == 3:
                    forward_corner(0, 1)
                    forward_pair(1, 2)
                    start_entries(0, 2)
                if k == 4:
                    share_hop(2).wait_recv()
                if k == 6:
                    forward_corner(1, 2)
                    forward_pair(1, 3)
                    start_entries(0, 3)
                if k == 8:
                    forward_corner(1, 3)
                    forward_pair(0, 2)
                if k == 9:
                    forward_corner(0, 2)
                if k == 10:
                    add_second(1)
                if k == 11:
                    forward_pair(0, 3)
                if k == 13:
                    forward_corner(0, 3)
                    finish(1)
                if k == 15:
                    add_second(2)
                if whose == 3:
                    wait_corner(pair)

        x = xr[q, pl.ds(2 * c, 2)].reshape(rows, width)
        g = gr[q, pl.ds(2 * c, 2)].reshape(rows, width)
        share = jnp.concatenate([jnp.transpose(sh[q, 2 * c + i])[0:cap, 0:1] for i in range(2)], axis=0)
        gate = contract(x, wg[...], ((1,), (1,)))
        up = contract(x, wu[...], ((1,), (1,)))
        ag = contract(g, wd[...], ((1,), (1,))) * share
        value, slope = gelu_parts(gate)
        active = value * up
        gate_back = (ag * up * slope).astype(low)
        up_back = (ag * value).astype(low)
        act[q, c] = (active * share).astype(low)
        gb[q, c] = gate_back
        ub[q, c] = up_back
        out = contract(active.astype(low), wd[...], ((1,), (0,)))
        dots = lax.dot_general(jnp.ones((8, width), full), out * g.astype(full), (((1,), (1,)), ((), ())),
                               precision=lax.Precision.HIGHEST, preferred_element_type=full)
        sd[q, c, :, 0:rows] = dots
        weighted = (out * share).astype(low)
        into = contract(gate_back, wg[...], ((1,), (0,))) + contract(up_back, wu[...], ((1,), (0,)))
        for half in range(2):
            po[q, half, c] = weighted[half * cap:(half + 1) * cap]
            pb[q, half, c] = into[half * cap:(half + 1) * cap].astype(low)
        put_out(u, q, c).start()

        for k, (whose, pair) in enumerate(UNITS):
            if whose == 3 and pair:
                @pl.when(u == k)
                def _():
                    start_sums(pair)
            elif pair == 3 and whose:
                @pl.when(u == k)
                def _():
                    give_dots(whose).start()
        return carry

    def give_dots(q):
        return remote(sd.at[q], sd_got.at[q - 1], sd_send.at[q - 1], sd_recv.at[q - 1], around[q - 1])

    def return_dots(place):
        return remote(sd_out.at[place], ret_s.at[e], sr_send.at[place], sr_recv.at[place], (e ^ ORDER[place], s))

    def own_dots():
        return pltpu.make_async_copy(sd_out.at[0], ret_s.at[e], own_sem.at[3])

    sd[...] = jnp.zeros_like(sd)
    lax.fori_loop(0, len(UNITS), unit, 0)
    give_dots(3).start()

    def grads(left, right, dst):
        def part(u):
            q, c = lax.rem(u, 4), u // 4
            return contract(left[q, pl.ds(2 * c, 2)].reshape(2 * rows, wg.shape[0]),
                            right[q, pl.ds(4 * c, 4)].reshape(2 * rows, width), ((0,), (0,)))

        def more(u, carry):
            stage[...] += part(u)
            return carry

        stage[...] = part(0)
        lax.fori_loop(1, 8, more, 0)
        rounded[...] = stage[...].astype(low)
        done = pltpu.make_async_copy(rounded, dst, stage_sem)
        done.start()
        return done

    finish(2)
    done = grads(gb, xr, dwg)
    add_second(3)
    start_sums(0)
    for q in range(1, 4):
        give_dots(q).wait_recv()
    for c in range(4):
        dots = sd[0, c] + sd_got[0, c] + sd_got[1, c] + sd_got[2, c]
        for i in range(2):
            sd_out[2 * c + i] = jnp.zeros((8, 128), full)
            sd_out[2 * c + i, :, 0:cap] = dots[:, i * cap:(i + 1) * cap]
    for place in range(1, 8):
        return_dots(place).start()
    own_dots().start()
    done.wait()
    done = grads(ub, xr, dwu)
    finish(3)
    add_second(0)
    done.wait()
    done = grads(act, gr, dwd)
    finish(0)
    done.wait()

    own_back().wait()
    own_dots().wait()
    for place in range(1, 8):
        back(place).wait()
        return_dots(place).wait()
        share_entry(place).wait_send()
        for kind in range(2 if place >= 4 else 1):
            entry(kind, place).wait_send()
    for which in range(3):
        share_hop(which).wait_send()
        give_dots(1 + which).wait_send()
    for pair in range(4):
        for kind in range(2 if pair >= 2 else 1):
            for which in range(4):
                hop(kind, which, pair).wait_send()
        for half in range(2):
            for which in range(3):
                rs(half, which, pair).wait_send()
    for k, (whose, pair) in enumerate(UNITS):
        put_out(k, whose, pair).wait()


def experts(send_rows, grad_rows, shares, g_early, gate_weight, up_weight, down_weight):
    rows, width = send_rows.shape
    units = gate_weight.shape[0]
    cap = rows // 8
    low, full = jnp.bfloat16, jnp.float32
    hbm = pl.BlockSpec(memory_space=pl.ANY)
    dma = pltpu.SemaphoreType.DMA
    part = (4, 2, 4, cap, width)
    return pl.pallas_call(
        expert_kernel,
        out_shape=(
            jax.ShapeDtypeStruct(part, low),
            jax.ShapeDtypeStruct((rows, width), low),
            jax.ShapeDtypeStruct((8, 8, 128), full),
        ) + (jax.ShapeDtypeStruct((units, width), low),) * 3,
        in_specs=[hbm] * 7,
        out_specs=(hbm,) * 6,
        scratch_shapes=[
            pltpu.VMEM((4, 8, cap, width), low),
            pltpu.VMEM((4, 8, cap, width), low),
            pltpu.VMEM((4, 8, 8, 128), full),
            pltpu.VMEM((4, 4, 2 * cap, units), low),
            pltpu.VMEM((4, 4, 2 * cap, units), low),
            pltpu.VMEM((4, 4, 2 * cap, units), low),
            pltpu.VMEM(part, low),
            pltpu.VMEM(part, low),
            pltpu.VMEM((2, 2, 4, cap, width), low),
            pltpu.VMEM((2, 4, cap, width), low),
            pltpu.VMEM((4, 4, 8, 256), full),
            pltpu.VMEM((3, 4, 8, 256), full),
            pltpu.VMEM((8, 8, 128), full),
            pltpu.VMEM((units, width), full),
            pltpu.VMEM((units, width), low),
            pltpu.VMEM((units, width), low),
            pltpu.VMEM((units, width), low),
            pltpu.VMEM((units, width), low),
            dma((2, 8)), dma((2, 8)),
            dma((2, 4, 4)), dma((2, 4, 4)),
            dma((11,)), dma((11,)),
            dma((2, 3, 4)), dma((2, 3, 4)),
            dma((8,)), dma((8,)),
            dma((3,)), dma((3,)),
            dma((8,)), dma((8,)),
            dma((len(UNITS),)), dma, dma((4,)), dma((4,)),
        ],
        compiler_params=pltpu.CompilerParams(
            collective_id=1, has_side_effects=True, vmem_limit_bytes=VMEM_LIMIT
        ),
        cost_estimate=pl.CostEstimate(flops=2 * 9 * 4 * rows * units * width, bytes_accessed=20 << 20, transcendentals=4 * rows * units),
        name="experts",
    )(send_rows, grad_rows, shares, g_early, gate_weight, up_weight, down_weight)


def segment_scalars(lengths, parents, before_mem, reach_mem):
    count = lengths.shape[1]
    start = jnp.int32(0)
    found = []
    for k in range(count):
        length = lengths[0, k]
        if k == 0:
            before, reach = jnp.int32(0), jnp.int32(1)
        else:
            parent = parents[0, k]
            before = before_mem[parent] + lengths[0, parent]
            reach = reach_mem[parent] | (1 << k)
        before_mem[k] = before
        reach_mem[k] = reach
        found.append((start, before, reach, length))
        start = start + length
    return found


def token_columns(found, ids):
    offset = jnp.zeros(ids.shape, jnp.int32)
    reach = jnp.full(ids.shape, 1, jnp.int32)
    own = jnp.full(ids.shape, 1, jnp.int32)
    for k, (start, before, bits, _) in enumerate(found):
        if k:
            after = ids >= start
            offset = jnp.where(after, before - start, offset)
            reach = jnp.where(after, bits, reach)
            own = jnp.where(after, 1 << k, own)
    return ids + offset, reach, own


LAST = 127


def bias_tables(params, s):
    flat = params[2:3, 0:BUCKETS * HEADS]
    lane = lax.broadcasted_iota(jnp.int32, (8, BUCKETS * HEADS), 1)
    head = lax.broadcasted_iota(jnp.int32, (8, BUCKETS * HEADS), 0)
    heads_here = HEADS // 4
    chosen = jnp.where((lane % HEADS) == s * heads_here + head, jnp.broadcast_to(flat, lane.shape), 0.0)
    entry = lax.broadcasted_iota(jnp.int32, (BUCKETS * HEADS, LAST + 1), 0) // HEADS
    distance = lax.broadcasted_iota(jnp.int32, (BUCKETS * HEADS, LAST + 1), 1)
    hot = jnp.where(entry == bucket_of(distance), 1.0, 0.0)
    table = contract(chosen.astype(jnp.bfloat16), hot.astype(jnp.bfloat16), ((1,), (0,)))
    spot = lax.broadcasted_iota(jnp.int32, table.shape, 1)
    return jnp.where(spot == LAST, NEGATIVE, table)


def pair_index(found, first, rows, count):
    ids = first + lax.broadcasted_iota(jnp.int32, (rows, 1), 0)
    keys = lax.broadcasted_iota(jnp.int32, (1, count), 1)
    place, reach, _ = token_columns(found, ids)
    key_place, _, key_own = token_columns(found, keys)
    seen = ((reach & key_own) != 0) & (keys <= ids)
    return jnp.where(seen, jnp.minimum(place - key_place, LAST - 1), LAST), place, reach


def looked_up(row, index):
    rows, count = index.shape
    table = jnp.broadcast_to(row, (rows, LAST + 1))
    pieces = [
        jnp.take_along_axis(table, index[:, k * 128:(k + 1) * 128], axis=1)
        for k in range(count // 128)
    ]
    return jnp.concatenate(pieces, axis=1)


def slots_of(ids_row, cap):
    rows = ids_row.shape[1]
    full, low = jnp.float32, jnp.bfloat16
    level = lax.broadcasted_iota(jnp.int32, (8, rows), 0)
    hot_row = [jnp.where(ids_row[k:k + 1] == level, 1.0, 0.0).astype(full) for k in range(2)]
    down = lax.broadcasted_iota(jnp.int32, (rows, rows), 0)
    across = lax.broadcasted_iota(jnp.int32, (rows, rows), 1)
    after = jnp.where(down < across, 1.0, 0.0).astype(low)
    earlier = contract((hot_row[0] + hot_row[1]).astype(low), after, ((1,), (0,)))
    slot_row = [jnp.sum(h * earlier, axis=0, keepdims=True) for h in hot_row]
    spot_row = [
        jnp.where(slot_row[k] < cap, ids_row[k:k + 1].astype(full) * cap + slot_row[k], -1.0) for k in range(2)
    ]
    columns = jnp.transpose(jnp.concatenate(spot_row + slot_row + [jnp.zeros((4, rows), full)], axis=0))
    target = [columns[:, k:k + 1].astype(jnp.int32) for k in range(2)]
    slot = [columns[:, 2 + k:3 + k].astype(jnp.int32) for k in range(2)]
    hot = [jnp.transpose(h) for h in hot_row]
    target_row = [spot.astype(jnp.int32) for spot in spot_row]
    return hot_row, hot, slot, target, target_row


def router_of(residual, params, hot):
    low = jnp.bfloat16
    scale = norm_factor(residual)
    unit = residual * scale
    normed = (unit * params[1:2]).astype(low)
    router = params[8:16]
    logits = contract(normed, router.astype(low), ((1,), (1,)))
    expo = jnp.exp(logits - jnp.max(logits, axis=1, keepdims=True))
    prob = expo / jnp.sum(expo, axis=1, keepdims=True)
    chosen = [jnp.sum(h * prob, axis=1, keepdims=True) for h in hot]
    chosen_sum = chosen[0] + chosen[1]
    shares = [c / chosen_sum for c in chosen]
    return scale, unit, normed, router, prob, chosen_sum, shares


def front_kernel(
    lengths, parents, tokens, cotangent, ids_row, wq, wk, wv, wo, gain_one, gain_two, bias, router_row,
    xs, gs_far, shares, residual, all_tokens_far, qkv_far, cols_far, params, att_far, probs_far, wo_far, g_far,
    all_tokens, qkv, cols, wo_full, att, probs, got, part, normed, misc, tags, tag_sum, all_tags, index, table, landed, gs, g_early,
    before_mem, reach_mem,
    t_send, t_recv, w_send, w_recv, m_send, m_recv, c_send, c_recv, n_send, n_recv,
    h_send, h_recv, a_send, a_recv,
    e_send, e_recv, j_send, j_recv, far_sem, save_sem,
):
    e, s = lax.axis_index(EXPERT), lax.axis_index(SEQ)
    near_x, near_y, corner = (e, s ^ 1), (e, s ^ 2), (e, s ^ 3)
    around = (near_x, near_y, corner)
    hops = (1,) + ZHOPS
    low, full = jnp.bfloat16, jnp.float32
    rows, width = tokens.shape
    slim = wq.shape[0]
    shard = width // 4
    weights = (wq, wk, wv)
    place = e * 4 + s

    at_gain = lax.broadcasted_iota(jnp.int32, (slim, width), 1) == place * slim + lax.broadcasted_iota(
        jnp.int32, (slim, width), 0)
    gain_spot = jnp.where(at_gain, 1.0, 0.0).astype(low)
    few = bias.shape[1]
    at_bias = lax.broadcasted_iota(jnp.int32, (few, width), 1) == place * few + lax.broadcasted_iota(
        jnp.int32, (few, width), 0)
    bias_spot = jnp.where(at_bias, 1.0, 0.0).astype(low)
    two_gains = [contract(one[...], gain_spot, ((1,), (0,))) for one in (gain_one, gain_two)]
    one_bias = contract(bias[...], bias_spot, ((1,), (0,)))
    misc[...] = jnp.concatenate(
        two_gains + [one_bias, jnp.zeros((5, width), full), contract(router_row[...], gain_spot, ((1,), (0,)))], axis=0
    ).astype(low)

    greet(list(around) + [(e ^ d, s) for d in (1, 2, 3, 4, 6)])

    def send_tokens(k):
        return remote(tokens, all_tokens.at[aligned(s, rows)], t_send.at[k], t_recv.at[k], around[k])

    def pass_tokens(k):
        piece = pl.ds(pl.multiple_of((s ^ (1 + k)) * rows + k * (rows // 2), rows // 2), rows // 2)
        view = all_tokens.at[piece]
        return remote(view, view, t_send.at[2 + k], t_recv.at[2 + k], around[1 - k])

    def send_cols(k, m):
        return remote(
            weights[m].at[:, aligned(s ^ (k + 1), shard)], got.at[m, aligned(s, slim)],
            w_send.at[k, m], w_recv.at[k, m], around[k],
        )

    def send_tags(k):
        return remote(misc, tags.at[k], m_send.at[k], m_recv.at[k], around[k])

    def share(k, p):
        return remote(part.at[p], cols.at[p, aligned(e, 4 * slim)], c_send.at[p, k], c_recv.at[p, k], (e ^ hops[k], s))

    def share_tags(k):
        return remote(tag_sum, all_tags.at[k], n_send.at[k], n_recv.at[k], (e ^ hops[k], s))

    def relay(k, p):
        view = cols.at[p, aligned(e ^ hops[k], 4 * slim)]
        return remote(view, view, c_send.at[p, 3 + k], c_recv.at[p, 3 + k], (e ^ 1, s))

    def relay_tags(k):
        return remote(all_tags.at[k], all_tags.at[3 + k], n_send.at[3 + k], n_recv.at[3 + k], (e ^ 1, s))

    def early_out(k):
        return remote(wo, wo_full.at[e, s], h_send.at[k], h_recv.at[k], around[k])

    def along_out(k):
        view = wo_full.at[e]
        return remote(view, view, h_send.at[3 + k], h_recv.at[3 + k], (e ^ hops[k], s))

    def relay_along(k):
        view = wo_full.at[e ^ hops[k]]
        return remote(view, view, h_send.at[6 + k], h_recv.at[6 + k], (e ^ 1, s))

    def give(r):
        return remote(att.at[pl.ds(r * rows, rows)], landed.at[s], a_send.at[r], a_recv.at[s ^ r], (e, r))

    cap = xs.shape[0] // 8

    def g_entry(place):
        return remote(gs.at[pl.ds(pl.multiple_of((e ^ ORDER[place]) * cap, 16), cap)], g_early.at[0, place],
                      e_send.at[place], e_recv.at[place], (e ^ ORDER[place], s))

    def g_hop(which, pair):
        places = pl.ds(2 * pair, 2) if which < 2 else pl.ds(2 * pair + which - 2, 1)
        return remote(g_early.at[(0, 0, 1, 2)[which], places], g_early.at[(1, 2, 3, 3)[which], places],
                      j_send.at[which, pair], j_recv.at[which, pair], (near_x, near_y, near_y, near_x)[which])

    def g_corner(pair):
        for which in range(2):
            g_hop(which, pair).wait_recv()
            g_hop(2 + which, pair).start()

    far = []

    def keep(src, dst):
        copy = pltpu.make_async_copy(src, dst, far_sem.at[len(far)])
        copy.start()
        far.append(copy)

    for k in range(3):
        for m in range(3):
            send_cols(k, m).start()
        send_tags(k).start()
    for k in range(2):
        send_tokens(k).start()
    for k in range(3):
        early_out(k).start()
    for m in range(3):
        got[m, aligned(s, slim), :] = weights[m][:, aligned(s, shard)]
    all_tokens[aligned(s, rows), :] = tokens[...]
    wo_full[e, s] = wo[...]
    hot_row, hot, slot, _, target_row = slots_of(ids_row[...], cap)
    level = lax.broadcasted_iota(jnp.int32, (8 * cap, rows), 0)
    takes = jnp.where((level == target_row[0]) | (level == target_row[1]), 1.0, 0.0).astype(low)
    total = misc[...].astype(full)
    for k in range(3):
        send_tags(k).wait_recv()
        total += tags[k].astype(full)
    tag_sum[...] = total.astype(low)
    for k in range(4):
        share_tags(k).start()
    for k in range(3):
        for m in range(3):
            send_cols(k, m).wait_recv()
    for p in range(2):
        for m in range(3):
            part[p, :, m * 128:(m + 1) * 128] = got[m, :, p * 128:(p + 1) * 128]
    for k in (3, 2, 1, 0):
        share(k, 0).start()
    for p in range(2):
        cols[p, aligned(e, 4 * slim), :] = part[p]
    gs[...] = contract(takes, cotangent[...], ((1,), (0,))).astype(low)
    for place in range(1, 4):
        g_entry(place).start()
    g_early[0, 0] = gs[pl.ds(pl.multiple_of(e * cap, 16), cap), :]
    keep(gs, gs_far)
    found = segment_scalars(lengths, parents, before_mem, reach_mem)
    for r in range(4):
        index[r, :, :(r + 1) * rows] = pair_index(found, r * rows, rows, (r + 1) * rows)[0]
    for k in range(1, 4):
        share_tags(k).wait_recv()
        relay_tags(k).start()
    for k in range(2):
        send_tokens(k).wait_recv()
        pass_tokens(k).start()
    g_entry(1).wait_recv()
    for which in range(2):
        g_hop(which, 0).start()
    for k in range(1, 4):
        share(k, 0).wait_recv()
        relay(k, 0).start()
    for k in (3, 2, 1, 0):
        share(k, 1).start()
    for k in range(3):
        early_out(k).wait_recv()
    for k in (3, 2, 1, 0):
        along_out(k).start()
    share_tags(0).wait_recv()
    for k in range(1, 4):
        relay_tags(k).wait_recv()
    for k in range(7):
        total += all_tags[k].astype(full)
    params[...] = total
    gain = total[0:1]
    table[...] = bias_tables(params, s)

    def norm_block(q, carry):
        spot = aligned(s ^ q, rows)
        values = all_tokens[spot, :].astype(full)
        normed[spot, :] = (values * norm_factor(values) * gain).astype(low)
        return carry

    lax.fori_loop(0, 3, norm_block, 0)
    for k in range(2):
        pass_tokens(k).wait_recv()
    lax.fori_loop(3, 4, norm_block, 0)
    keep(all_tokens, all_tokens_far)

    def save_probs(p, r):
        piece = probs.at[pl.ds(2 * p, 2), r, :, pl.ds(0, (r + 1) * rows)]
        return pltpu.make_async_copy(piece, probs_far.at[pl.ds(2 * p, 2), r, :, pl.ds(0, (r + 1) * rows)], save_sem.at[p, r])

    def pair(p, carry):
        for which in range(2):
            @pl.when(p == which)
            def _():
                share(0, which).wait_recv()
                for k in range(1, 4):
                    relay(k, which).wait_recv()

        for r in range(4):
            out = contract(normed[r * rows:(r + 1) * rows, :], cols[p], ((1,), (0,)))
            first_part = out[:, 0:128].astype(low).astype(full) * HDIM ** (-0.5)
            qkv[p, r * rows:(r + 1) * rows, :] = jnp.concatenate([first_part, out[:, 128:]], axis=1).astype(low)

        for r in (3, 2, 1, 0):
            first, count = r * rows, (r + 1) * rows
            q = qkv[p, first:count, 0:128]
            k = qkv[p, 0:count, 128:256]
            v = qkv[p, 0:count, 256:384]
            lane = lax.broadcasted_iota(jnp.int32, (rows, 128), 1)
            results = []
            for side in range(2):
                mine = (lane // HDIM) == side
                scores = contract(jnp.where(mine, q, jnp.zeros_like(q)), k, ((1,), (1,)))
                scores = scores + looked_up(table[pl.ds(2 * p + side, 1), :], index[r, :, :count])
                expo = jnp.exp(scores - jnp.max(scores, axis=1, keepdims=True))
                soft = (expo * (1.0 / jnp.sum(expo, axis=1, keepdims=True))).astype(low)
                probs[2 * p + side, r, :, :count] = soft
                results.append(contract(soft, v, ((1,), (0,))))
            att[first:count, aligned(p, 128)] = jnp.where((lane // HDIM) == 0, results[0], results[1]).astype(low)

            save_probs(p, r).start()

            @pl.when((p == 1) & (s != r))
            def _():
                give(r).start()

            if r == 2:
                @pl.when(p == 0)
                def _():
                    for i in (2, 3):
                        g_entry(i).wait_recv()
                    for which in range(2):
                        g_hop(which, 1).start()
            if r == 1:
                @pl.when(p == 0)
                def _():
                    g_corner(0)
                    for i in range(1, 4):
                        share(i, 1).wait_recv()
                        relay(i, 1).start()

                @pl.when(p == 1)
                def _():
                    for i in range(1, 4):
                        along_out(i).wait_recv()
                        relay_along(i).start()
            if r == 0:
                @pl.when(p == 1)
                def _():
                    g_corner(1)
        return carry

    lax.fori_loop(0, 2, pair, 0)
    keep(qkv, qkv_far)
    keep(cols, cols_far)
    along_out(0).wait_recv()
    for k in range(1, 4):
        relay_along(k).wait_recv()
    keep(wo_full, wo_far)
    landed[s] = att[aligned(s, rows), :]
    total = tokens[...].astype(full)

    def out_rows(index):
        return wo_full[pl.ds(2 * index, 2)].reshape(shard, width)

    total += contract(landed[s], out_rows(s), ((1,), (0,)))
    for k in range(1, 4):
        remote(landed.at[s], landed.at[s ^ k], a_send.at[0], a_recv.at[k], (e, s ^ k)).wait_recv()
        total += contract(landed[s ^ k], out_rows(s ^ k), ((1,), (0,)))
    residual[...] = total
    keep(landed, att_far)
    _, _, normed, _, _, _, given = router_of(total, params[...], hot)
    xs[...] = contract(takes, normed, ((1,), (0,))).astype(low)
    at_slot = lax.broadcasted_iota(jnp.int32, (rows, 128), 1)
    by_slot = jnp.zeros((8, 128), full)
    for k in range(2):
        placed = jnp.where((at_slot == slot[k]) & (slot[k] < cap), given[k], 0.0)
        by_slot += lax.dot_general(hot_row[k], placed, (((1,), (0,)), ((), ())),
                                   precision=lax.Precision.HIGHEST, preferred_element_type=full)
    shares[...] = jnp.zeros_like(shares)
    for k in range(8):
        shares[k, 0:1, :] = by_slot[k:k + 1]
    for pair in range(2):
        for which in range(2):
            g_hop(2 + which, pair).wait_recv()
    keep(g_early, g_far)

    for place in range(1, 4):
        g_entry(place).wait_send()
    for pair in range(2):
        for which in range(4):
            g_hop(which, pair).wait_send()
    for k in range(2):
        send_tokens(k).wait_send()
        pass_tokens(k).wait_send()
    for k in range(3):
        for m in range(3):
            send_cols(k, m).wait_send()
        send_tags(k).wait_send()
        early_out(k).wait_send()
    for k in range(4):
        share_tags(k).wait_send()
        along_out(k).wait_send()
        for p in range(2):
            share(k, p).wait_send()
    for k in range(1, 4):
        relay_tags(k).wait_send()
        relay_along(k).wait_send()
        for p in range(2):
            relay(k, p).wait_send()
    for r in range(4):
        @pl.when(s != r)
        def _():
            give(r).wait_send()
    for copy in far:
        copy.wait()
    for p in range(2):
        for r in range(4):
            save_probs(p, r).wait()


def front(lengths, parents, tokens, cotangent, ids_row, wq, wk, wv, wo, gain_one, gain_two, bias, router_row):
    rows, width = tokens.shape
    slim, shard = wq.shape[0], width // 4
    cap = 10 * rows // 32
    low, full = jnp.bfloat16, jnp.float32
    vmem, smem, hbm = (pl.BlockSpec(memory_space=m) for m in (pltpu.VMEM, pltpu.SMEM, pl.ANY))
    dma = pltpu.SemaphoreType.DMA
    kept = (
        jax.ShapeDtypeStruct((4 * rows, width), low),
        jax.ShapeDtypeStruct((2, 4 * rows, 3 * shard // 2), low),
        jax.ShapeDtypeStruct((2, width, 3 * shard // 2), low),
        jax.ShapeDtypeStruct((16, width), full),
        jax.ShapeDtypeStruct((4, rows, shard), low),
        jax.ShapeDtypeStruct((4, 4, rows, 4 * rows), low),
        jax.ShapeDtypeStruct((8, 4, slim, width), low),
    )
    return pl.pallas_call(
        front_kernel,
        out_shape=(
            jax.ShapeDtypeStruct((8 * cap, width), low),
            jax.ShapeDtypeStruct((8 * cap, width), low),
            jax.ShapeDtypeStruct((8, 8, 128), full),
            jax.ShapeDtypeStruct((rows, width), full),
        ) + kept + (jax.ShapeDtypeStruct((4, 4, cap, width), low),),
        in_specs=[smem, smem] + [vmem] * 11,
        out_specs=(vmem, hbm, vmem, vmem, hbm, hbm, hbm, vmem, hbm, hbm, hbm, hbm),
        scratch_shapes=[
            pltpu.VMEM(kept[0].shape, low), pltpu.VMEM(kept[1].shape, low), pltpu.VMEM(kept[2].shape, low),
            pltpu.VMEM(kept[6].shape, low), pltpu.VMEM((4 * rows, shard), low), pltpu.VMEM(kept[5].shape, low),
            pltpu.VMEM((3, 4 * slim, shard), low), pltpu.VMEM((2, 4 * slim, 3 * shard // 2), low),
            pltpu.VMEM((4 * rows, width), low),
            pltpu.VMEM((16, width), low), pltpu.VMEM((3, 16, width), low), pltpu.VMEM((16, width), low),
            pltpu.VMEM((7, 16, width), low),
            pltpu.VMEM((4, rows, 4 * rows), jnp.int32), pltpu.VMEM((8, 128), full),
            pltpu.VMEM((4, rows, shard), low),
            pltpu.VMEM((8 * cap, width), low), pltpu.VMEM((4, 4, cap, width), low),
            pltpu.SMEM((16,), jnp.int32), pltpu.SMEM((16,), jnp.int32),
            dma((4,)), dma((4,)), dma((3, 3)), dma((3, 3)), dma((3,)), dma((3,)),
            dma((2, 7)), dma((2, 7)), dma((7,)), dma((7,)),
            dma((10,)), dma((10,)), dma((4,)), dma((4,)),
            dma((4,)), dma((4,)), dma((4, 2)), dma((4, 2)), dma((8,)), dma((2, 4)),
        ],
        compiler_params=pltpu.CompilerParams(
            collective_id=2, has_side_effects=True, vmem_limit_bytes=VMEM_LIMIT
        ),
        cost_estimate=pl.CostEstimate(flops=40 * rows * width * shard, bytes_accessed=24 << 20, transcendentals=8 * rows * rows * 16),
        name="front",
    )(lengths, parents, tokens, cotangent, ids_row, wq, wk, wv, wo, gain_one, gain_two, bias, router_row)


def near_keys(found, first, rows):
    ids = first + lax.broadcasted_iota(jnp.int32, (rows, 1), 0)
    place, reach, _ = token_columns(found, ids)
    step = lax.broadcasted_iota(jnp.int32, (rows, LAST + 1), 1)
    wanted = place - step
    spot = jnp.full((rows, LAST + 1), -1, jnp.int32)
    for k, (start, before, _, length) in enumerate(found):
        inside = ((reach & (1 << k)) != 0) & (wanted >= before) & (wanted < before + length)
        spot = jnp.where(inside, wanted + (start - before), spot)
    return jnp.where(step == LAST, -1, spot)


GROUPS = ((0, 3), (3, 3))


def back_kernel(
    lengths, parents, ids_row, params, ret_s, po_far, ret_b_far, residual_far, cotangent_far,
    wo_far, qkv_far, cols_far, all_tokens_far, att_far, probs_far,
    layer_out_far, tokens_grad, dwq, dwk, dwv, dwo, small_sum,
    po0, po2, ro, ro2, ret_o, ret_b, residual, cotangent, layer_out, wo, qkv, cols, all_tokens, att, probs, datt, datt_own, aog_own, residual_grad,
    takes, o_halves, o_core, o_sums, o_z, o_final, o_seq, spots, near, dk, dv, dqkv, normed,
    halves, core_got, sums, z_got, final, final_got, parts, first_got, second_got, mine, tally, tally_got, square, square_got,
    before_mem, reach_mem,
    load_sem, d_send, d_recv, w_send, w_recv, core_send, core_recv, z_send, z_recv, a_send, a_recv,
    n_send, n_recv, m_send, m_recv, o_send, o_recv, r_send, r_recv, q_send, q_recv, own_sem, probs_sem,
):
    e, s = lax.axis_index(EXPERT), lax.axis_index(SEQ)
    z, c = e // 2, lax.rem(e, 2)
    near_x, near_y = (e, s ^ 1), (e, s ^ 2)
    around = [(e, s ^ k) for k in range(1, 4)]
    hops = (1,) + ZHOPS
    full, low = jnp.float32, jnp.bfloat16
    high = lax.Precision.HIGHEST
    rows, width = residual.shape
    shard = att.shape[2]
    slim = dwq.shape[0]
    cap = ret_b.shape[0] // 8
    half = shard // 2
    pairs = (
        (residual_far, residual), (cotangent_far, cotangent), (ret_b_far, ret_b), (wo_far, wo), (po_far.at[0], po0),
        (att_far, att), (qkv_far, qkv), (all_tokens_far, all_tokens), (cols_far, cols),
        (po_far.at[2, 0], po2.at[0]), (po_far.at[1, 1], po2.at[1]),
    )
    loads = [pltpu.make_async_copy(src, dst, load_sem.at[k]) for k, (src, dst) in enumerate(pairs)]
    for load in loads[:4]:
        load.start()
    peers = around + [(e ^ d, s) for d in range(1, 8)]
    announce(peers)
    early_probs = [
        pltpu.make_async_copy(probs_far.at[:, r, :, pl.ds(0, (r + 1) * rows)], probs.at[:, r, :, pl.ds(0, (r + 1) * rows)],
                              probs_sem.at[r])
        for r in range(4)
    ]
    _, hot, slot, target, _ = slots_of(ids_row[...], cap)
    place = lax.broadcasted_iota(jnp.int32, (rows, 8 * cap), 1)
    takes[...] = jnp.where((place == target[0]) | (place == target[1]), 1.0, 0.0).astype(low)
    pl.semaphore_wait(pltpu.get_barrier_semaphore(), len(peers))

    def o_copy(side, which, zone):
        first, second = ((near_x, near_y), (near_y, near_x))[side]
        two = pl.ds(2 * zone, 2)
        if which == 2:
            src, dst = po2.at[side, two], ro2.at[side, two]
        else:
            src, dst = po_far.at[(1 + side, 3)[which], side, two], ro.at[which, side, two]
        return remote(src, dst, o_send.at[side, which, zone], o_recv.at[side, which, zone], second if which == 2 else first)

    def block(index):
        return pl.ds(pl.multiple_of(index * cap, 16), cap)

    def return_rows(place):
        return remote(po0.at[place % 2, place // 2], ret_o.at[block(e)], r_send.at[place], r_recv.at[place],
                      (e ^ ORDER[place], s))

    def start_outs(zone, which):
        for side in range(2):
            o_copy(side, which, zone).start()

    def add_outs(zone):
        for side in range(2):
            o_copy(side, 1, zone).wait_recv()
            for i in (2 * zone, 2 * zone + 1):
                po2[side, i] = (po2[side, i].astype(full) + ro[1, side, i].astype(full)).astype(low)
            o_copy(side, 2, zone).start()

    def finish_outs(zone):
        for side in range(2):
            o_copy(side, 0, zone).wait_recv()
            o_copy(side, 2, zone).wait_recv()
            for i in (2 * zone, 2 * zone + 1):
                po0[side, i] = (
                    po0[side, i].astype(full) + ro[0, side, i].astype(full) + ro2[side, i].astype(full)
                ).astype(low)
                if 2 * i + side:
                    return_rows(2 * i + side).start()
                else:
                    ret_o[block(e), :] = po0[0, 0]

    start_outs(1, 1)
    loads[0].wait()

    held = residual[...]
    scale, unit, unrouted, router, prob, chosen_sum, shares = router_of(held, params[...], hot)
    at_slot = lax.broadcasted_iota(jnp.int32, (rows, 128), 1)
    dots = jnp.concatenate([ret_s[k, 0:1, :] for k in range(8)], axis=0)
    share_grad = []
    for k in range(2):
        mine_dots = lax.dot_general(hot[k], dots, (((1,), (0,)), ((), ())), precision=high, preferred_element_type=full)
        share_grad.append(jnp.sum(
            jnp.where((at_slot == slot[k]) & (slot[k] < cap), mine_dots, 0.0), axis=1, keepdims=True))
    for load in loads[1:4]:
        load.wait()
    for load in loads[4:] + early_probs:
        load.start()
    grad = cotangent[...].astype(full)
    inner = shares[0] * share_grad[0] + shares[1] * share_grad[1]
    prob_grad = sum(hot[k] * ((share_grad[k] - inner) / chosen_sum) for k in range(2))
    logit_grad = prob * (prob_grad - jnp.sum(prob * prob_grad, axis=1, keepdims=True))
    normed_grad = contract(takes[...], ret_b[...], ((1,), (0,))) + lax.dot_general(
        logit_grad, router, (((1,), (0,)), ((), ())), precision=high, preferred_element_type=full
    )
    unit_grad = normed_grad * params[1:2]
    passed = grad + scale * (unit_grad - unit * jnp.mean(unit_grad * unit, axis=1, keepdims=True))
    residual_grad[...] = passed
    aog_own[...] = passed.astype(low)
    datt_own[...] = contract(aog_own[...], wo[...], ((1,), (1,))).astype(low)

    def give(k):
        return remote(datt_own.at[:, aligned(s ^ (k + 1), shard)], datt.at[aligned(s, rows)],
                      d_send.at[k], d_recv.at[k], around[k])

    for k in (2, 0, 1):
        give(k).start()

    def wide_core():
        return remote(o_halves.at[1 - c], o_core, w_send.at[0], w_recv.at[0], (e ^ 1, s))

    def wide_z(k):
        return remote(o_sums.at[z ^ (1, 3, 2)[k - 1]], o_z.at[k - 1], w_send.at[k], w_recv.at[k],
                      (e ^ (2, 2, 4)[k - 1], s))

    def wide_on():
        wide_z(2).wait_recv()
        o_sums[z ^ 2] = (o_sums[z ^ 2].astype(full) + o_z[1].astype(full)).astype(low)
        wide_z(3).start()

    def wide_seq(k):
        return remote(o_final.at[aligned(s ^ (k + 1), slim)], o_seq.at[k], w_send.at[4 + k], w_recv.at[4 + k], around[k])

    for load in loads[4:]:
        load.wait()

    def output_zone(j, carry):
        part = contract(att[j], aog_own[...], ((0,), (0,)))
        for i in range(2):
            o_halves[i, j] = part[i * half:(i + 1) * half].astype(low)
        return carry

    lax.fori_loop(0, 4, output_zone, 0)
    wide_core().start()
    datt[aligned(s, rows), :] = datt_own[:, aligned(s, shard)]
    tally[0] = jnp.zeros((16, width), full)
    tally[0, 1:2] = jnp.sum(normed_grad * unit, axis=0, keepdims=True)
    lane = lax.broadcasted_iota(jnp.int32, (1, width), 1)
    tally[0, 3:4] = jnp.where(lane == 0, jnp.sum(held * held), 0.0)
    tally[0, 8:16] = lax.dot_general(logit_grad, unrouted.astype(full), (((0,), (0,)), ((), ())),
                                     precision=high, preferred_element_type=full)
    wide_core().wait_recv()
    for j in range(4):
        o_sums[j] = (o_halves[c, j].astype(full) + o_core[j].astype(full)).astype(low)
    for k in (2, 1):
        wide_z(k).start()
    found = segment_scalars(lengths, parents, before_mem, reach_mem)
    near[...] = jnp.zeros_like(near)
    for r in range(4):
        spots[r] = near_keys(found, r * rows, rows)
    gain = params[0:1]

    def units(q):
        values = all_tokens[aligned(s ^ q, rows), :].astype(full)
        factor = norm_factor(values)
        return values * factor, factor

    def norm_block(q, carry):
        normed[aligned(s ^ q, rows), :] = (units(q)[0] * gain).astype(low)
        return carry

    lax.fori_loop(0, 4, norm_block, 0)

    def core_copy(g):
        slots = pl.ds(*GROUPS[g])
        return remote(halves.at[1 - c, slots], core_got.at[slots], core_send.at[g], core_recv.at[g], (e ^ 1, s))

    def z_copy(g, k):
        slots = pl.ds(*GROUPS[g])
        return remote(sums.at[slots, z ^ k], z_got.at[k - 1, slots], z_send.at[g, k - 1], z_recv.at[g, k - 1],
                      (e ^ (2 * k), s))

    def a_copy(g, k):
        slots = pl.ds(*GROUPS[g])
        return remote(final.at[slots, aligned(s ^ (k + 1), slim)], final_got.at[s, slots],
                      a_send.at[g, k], a_recv.at[g, k], around[k])

    def add_core(g):
        core_copy(g).wait_recv()
        first, amount = GROUPS[g]
        for slot in range(first, first + amount):
            for j in range(4):
                sums[slot, j] = (halves[c, slot, j].astype(full) + core_got[slot, j].astype(full)).astype(low)
        for k in range(1, 4):
            z_copy(g, k).start()

    def finish_grad(g):
        first, amount = GROUPS[g]
        for k in range(1, 4):
            z_copy(g, k).wait_recv()
        for slot in range(first, first + amount):
            block = sums[slot, z].astype(full)
            for k in range(1, 4):
                block += z_got[k - 1, slot].astype(full)
            final[slot] = block
        for k in range(3):
            a_copy(g, k).start()
        for slot in range(first, first + amount):
            final_got[s, slot] = final[slot, aligned(s, slim)]

    for load in early_probs:
        load.wait()
    for k in range(3):
        give(k).wait_recv()
    add_outs(1)
    start_outs(1, 0)

    def pair(p, carry):
        lanes = aligned(p, 128)
        dk[...] = jnp.zeros_like(dk)
        dv[...] = jnp.zeros_like(dv)
        for r in (3, 2, 1, 0):
            first, count = r * rows, (r + 1) * rows
            q = qkv[p, first:count, 0:128]
            k = qkv[p, 0:count, 128:256]
            v = qkv[p, 0:count, 256:384]
            g = datt[first:count, lanes]
            lane = lax.broadcasted_iota(jnp.int32, (rows, 128), 1)
            lane_long = lax.broadcasted_iota(jnp.int32, (count, 128), 1)
            spot = spots[r]
            spot_lane, spot_block = spot & 127, jnp.where(spot < 0, -1, spot >> 7)
            dq = []
            key_sum, value_sum = 0.0, 0.0
            for side in range(2):
                mine_lanes = (lane // HDIM) == side
                q_side = jnp.where(mine_lanes, q, jnp.zeros_like(q))
                g_side = jnp.where(mine_lanes, g, jnp.zeros_like(g))
                soft = probs[2 * p + side, r, :, :count]
                wide_soft = soft.astype(full)
                dprob = contract(g_side, v, ((1,), (1,)))
                delta = jnp.sum(wide_soft * dprob, axis=1, keepdims=True)
                wide = wide_soft * (dprob - delta)
                score_grad = wide.astype(low)
                key_sum = key_sum + contract(score_grad, q_side, ((0,), (0,)))
                value_sum = value_sum + contract(soft, g_side, ((0,), (0,)))
                with_ones = jnp.where((lane_long // HDIM) == side, k, jnp.ones_like(k))
                part = contract(score_grad, with_ones, ((1,), (0,)))
                dq.append(part)
                close = jnp.zeros((rows, 128), full)
                for b in range(count // 128):
                    taken = jnp.take_along_axis(wide[:, b * 128:(b + 1) * 128], spot_lane, axis=1)
                    close = jnp.where(spot_block == b, taken, close)
                near[0, 2 * p + side] += jnp.sum(close.reshape(rows // 8, 8, 128), axis=0)
                rest = jnp.where(mine_lanes, 0.0, part)
                near[1, 2 * p + side] += jnp.sum(rest.reshape(rows // 8, 8, 128), axis=0)
            dqkv[p, first:count, 0:128] = (jnp.where((lane // HDIM) == 0, dq[0], dq[1]) * HDIM ** (-0.5)).astype(low)
            dk[0:count] += key_sum
            dv[0:count] += value_sum

            if r == 3:
                @pl.when(p == 0)
                def _():
                    start_outs(0, 1)
                    start_outs(0, 0)
                    wide_on()

                @pl.when(p == 1)
                def _():
                    add_core(0)
            if r == 2:
                @pl.when(p == 0)
                def _():
                    finish_outs(1)
            if r == 1:
                @pl.when(p == 1)
                def _():
                    add_outs(0)
        dqkv[p, :, 128:256] = dk[...].astype(low)
        dqkv[p, :, 256:384] = dv[...].astype(low)

        def qkv_zone(j, carry):
            block = contract(normed[:, aligned(j, shard)], dqkv[p], ((0,), (0,)))
            for m in range(3):
                for i in range(2):
                    halves[i, 3 * p + m, j] = block[i * half:(i + 1) * half, m * 128:(m + 1) * 128].astype(low)
            return carry

        lax.fori_loop(0, 4, qkv_zone, 0)

        @pl.when(p == 0)
        def _():
            core_copy(0).start()

        @pl.when(p == 1)
        def _():
            core_copy(1).start()
        return carry

    lax.fori_loop(0, 2, pair, 0)

    def n_copy(kind, which):
        one, two = ((near_x, near_y), (near_y, near_x))[kind]
        if which < 2:
            src = parts.at[(1 + kind, 3)[which], kind]
            return remote(src, first_got.at[kind, which], n_send.at[kind, which], n_recv.at[kind, which], one)
        return remote(parts.at[2 - kind, kind], second_got.at[kind], n_send.at[kind, 2], n_recv.at[kind, 2], two)

    def back_block(i, carry):
        q = 3 - i
        total = jnp.zeros((rows, width), full)
        for p in range(2):
            total += contract(dqkv[p, aligned(s ^ q, rows), :], cols[p], ((1,), (1,)))
        tally[0, 0:1] += jnp.sum(total * units(q)[0], axis=0, keepdims=True)
        mine[...] = total
        for kind in range(2):
            parts[q, kind] = total[:, kind * (width // 2):(kind + 1) * (width // 2)].astype(low)

        @pl.when(i == 0)
        def _():
            n_copy(0, 1).start()
            n_copy(1, 1).start()
            add_core(1)

        @pl.when(i == 1)
        def _():
            n_copy(1, 0).start()

        @pl.when(i == 2)
        def _():
            n_copy(0, 0).start()
        return carry

    lax.fori_loop(0, 4, back_block, 0)
    finish_outs(0)
    wide_z(1).wait_recv()
    wide_z(3).wait_recv()
    whole = o_sums[z].astype(full) + o_z[0].astype(full) + o_z[2].astype(full)
    o_final[...] = whole.astype(low)
    for k in range(3):
        wide_seq(k).start()

    close, rest = (
        jnp.concatenate([jnp.sum(near[kind, h], axis=0, keepdims=True) for h in range(8)], axis=0) for kind in range(2)
    )
    far = jnp.sum(rest, axis=1, keepdims=True) / HDIM - jnp.sum(close, axis=1, keepdims=True)
    spot = lax.broadcasted_iota(jnp.int32, close.shape, 1)
    by_distance = jnp.where(spot == LAST, far, close)
    lane = lax.broadcasted_iota(jnp.int32, (128, BUCKETS * HEADS), 1)
    distance = lax.broadcasted_iota(jnp.int32, (128, BUCKETS * HEADS), 0)
    hot_bucket = jnp.where((lane // HEADS) == bucket_of(distance), 1.0, 0.0)
    spread = lax.dot_general(by_distance, hot_bucket, (((1,), (0,)), ((), ())), precision=high, preferred_element_type=full)
    head = lax.broadcasted_iota(jnp.int32, spread.shape, 0)
    lane = lax.broadcasted_iota(jnp.int32, spread.shape, 1)
    here = ((lane % HEADS) == s * (HEADS // 4) + head) & (head < HEADS // 4)
    tally[0, 2:3, 0:BUCKETS * HEADS] = jnp.sum(jnp.where(here, spread, 0.0), axis=0, keepdims=True)

    def m_copy(stage, k):
        slot = (0, 3, 4)[stage] + k
        peer = (around[k], (e ^ 1, s), (e ^ (2 * (k + 1)), s))[stage]
        return remote(tally.at[stage], tally_got.at[slot], m_send.at[slot], m_recv.at[slot], peer)

    for k in range(3):
        m_copy(0, k).start()
    for kind in range(2):
        n_copy(kind, 1).wait_recv()
        group = 2 - kind
        parts[group, kind] = (parts[group, kind].astype(full) + first_got[kind, 1].astype(full)).astype(low)
        n_copy(kind, 2).start()
    finish_grad(0)
    total = tally[0]
    for k in range(3):
        m_copy(0, k).wait_recv()
        total += tally_got[k]
    tally[1] = total
    m_copy(1, 0).start()

    for place in range(1, 8):
        return_rows(place).wait_recv()
    mixture = contract(takes[...], ret_o[...], ((1,), (0,)))
    layer_out[...] = (residual[...] + mixture).astype(low)
    layer_done = pltpu.make_async_copy(layer_out, layer_out_far, own_sem)
    layer_done.start()
    squares = jnp.full((8, 128), jnp.sum(mixture * mixture), full)

    def q_copy(stage, k):
        slot = (0, 3, 4)[stage] + k
        peer = (around[k], (e ^ 1, s), (e ^ (2 * (k + 1)), s))[stage]
        return remote(square.at[stage], square_got.at[slot], q_send.at[slot], q_recv.at[slot], peer)

    square[0] = squares
    for k in range(3):
        q_copy(0, k).start()
    finish_grad(1)
    m_copy(1, 0).wait_recv()
    total = total + tally_got[3]
    tally[2] = total
    for k in range(3):
        m_copy(2, k).start()
    for k in range(3):
        q_copy(0, k).wait_recv()
        squares += square_got[k]
    square[1] = squares
    q_copy(1, 0).start()
    for kind in range(2):
        n_copy(kind, 0).wait_recv()
        n_copy(kind, 2).wait_recv()
        lanes = slice(kind * (width // 2), (kind + 1) * (width // 2))
        mine[:, lanes] += first_got[kind, 0].astype(full) + second_got[kind].astype(full)
    unit, scale = units(0)
    unit_grad = mine[...] * gain
    tokens_grad[...] = residual_grad[...] + scale * (
        unit_grad - unit * jnp.mean(unit_grad * unit, axis=1, keepdims=True)
    )
    q_copy(1, 0).wait_recv()
    squares += square_got[3]
    square[2] = squares
    for k in range(3):
        q_copy(2, k).start()
    for g in range(2):
        for k in range(3):
            a_copy(g, k).wait_recv()
    for m, out in enumerate((dwq, dwk, dwv)):
        for i in range(2):
            for j in range(4):
                out[:, j * shard + i * 128:j * shard + (i + 1) * 128] = final_got[j, m + 3 * i]
    whole = o_final[aligned(s, slim), :].astype(full)
    for k in range(3):
        wide_seq(k).wait_recv()
        whole += o_seq[k].astype(full)
    dwo[...] = whole
    for k in range(3):
        m_copy(2, k).wait_recv()
        total += tally_got[4 + k]
    for k in range(3):
        q_copy(2, k).wait_recv()
        squares += square_got[4 + k]
    lane = lax.broadcasted_iota(jnp.int32, (1, 128), 1)
    small_sum[...] = total
    small_sum[3:4, 0:128] = jnp.where(lane == 1, squares[0:1], total[3:4, 0:128])
    layer_done.wait()
    wide_core().wait_send()
    for k in range(3):
        give(k).wait_send()
        wide_z(k + 1).wait_send()
        wide_seq(k).wait_send()
        for g in range(2):
            z_copy(g, k + 1).wait_send()
            a_copy(g, k).wait_send()
    for g in range(2):
        core_copy(g).wait_send()
    for kind in range(2):
        for which in range(3):
            n_copy(kind, which).wait_send()
    for stage, amount in ((0, 3), (1, 1), (2, 3)):
        for k in range(amount):
            m_copy(stage, k).wait_send()
            q_copy(stage, k).wait_send()
    for place in range(1, 8):
        return_rows(place).wait_send()
    for side in range(2):
        for which in range(3):
            for zone in range(2):
                o_copy(side, which, zone).wait_send()


def back(lengths, parents, ids_row, params, ret_s, part_o, ret_b, residual, cotangent, wo, qkv, cols, all_tokens, att, probs):
    rows, width = residual.shape
    shard = att.shape[2]
    slim = width // 32
    low, full = jnp.bfloat16, jnp.float32
    vmem, smem, hbm = (pl.BlockSpec(memory_space=m) for m in (pltpu.VMEM, pltpu.SMEM, pl.ANY))
    dma = pltpu.SemaphoreType.DMA
    half = shard // 2
    return pl.pallas_call(
        back_kernel,
        out_shape=(
            jax.ShapeDtypeStruct((rows, width), low),
            jax.ShapeDtypeStruct((rows, width), full),
        ) + (jax.ShapeDtypeStruct((slim, width), full),) * 4 + (jax.ShapeDtypeStruct((16, width), full),),
        in_specs=[smem, smem] + [vmem] * 3 + [hbm] * 10,
        out_specs=(hbm,) + (vmem,) * 6,
        scratch_shapes=[
            pltpu.VMEM(part_o.shape[1:], low), pltpu.VMEM(part_o.shape[1:], low), pltpu.VMEM((2,) + part_o.shape[1:], low),
            pltpu.VMEM(part_o.shape[1:], low),
            pltpu.VMEM(ret_b.shape, low), pltpu.VMEM(ret_b.shape, low), pltpu.VMEM((rows, width), full),
            pltpu.VMEM((rows, width), low), pltpu.VMEM((rows, width), low),
            pltpu.VMEM((width, width), low), pltpu.VMEM(qkv.shape, low), pltpu.VMEM(cols.shape, low),
            pltpu.VMEM(all_tokens.shape, low), pltpu.VMEM(att.shape, low), pltpu.VMEM(probs.shape, low),
            pltpu.VMEM((4 * rows, shard), low), pltpu.VMEM((rows, width), low),
            pltpu.VMEM((rows, width), low), pltpu.VMEM((rows, width), full),
            pltpu.VMEM((rows, ret_b.shape[0]), low),
            pltpu.VMEM((2, 4, half, width), low), pltpu.VMEM((4, half, width), low),
            pltpu.VMEM((4, half, width), low), pltpu.VMEM((3, half, width), low),
            pltpu.VMEM((half, width), low), pltpu.VMEM((3, slim, width), low),
            pltpu.VMEM((4, rows, 128), jnp.int32), pltpu.VMEM((2, 8, 8, 128), full),
            pltpu.VMEM((4 * rows, 128), full), pltpu.VMEM((4 * rows, 128), full),
            pltpu.VMEM((2, 4 * rows, 3 * shard // 2), low), pltpu.VMEM((4 * rows, width), low),
            pltpu.VMEM((2, 6, 4, half, half), low), pltpu.VMEM((6, 4, half, half), low),
            pltpu.VMEM((6, 4, half, half), low), pltpu.VMEM((3, 6, half, half), low),
            pltpu.VMEM((6, half, half), full), pltpu.VMEM((4, 6, slim, half), full),
            pltpu.VMEM((4, 2, rows, width // 2), low), pltpu.VMEM((2, 2, rows, width // 2), low),
            pltpu.VMEM((2, rows, width // 2), low), pltpu.VMEM((rows, width), full),
            pltpu.VMEM((3, 16, width), full), pltpu.VMEM((7, 16, width), full),
            pltpu.VMEM((3, 8, 128), full), pltpu.VMEM((7, 8, 128), full),
            pltpu.SMEM((16,), jnp.int32), pltpu.SMEM((16,), jnp.int32),
            dma((12,)), dma((3,)), dma((3,)), dma((7,)), dma((7,)), dma((2,)), dma((2,)),
            dma((2, 3)), dma((2, 3)), dma((2, 3)), dma((2, 3)), dma((2, 3)), dma((2, 3)), dma((7,)), dma((7,)),
            dma((2, 3, 2)), dma((2, 3, 2)), dma((8,)), dma((8,)), dma((7,)), dma((7,)), dma, dma((4,)),
        ],
        compiler_params=pltpu.CompilerParams(
            collective_id=5, has_side_effects=True, vmem_limit_bytes=VMEM_LIMIT
        ),
        cost_estimate=pl.CostEstimate(flops=120 * rows * width * shard, bytes_accessed=20 << 20, transcendentals=8 * rows * rows * 16),
        name="back",
    )(lengths, parents, ids_row, params, ret_s, part_o, ret_b, residual, cotangent, wo, qkv, cols, all_tokens, att, probs)


def emit_kernel(*refs):
    large, small = refs[:9], refs[9]
    out, (gain_one, gain_two, bias, router, roots) = refs[10:19], refs[19:24]
    held, wide, in_sem, out_sem = refs[24:33], refs[33:36], refs[36], refs[37]
    comes, goes = [], []
    for k, (src, mid, dst) in enumerate(zip(large, held, out)):
        pieces = 4 if k >= 6 else 1
        amount = src.shape[0] // pieces
        for i in range(pieces):
            part = pl.ds(i * amount, amount)
            comes.append(pltpu.make_async_copy(src.at[part], mid.at[part], in_sem.at[len(comes)]))
            last = wide[k - 6] if k >= 6 else mid
            goes.append(pltpu.make_async_copy(last.at[part], dst.at[part], out_sem.at[len(goes)]))
    order = list(range(6, 18)) + list(range(6))
    for k in order:
        comes[k].start()
    place = lax.axis_index(EXPERT) * 4 + lax.axis_index(SEQ)
    width = small.shape[1]

    def own(length):
        lane = lax.broadcasted_iota(jnp.int32, (length, width), 1)
        down = lax.broadcasted_iota(jnp.int32, (length, width), 0)
        return jnp.where(lane == place * length + down, 1.0, 0.0)

    def picked(left, right):
        return lax.dot_general(left, right, (((1,), (1,)), ((), ())),
                               precision=lax.Precision.HIGHEST, preferred_element_type=jnp.float32)

    for k in order:
        comes[k].wait()
        if k >= 6:
            which, i = (k - 6) // 4, (k - 6) % 4
            amount = held[6].shape[0] // 4
            part = slice(i * amount, (i + 1) * amount)
            wide[which][part] = held[6 + which][part].astype(jnp.float32)
        goes[k].start()
    slim = gain_one.shape[1]
    ours = own(slim)
    gains = picked(small[0:8], ours)
    gain_one[...] = gains[0:1]
    gain_two[...] = gains[1:2]
    bias[...] = picked(small[0:8], own(bias.shape[1]))[2:3]
    router[...] = picked(small[8:16], ours)
    roots[...] = jnp.sqrt(small[3:4, 0:2] / (32 * large[0].shape[0] * width))
    for copy in goes:
        copy.wait()


def emit(large, small):
    full = jnp.float32
    width = small.shape[1]
    vmem, hbm = pl.BlockSpec(memory_space=pltpu.VMEM), pl.BlockSpec(memory_space=pl.ANY)
    slim = width // 32
    shapes = ((1, slim), (1, slim), (1, BUCKETS * HEADS // 32), (8, slim), (1, 2))
    return pl.pallas_call(
        emit_kernel,
        out_shape=tuple(jax.ShapeDtypeStruct(x.shape, x.dtype) for x in large[:6])
        + tuple(jax.ShapeDtypeStruct(x.shape, full) for x in large[6:])
        + tuple(jax.ShapeDtypeStruct(shape, full) for shape in shapes),
        in_specs=[hbm] * 9 + [vmem],
        out_specs=(hbm,) * 9 + (vmem,) * 5,
        scratch_shapes=[pltpu.VMEM(x.shape, x.dtype) for x in large]
        + [pltpu.VMEM(x.shape, full) for x in large[6:]]
        + [pltpu.SemaphoreType.DMA((18,)), pltpu.SemaphoreType.DMA((18,))],
        compiler_params=pltpu.CompilerParams(vmem_limit_bytes=VMEM_LIMIT),
        name="emit",
    )(*large, small)


def per_device_kernels(
    tokens, cotangent, expert_ids, segment_lengths, segment_parents, attention_gain,
    query_weight, key_weight, value_weight, output_weight, bias_table, feedforward_gain,
    router_weight, gate_weight, up_weight, down_weight,
):
    ids_row = expert_ids.T
    send_rows, grad_rows, shares, residual, all_tokens, qkv, cols, params, att, probs, wo, g_early = front(
        segment_lengths, segment_parents, tokens, cotangent, ids_row, query_weight, key_weight, value_weight,
        output_weight, attention_gain[None], feedforward_gain[None], bias_table[None], router_weight.T,
    )
    part_out, grad_back, dots, gate_term, up_term, down_term = experts(
        send_rows, grad_rows, shares, g_early, gate_weight[0], up_weight[0], down_weight[0]
    )
    layer_out, tokens_grad, dwq, dwk, dwv, dwo, totals = back(
        segment_lengths, segment_parents, ids_row, params, dots, part_out, grad_back, residual, cotangent,
        wo.reshape(D, D), qkv, cols, all_tokens, att, probs,
    )
    large = (layer_out, tokens_grad, dwq, dwk, dwv, dwo, gate_term, up_term, down_term)
    *large, gain_one, gain_two, bias, router, roots = emit(large, totals)
    layer_out, tokens_grad, dwq, dwk, dwv, dwo, gate_term, up_term, down_term = large
    return (
        layer_out, tokens_grad, gain_one[0], dwq, dwk, dwv, dwo, bias[0], gain_two[0], router.T,
        gate_term[None], up_term[None], down_term[None], roots[0],
    )


def per_device_general(
    tokens,
    cotangent,
    expert_ids,
    segment_lengths,
    segment_parents,
    attention_gain,
    query_weight,
    key_weight,
    value_weight,
    output_weight,
    bias_table,
    feedforward_gain,
    router_weight,
    gate_weight,
    up_weight,
    down_weight,
):
    seq_count = lax.axis_size(SEQ)
    seq_place = lax.axis_index(SEQ)
    all_count = lax.axis_size(EXPERT) * seq_count
    row_count = tokens.shape[0]
    experts = lax.axis_size(EXPERT) * gate_weight.shape[0]
    capacity = 10 * row_count // (4 * experts)
    score_scale = HDIM ** (-0.5)
    gathered = (
        lax.all_gather(attention_gain, BOTH, axis=0, tiled=True),
        lax.all_gather(query_weight, BOTH, axis=0, tiled=True),
        lax.all_gather(key_weight, BOTH, axis=0, tiled=True),
        lax.all_gather(value_weight, BOTH, axis=0, tiled=True),
        lax.all_gather(output_weight, BOTH, axis=0, tiled=True),
        lax.all_gather(bias_table, BOTH, axis=0, tiled=True),
        lax.all_gather(feedforward_gain, BOTH, axis=0, tiled=True),
        lax.all_gather(router_weight, BOTH, axis=0, tiled=True),
    )
    gain_one, query_full, key_full, value_full, output_full, bias_flat, gain_two, router_full = (
        gathered
    )
    bias_grid = bias_flat.reshape(BUCKETS, HEADS)
    starts, before, reaches = tree_tables(segment_lengths[0], segment_parents[0])
    own_rows = seq_place * row_count + jnp.arange(row_count, dtype=jnp.int32)
    own_meta = token_info(own_rows, starts, before, reaches)
    tokens_float = tokens.astype(jnp.float32)
    scale_one = norm_factor(tokens_float)
    unit_one = tokens_float * scale_one
    normed_one = (unit_one * gain_one.astype(jnp.float32)).astype(jnp.bfloat16)
    queries = (
        jnp.dot(normed_one, query_full, preferred_element_type=jnp.float32)
        .astype(jnp.bfloat16)
        .reshape(row_count, HEADS, HDIM)
    )
    keys_own = (
        jnp.dot(normed_one, key_full, preferred_element_type=jnp.float32)
        .astype(jnp.bfloat16)
        .reshape(row_count, HEADS, HDIM)
    )
    values_own = (
        jnp.dot(normed_one, value_full, preferred_element_type=jnp.float32)
        .astype(jnp.bfloat16)
        .reshape(row_count, HEADS, HDIM)
    )
    row_peak = jnp.full((HEADS, row_count), NEGATIVE, jnp.float32)
    key_piece = lax.all_gather(keys_own, SEQ, axis=0, tiled=True)
    value_piece = lax.all_gather(values_own, SEQ, axis=0, tiled=True)
    key_rows = jnp.arange(key_piece.shape[0], dtype=jnp.int32)
    visible, onehot, pair_bias = pair_terms(
        own_meta, token_info(key_rows, starts, before, reaches), own_rows, key_rows, bias_grid
    )
    scores = masked_scores(queries, key_piece, visible, pair_bias)
    new_peak = jnp.maximum(row_peak, jnp.max(scores, axis=-1))
    expo = jnp.exp(scores - new_peak[:, :, None])
    row_total = jnp.sum(expo, axis=-1)
    summed = jnp.einsum(
        SPEC_2, expo.astype(jnp.bfloat16), value_piece, preferred_element_type=jnp.float32
    )
    row_peak, row_total, summed = (new_peak, row_total, summed)
    log_total = row_peak + jnp.log(row_total)
    attended_float = summed / jnp.transpose(row_total)[:, :, None]
    attended = attended_float.astype(jnp.bfloat16).reshape(row_count, D)
    residual = tokens_float + jnp.dot(attended, output_full, preferred_element_type=jnp.float32)
    scale_two = norm_factor(residual)
    unit_two = residual * scale_two
    normed_two = (unit_two * gain_two.astype(jnp.float32)).astype(jnp.bfloat16)
    router_prob = jax.nn.softmax(
        jnp.dot(normed_two, router_full, preferred_element_type=jnp.float32), axis=-1
    )
    pick_hot = (
        expert_ids[:, :, None] == jnp.arange(experts, dtype=jnp.int32)[None, None, :]
    ).astype(jnp.float32)
    chosen = jnp.sum(pick_hot * router_prob[:, None, :], axis=2)
    chosen_total = jnp.sum(chosen, axis=1, keepdims=True)
    gate_shares = chosen / chosen_total
    hot_int = pick_hot.astype(jnp.int32).reshape(row_count * 2, experts)
    earlier = jnp.cumsum(hot_int, axis=0) - hot_int
    slot_number = jnp.sum(earlier * hot_int, axis=1).reshape(row_count, 2)
    kept_copy = slot_number < capacity
    kept_float = kept_copy.astype(jnp.float32)
    target = jnp.where(kept_copy, expert_ids * capacity + slot_number, experts * capacity)
    copy_ids = jnp.arange(row_count * 2, dtype=jnp.int32)
    slot_copy = (
        jnp.full((experts * capacity + 1,), row_count * 2, jnp.int32)
        .at[target.reshape(-1)]
        .set(copy_ids)[: experts * capacity]
    )
    fetch_index = jnp.minimum(target, experts * capacity - 1).reshape(-1)
    token_of_slot = jnp.where(slot_copy < row_count * 2, slot_copy // 2, row_count)
    padded = jnp.concatenate([normed_two, jnp.zeros((1, D), jnp.bfloat16)], axis=0)
    send_rows = padded[token_of_slot].reshape(experts, capacity, D)
    expert_in = lax.all_to_all(send_rows, EXPERT, split_axis=0, concat_axis=1, tiled=True)[0]
    gate_piece = lax.all_gather(gate_weight, SEQ, axis=1, tiled=True)
    up_piece = lax.all_gather(up_weight, SEQ, axis=1, tiled=True)
    down_piece = lax.all_gather(down_weight, SEQ, axis=1, tiled=True)
    gate_pre = jnp.einsum(SPEC_3, expert_in, gate_piece[0], preferred_element_type=jnp.float32)
    up_pre = jnp.einsum(SPEC_3, expert_in, up_piece[0], preferred_element_type=jnp.float32)
    active = (gelu_tanh(gate_pre) * up_pre).astype(jnp.bfloat16)
    expert_sum = jnp.dot(active, down_piece[0], preferred_element_type=jnp.float32)
    returned = lax.all_to_all(
        expert_sum.astype(jnp.bfloat16)[None], EXPERT, split_axis=1, concat_axis=0, tiled=True
    )
    picked = (
        returned.reshape(experts * capacity, D)[fetch_index]
        .reshape(row_count, 2, D)
        .astype(jnp.float32)
    )
    weighted = gate_shares * kept_float
    mixture = jnp.sum(weighted[:, :, None] * picked, axis=1)
    layer_out = (residual + mixture).astype(jnp.bfloat16)
    local_sums = jnp.stack([jnp.sum(residual * residual), jnp.sum(mixture * mixture)])
    again = (
        lax.all_gather(attention_gain, BOTH, axis=0, tiled=True),
        lax.all_gather(query_weight, BOTH, axis=0, tiled=True),
        lax.all_gather(key_weight, BOTH, axis=0, tiled=True),
        lax.all_gather(value_weight, BOTH, axis=0, tiled=True),
        lax.all_gather(output_weight, BOTH, axis=0, tiled=True),
        lax.all_gather(bias_table, BOTH, axis=0, tiled=True),
        lax.all_gather(feedforward_gain, BOTH, axis=0, tiled=True),
        lax.all_gather(router_weight, BOTH, axis=0, tiled=True),
    )
    gain_one, query_full, key_full, value_full, output_full, bias_flat, gain_two, router_full = (
        again
    )
    bias_grid = bias_flat.reshape(BUCKETS, HEADS)
    grad_out = cotangent.astype(jnp.float32)
    copy_grad = (
        (weighted[:, :, None] * grad_out[:, None, :]).astype(jnp.bfloat16).reshape(row_count * 2, D)
    )
    copy_padded = jnp.concatenate([copy_grad, jnp.zeros((1, D), jnp.bfloat16)], axis=0)
    grad_send = copy_padded[slot_copy].reshape(experts, capacity, D)
    grad_in = lax.all_to_all(grad_send, EXPERT, split_axis=0, concat_axis=1, tiled=True)[0]
    gate_piece = lax.all_gather(gate_weight, SEQ, axis=1, tiled=True)
    up_piece = lax.all_gather(up_weight, SEQ, axis=1, tiled=True)
    down_piece = lax.all_gather(down_weight, SEQ, axis=1, tiled=True)
    gate_pre = jnp.einsum(SPEC_3, expert_in, gate_piece[0], preferred_element_type=jnp.float32)
    up_pre = jnp.einsum(SPEC_3, expert_in, up_piece[0], preferred_element_type=jnp.float32)
    gelu_out, gelu_pull = jax.vjp(gelu_tanh, gate_pre)
    act_grad = jnp.einsum(SPEC_3, grad_in, down_piece[0], preferred_element_type=jnp.float32)
    gate_back = gelu_pull(act_grad * up_pre)[0].astype(jnp.bfloat16)
    up_back = (act_grad * gelu_out).astype(jnp.bfloat16)
    input_grad = jnp.dot(gate_back, gate_piece[0], preferred_element_type=jnp.float32) + jnp.dot(
        up_back, up_piece[0], preferred_element_type=jnp.float32
    )
    active = (gelu_out * up_pre).astype(jnp.bfloat16)
    input_grad, gate_backs, up_backs, actives = (input_grad, gate_back, up_back, active)
    grad_back = lax.all_to_all(
        input_grad.astype(jnp.bfloat16)[None], EXPERT, split_axis=1, concat_axis=0, tiled=True
    )
    expert_back = (
        grad_back.reshape(experts * capacity, D)[fetch_index]
        .reshape(row_count, 2, D)
        .astype(jnp.float32)
    )
    normed_two_grad = jnp.sum(expert_back * kept_float[:, :, None], axis=1)
    expert_grads = lax.psum_scatter(
        jnp.stack(
            [
                jnp.einsum(SPEC_4, gate_backs, expert_in, preferred_element_type=jnp.float32),
                jnp.einsum(SPEC_4, up_backs, expert_in, preferred_element_type=jnp.float32),
                jnp.einsum(SPEC_4, actives, grad_in, preferred_element_type=jnp.float32),
            ],
            axis=1,
        ).astype(jnp.bfloat16),
        SEQ,
        scatter_dimension=0,
        tiled=True,
    ).astype(jnp.float32)
    share_grad = jnp.sum(grad_out[:, None, :] * picked, axis=2) * kept_float
    chosen_grad = (
        share_grad - jnp.sum(gate_shares * share_grad, axis=1, keepdims=True)
    ) / chosen_total
    prob_grad = jnp.sum(pick_hot * chosen_grad[:, :, None], axis=1)
    logit_grad = router_prob * (prob_grad - jnp.sum(router_prob * prob_grad, axis=1, keepdims=True))
    router_float = router_full.astype(jnp.float32)
    router_term = jnp.einsum(
        SPEC_5, normed_two.astype(jnp.float32), logit_grad, precision=lax.Precision.HIGHEST
    )
    normed_two_grad = normed_two_grad + jnp.einsum(
        SPEC_6, logit_grad, router_float, precision=lax.Precision.HIGHEST
    )
    gain_two_term = jnp.sum(normed_two_grad * unit_two, axis=0)
    unit_grad_two = normed_two_grad * gain_two.astype(jnp.float32)
    residual_grad = grad_out + scale_two * (
        unit_grad_two - unit_two * jnp.mean(unit_grad_two * unit_two, axis=-1, keepdims=True)
    )
    attention_out_grad = residual_grad.astype(jnp.bfloat16)
    output_term = jnp.einsum(
        SPEC_5, attended, attention_out_grad, preferred_element_type=jnp.float32
    )
    attended_grad = (
        jnp.einsum(SPEC_6, attention_out_grad, output_full, preferred_element_type=jnp.float32)
        .astype(jnp.bfloat16)
        .reshape(row_count, HEADS, HDIM)
    )
    row_delta = jnp.transpose(jnp.sum(attended_grad.astype(jnp.float32) * attended_float, axis=-1))
    total_all, delta_all = (
        lax.all_gather(log_total, SEQ, axis=1, tiled=True),
        lax.all_gather(row_delta, SEQ, axis=1, tiled=True),
    )
    key_piece = lax.all_gather(keys_own, SEQ, axis=0, tiled=True)
    value_piece = lax.all_gather(values_own, SEQ, axis=0, tiled=True)
    key_rows = jnp.arange(key_piece.shape[0], dtype=jnp.int32)
    visible, onehot, pair_bias = pair_terms(
        own_meta, token_info(key_rows, starts, before, reaches), own_rows, key_rows, bias_grid
    )
    scores = masked_scores(queries, key_piece, visible, pair_bias)
    soft_weights = jnp.exp(scores - log_total[:, :, None])
    dprob = jnp.einsum(
        SPEC_1, attended_grad, value_piece, preferred_element_type=jnp.float32
    )
    score_grad = (soft_weights * (dprob - row_delta[:, :, None])).astype(jnp.bfloat16)
    query_acc = jnp.einsum(
        SPEC_2, score_grad, key_piece, preferred_element_type=jnp.float32
    )
    bias_acc = jnp.einsum(SPEC_7, onehot, score_grad, preferred_element_type=jnp.float32)
    query_acc, bias_acc = (query_acc, bias_acc)
    query_piece = lax.all_gather(queries, SEQ, axis=0, tiled=True)
    grad_piece = lax.all_gather(attended_grad, SEQ, axis=0, tiled=True)
    piece_rows = query_piece.shape[0]
    query_rows = jnp.arange(piece_rows, dtype=jnp.int32)
    visible, onehot, pair_bias = pair_terms(
        token_info(query_rows, starts, before, reaches), own_meta, query_rows, own_rows, bias_grid
    )
    scores = masked_scores(query_piece, keys_own, visible, pair_bias)
    soft_weights = jnp.exp(scores - total_all[:, :, None])
    value_acc = jnp.einsum(
        SPEC_8,
        soft_weights.astype(jnp.bfloat16),
        grad_piece,
        preferred_element_type=jnp.float32,
    )
    dprob = jnp.einsum(SPEC_1, grad_piece, values_own, preferred_element_type=jnp.float32)
    score_grad = (soft_weights * (dprob - delta_all[:, :, None])).astype(jnp.bfloat16)
    key_acc = jnp.einsum(
        SPEC_8, score_grad, query_piece, preferred_element_type=jnp.float32
    )
    key_acc, value_acc = (key_acc, value_acc)
    query_back = (query_acc * score_scale).astype(jnp.bfloat16).reshape(row_count, D)
    key_back = (key_acc * score_scale).astype(jnp.bfloat16).reshape(row_count, D)
    value_back = value_acc.astype(jnp.bfloat16).reshape(row_count, D)
    query_term = jnp.einsum(SPEC_5, normed_one, query_back, preferred_element_type=jnp.float32)
    key_term = jnp.einsum(SPEC_5, normed_one, key_back, preferred_element_type=jnp.float32)
    value_term = jnp.einsum(SPEC_5, normed_one, value_back, preferred_element_type=jnp.float32)
    normed_one_grad = jnp.einsum(
        SPEC_6, query_back, query_full, preferred_element_type=jnp.float32
    )
    normed_one_grad = normed_one_grad + jnp.einsum(
        SPEC_6, key_back, key_full, preferred_element_type=jnp.float32
    )
    normed_one_grad = normed_one_grad + jnp.einsum(
        SPEC_6, value_back, value_full, preferred_element_type=jnp.float32
    )
    gain_one_term = jnp.sum(normed_one_grad * unit_one, axis=0)
    unit_grad_one = normed_one_grad * gain_one.astype(jnp.float32)
    tokens_grad = residual_grad + scale_one * (
        unit_grad_one - unit_one * jnp.mean(unit_grad_one * unit_one, axis=-1, keepdims=True)
    )
    stats_term = jnp.broadcast_to(local_sums[None, :], (all_count, 2))
    reduced = (
        lax.psum_scatter(gain_one_term, BOTH, scatter_dimension=0, tiled=True),
        lax.psum_scatter(query_term, BOTH, scatter_dimension=0, tiled=True),
        lax.psum_scatter(key_term, BOTH, scatter_dimension=0, tiled=True),
        lax.psum_scatter(value_term, BOTH, scatter_dimension=0, tiled=True),
        lax.psum_scatter(output_term, BOTH, scatter_dimension=0, tiled=True),
        lax.psum_scatter(
            bias_acc.reshape(BUCKETS * HEADS), BOTH, scatter_dimension=0, tiled=True
        ),
        lax.psum_scatter(gain_two_term, BOTH, scatter_dimension=0, tiled=True),
        lax.psum_scatter(router_term, BOTH, scatter_dimension=0, tiled=True),
        lax.psum_scatter(stats_term, BOTH, scatter_dimension=0, tiled=True),
    )
    roots = jnp.sqrt(reduced[8][0] / (row_count * all_count * D))
    return (
        layer_out,
        tokens_grad,
        reduced[0],
        reduced[1],
        reduced[2],
        reduced[3],
        reduced[4],
        reduced[5],
        reduced[6],
        reduced[7],
        expert_grads[None, :, 0, :],
        expert_grads[None, :, 1, :],
        expert_grads[None, :, 2, :],
        roots,
    )


def solution(mesh):
    kernels_fit = mesh.shape[EXPERT] == len(ORDER) and mesh.shape[SEQ] == 4
    return jax.shard_map(
        per_device_kernels if kernels_fit else per_device_general,
        mesh=mesh,
        in_specs=(
            P(BOTH, None),
            P(BOTH, None),
            P(BOTH, None),
            P(EXPERT, None),
            P(EXPERT, None),
            P(BOTH),
            P(BOTH, None),
            P(BOTH, None),
            P(BOTH, None),
            P(BOTH, None),
            P(BOTH),
            P(BOTH),
            P(BOTH, None),
            P(EXPERT, SEQ, None),
            P(EXPERT, SEQ, None),
            P(EXPERT, SEQ, None),
        ),
        out_specs=(
            P(BOTH, None),
            P(BOTH, None),
            P(BOTH),
            P(BOTH, None),
            P(BOTH, None),
            P(BOTH, None),
            P(BOTH, None),
            P(BOTH),
            P(BOTH),
            P(BOTH, None),
            P(EXPERT, SEQ, None),
            P(EXPERT, SEQ, None),
            P(EXPERT, SEQ, None),
            P(),
        ),
        check_vma=False,
    )
```
